32 devices in a mesh: section: 2 (over core), dp: 16 (over z, y, x).
Axes of the slice: x: 2, y: 2, z: 4, core: 2. Of those that a mesh axis runs over, the one named last changes fastest.
Arguments:
- patches: bfloat16 [192, 196, 768], P('dp'), may hold values from -6 to 6
- keep: int32 [192], P('dp'), may hold values from 40 to 98, as said below
- perm: int32 [192, 196], P('dp'), may hold values from 0 to 195, as said below
- master: float32 [2, 7673856], P('section', 'dp')
- first: float32 [2, 7673856], P('section', 'dp'), may hold values from -4.7683716e-06 to 4.7683716e-06
- second: float32 [2, 7673856], P('section', 'dp'), may hold values from 8.614131e-15 to 3.4456524e-14
- ema: float32 [2, 7673856], P('section', 'dp')
Outputs:
- new_master: float32 [2, 7673856], P('section', 'dp')
- new_first: float32 [2, 7673856], P('section', 'dp')
- new_second: float32 [2, 7673856], P('section', 'dp')
- new_ema: float32 [2, 7673856], P('section', 'dp')
- grad_norm: float32 [], replicated
- loss_sum: float32 [], replicated
- loss_count: float32 [], replicated
The draws below stay inside these ranges and needn't reach their ends.
Inputs may be any that keep to these rules, and one draw needn't show every extreme that they name: `keep`: some image keeps exactly 98 patches. `perm`: each row is a permutation of 0 to 195; its first keep entries are the visible patches.
All inputs are finite; a program needn't handle non-finite values.
Results may differ from the reference program's by a relative error of at most 0.00035.
The reference program's roundings to bfloat16 on the way count: a program that leaves them out, or rounds other values in their place, can miss the bound.
Values may be sent and summed in bfloat16 or wider, within the bound.
No kernel may reach another device: no remote copies, remote signals or barrier semaphores. Data moves between devices by JAX's collectives and lax.ppermute only.
A program may use at most 704 MiB of HBM per device.

```python
import math
import jax
import jax.numpy as jnp
from jax import lax

D = 768
HEADS_E = 12
FF_E = 3072
DD = 512
HEADS_D = 16
FF_D = 2048
PIX = 768
NP = 196
SLOTS = 98
IMG = 4
STEP = 10
IMAGES = 192
P_ENC = 7673088
P_DEC = 3935744
FLAT = 7673856


def section_specs():
    encoder = [((PIX, D), PIX ** (-0.5), False), ((D,), 0.3, False), ((D,), 0.0, True), ((D,), 0.2, False), ((D, 3 * D), D ** (-0.5), False), ((D, D), 4.0 * D ** (-0.5), False), ((D,), 0.0, True), ((D,), 0.2, False), ((D, FF_E), D ** (-0.5), False), ((FF_E, D), FF_E ** (-0.5), False), ((D,), 0.0, True), ((D,), 0.2, False)]
    decoder = [((D, DD), D ** (-0.5), False), ((DD,), 1.0, False), ((DD,), 0.0, True), ((DD,), 0.2, False), ((DD, 3 * DD), DD ** (-0.5), False), ((DD, DD), 4.0 * DD ** (-0.5), False), ((DD,), 0.0, True), ((DD,), 0.2, False), ((DD, FF_D), DD ** (-0.5), False), ((FF_D, DD), FF_D ** (-0.5), False), ((DD,), 0.0, True), ((DD,), 0.2, False), ((DD, PIX), DD ** (-0.5), False)]
    return [encoder, decoder]


def section_scales(specs):
    offsets = []
    scales = []
    used = 0
    for shape, scale, ramp in specs:
        amount = math.prod(shape)
        used += amount
        if ramp:
            rising = 0.6 + 1.2 * jnp.arange(amount).astype(jnp.float32) / amount
            offsets.append(rising)
            scales.append(0.1 * rising)
        else:
            offsets.append(jnp.zeros((amount,), jnp.float32))
            scales.append(jnp.full((amount,), scale, jnp.float32))
    offsets.append(jnp.zeros((FLAT - used,), jnp.float32))
    scales.append(jnp.full((FLAT - used,), 0.02, jnp.float32))
    return (jnp.concatenate(offsets), jnp.concatenate(scales))


def layered_values(noise):
    rows = []
    for index, specs in enumerate(section_specs()):
        offset, scale = section_scales(specs)
        rows.append(offset + scale * noise[index])
    return jnp.stack(rows)


def draw_master(key, part):
    key = jax.random.fold_in(key, 1)
    noise = jax.random.normal(key, (2, FLAT), jnp.float32)
    return layered_values(noise)


def draw_ema(key, part):
    key = jax.random.fold_in(key, 2)
    noise = jax.random.normal(key, (2, FLAT), jnp.float32)
    return layered_values(noise)


def draw_keep(key, part):
    key = jax.random.fold_in(key, 3)
    first_key, second_key = jax.random.split(key)
    counts = jax.random.randint(first_key, (IMAGES,), (NP + 4) // 5, SLOTS + 1)
    fullest = jax.random.randint(second_key, (), 0, IMAGES)
    return counts.at[fullest].set(SLOTS).astype(jnp.int32)


def draw_perm(key, part):
    key = jax.random.fold_in(key, 4)
    keys = jax.random.split(key, IMAGES)
    return jax.vmap(lambda single: jax.random.permutation(single, NP))(keys).astype(jnp.int32)


def level_of(key, extent, cuts, low, high):
    def one(axis_at, blocks):
        draws = jax.random.uniform(jax.random.fold_in(jax.random.fold_in(key, 6), axis_at), (blocks,), jnp.float32, low / len(cuts), high / len(cuts))
        return jnp.repeat(jnp.exp(draws), extent[axis_at] // blocks).reshape((-1,) + (1,) * (len(extent) - axis_at - 1))

    level = one(*cuts[0])
    for cut in cuts[1:]:
        level = level * one(*cut)
    return level


def normal_values(rng, shape, scale, bound, cuts=(), kind=jnp.bfloat16):
    values = jax.random.normal(rng, shape, jnp.float32) * scale
    if len(cuts) > 0:
        values = level_of(rng, shape, cuts, -0.22, 0.18) * values
    return jnp.clip(values, min=-bound, max=bound).astype(kind)


def setup_inputs(seed: int = 0) -> dict:
    arg_keys = jax.random.split(jax.random.key(seed), 8)
    patches = normal_values(arg_keys[0], (IMAGES, NP, PIX), 1.0, 6.0, ((0, 16),))
    keep = draw_keep(jax.random.fold_in(arg_keys[7], 71), 0)
    perm = draw_perm(jax.random.fold_in(arg_keys[7], 71), 0)
    master = draw_master(jax.random.fold_in(arg_keys[7], 71), 0)
    first = normal_values(arg_keys[4], (2, FLAT), (0.0011 * (P_ENC + P_DEC) ** -0.5), 4.76837158203125e-06, ((0, 2), (1, 16)), jnp.float32)
    second = jnp.clip(jnp.exp(math.log(3.445652441212525e-14) - 1.3862944 * jax.random.uniform(arg_keys[5], (2, FLAT), jnp.float32) ** level_of(arg_keys[5], (2, FLAT), ((0, 2), (1, 16)), -0.2, 0.2)), 8.614131103031313e-15, 3.445652441212525e-14)
    ema = draw_ema(jax.random.fold_in(arg_keys[7], 71), 0)
    return dict(patches=patches, keep=keep, perm=perm, master=master, first=first, second=second, ema=ema)


norm_epsilon = 1e-06
clip_limit = 0.01
learn_rate = 0.02
beta_one = 0.9
beta_two = 0.999
adam_epsilon = 1e-08
weight_decay = 0.05
average_keep = 0.8
HIGH = lax.Precision.HIGHEST

@jax.custom_vjp
def low(v):
    return lax.optimization_barrier(v.astype(jnp.bfloat16)).astype(jnp.float32)

@jax.custom_vjp
def low_back(v):
    return v

def low_keep(v):
    return (low(v), None)

def low_pass(kept, grad):
    return (grad,)

def back_keep(v):
    return (v, None)

def back_low(kept, grad):
    return (low(grad),)
low.defvjp(low_keep, low_pass)
low_back.defvjp(back_keep, back_low)

def encoder_layout():
    return [(PIX, D), (D,), (D,), (D,), (D, 3 * D), (D, D), (D,), (D,), (D, FF_E), (FF_E, D), (D,), (D,)]

def decoder_layout():
    return [(D, DD), (DD,), (DD,), (DD,), (DD, 3 * DD), (DD, DD), (DD,), (DD,), (DD, FF_D), (FF_D, DD), (DD,), (DD,), (DD, PIX)]

def unpack(flat, layout):
    pieces = []
    offset = 0
    for shape in layout:
        amount = math.prod(shape)
        pieces.append(flat[offset:offset + amount].reshape(shape))
        offset += amount
    return pieces

def sincos(width):
    places = jnp.arange(NP).astype(jnp.float32)[:, None]
    column = jnp.arange(width)
    rates = jnp.exp(-(2.0 * (column // 2).astype(jnp.float32) / width) * math.log(10000.0))
    phases = places * rates[None, :]
    return jnp.where(column[None, :] % 2 == 0, jnp.sin(phases), jnp.cos(phases))

def normalize(values, gain, shift):
    centre = values - lax.optimization_barrier(jnp.mean(values, axis=-1, keepdims=True))
    spread = lax.optimization_barrier(jnp.mean(centre * centre, axis=-1, keepdims=True))
    return centre * lax.rsqrt(spread + norm_epsilon) * gain + shift

def block(stream, weights, heads, valid):
    gain_one, bias_one, qkv_w, proj_w, gain_two, bias_two, fc_one, fc_two = weights
    batch, length, width = stream.shape
    size = width // heads
    normed = low(normalize(stream, gain_one, bias_one))
    mixed = low_back(jnp.einsum('blw,wk->blk', normed, qkv_w, precision=HIGH))
    query = low(mixed[..., :width] * (1.0 / math.sqrt(size))).reshape(batch, length, heads, size)
    keys = low(mixed[..., width:2 * width]).reshape(batch, length, heads, size)
    values = low(mixed[..., 2 * width:]).reshape(batch, length, heads, size)
    scores = low_back(jnp.einsum('bqhd,bkhd->bhqk', query, keys, precision=HIGH))
    scores = jnp.where(valid[:, None, None, :], scores, -1e+30)
    probs = low(jax.nn.softmax(scores, axis=-1))
    attended = low(low_back(jnp.einsum('bhqk,bkhd->bqhd', probs, values, precision=HIGH)))
    attended = attended.reshape(batch, length, width)
    stream = stream + low_back(jnp.einsum('blw,wk->blk', attended, proj_w, precision=HIGH))
    normed = low(normalize(stream, gain_two, bias_two))
    hidden = low_back(jnp.einsum('blw,wk->blk', normed, fc_one, precision=HIGH))
    hidden = low(jax.nn.gelu(hidden, approximate=False))
    return stream + low_back(jnp.einsum('blk,kw->blw', hidden, fc_two, precision=HIGH))

def encode(flat, pixels, kept_count, order):
    pieces = unpack(flat, encoder_layout())
    chosen = order[:, :SLOTS]
    visible = jnp.take_along_axis(pixels, chosen[:, :, None], axis=1)
    embedded = low_back(jnp.einsum('bsp,pw->bsw', visible, pieces[0], precision=HIGH))
    embedded = embedded + pieces[1] + sincos(D)[chosen]
    valid = jnp.arange(SLOTS)[None, :] < kept_count[:, None]
    stream = block(embedded, pieces[2:10], HEADS_E, valid)
    return normalize(stream, pieces[10], pieces[11])

def decode(flat, latent, pixels, kept_count, order):
    pieces = unpack(flat, decoder_layout())
    embedded = low_back(jnp.einsum('bsw,wk->bsk', latent, pieces[0], precision=HIGH))
    ranks = jnp.argsort(order, axis=1).astype(jnp.int32)
    kept = ranks < kept_count[:, None]
    placed = jnp.take_along_axis(embedded, jnp.minimum(ranks, SLOTS - 1)[:, :, None], axis=1)
    tokens = jnp.where(kept[:, :, None], placed, pieces[1]) + sincos(DD)
    stream = block(tokens, pieces[2:10], HEADS_D, jnp.ones(kept.shape, dtype=bool))
    normed = low(normalize(stream, pieces[10], pieces[11]))
    predicted = low_back(jnp.einsum('bpk,kx->bpx', normed, pieces[12], precision=HIGH))
    centre = pixels - lax.optimization_barrier(jnp.mean(pixels, axis=-1, keepdims=True))
    target = centre * lax.rsqrt(lax.optimization_barrier(jnp.mean(centre * centre, axis=-1, keepdims=True)) + norm_epsilon)
    error = lax.optimization_barrier(jnp.mean((predicted - target) ** 2, axis=-1))
    return jnp.sum(jnp.where(kept, 0.0, error))

def reference(patches, keep, perm, master, first, second, ema):
    images = patches.astype(jnp.float32)
    count = jnp.sum(NP - keep).astype(jnp.float32)
    groups = IMAGES // IMG

    def loss_of(params):
        rounded = low(params)

        def one_group(total, index):
            start = (index * IMG).astype(jnp.int32)
            pixels = lax.dynamic_slice_in_dim(images, start, IMG, 0)
            counts = lax.dynamic_slice_in_dim(keep, start, IMG, 0)
            order = lax.dynamic_slice_in_dim(perm, start, IMG, 0)
            latent = low(low_back(encode(rounded[0], pixels, counts, order)))
            return (total + decode(rounded[1], latent, pixels, counts, order), None)
        total, _ = lax.scan(jax.checkpoint(one_group), jnp.zeros((), jnp.float32), jnp.arange(groups))
        return (total / count, total)
    loss, pull, total = jax.vjp(loss_of, master, has_aux=True)
    grads = pull(jnp.ones((), jnp.float32))[0]
    norm = jnp.sqrt(jnp.sum(grads * grads))
    factor = jnp.minimum(1.0, clip_limit / (norm + norm_epsilon))
    clipped = grads * factor
    new_first = beta_one * first + (1.0 - beta_one) * clipped
    new_second = beta_two * second + (1.0 - beta_two) * clipped * clipped
    first_hat = new_first / (1.0 - beta_one ** STEP)
    second_hat = new_second / (1.0 - beta_two ** STEP)
    new_master = master - learn_rate * (first_hat / (jnp.sqrt(second_hat) + adam_epsilon) + weight_decay * master)
    new_ema = average_keep * ema + (1.0 - average_keep) * new_master
    return (new_master, new_first, new_second, new_ema, norm, total, count)
```

```python
import math

import jax
import jax.numpy as jnp
import numpy as np
from jax import lax
from jax.experimental import pallas as pl
from jax.experimental.pallas import tpu as pltpu
from jax.sharding import PartitionSpec as P

D = 768
HEADS_E = 12
FF_E = 3072
DD = 512
HEADS_D = 16
FF_D = 2048
PIX = 768
NP = 196
SLOTS = 98
STEP = 10

norm_epsilon = 1e-06
clip_limit = 0.01
learn_rate = 0.02
beta_one = 0.9
beta_two = 0.999
adam_epsilon = 1e-08
weight_decay = 0.05
average_keep = 0.8

F32 = jnp.float32
BF16 = jnp.bfloat16
ROWS_E = 112
ROWS_D = 208
GROUP = 16
VEC_UNITS = 2
VMEM_BYTES = 60 * 1024 * 1024

ENC = [
    ("patch", (PIX, D)),
    ("patch_b", (D,)),
    ("g1", (D,)),
    ("b1", (D,)),
    ("qkv", (D, 3 * D)),
    ("proj", (D, D)),
    ("g2", (D,)),
    ("b2", (D,)),
    ("fc1", (D, FF_E)),
    ("fc2", (FF_E, D)),
    ("gf", (D,)),
    ("bf", (D,)),
]
DEC = [
    ("embed", (D, DD)),
    ("mask", (DD,)),
    ("g1", (DD,)),
    ("b1", (DD,)),
    ("qkv", (DD, 3 * DD)),
    ("proj", (DD, DD)),
    ("g2", (DD,)),
    ("b2", (DD,)),
    ("fc1", (DD, FF_D)),
    ("fc2", (FF_D, DD)),
    ("gf", (DD,)),
    ("bf", (DD,)),
    ("head", (DD, PIX)),
]


class Section:
    def __init__(self, layout, dp, shard_rows):
        self.dp = dp
        self.shard_rows = shard_rows
        self.groups = []
        self.vectors = {}
        self.panels = {}
        fill = [0] * dp
        vector_fill = [0] * dp
        row = 0
        for name, shape in layout:
            panels = shape[-1] // 128
            self.panels[name] = panels
            if len(shape) == 2:
                for group in range(shape[0] // GROUP):
                    block = row // shard_rows
                    self.groups.append((name, group, row, panels, block, fill[block]))
                    fill[block] += panels
                    row += GROUP * panels
            else:
                block = row // shard_rows
                self.vectors[name] = (row, panels, block, vector_fill[block])
                vector_fill[block] += panels
                row += panels
        self.rows = row
        self.fill = fill
        assert max(vector_fill) <= 16 * VEC_UNITS
        self.blocks_used = max(b for b in range(dp) if fill[b] or vector_fill[b]) + 1

    def pieces(self, name, first=0, count=None):
        out = []
        for tensor, group, _, panels, block, unit in self.groups:
            if tensor != name or group < first or (count is not None and group >= first + count):
                continue
            if out and out[-1][0] == block and out[-1][1] + out[-1][3] * panels == unit:
                out[-1][3] += 1
            else:
                out.append([block, unit, group, 1])
        return [tuple(p) for p in out]


class Plan:
    def __init__(self, dp, shard_rows):
        self.dp = dp
        self.shard_rows = shard_rows
        self.sections = [Section(ENC, dp, shard_rows), Section(DEC, dp, shard_rows)]
        units = max(max(s.fill) for s in self.sections)
        units += (units + VEC_UNITS) % 2
        self.vec_unit = units
        self.units = units + VEC_UNITS
        self.half = self.units // 2
        self.head_rows = 8 * -(-max(16 * max(s.panels.values()) for s in self.sections) // 8)
        self.tail_units = max(max(s.panels.values()) for s in self.sections)
        self.pack_rows = shard_rows + self.head_rows
        self.pack_index = np.zeros((2, dp, self.units * 16), np.int32)
        self.tail_rows = 16 * (self.tail_units + VEC_UNITS)
        self.zero_row = self.units * 16 + self.tail_rows
        self.unpack_index = np.full((2, dp, shard_rows), self.zero_row, np.int32)
        self.tail_start = np.zeros((2, dp), np.int32)
        for s, section in enumerate(self.sections):
            for b in range(dp):
                self.tail_start[s, b] = max(section.fill[b] - self.tail_units, 0)
            for name, group, row, panels, block, unit in section.groups:
                for panel in range(panels):
                    for r in range(GROUP):
                        self.place(s, block, (unit + panel) * 16 + r, row + r * panels + panel)
            for row, panels, block, at in section.vectors.values():
                for panel in range(panels):
                    self.place(s, block, self.vec_unit * 16 + at + panel, row + panel)

    def place(self, s, block, block_row, flat_row):
        local = flat_row - block * self.shard_rows
        assert 0 <= local < self.pack_rows
        self.pack_index[s, block, block_row] = local
        owner, at = divmod(flat_row, self.shard_rows)
        if owner == block:
            self.unpack_index[s, owner, at] = block_row
        else:
            assert owner == block + 1
            if block_row >= self.vec_unit * 16:
                source = self.tail_units * 16 + block_row - self.vec_unit * 16
            else:
                source = block_row - int(self.tail_start[s, block]) * 16
                assert 0 <= source < self.tail_units * 16
            self.unpack_index[s, owner, at] = self.units * 16 + source


def factors(dp):
    if dp == 16:
        return (4, 2, 2)
    if dp == 64:
        return (4, 4, 4)
    return (dp, 1, 1)


def move_rows_kernel(index_ref, *refs, count, sizes, zero_at):
    sources, out_ref, held, done = refs[: len(sizes)], refs[-3], refs[-2], refs[-1]
    at = 0
    for source, size in zip(sources, sizes):
        held[pl.ds(at, size), :] = source[...].reshape(size, 128)
        at += size
    if zero_at is not None:
        held[pl.ds(zero_at, 8), :] = jnp.zeros((8, 128), F32)

    def eight(i, carry):
        for j in range(8):
            row = i * 8 + j
            done[pl.ds(row, 1), :] = held[pl.ds(index_ref[row], 1), :]
        return carry

    lax.fori_loop(0, count // 8, eight, 0)
    for row in range(count // 8 * 8, count):
        done[pl.ds(row, 1), :] = held[pl.ds(index_ref[row], 1), :]
    out_ref[...] = done[...].reshape(out_ref.shape).astype(out_ref.dtype)


def move_rows(index, sources, out_shape, dtype, zero_at=None):
    sizes = [math.prod(s.shape) // 128 for s in sources]
    count = math.prod(out_shape) // 128
    total = sum(sizes) + 8
    import functools

    return pl.pallas_call(
        functools.partial(move_rows_kernel, count=count, sizes=sizes, zero_at=zero_at),
        out_shape=jax.ShapeDtypeStruct(out_shape, dtype),
        in_specs=[pl.BlockSpec(memory_space=pltpu.SMEM)]
        + [pl.BlockSpec(memory_space=pltpu.VMEM)] * len(sources),
        out_specs=pl.BlockSpec(memory_space=pltpu.VMEM),
        scratch_shapes=[pltpu.VMEM((total, 128), F32), pltpu.VMEM((count, 128), F32)],
        compiler_params=pltpu.CompilerParams(vmem_limit_bytes=32 * 1024 * 1024),
        name="move_rows",
    )(index, *sources)


def dot(a, b):
    return lax.dot_general(a, b, (((1,), (0,)), ((), ())), preferred_element_type=F32)


def dot_nt(a, b):
    return lax.dot_general(a, b, (((1,), (1,)), ((), ())), preferred_element_type=F32)


def dot_tn(a, b):
    return lax.dot_general(a, b, (((0,), (0,)), ((), ())), preferred_element_type=F32)


def for_rows(count, size, step, unroll=1):
    def body(i, carry):
        step(pl.multiple_of(i * size, size))
        return carry

    lax.fori_loop(0, count // size, body, 0, unroll=unroll)


def columns(weight, panels, depth, pair):
    halves = [
        weight[:, 2 * pair + i].reshape(depth, 128)
        for i in range(2)
    ]
    return jnp.concatenate(halves, axis=1)


def row_band(weight, panels, band):
    parts = [weight[pl.ds(band * 16, 16), i].reshape(256, 128) for i in range(panels)]
    return jnp.concatenate(parts, axis=1)


def times_columns(left, weight, panels, depth, acc, finish):
    def body(pair, carry):
        acc[...] = dot(left[...], columns(weight, panels, depth, pair))
        finish(pair)
        return carry

    lax.fori_loop(0, panels // 2, body, 0)


def lanes(pair):
    return pl.ds(pl.multiple_of(pair * 256, 256), 256)


def norm_rows(x, width):
    mean = jnp.sum(x, axis=1, keepdims=True) * (1.0 / width)
    centre = x - mean
    spread = jnp.sum(centre * centre, axis=1, keepdims=True) * (1.0 / width)
    rstd = lax.rsqrt(spread + norm_epsilon)
    return centre * rstd, rstd


def norm_forward(x_ref, gain, shift, out_ref, count, width, size=16):
    def step(at):
        hat, _ = norm_rows(x_ref[pl.ds(at, size), :], width)
        out_ref[pl.ds(at, size), :] = (hat * gain + shift).astype(out_ref.dtype)

    for_rows(count, size, step, 2)


def norm_backward(x_ref, gain, grad_of, put, count, width, size=16):
    def body(i, carry):
        gain_sum, shift_sum = carry
        at = pl.multiple_of(i * size, size)
        hat, rstd = norm_rows(x_ref[pl.ds(at, size), :], width)
        grad = grad_of(at, size)
        gain_sum = gain_sum + jnp.sum((grad * hat).reshape(size // 8, 8, width), axis=0)
        shift_sum = shift_sum + jnp.sum(grad.reshape(size // 8, 8, width), axis=0)
        scaled = grad * gain
        first = jnp.sum(scaled, axis=1, keepdims=True) * (1.0 / width)
        second = jnp.sum(scaled * hat, axis=1, keepdims=True) * (1.0 / width)
        put(at, size, rstd * (scaled - first - hat * second))
        return gain_sum, shift_sum

    zero = jnp.zeros((8, width), F32)
    gain_sum, shift_sum = lax.fori_loop(0, count // size, body, (zero, zero))
    return jnp.sum(gain_sum, axis=0, keepdims=True), jnp.sum(shift_sum, axis=0, keepdims=True)


def head_masks(size):
    lane = lax.broadcasted_iota(jnp.int32, (1, 128), 1)
    return [
        jnp.where((lane >= h * size) & (lane < (h + 1) * size), 1.0, 0.0).astype(BF16)
        for h in range(128 // size)
    ]


def softmax_rows(scores, limit):
    key = lax.broadcasted_iota(jnp.int32, scores.shape, 1)
    scores = jnp.where(key < limit, scores, -1e30)
    top = jnp.max(scores, axis=1, keepdims=True)
    raised = jnp.exp(scores - top)
    return raised * (1.0 / jnp.sum(raised, axis=1, keepdims=True))


def attention_forward(mixed, out, limit_of, images, rows, width, size):
    panels = width // 128
    masks = head_masks(size)

    def body(step, carry):
        image, panel = step // panels, step % panels
        here = pl.ds(pl.multiple_of(image * rows, 16), rows)

        def part(third):
            return mixed[here, pl.ds(pl.multiple_of((third * panels + panel) * 128, 128), 128)]

        query, keys, values = part(0), part(1), part(2)
        limit = limit_of(image)
        total = jnp.zeros((rows, 128), F32)
        for mask in masks:
            probs = softmax_rows(dot_nt(query * mask, keys), limit).astype(BF16)
            total = total + dot(probs, values * mask)
        out[here, pl.ds(pl.multiple_of(panel * 128, 128), 128)] = total.astype(BF16)
        return carry

    lax.fori_loop(0, images * panels, body, 0)


def attention_backward(mixed, grad_out, grad_mixed, limit_of, images, rows, width, size):
    panels = width // 128
    masks = head_masks(size)

    def body(step, carry):
        image, panel = step // panels, step % panels
        here = pl.ds(pl.multiple_of(image * rows, 16), rows)

        def place(third):
            return pl.ds(pl.multiple_of((third * panels + panel) * 128, 128), 128)

        query, keys, values = (mixed[here, place(third)] for third in range(3))
        grad = grad_out[here, place(0)]
        limit = limit_of(image)
        zero = jnp.zeros((rows, 128), F32)
        grad_query, grad_keys, grad_values = zero, zero, zero
        for mask in masks:
            masked_query = query * mask
            masked_grad = grad * mask
            probs = softmax_rows(dot_nt(masked_query, keys), limit)
            grad_probs = dot_nt(masked_grad, values)
            inner = jnp.sum(probs * grad_probs, axis=1, keepdims=True)
            grad_scores = (probs * (grad_probs - inner)).astype(BF16)
            grad_values = grad_values + dot_tn(probs.astype(BF16), masked_grad)
            grad_query = grad_query + dot(grad_scores, keys * mask)
            grad_keys = grad_keys + dot_tn(grad_scores, masked_query)
        grad_mixed[here, place(0)] = (grad_query * (1.0 / math.sqrt(size))).astype(BF16)
        grad_mixed[here, place(1)] = grad_keys.astype(BF16)
        grad_mixed[here, place(2)] = grad_values.astype(BF16)
        return carry

    lax.fori_loop(0, images * panels, body, 0)


def gelu_parts(value):
    bell = 0.5 * (1.0 + lax.erf(value * math.sqrt(0.5)))
    slope = bell + value * (jnp.exp(value * value * -0.5) * (1.0 / math.sqrt(2.0 * math.pi)))
    return value * bell, slope


class Shape:
    def __init__(self, images, rows, width, heads, hidden):
        self.images, self.rows, self.width = images, rows, width
        self.size = width // heads
        self.hidden = hidden
        self.count = images * rows


def block_forward(sh, x0, n1, mixed, o, x1, n2, g, gp, y, w, vec, limit_of, acc, ready, saved):
    width, hidden, count = sh.width, sh.hidden, sh.count
    panels = width // 128
    norm_forward(x0, vec("g1"), vec("b1"), n1, count, width)
    saved(n1)
    ready("qkv")

    def put_mixed(pair):
        scale = jnp.where(pair < panels // 2, 1.0 / math.sqrt(sh.size), 1.0)

        def step(at):
            mixed[pl.ds(at, 16), lanes(pair)] = (acc[pl.ds(at, 16), :] * scale).astype(BF16)

        for_rows(count, 16, step, 4)

    times_columns(n1, w["qkv"], 3 * panels, width, acc, put_mixed)
    saved(mixed)
    attention_forward(mixed, o, limit_of, sh.images, sh.rows, width, sh.size)
    saved(o)
    ready("proj")

    def put_sum(base, out):
        def finish(pair):
            def step(at):
                here = pl.ds(at, 16)
                out[here, lanes(pair)] = base[here, lanes(pair)] + acc[here, :]

            for_rows(count, 16, step, 4)

        return finish

    times_columns(o, w["proj"], panels, width, acc, put_sum(x0, x1))
    saved(x1)
    norm_forward(x1, vec("g2"), vec("b2"), n2, count, width)
    saved(n2)
    ready("fc1")

    def put_hidden(pair):
        def step(at):
            here = pl.ds(at, 16)
            value, slope = gelu_parts(acc[here, :])
            g[here, lanes(pair)] = value.astype(BF16)
            gp[here, lanes(pair)] = slope

        for_rows(count, 16, step, 2)

    times_columns(n2, w["fc1"], hidden // 128, width, acc, put_hidden)
    saved(g)
    saved(gp)
    ready("fc2")
    times_columns(g, w["fc2"], panels, hidden, acc, put_sum(x1, y))
    saved(y)


class Gradients:
    def __init__(self, section, half, own, stage, sems, keep, send):
        self.section, self.half, self.own = section, half, own
        self.stage, self.sems, self.keep, self.send = stage, sems, keep, send
        self.turn = 0
        self.flying = [[], []]

    def pieces(self, name, first, count):
        panels = self.section.panels[name]
        out = []
        for block, unit, group, groups in self.section.pieces(name, first, count):
            start, left = unit, groups * panels
            at = (group - first) * panels
            while left:
                side = 0 if start < self.half else 1
                take = min(left, self.half - start) if side == 0 else left
                out.append((block, side, start - side * self.half, at, take))
                start, at, left = start + take, at + take, left - take
        return out

    def copy_out(self, source, block, side, unit, take, sem):
        def to(target):
            return pltpu.make_async_copy(source, target.at[block, pl.ds(unit, take)], sem)

        @pl.when(self.own == side)
        def _():
            to(self.keep).start()

        @pl.when(self.own != side)
        def _():
            to(self.send).start()

        return to(self.keep)

    def drain(self, slot):
        for copy in self.flying[slot]:
            copy.wait()
        self.flying[slot] = []

    def weight(self, name, left, depth, right, turned):
        panels = self.section.panels[name]
        for band in range(depth // 256):
            slot = self.turn % 2
            self.turn += 1
            self.drain(slot)
            stage = self.stage.at[slot]
            turned[...] = left[:, band * 256 : band * 256 + 256].T

            def body(pair, carry):
                value = dot(turned[...], right[:, lanes(pair)])
                for i in range(2):
                    stage[pl.ds(2 * pair + i, 16, stride=panels)] = value[
                        :, i * 128 : i * 128 + 128
                    ].reshape(16, 16, 128)
                return carry

            lax.fori_loop(0, panels // 2, body, 0)
            for block, side, unit, at, take in self.pieces(name, band * 16, 16):
                self.flying[slot].append(
                    self.copy_out(
                        stage.at[pl.ds(at, take)], block, side, unit, take, self.sems.at[slot]
                    )
                )

    def vectors(self, values, scratch, vec_unit):
        blocks = sorted({v[2] for v in self.section.vectors.values()})
        for k, block in enumerate(blocks):
            scratch[k] = jnp.zeros((16 * VEC_UNITS, 128), F32).reshape(VEC_UNITS, 16, 128)
            for name, (_, panels, at_block, at) in self.section.vectors.items():
                if at_block != block:
                    continue
                for panel in range(panels):
                    unit, row = divmod(at + panel, 16)
                    scratch[k, unit, row : row + 1, :] = values[name][
                        :, panel * 128 : panel * 128 + 128
                    ]
        copies = [
            self.copy_out(
                scratch.at[k], block, 1, vec_unit - self.half, VEC_UNITS, self.sems.at[2]
            )
            for k, block in enumerate(blocks)
        ]
        for copy in copies:
            copy.wait()
        self.drain(0)
        self.drain(1)


def block_backward(sh, dy, x0, n1, mixed, o, x1, n2, g, gp, dyb, dn, dmixed, acc, turned, w, vec,
                   limit_of, grads, values, ready):
    width, hidden, count = sh.width, sh.hidden, sh.count
    panels = width // 128

    def round_stream():
        def step(at):
            dyb[pl.ds(at, 16), :] = dy[pl.ds(at, 16), :].astype(BF16)

        for_rows(count, 16, step, 2)

    def into_stream(at, size, value):
        dy[pl.ds(at, size), :] = dy[pl.ds(at, size), :] + value

    def from_dn(at, size):
        return dn[pl.ds(at, size), :]

    round_stream()
    ready("fc2", g)
    grads.weight("fc2", g, hidden, dyb, turned)
    ready("gp", gp)

    def hidden_band(band, carry):
        acc[...] = dot_nt(dyb[...], row_band(w["fc2"], panels, band))

        def step(at):
            here = pl.ds(at, 16)
            g[here, lanes(band)] = (acc[here, :] * gp[here, lanes(band)]).astype(BF16)

        for_rows(count, 16, step, 4)
        return carry

    lax.fori_loop(0, hidden // 256, hidden_band, 0)
    ready("fc1", n2)
    grads.weight("fc1", n2, width, g, turned)

    def back_through(left, name):
        def body(band, carry):
            acc[...] = dot_nt(left[...], row_band(w[name], grads.section.panels[name], band))

            def step(at):
                dn[pl.ds(at, 16), lanes(band)] = acc[pl.ds(at, 16), :]

            for_rows(count, 16, step, 4)
            return carry

        lax.fori_loop(0, width // 256, body, 0)

    back_through(g, "fc1")
    ready("x1", x1)
    values["g2"], values["b2"] = norm_backward(x1, vec("g2"), from_dn, into_stream, count, width)
    round_stream()
    ready("proj", o)
    grads.weight("proj", o, width, dyb, turned)

    def out_band(band, carry):
        acc[...] = dot_nt(dyb[...], row_band(w["proj"], panels, band))

        def step(at):
            o[pl.ds(at, 16), lanes(band)] = acc[pl.ds(at, 16), :].astype(BF16)

        for_rows(count, 16, step, 4)
        return carry

    lax.fori_loop(0, width // 256, out_band, 0)
    ready("mixed", mixed)
    attention_backward(mixed, o, dmixed, limit_of, sh.images, sh.rows, width, sh.size)
    ready("qkv", n1)
    grads.weight("qkv", n1, width, dmixed, turned)
    back_through(dmixed, "qkv")
    ready("x0", x0)
    values["g1"], values["b1"] = norm_backward(x0, vec("g1"), from_dn, into_stream, count, width)


def load_vectors(section, vec_unit, own_section, gathered, held, vec_ref, sem):
    blocks = sorted({v[2] for v in section.vectors.values()})
    copies = [
        pltpu.make_async_copy(
            gathered.at[own_section, block, pl.ds(vec_unit, VEC_UNITS)], held.at[k], sem
        )
        for k, block in enumerate(blocks)
    ]
    for copy in copies:
        copy.start()

    def finish():
        for copy in copies:
            copy.wait()
        names = {}
        for k, block in enumerate(blocks):
            rows = held[k].reshape(16 * VEC_UNITS, 128).astype(F32)
            for i, (name, (_, panels, at_block, at)) in enumerate(section.vectors.items()):
                names[name] = i
                if at_block != block:
                    continue
                for panel in range(panels):
                    vec_ref[i : i + 1, panel * 128 : panel * 128 + 128] = rows[
                        at + panel : at + panel + 1, :
                    ]
        return lambda name: vec_ref[names[name] : names[name] + 1, :]

    return finish


def load_weights(section, own_section, gathered, w, sems):
    copies = {}
    for k, (name, ref) in enumerate(w.items()):
        panels = section.panels[name]
        copies[name] = [
            pltpu.make_async_copy(
                gathered.at[own_section, block, pl.ds(unit, groups * panels)],
                ref.reshape(ref.shape[0] * panels, 16, 128).at[
                    pl.ds(group * panels, groups * panels)
                ],
                sems.at[k],
            )
            for block, unit, group, groups in section.pieces(name)
        ]
        for copy in copies[name]:
            copy.start()

    def ready(name):
        for copy in copies.get(name, ()):
            copy.wait()

    return ready


def weight_scratch(layout, names):
    shapes = dict(layout)
    return [
        pltpu.VMEM((shapes[n][0] // GROUP, shapes[n][1] // 128, GROUP, 128), BF16)
        for n in names
    ]


def picks(perm_ref, image):
    here = pl.ds(pl.multiple_of(image * ROWS_D, 16), ROWS_D)
    patch = lax.broadcasted_iota(jnp.int32, (ROWS_D, ROWS_D), 1)
    return jnp.where(perm_ref[here, :] == patch, 1.0, 0.0).astype(BF16)


W_ENC = ["patch", "qkv", "proj", "fc1", "fc2"]


def encoder_kernel(plan, sh, refs):
    section = plan.sections[0]
    (info, gathered, patches, perm, pos, pp_out, x0_out, n1_out, mixed_out, o_out, x1_out, n2_out,
     g_out, gp_out, y_out, latent_out, w_patch, w_qkv, w_proj, w_fc1, w_fc2, held, vec_ref, pp, xe,
     x0, n1, mixed, o, x1, n2, g, gp, y, latent, acc, w_sems, out_sems) = refs
    w = dict(zip(W_ENC, (w_patch, w_qkv, w_proj, w_fc1, w_fc2)))
    finish_vec = load_vectors(section, plan.vec_unit, 0, gathered, held, vec_ref, w_sems.at[5])
    ready = load_weights(section, 0, gathered, w, w_sems)
    outs = []

    targets = [(pp, pp_out), (x0, x0_out), (n1, n1_out), (mixed, mixed_out), (o, o_out),
               (x1, x1_out), (n2, n2_out), (g, g_out), (gp, gp_out), (y, y_out),
               (latent, latent_out)]

    def saved(ref):
        for k, (source, target) in enumerate(targets):
            if source is ref:
                copy = pltpu.make_async_copy(source, target, out_sems.at[k])
                copy.start()
                outs.append(copy)

    def gather(image, carry):
        chosen = picks(perm, image)
        pp[image] = dot(chosen, patches[image]).astype(BF16)
        here = pl.ds(pl.multiple_of(image * ROWS_E, 16), ROWS_E)
        xe[here, :] = pp[image, 0:ROWS_E, :]
        few = chosen[0:ROWS_E, :]
        x0[here, :] = (dot(few, pos[0]) + dot(few, pos[1])) + dot(few, pos[2])
        return carry

    lax.fori_loop(0, sh.images, gather, 0)
    saved(pp)
    vec = finish_vec()
    ready("patch")
    bias = vec("patch_b")

    def put(pair):
        part = vec_ref[0:1, lanes(pair)]

        def step(at):
            here = pl.ds(at, 16)
            x0[here, lanes(pair)] = (acc[here, :] + part) + x0[here, lanes(pair)]

        for_rows(sh.count, 16, step, 4)

    del bias
    times_columns(xe, w["patch"], D // 128, PIX, acc, put)
    saved(x0)
    block_forward(
        sh, x0, n1, mixed, o, x1, n2, g, gp, y, w, vec, lambda i: info[1 + i], acc, ready, saved
    )
    norm_forward(y, vec("gf"), vec("bf"), latent, sh.count, D)
    saved(latent)
    for copy in outs:
        copy.wait()


ANY = pl.BlockSpec(memory_space=pl.ANY)
IN_VMEM = pl.BlockSpec(memory_space=pltpu.VMEM)
IN_SMEM = pl.BlockSpec(memory_space=pltpu.SMEM)


def saved_shapes(sh):
    count, width, hidden = sh.count, sh.width, sh.hidden
    return [
        ((count, width), F32),
        ((count, width), BF16),
        ((count, 3 * width), BF16),
        ((count, width), BF16),
        ((count, width), F32),
        ((count, width), BF16),
        ((count, hidden), BF16),
        ((count, hidden), F32),
        ((count, width), F32),
    ]


def encoder(plan, sh, info, gathered, patches, perm, pos):
    saved = saved_shapes(sh)
    pp_shape = ((sh.images, ROWS_D, PIX), BF16)
    latent_shape = ((sh.count, D), BF16)
    outs = [pp_shape, *saved, latent_shape]
    holders = len({v[2] for v in plan.sections[0].vectors.values()})
    return pl.pallas_call(
        lambda *refs: encoder_kernel(plan, sh, refs),
        out_shape=[jax.ShapeDtypeStruct(*s) for s in outs],
        in_specs=[IN_SMEM, ANY, IN_VMEM, IN_VMEM, IN_VMEM],
        out_specs=[ANY] * len(outs),
        scratch_shapes=[
            *weight_scratch(ENC, W_ENC),
            pltpu.VMEM((holders, VEC_UNITS, 16, 128), BF16),
            pltpu.VMEM((8, D), F32),
            pltpu.VMEM(*pp_shape),
            pltpu.VMEM((sh.count, PIX), BF16),
            *[pltpu.VMEM(*s) for s in saved],
            pltpu.VMEM(*latent_shape),
            pltpu.VMEM((sh.count, 256), F32),
            pltpu.SemaphoreType.DMA((6,)),
            pltpu.SemaphoreType.DMA((len(outs),)),
        ],
        compiler_params=pltpu.CompilerParams(vmem_limit_bytes=VMEM_BYTES),
        name="encoder_forward",
    )(info, gathered, patches, perm, pos)


W_DEC = ["embed", "qkv", "proj", "fc1", "fc2", "head"]


def decoder_kernel(plan, sh, refs):
    section = plan.sections[1]
    (info, scale, gathered, latent_in, pp_in, perm, pos, keep_out, send_out, grad_latent, loss_out,
     w_embed, w_qkv, w_proj, w_fc1, w_fc2, w_head, held, vec_ref, pp, latent, embedded, x0, n1,
     mixed, o, x1, n2, g, gp, y, f, dn, guess, acc, acc_e, turned, turned_e, stage, vec_stage, w_sems,
     in_sems, grad_sems) = refs
    w = dict(zip(W_DEC, (w_embed, w_qkv, w_proj, w_fc1, w_fc2, w_head)))
    copy_latent = pltpu.make_async_copy(latent_in, latent, in_sems.at[0])
    copy_pp = pltpu.make_async_copy(pp_in, pp, in_sems.at[1])
    copy_latent.start()
    finish_vec = load_vectors(section, plan.vec_unit, 1, gathered, held, vec_ref, w_sems.at[6])
    ready = load_weights(section, 1, gathered, w, w_sems)
    copy_pp.start()
    images, count = sh.images, sh.count
    count_e = images * ROWS_E
    vec = finish_vec()
    copy_latent.wait()
    ready("embed")

    def put_embedded(pair):
        def step(at):
            embedded[pl.ds(at, 16), lanes(pair)] = acc_e[pl.ds(at, 16), :]

        for_rows(count_e, 16, step, 4)

    times_columns(latent, w["embed"], DD // 128, D, acc_e, put_embedded)

    def tokens(image, carry):
        chosen = picks(perm, image)
        place = (dot(chosen, pos[0]) + dot(chosen, pos[1])) + dot(chosen, pos[2])
        start = pl.multiple_of(image * ROWS_D, 16)
        kept = info[1 + image]
        token = vec_ref[0:1, :]
        few = embedded[pl.ds(pl.multiple_of(image * ROWS_E, 16), ROWS_E), :]
        rank = lax.broadcasted_iota(jnp.int32, (ROWS_E, DD), 0)
        x0[pl.ds(start, ROWS_E), :] = jnp.where(rank < kept, few, token) + place[:ROWS_E, :]
        x0[pl.ds(start + ROWS_E, ROWS_D - ROWS_E), :] = token + place[ROWS_E:, :]
        return carry

    lax.fori_loop(0, images, tokens, 0)
    block_forward(
        sh, x0, n1, mixed, o, x1, n2, g, gp, y, w, vec, lambda i: NP, acc, ready, lambda ref: None
    )
    norm_forward(y, vec("gf"), vec("bf"), f, count, DD)
    ready("head")
    copy_pp.wait()
    factor = scale[0]

    def predict_image(image, total):
        start = pl.multiple_of(image * ROWS_D, 16)
        kept = info[1 + image]
        here = pl.ds(start, ROWS_D)
        for pair in range(PIX // 256):
            guess[:, pair * 256 : pair * 256 + 256] = dot(
                f[here, :], columns(w["head"], PIX // 128, DD, pair)
            )

        def rows(i, total):
            at = pl.multiple_of(i * 16, 16)
            target, _ = norm_rows(pp[image, pl.ds(at, 16), :].astype(F32), PIX)
            off = guess[pl.ds(at, 16), :] - target
            rank = lax.broadcasted_iota(jnp.int32, (16, PIX), 0) + at
            off = jnp.where((rank >= kept) & (rank < NP), off, 0.0)
            pp[image, pl.ds(at, 16), :] = (off * factor).astype(BF16)
            return total + jnp.sum((off * off).reshape(2, 8, PIX), axis=0)

        return lax.fori_loop(0, ROWS_D // 16, rows, total)

    total = lax.fori_loop(0, images, predict_image, jnp.zeros((8, PIX), F32))
    total = jnp.sum(jnp.sum(total, axis=0, keepdims=True), axis=1, keepdims=True)
    loss_out[...] = jnp.broadcast_to(total * (1.0 / PIX), (8, 128))

    own = info[0]
    grads = Gradients(section, plan.half, own, stage, grad_sems, keep_out, send_out)
    dpred = pp.reshape(count, PIX)
    grads.weight("head", f, DD, dpred, turned)

    def final_band(band, carry):
        acc[...] = dot_nt(dpred[...], row_band(w["head"], PIX // 128, band))

        def step(at):
            dn[pl.ds(at, 16), lanes(band)] = acc[pl.ds(at, 16), :]

        for_rows(count, 16, step, 4)
        return carry

    lax.fori_loop(0, DD // 256, final_band, 0)
    values = {}

    def from_dn(at, size):
        return dn[pl.ds(at, size), :]

    def put_y(at, size, value):
        y[pl.ds(at, size), :] = value

    values["gf"], values["bf"] = norm_backward(y, vec("gf"), from_dn, put_y, count, DD)
    block_backward(
        sh, y, x0, n1, mixed, o, x1, n2, g, gp, f, dn, g.at[:, pl.ds(0, 3 * DD)], acc, turned, w, vec, lambda i: NP,
        grads, values, lambda *a: None,
    )

    def split(image, total):
        start = pl.multiple_of(image * ROWS_D, 16)
        kept = info[1 + image]

        def rows(i, total):
            at = pl.multiple_of(i * 16, 16)
            grad = y[pl.ds(start + at, 16), :]
            rank = lax.broadcasted_iota(jnp.int32, (16, DD), 0) + at
            free = jnp.where(rank >= kept, grad, 0.0)

            @pl.when(i < ROWS_E // 16)
            def _():
                taken = jnp.where(rank < kept, grad, 0.0).astype(BF16)
                n1[pl.ds(pl.multiple_of(image * ROWS_E, 16) + at, 16), :] = taken

            return total + jnp.sum(free.reshape(2, 8, DD), axis=0)

        return lax.fori_loop(0, ROWS_D // 16, rows, total)

    total = lax.fori_loop(0, images, split, jnp.zeros((8, DD), F32))
    values["mask"] = jnp.sum(total, axis=0, keepdims=True)
    placed = n1.at[pl.ds(0, count_e)]
    grads.weight("embed", latent, D, placed, turned_e)

    def latent_band(band, carry):
        acc_e[...] = dot_nt(placed[...], row_band(w["embed"], DD // 128, band))

        def step(at):
            grad_latent[pl.ds(at, 16), lanes(band)] = acc_e[pl.ds(at, 16), :].astype(BF16)

        for_rows(count_e, 16, step, 4)
        return carry

    lax.fori_loop(0, D // 256, latent_band, 0)
    grads.vectors(values, vec_stage, plan.vec_unit)


def grad_shapes(plan, section):
    blocks = plan.sections[section].blocks_used
    inner = factors(plan.dp)[1] * factors(plan.dp)[2]
    blocks = -(-blocks // inner) * inner
    return [jax.ShapeDtypeStruct((blocks, plan.half, 16, 128), F32)] * 2


def decoder(plan, sh, info, scale, gathered, latent, pp, perm, pos):
    count_e = sh.images * ROWS_E
    holders = len({v[2] for v in plan.sections[1].vectors.values()})
    saved = saved_shapes(sh)
    most = max(plan.sections[1].panels.values())
    return pl.pallas_call(
        lambda *refs: decoder_kernel(plan, sh, refs),
        out_shape=[
            *grad_shapes(plan, 1),
            jax.ShapeDtypeStruct((count_e, D), BF16),
            jax.ShapeDtypeStruct((8, 128), F32),
        ],
        in_specs=[IN_SMEM, IN_SMEM, ANY, ANY, ANY, IN_VMEM, IN_VMEM],
        out_specs=[ANY, ANY, IN_VMEM, IN_VMEM],
        scratch_shapes=[
            *weight_scratch(DEC, W_DEC),
            pltpu.VMEM((holders, VEC_UNITS, 16, 128), BF16),
            pltpu.VMEM((8, DD), F32),
            pltpu.VMEM((sh.images, ROWS_D, PIX), BF16),
            pltpu.VMEM((count_e, D), BF16),
            pltpu.VMEM((count_e, DD), F32),
            *[pltpu.VMEM(*s) for s in saved],
            pltpu.VMEM((sh.count, DD), BF16),
            pltpu.VMEM((sh.count, DD), F32),
            pltpu.VMEM((ROWS_D, PIX), F32),
            pltpu.VMEM((sh.count, 256), F32),
            pltpu.VMEM((count_e, 256), F32),
            pltpu.VMEM((256, sh.count), BF16),
            pltpu.VMEM((256, count_e), BF16),
            pltpu.VMEM((2, 16 * most, 16, 128), F32),
            pltpu.VMEM((holders, VEC_UNITS, 16, 128), F32),
            pltpu.SemaphoreType.DMA((7,)),
            pltpu.SemaphoreType.DMA((2,)),
            pltpu.SemaphoreType.DMA((3,)),
        ],
        compiler_params=pltpu.CompilerParams(vmem_limit_bytes=VMEM_BYTES),
        name="decoder_both",
    )(info, scale, gathered, latent, pp, perm, pos)


W_BACK = ["fc2", "fc1", "proj", "qkv"]


def encoder_back_kernel(plan, sh, refs):
    section = plan.sections[0]
    (info, gathered, grad_latent, pp_in, x0_in, n1_in, mixed_in, o_in, x1_in, n2_in, g_in, gp_in,
     y_in, keep_out, send_out, w_fc2, w_fc1, w_proj, w_qkv, held, vec_ref, xe, x0, n1, mixed, o, x1,
     n2, g, gp, y, dyb, dn, dmixed, acc, turned, stage, vec_stage, w_sems, in_sems,
     grad_sems) = refs
    w = dict(zip(W_BACK, (w_fc2, w_fc1, w_proj, w_qkv)))
    finish_vec = load_vectors(section, plan.vec_unit, 0, gathered, held, vec_ref, w_sems.at[4])
    loads = {}
    pairs = [(y, y_in), (g, g_in), (gp, gp_in), (n2, n2_in), (x1, x1_in), (o, o_in),
             (mixed, mixed_in), (n1, n1_in), (x0, x0_in)]
    for k, (ref, source) in enumerate(pairs):
        loads[id(ref)] = pltpu.make_async_copy(source, ref, in_sems.at[k])
        loads[id(ref)].start()
    weights_ready = load_weights(section, 0, gathered, w, w_sems)
    patch_loads = [
        pltpu.make_async_copy(
            pp_in.at[i, pl.ds(0, ROWS_E)], xe.at[pl.ds(i * ROWS_E, ROWS_E)], in_sems.at[9]
        )
        for i in range(sh.images)
    ]
    for copy in patch_loads:
        copy.start()

    def ready(name, ref):
        loads[id(ref)].wait()
        weights_ready(name)

    vec = finish_vec()
    loads[id(y)].wait()
    values = {}

    def from_latent(at, size):
        return grad_latent[pl.ds(at, size), :].astype(F32)

    def put_y(at, size, value):
        y[pl.ds(at, size), :] = value

    values["gf"], values["bf"] = norm_backward(y, vec("gf"), from_latent, put_y, sh.count, D)
    grads = Gradients(section, plan.half, info[0], stage, grad_sems, keep_out, send_out)
    block_backward(
        sh, y, x0, n1, mixed, o, x1, n2, g, gp, dyb, dn, dmixed, acc, turned, w, vec,
        lambda i: info[1 + i], grads, values, ready,
    )

    def body(i, total):
        at = pl.multiple_of(i * 16, 16)
        grad = y[pl.ds(at, 16), :]
        dyb[pl.ds(at, 16), :] = grad.astype(BF16)
        return total + jnp.sum(grad.reshape(2, 8, D), axis=0)

    total = lax.fori_loop(0, sh.count // 16, body, jnp.zeros((8, D), F32))
    values["patch_b"] = jnp.sum(total, axis=0, keepdims=True)
    for copy in patch_loads:
        copy.wait()
    grads.weight("patch", xe, PIX, dyb, turned)
    grads.vectors(values, vec_stage, plan.vec_unit)


def encoder_back(plan, sh, info, gathered, grad_latent, pp, saved):
    shapes = saved_shapes(sh)
    holders = len({v[2] for v in plan.sections[0].vectors.values()})
    most = max(plan.sections[0].panels.values())
    return pl.pallas_call(
        lambda *refs: encoder_back_kernel(plan, sh, refs),
        out_shape=grad_shapes(plan, 0),
        in_specs=[IN_SMEM, ANY, IN_VMEM, *[ANY] * 10],
        out_specs=[ANY, ANY],
        scratch_shapes=[
            *weight_scratch(ENC, W_BACK),
            pltpu.VMEM((holders, VEC_UNITS, 16, 128), BF16),
            pltpu.VMEM((8, D), F32),
            pltpu.VMEM((sh.count, PIX), BF16),
            *[pltpu.VMEM(*s) for s in shapes],
            pltpu.VMEM((sh.count, D), BF16),
            pltpu.VMEM((sh.count, D), F32),
            pltpu.VMEM((sh.count, 3 * D), BF16),
            pltpu.VMEM((sh.count, 256), F32),
            pltpu.VMEM((256, sh.count), BF16),
            pltpu.VMEM((2, 16 * most, 16, 128), F32),
            pltpu.VMEM((holders, VEC_UNITS, 16, 128), F32),
            pltpu.SemaphoreType.DMA((5,)),
            pltpu.SemaphoreType.DMA((10,)),
            pltpu.SemaphoreType.DMA((3,)),
        ],
        compiler_params=pltpu.CompilerParams(vmem_limit_bytes=VMEM_BYTES),
        name="encoder_backward",
    )(info, gathered, grad_latent, pp, *saved)


class Grid:
    def __init__(self, dp):
        self.sizes = factors(dp)
        self.dp = dp
        me = lax.axis_index("dp")
        _, b, c = self.sizes
        self.at = (me // (b * c), me // c % b, me % c)

    def shift(self, axis, by, held=None):
        a, b, c = self.sizes
        pairs = []
        for me in range(self.dp):
            at = [me // (b * c), me // c % b, me % c]
            if held is not None and at[axis] not in held:
                continue
            at[axis] += by
            if 0 <= at[axis] < self.sizes[axis]:
                pairs.append((me, (at[0] * b + at[1]) * c + at[2]))
        return pairs


def pick(value, index, axis):
    return lax.dynamic_index_in_dim(value, index, axis, keepdims=False)


def scatter_axis(grid, terms, axis, dim, targets):
    size, at = grid.sizes[axis], grid.at[axis]

    def own(target):
        target = jnp.clip(target, 0, targets - 1)
        total = pick(terms[0], target, dim)
        for term in terms[1:]:
            total = total + pick(term, target, dim)
        return total

    if size == 1:
        return [pick(term, jnp.zeros((), jnp.int32), dim) for term in terms]
    if size == 2 and targets == 2:
        got = lax.ppermute(own(1 - at), "dp", grid.shift(axis, 1) + grid.shift(axis, -1))
        return [pick(term, at, dim) for term in terms] + [got]
    up = None
    down = None
    for step in range(1, size):
        held = [z for z in range(step) if size - step + z < targets and z < size - 1]
        mine = own(size - step + at)
        if up is not None:
            mine = mine + up
        up = lax.ppermute(mine, "dp", grid.shift(axis, 1, held)) if held else None
        held = [z for z in range(1, size) if 0 <= step - 1 - (size - 1 - z) < targets]
        mine = own(step - 1 - (size - 1 - at))
        if down is not None:
            mine = mine + down
        down = lax.ppermute(mine, "dp", grid.shift(axis, -1, held)) if held else None
    last = jnp.clip(at, 0, targets - 1)
    out = [pick(term, last, dim) for term in terms]
    return out + [v for v in (up, down) if v is not None]


def scatter_sum(grid, keep, got):
    a, b, c = grid.sizes
    half = keep.shape[1]
    targets = keep.shape[0] // (b * c)
    cut = [0, -(-half // 3), -(-2 * half // 3), half]
    orders = [(2, 1, 0), (1, 0, 2), (0, 2, 1)]
    parts = []
    for part, order in enumerate(orders):
        terms = [
            v.reshape((targets, b, c) + v.shape[1:])[:, :, :, cut[part] : cut[part + 1]]
            for v in (keep, got)
        ]
        left = [0, 1, 2]
        for axis in order:
            dim = left.index(axis)
            terms = scatter_axis(grid, terms, axis, dim, (targets, b, c)[axis])
            left.remove(axis)
        total = terms[0]
        for term in terms[1:]:
            total = total + term
        parts.append(total)
    return jnp.concatenate(parts, axis=0)


def sum_everywhere(grid, value):
    value = value + lax.ppermute(value, "section", [(0, 1), (1, 0)])
    for axis, size in enumerate(grid.sizes):
        step = 1
        stride = math.prod(grid.sizes[axis + 1 :])
        while step < size:
            pairs = [
                (i, i + (step if i // stride // step % 2 == 0 else -step) * stride)
                for i in range(grid.dp)
            ]
            value = value + lax.ppermute(value, "dp", pairs)
            step *= 2
    return value


def sincos(width):
    places = np.arange(NP).astype(np.float32)[:, None]
    column = np.arange(width)
    rates = np.exp(
        -(np.float32(2.0) * (column // 2).astype(np.float32) / np.float32(width))
        * np.float32(math.log(10000.0))
    ).astype(np.float32)
    phases = (places * rates[None, :]).astype(np.float32)
    table = np.where(
        column[None, :] % 2 == 0, np.sin(phases.astype(np.float64)), np.cos(phases.astype(np.float64))
    ).astype(np.float32)
    parts = []
    left = np.zeros((ROWS_D, width), np.float32)
    left[:NP] = table
    for _ in range(3):
        high = left.astype(jnp.bfloat16)
        parts.append(high)
        left = left - high.astype(np.float32)
    return np.stack(parts)


def on_device(patches, keep, perm, master, first, second, ema):
    dp = lax.axis_size("dp")
    section = lax.axis_index("section")
    me = lax.axis_index("dp")
    shard = master.shape[1]
    plan = Plan(dp, shard // 128)
    grid = Grid(dp)
    rows = plan.shard_rows

    flat = master.reshape(rows, 128)
    following = lax.ppermute(
        flat[: plan.head_rows], "dp", [(i, i - 1) for i in range(1, dp)]
    )
    index = jnp.asarray(plan.pack_index)[section, me]
    packed = move_rows(index, [flat, following], (plan.units, 16, 128), BF16)
    gathered = lax.all_gather(packed, ("section", "dp"), axis=0, tiled=True)
    gathered = gathered.reshape(2, dp, plan.units, 16, 128)

    count = sum_everywhere(grid, jnp.sum(NP - keep).astype(F32)) * 0.5
    images = patches.shape[0] // 2
    mine = section * images
    patches = lax.dynamic_slice_in_dim(patches, mine, images, 0)
    patches = jnp.pad(patches, ((0, 0), (0, ROWS_D - NP), (0, 0)))
    order = lax.dynamic_slice_in_dim(perm, mine, images, 0)
    order = jnp.pad(order, ((0, 0), (0, ROWS_D - NP)), constant_values=ROWS_D - 1)
    order = order.reshape(images * ROWS_D, 1)
    kept = lax.dynamic_slice_in_dim(keep, mine, images, 0)
    info = jnp.concatenate([section[None].astype(jnp.int32), kept])
    scale = ((1.0 / count) * (1.0 / PIX) * 2.0).reshape(1)

    shape_e = Shape(images, ROWS_E, D, HEADS_E, FF_E)
    shape_d = Shape(images, ROWS_D, DD, HEADS_D, FF_D)
    pp, *saved, latent = encoder(
        plan, shape_e, info, gathered, patches, order, jnp.asarray(sincos(D))
    )
    keep_d, send_d, grad_latent, loss = decoder(
        plan, shape_d, info, scale, gathered, latent, pp, order, jnp.asarray(sincos(DD))
    )
    swap = [(0, 1), (1, 0)]
    sum_d = scatter_sum(grid, keep_d, lax.ppermute(send_d, "section", swap))
    keep_e, send_e = encoder_back(plan, shape_e, info, gathered, grad_latent, pp, saved)
    sum_e = scatter_sum(grid, keep_e, lax.ppermute(send_e, "section", swap))

    half_mine = jnp.where(section == 0, sum_e, sum_d)
    half_other = lax.ppermute(jnp.where(section == 0, sum_d, sum_e), "section", swap)
    block = jnp.where(
        section == 0,
        jnp.concatenate([half_mine, half_other], axis=0),
        jnp.concatenate([half_other, half_mine], axis=0),
    )
    start = jnp.asarray(plan.tail_start)[section, me]
    tail = jnp.concatenate(
        [
            lax.dynamic_slice_in_dim(block, start, plan.tail_units, 0),
            block[plan.vec_unit :],
        ],
        axis=0,
    )
    tail = lax.ppermute(tail, "dp", [(i, i + 1) for i in range(dp - 1)])
    index = jnp.asarray(plan.unpack_index)[section, me]
    shard_total = move_rows(index, [block, tail], (rows, 128), F32, zero_at=plan.zero_row)

    squares = jnp.sum(shard_total * shard_total)
    sums = sum_everywhere(grid, jnp.stack([squares, loss[0, 0]]))
    loss_sum = sums[1]
    norm = jnp.sqrt(sums[0])
    factor = jnp.minimum(1.0, clip_limit / (norm + norm_epsilon))
    clipped = (shard_total * factor).reshape(master.shape)
    new_first = beta_one * first + (1.0 - beta_one) * clipped
    new_second = beta_two * second + (1.0 - beta_two) * clipped * clipped
    first_hat = new_first / (1.0 - beta_one**STEP)
    second_hat = new_second / (1.0 - beta_two**STEP)
    new_master = master - learn_rate * (
        first_hat / (jnp.sqrt(second_hat) + adam_epsilon) + weight_decay * master
    )
    new_ema = average_keep * ema + (1.0 - average_keep) * new_master
    return (new_master, new_first, new_second, new_ema, norm, loss_sum, count)


def solution(mesh):
    return jax.shard_map(
        on_device,
        mesh=mesh,
        in_specs=(
            P("dp", None, None),
            P("dp"),
            P("dp", None),
            P("section", "dp"),
            P("section", "dp"),
            P("section", "dp"),
            P("section", "dp"),
        ),
        out_specs=(
            P("section", "dp"),
            P("section", "dp"),
            P("section", "dp"),
            P("section", "dp"),
            P(),
            P(),
            P(),
        ),
        check_vma=False,
    )
```

```python
import functools
import math

import jax
import jax.numpy as jnp
import numpy as np
from jax import lax
from jax.experimental import pallas as pl
from jax.experimental.pallas import tpu as pltpu
from jax.sharding import PartitionSpec as P

D = 768
HEADS_E = 12
FF_E = 3072
DD = 512
HEADS_D = 16
FF_D = 2048
PIX = 768
NP = 196
SLOTS = 98
STEP = 10

norm_epsilon = 1e-06
clip_limit = 0.01
learn_rate = 0.02
beta_one = 0.9
beta_two = 0.999
adam_epsilon = 1e-08
weight_decay = 0.05
average_keep = 0.8

F32 = jnp.float32
BF16 = jnp.bfloat16
ROWS_E = 112
ROWS_D = 208
GROUP = 16
VEC_UNITS = 2
VMEM_BYTES = 60 * 1024 * 1024
ANY = pl.BlockSpec(memory_space=pl.ANY)
IN_VMEM = pl.BlockSpec(memory_space=pltpu.VMEM)
IN_SMEM = pl.BlockSpec(memory_space=pltpu.SMEM)

ENC = [
    ("patch", (PIX, D)),
    ("patch_b", (D,)),
    ("g1", (D,)),
    ("b1", (D,)),
    ("qkv", (D, 3 * D)),
    ("proj", (D, D)),
    ("g2", (D,)),
    ("b2", (D,)),
    ("fc1", (D, FF_E)),
    ("fc2", (FF_E, D)),
    ("gf", (D,)),
    ("bf", (D,)),
]
DEC = [
    ("embed", (D, DD)),
    ("mask", (DD,)),
    ("g1", (DD,)),
    ("b1", (DD,)),
    ("qkv", (DD, 3 * DD)),
    ("proj", (DD, DD)),
    ("g2", (DD,)),
    ("b2", (DD,)),
    ("fc1", (DD, FF_D)),
    ("fc2", (FF_D, DD)),
    ("gf", (DD,)),
    ("bf", (DD,)),
    ("head", (DD, PIX)),
]


class Section:
    def __init__(self, layout, dp, shard_rows):
        self.dp = dp
        self.shard_rows = shard_rows
        self.groups = []
        self.vectors = {}
        self.panels = {}
        fill = [0] * dp
        vector_fill = [0] * dp
        row = 0
        for name, shape in layout:
            panels = shape[-1] // 128
            self.panels[name] = panels
            if len(shape) == 2:
                for group in range(shape[0] // GROUP):
                    block = row // shard_rows
                    self.groups.append((name, group, row, panels, block, fill[block]))
                    fill[block] += panels
                    row += GROUP * panels
            else:
                block = row // shard_rows
                self.vectors[name] = (row, panels, block, vector_fill[block])
                vector_fill[block] += panels
                row += panels
        self.rows = row
        self.fill = fill
        assert max(vector_fill) <= 16 * VEC_UNITS
        self.blocks_used = max(b for b in range(dp) if fill[b] or vector_fill[b]) + 1

    def pieces(self, name, first=0, count=None):
        out = []
        for tensor, group, _, panels, block, unit in self.groups:
            if tensor != name or group < first or (count is not None and group >= first + count):
                continue
            if out and out[-1][0] == block and out[-1][1] + out[-1][3] * panels == unit:
                out[-1][3] += 1
            else:
                out.append([block, unit, group, 1])
        return [tuple(p) for p in out]

    def runs(self, name, cuts, first=0, count=None):
        panels = self.panels[name]
        out = []
        for block, unit, group, groups in self.pieces(name, first, count):
            at, left = (group - first) * panels, groups * panels
            while left:
                place = max(i for i in range(len(cuts) - 1) if cuts[i] <= unit)
                take = min(left, cuts[place + 1] - unit)
                out.append((block, place, unit - cuts[place], at, take))
                unit, at, left = unit + take, at + take, left - take
        return out


class Plan:
    def __init__(self, dp, shard_rows):
        self.dp = dp
        self.shard_rows = shard_rows
        self.sections = [Section(ENC, dp, shard_rows), Section(DEC, dp, shard_rows)]
        units = max(max(s.fill) for s in self.sections)
        units += (units + VEC_UNITS) % 2
        self.vec_unit = units
        self.units = units + VEC_UNITS
        self.half = self.units // 2
        half = self.half
        self.part_cuts = [0, -(-half // 3), -(-2 * half // 3), half]
        self.cuts = self.part_cuts[:-1] + [half + c for c in self.part_cuts]
        self.half_cuts = [0, half, self.units]
        self.head_rows = 8 * -(-max(16 * max(s.panels.values()) for s in self.sections) // 8)
        self.tail_units = max(max(s.panels.values()) for s in self.sections)
        self.pack_base = 8 * -(-shard_rows // 8)
        self.pack_rows = shard_rows + self.head_rows
        self.pack_index = np.zeros((2, dp, self.units * 16), np.int32)
        self.tail_rows = 16 * (self.tail_units + VEC_UNITS)
        self.zero_row = self.units * 16 + self.tail_rows
        self.unpack_index = np.full((2, dp, shard_rows), self.zero_row, np.int32)
        self.tail_start = np.zeros((2, dp), np.int32)
        for s, section in enumerate(self.sections):
            for b in range(dp):
                self.tail_start[s, b] = max(section.fill[b] - self.tail_units, 0)
            for name, group, row, panels, block, unit in section.groups:
                for panel in range(panels):
                    for r in range(GROUP):
                        self.place(s, block, (unit + panel) * 16 + r, row + r * panels + panel)
            for row, panels, block, at in section.vectors.values():
                for panel in range(panels):
                    self.place(s, block, self.vec_unit * 16 + at + panel, row + panel)

    def bins(self, s):
        if s == 0:
            return [(0, self.dp // 2), (self.dp // 2, self.dp - self.dp // 2)]
        used = self.sections[1].blocks_used
        main = 1 << (used.bit_length() - 1)
        return [(0, main), (main, max(used - main, 1))]

    def tail_parts(self):
        first, count = self.bins(1)[1]
        section = self.sections[1]
        most = max(section.fill[first : first + count], default=0)
        if any(v[2] >= first for v in section.vectors.values()):
            most = self.units
        held = [u % self.half for u in range(most)]
        cuts = self.part_cuts
        return [p for p in range(3) if any(cuts[p] <= u < cuts[p + 1] for u in held)]

    def place(self, s, block, block_row, flat_row):
        local = flat_row - block * self.shard_rows
        assert 0 <= local < self.pack_rows
        gap = self.pack_base - self.shard_rows if local >= self.shard_rows else 0
        self.pack_index[s, block, block_row] = local + gap
        owner, at = divmod(flat_row, self.shard_rows)
        if owner == block:
            self.unpack_index[s, owner, at] = block_row
        else:
            assert owner == block + 1
            if block_row >= self.vec_unit * 16:
                source = self.tail_units * 16 + block_row - self.vec_unit * 16
            else:
                source = block_row - int(self.tail_start[s, block]) * 16
                assert 0 <= source < self.tail_units * 16
            self.unpack_index[s, owner, at] = self.units * 16 + source


def move_rows_in(index_ref, held, done, count):
    def eight(i, carry):
        for j in range(8):
            row = i * 8 + j
            done[pl.ds(row, 1), :] = held[pl.ds(index_ref[row], 1), :]
        return carry

    lax.fori_loop(0, count // 8, eight, 0)
    for row in range(count // 8 * 8, count):
        done[pl.ds(row, 1), :] = held[pl.ds(index_ref[row], 1), :]


def pack_kernel(base, index_ref, flat, following, out_ref, held, done, sems):
    rows, more = flat.shape[0], following.shape[0]
    copies = [
        pltpu.make_async_copy(flat.at[:, 0], held.at[pl.ds(0, rows)], sems.at[0]),
        pltpu.make_async_copy(following.at[:, 0], held.at[pl.ds(base, more)], sems.at[1]),
    ]
    for copy in copies:
        copy.start()
    for copy in copies:
        copy.wait()
    count = done.shape[0]
    move_rows_in(index_ref, held, done, count)
    out_ref[...] = done[...].reshape(out_ref.shape).astype(BF16)


def pack(plan, index, flat, following):
    count = plan.units * 16
    return pl.pallas_call(
        functools.partial(pack_kernel, plan.pack_base),
        out_shape=jax.ShapeDtypeStruct((plan.units, 16, 128), BF16),
        in_specs=[IN_SMEM, ANY, ANY],
        out_specs=IN_VMEM,
        scratch_shapes=[
            pltpu.VMEM((plan.pack_base + plan.head_rows, 128), F32),
            pltpu.VMEM((count, 128), F32),
            pltpu.SemaphoreType.DMA((2,)),
        ],
        compiler_params=pltpu.CompilerParams(vmem_limit_bytes=32 * 1024 * 1024),
        name="pack_rows",
    )(index, flat, following)


def unpack_kernel(zero_row, rows, index_ref, block, tail, out_ref, squares, held):
    at = 0
    for source in (block, tail):
        size = source.shape[0] * 16
        held[pl.ds(at, size), :] = source[...].reshape(size, 128)
        at += size
    held[pl.ds(zero_row, 8), :] = jnp.zeros((8, 128), F32)
    out_ref[pl.ds(out_ref.shape[0] - 16, 16), :] = jnp.zeros((16, 128), F32)
    move_rows_in(index_ref, held, out_ref, rows)

    def body(i, total):
        value = out_ref[pl.ds(pl.multiple_of(i * 8, 8), 8), :]
        return total + value * value

    squares[...] = lax.fori_loop(
        0, out_ref.shape[0] // 8, body, jnp.zeros((8, 128), F32), unroll=8
    )


def unpack(plan, index, block, tail):
    rows = plan.shard_rows
    padded = 16 * -(-rows // 16)
    return pl.pallas_call(
        functools.partial(unpack_kernel, plan.zero_row, rows),
        out_shape=[
            jax.ShapeDtypeStruct((padded, 128), F32),
            jax.ShapeDtypeStruct((8, 128), F32),
        ],
        in_specs=[IN_SMEM, IN_VMEM, IN_VMEM],
        out_specs=[IN_VMEM, IN_VMEM],
        scratch_shapes=[pltpu.VMEM((plan.zero_row + 8, 128), F32)],
        compiler_params=pltpu.CompilerParams(vmem_limit_bytes=32 * 1024 * 1024),
        name="unpack_rows",
    )(index, block, tail)


def update_kernel(rows, chunk, factor_ref, total, *refs):
    states, outs, held, made, in_sems, out_sems = (
        refs[:4], refs[4:8], refs[8:12], refs[12:16], refs[16], refs[17],
    )
    starts = list(range(0, rows, chunk))
    sizes = [min(chunk, rows - at) for at in starts]
    loads = [
        [
            pltpu.make_async_copy(
                source.at[pl.ds(at, size), 0], ref.at[pl.ds(at, size)], in_sems.at[k, j]
            )
            for j, (source, ref) in enumerate(zip(states, held))
        ]
        for k, (at, size) in enumerate(zip(starts, sizes))
    ]
    for group in loads:
        for copy in group:
            copy.start()
    stores = []
    factor = factor_ref[0]
    for k, (at, size) in enumerate(zip(starts, sizes)):
        for copy in loads[k]:
            copy.wait()

        def body(i, carry):
            here = pl.ds(pl.multiple_of(at + i * 16, 8), 16)
            master, first, second, ema = (ref[here, :] for ref in held)
            clipped = total[here, :] * factor
            new_first = beta_one * first + (1.0 - beta_one) * clipped
            new_second = beta_two * second + (1.0 - beta_two) * clipped * clipped
            first_hat = new_first * (1.0 / (1.0 - beta_one**STEP))
            second_hat = new_second * (1.0 / (1.0 - beta_two**STEP))
            new_master = master - learn_rate * (
                first_hat / (jnp.sqrt(second_hat) + adam_epsilon) + weight_decay * master
            )
            made[0][here, :] = new_master
            made[1][here, :] = new_first
            made[2][here, :] = new_second
            made[3][here, :] = average_keep * ema + (1.0 - average_keep) * new_master
            return carry

        lax.fori_loop(0, -(-size // 16), body, 0, unroll=2)
        for j in range(4):
            copy = pltpu.make_async_copy(
                made[j].at[pl.ds(at, size)], outs[j].at[pl.ds(at, size), 0], out_sems.at[k, j]
            )
            copy.start()
            stores.append(copy)
    for copy in stores:
        copy.wait()


def update(plan, factor, total, states):
    rows = plan.shard_rows
    chunk = 16 * -(-rows // (16 * 4))
    padded = 16 * -(-rows // 16)
    count = -(-rows // chunk)
    return pl.pallas_call(
        functools.partial(update_kernel, rows, chunk),
        out_shape=[jax.ShapeDtypeStruct((rows, 1, 128), F32)] * 4,
        in_specs=[IN_SMEM, IN_VMEM, *[ANY] * 4],
        out_specs=[ANY] * 4,
        scratch_shapes=[
            *[pltpu.VMEM((padded, 128), F32)] * 8,
            pltpu.SemaphoreType.DMA((count, 4)),
            pltpu.SemaphoreType.DMA((count, 4)),
        ],
        compiler_params=pltpu.CompilerParams(vmem_limit_bytes=40 * 1024 * 1024),
        name="update_states",
    )(factor, total, *states)


def dot(a, b):
    return lax.dot_general(a, b, (((1,), (0,)), ((), ())), preferred_element_type=F32)


def dot_nt(a, b):
    return lax.dot_general(a, b, (((1,), (1,)), ((), ())), preferred_element_type=F32)


def dot_tn(a, b):
    return lax.dot_general(a, b, (((0,), (0,)), ((), ())), preferred_element_type=F32)


def for_rows(count, size, step, unroll=1):
    def body(i, carry):
        step(pl.multiple_of(i * size, size))
        return carry

    lax.fori_loop(0, count // size, body, 0, unroll=unroll)


def columns(weight, panels, depth, pair):
    halves = [
        weight[:, 2 * pair + i].reshape(depth, 128)
        for i in range(2)
    ]
    return jnp.concatenate(halves, axis=1)


def row_band(weight, panels, band):
    parts = [weight[pl.ds(band * 16, 16), i].reshape(256, 128) for i in range(panels)]
    return jnp.concatenate(parts, axis=1)


def times_columns(left, weight, panels, depth, acc, finish):
    def body(pair, carry):
        acc[...] = dot(left[...], columns(weight, panels, depth, pair))
        finish(pair)
        return carry

    lax.fori_loop(0, panels // 2, body, 0)


def lanes(pair):
    return pl.ds(pl.multiple_of(pair * 256, 256), 256)


def norm_block(count):
    return next(n for n in (224, 208, 112, 104, 16) if count % n == 0)


def norm_rows(x, width):
    mean = jnp.sum(x, axis=1, keepdims=True) * (1.0 / width)
    centre = x - mean
    spread = jnp.sum(centre * centre, axis=1, keepdims=True) * (1.0 / width)
    rstd = lax.rsqrt(spread + norm_epsilon)
    return centre * rstd, rstd


def norm_forward(x_ref, gain, shift, out_ref, count, width):
    size = norm_block(count)

    def step(at):
        hat, _ = norm_rows(x_ref[pl.ds(at, size), :], width)
        out_ref[pl.ds(at, size), :] = (hat * gain + shift).astype(out_ref.dtype)

    for_rows(count, size, step)


def norm_backward(x_ref, gain, grad_of, put, count, width):
    size = norm_block(count)

    def body(i, carry):
        gain_sum, shift_sum = carry
        at = pl.multiple_of(i * size, size)
        hat, rstd = norm_rows(x_ref[pl.ds(at, size), :], width)
        grad = grad_of(at, size)
        gain_sum = gain_sum + jnp.sum((grad * hat).reshape(size // 8, 8, width), axis=0)
        shift_sum = shift_sum + jnp.sum(grad.reshape(size // 8, 8, width), axis=0)
        scaled = grad * gain
        first = jnp.sum(scaled, axis=1, keepdims=True) * (1.0 / width)
        second = jnp.sum(scaled * hat, axis=1, keepdims=True) * (1.0 / width)
        put(at, size, rstd * (scaled - first - hat * second))
        return gain_sum, shift_sum

    zero = jnp.zeros((8, width), F32)
    gain_sum, shift_sum = lax.fori_loop(0, count // size, body, (zero, zero))
    return jnp.sum(gain_sum, axis=0, keepdims=True), jnp.sum(shift_sum, axis=0, keepdims=True)


def head_masks(size):
    lane = lax.broadcasted_iota(jnp.int32, (1, 128), 1)
    return [
        jnp.where((lane >= h * size) & (lane < (h + 1) * size), 1.0, 0.0).astype(BF16)
        for h in range(128 // size)
    ]


def softmax_rows(scores, limit):
    key = lax.broadcasted_iota(jnp.int32, scores.shape, 1)
    scores = jnp.where(key < limit, scores, -1e30)
    top = jnp.max(scores, axis=1, keepdims=True)
    raised = jnp.exp(scores - top)
    return raised * (1.0 / jnp.sum(raised, axis=1, keepdims=True))


def attention_forward(mixed, out, limit_of, images, rows, width, size):
    panels = width // 128
    masks = head_masks(size)

    def body(step, carry):
        image, panel = step // panels, step % panels
        here = pl.ds(pl.multiple_of(image * rows, 16), rows)

        def part(third):
            return mixed[here, pl.ds(pl.multiple_of((third * panels + panel) * 128, 128), 128)]

        query, keys, values = part(0), part(1), part(2)
        limit = limit_of(image)
        total = jnp.zeros((rows, 128), F32)
        for mask in masks:
            probs = softmax_rows(dot_nt(query * mask, keys), limit).astype(BF16)
            total = total + dot(probs, values * mask)
        out[here, pl.ds(pl.multiple_of(panel * 128, 128), 128)] = total.astype(BF16)
        return carry

    lax.fori_loop(0, images * panels, body, 0)


def attention_backward(mixed, grad_out, grad_mixed, limit_of, images, rows, width, size):
    panels = width // 128
    masks = head_masks(size)

    def body(step, carry):
        image, panel = step // panels, step % panels
        here = pl.ds(pl.multiple_of(image * rows, 16), rows)

        def place(third):
            return pl.ds(pl.multiple_of((third * panels + panel) * 128, 128), 128)

        query, keys, values = (mixed[here, place(third)] for third in range(3))
        grad = grad_out[here, place(0)]
        limit = limit_of(image)
        zero = jnp.zeros((rows, 128), F32)
        grad_query, grad_keys, grad_values = zero, zero, zero
        for mask in masks:
            masked_query = query * mask
            masked_grad = grad * mask
            probs = softmax_rows(dot_nt(masked_query, keys), limit)
            grad_probs = dot_nt(masked_grad, values)
            inner = jnp.sum(probs * grad_probs, axis=1, keepdims=True)
            grad_scores = (probs * (grad_probs - inner)).astype(BF16)
            grad_values = grad_values + dot_tn(probs.astype(BF16), masked_grad)
            grad_query = grad_query + dot(grad_scores, keys * mask)
            grad_keys = grad_keys + dot_tn(grad_scores, masked_query)
        grad_mixed[here, place(0)] = (grad_query * (1.0 / math.sqrt(size))).astype(BF16)
        grad_mixed[here, place(1)] = grad_keys.astype(BF16)
        grad_mixed[here, place(2)] = grad_values.astype(BF16)
        return carry

    lax.fori_loop(0, images * panels, body, 0)


def gelu_parts(value):
    bell = 0.5 * (1.0 + lax.erf(value * math.sqrt(0.5)))
    slope = bell + value * (jnp.exp(value * value * -0.5) * (1.0 / math.sqrt(2.0 * math.pi)))
    return value * bell, slope


class Shape:
    def __init__(self, images, rows, width, heads, hidden):
        self.images, self.rows, self.width = images, rows, width
        self.size = width // heads
        self.hidden = hidden
        self.count = images * rows


def block_forward(sh, x0, n1, mixed, o, x1, n2, g, gp, y, w, vec, limit_of, acc, ready, saved):
    width, hidden, count = sh.width, sh.hidden, sh.count
    panels = width // 128
    norm_forward(x0, vec("g1"), vec("b1"), n1, count, width)
    saved(n1)
    ready("qkv")

    def put_mixed(pair):
        scale = jnp.where(pair < panels // 2, 1.0 / math.sqrt(sh.size), 1.0)

        def step(at):
            mixed[pl.ds(at, 16), lanes(pair)] = (acc[pl.ds(at, 16), :] * scale).astype(BF16)

        for_rows(count, 16, step, 4)

    times_columns(n1, w["qkv"], 3 * panels, width, acc, put_mixed)
    saved(mixed)
    attention_forward(mixed, o, limit_of, sh.images, sh.rows, width, sh.size)
    saved(o)
    ready("proj")

    def put_sum(base, out):
        def finish(pair):
            def step(at):
                here = pl.ds(at, 16)
                out[here, lanes(pair)] = base[here, lanes(pair)] + acc[here, :]

            for_rows(count, 16, step, 4)

        return finish

    times_columns(o, w["proj"], panels, width, acc, put_sum(x0, x1))
    saved(x1)
    norm_forward(x1, vec("g2"), vec("b2"), n2, count, width)
    saved(n2)
    ready("fc1")

    def put_hidden(pair):
        def step(at):
            here = pl.ds(at, 16)
            value, slope = gelu_parts(acc[here, :])
            g[here, lanes(pair)] = value.astype(BF16)
            gp[here, lanes(pair)] = slope

        for_rows(count, 16, step, 2)

    times_columns(n2, w["fc1"], hidden // 128, width, acc, put_hidden)
    saved(g)
    saved(gp)
    ready("fc2")
    times_columns(g, w["fc2"], panels, hidden, acc, put_sum(x1, y))
    saved(y)


class Gradients:
    def __init__(self, plan, s, own, stage, sems, targets):
        self.plan, self.section, self.own = plan, plan.sections[s], own
        self.bins = plan.bins(s)
        self.stage, self.sems, self.targets = stage, sems, targets
        self.turn = 0
        self.flying = [[], []]

    def copy_out(self, source, block, place, unit, take, sem):
        which = max(i for i, (first, _) in enumerate(self.bins) if first <= block)
        block = block - self.bins[which][0]
        side, part = place // 3, place % 3
        keep, send = (self.targets[which * 6 + i * 3 + part] for i in range(2))

        def to(target):
            return pltpu.make_async_copy(source, target.at[block, pl.ds(unit, take)], sem)

        @pl.when(self.own == side)
        def _():
            to(keep).start()

        @pl.when(self.own != side)
        def _():
            to(send).start()

        return to(keep)

    def drain(self, slot):
        for copy in self.flying[slot]:
            copy.wait()
        self.flying[slot] = []

    def weight(self, name, left, depth, right, turned):
        panels = self.section.panels[name]
        for band in range(depth // 256):
            slot = self.turn % 2
            self.turn += 1
            self.drain(slot)
            stage = self.stage.at[slot]
            turned[...] = left[:, band * 256 : band * 256 + 256].T

            def body(pair, carry):
                value = dot(turned[...], right[:, lanes(pair)])
                for i in range(2):
                    stage[pl.ds(2 * pair + i, 16, stride=panels)] = value[
                        :, i * 128 : i * 128 + 128
                    ].reshape(16, 16, 128)
                return carry

            lax.fori_loop(0, panels // 2, body, 0)
            for block, place, unit, at, take in self.section.runs(
                name, self.plan.cuts, band * 16, 16
            ):
                self.flying[slot].append(
                    self.copy_out(
                        stage.at[pl.ds(at, take)], block, place, unit, take, self.sems.at[slot]
                    )
                )

    def finish(self, values, scratch):
        vectors = self.section.vectors
        blocks = sorted({vectors[name][2] for name in values})
        for k, block in enumerate(blocks):
            scratch[k] = jnp.zeros((VEC_UNITS, 16, 128), F32)
            for name, (_, panels, at_block, at) in vectors.items():
                if at_block != block:
                    continue
                for panel in range(panels):
                    unit, row = divmod(at + panel, 16)
                    scratch[k, unit, row : row + 1, :] = values[name][
                        :, panel * 128 : panel * 128 + 128
                    ]
        unit = self.plan.vec_unit - self.plan.cuts[5]
        assert unit >= 0
        copies = [
            self.copy_out(scratch.at[k], block, 5, unit, VEC_UNITS, self.sems.at[2])
            for k, block in enumerate(blocks)
        ]
        for copy in copies:
            copy.wait()
        self.drain(0)
        self.drain(1)


class Backward:
    def __init__(self, sh, w, vec, limit_of, grads, values, acc, turned, ready):
        self.sh, self.w, self.vec, self.limit_of = sh, w, vec, limit_of
        self.grads, self.values, self.acc, self.turned, self.ready = grads, values, acc, turned, ready
        self.panels = sh.width // 128

    def round_stream(self, dy, dyb):
        def step(at):
            dyb[pl.ds(at, 16), :] = dy[pl.ds(at, 16), :].astype(BF16)

        for_rows(self.sh.count, 16, step, 4)

    def bands(self, left, name, count, put):
        acc = self.acc
        panels = self.grads.section.panels[name]

        def body(band, carry):
            acc[...] = dot_nt(left[...], row_band(self.w[name], panels, band))

            def step(at):
                here = pl.ds(at, 16)
                put(here, lanes(band), acc[here, :])

            for_rows(self.sh.count, 16, step, 4)
            return carry

        lax.fori_loop(0, count // 256, body, 0)

    def through_norm(self, x, dn, dy, gain, shift, dn_is=None):
        def from_dn(at, size):
            return dn[pl.ds(at, size), :]

        def into_stream(at, size, value):
            dy[pl.ds(at, size), :] = dy[pl.ds(at, size), :] + value

        self.values[gain], self.values[shift] = norm_backward(
            x, self.vec(gain), from_dn, into_stream, self.sh.count, self.sh.width
        )

    def second_product(self, dy, dyb, g, gp):
        self.round_stream(dy, dyb)
        self.ready("fc2", g)
        self.grads.weight("fc2", g, self.sh.hidden, dyb, self.turned)
        self.ready(None, gp)

        def put(here, there, value):
            g[here, there] = (value * gp[here, there]).astype(BF16)

        self.bands(dyb, "fc2", self.sh.hidden, put)

    def first_product(self, dy, g, n2, x1, dn):
        def put(here, there, value):
            dn[here, there] = value

        self.ready("fc1", n2)
        self.grads.weight("fc1", n2, self.sh.width, g, self.turned)
        self.bands(g, "fc1", self.sh.width, put)
        self.ready(None, x1)
        self.through_norm(x1, dn, dy, "g2", "b2")

    def attention(self, dy, dyb, o, mixed, dmixed):
        sh = self.sh
        self.round_stream(dy, dyb)
        self.ready("proj", o)
        self.grads.weight("proj", o, sh.width, dyb, self.turned)

        def put(here, there, value):
            o[here, there] = value.astype(BF16)

        self.bands(dyb, "proj", sh.width, put)
        self.ready(None, mixed)
        attention_backward(mixed, o, dmixed, self.limit_of, sh.images, sh.rows, sh.width, sh.size)

    def mixing(self, dy, dmixed, n1, x0, dn):
        def put(here, there, value):
            dn[here, there] = value

        self.ready("qkv", n1)
        self.grads.weight("qkv", n1, self.sh.width, dmixed, self.turned)
        self.bands(dmixed, "qkv", self.sh.width, put)
        self.ready(None, x0)
        self.through_norm(x0, dn, dy, "g1", "b1")


def load_vectors(plan, s, gathered, held, vec_ref, sem):
    section = plan.sections[s]
    blocks = sorted({v[2] for v in section.vectors.values()})
    copies = [
        pltpu.make_async_copy(
            gathered.at[1, block, pl.ds(plan.vec_unit - plan.half, VEC_UNITS)], held.at[k], sem
        )
        for k, block in enumerate(blocks)
    ]
    for copy in copies:
        copy.start()
    names = {name: i for i, name in enumerate(section.vectors)}

    def finish():
        for copy in copies:
            copy.wait()
        for k, block in enumerate(blocks):
            rows = held[k].reshape(16 * VEC_UNITS, 128).astype(F32)
            for name, (_, panels, at_block, at) in section.vectors.items():
                if at_block != block:
                    continue
                i = names[name]
                for panel in range(panels):
                    vec_ref[i : i + 1, panel * 128 : panel * 128 + 128] = rows[
                        at + panel : at + panel + 1, :
                    ]
        return lambda name: vec_ref[names[name] : names[name] + 1, :]

    return finish


def load_weights(plan, s, gathered, w, sems):
    section = plan.sections[s]
    copies = {}
    for k, (name, ref) in enumerate(w.items()):
        panels = section.panels[name]
        flat = ref.reshape(ref.shape[0] * panels, 16, 128)
        copies[name] = [
            pltpu.make_async_copy(
                gathered.at[side, block, pl.ds(unit, take)], flat.at[pl.ds(at, take)], sems.at[k]
            )
            for block, side, unit, at, take in section.runs(name, plan.half_cuts)
        ]
        for copy in copies[name]:
            copy.start()

    def ready(name):
        for copy in copies.get(name, ()):
            copy.wait()

    return ready


def weight_scratch(layout, names):
    shapes = dict(layout)
    return [
        pltpu.VMEM((shapes[n][0] // GROUP, shapes[n][1] // 128, GROUP, 128), BF16)
        for n in names
    ]


def picks(perm_ref, image):
    here = pl.ds(pl.multiple_of(image * ROWS_D, 16), ROWS_D)
    patch = lax.broadcasted_iota(jnp.int32, (ROWS_D, ROWS_D), 1)
    return jnp.where(perm_ref[here, :] == patch, 1.0, 0.0).astype(BF16)


W_ENC = ["patch", "qkv", "proj", "fc1", "fc2"]


def encoder_kernel(plan, sh, refs):
    (info, gathered, patches, perm, pos, pp_out, x0_out, n1_out, mixed_out, o_out, x1_out, n2_out,
     g_out, gp_out, y_out, latent_out, w_patch, w_qkv, w_proj, w_fc1, w_fc2, held, vec_ref, pp, xe,
     x0, n1, mixed, o, x1, n2, g, gp, y, latent, acc, w_sems, out_sems) = refs
    w = dict(zip(W_ENC, (w_patch, w_qkv, w_proj, w_fc1, w_fc2)))
    finish_vec = load_vectors(plan, 0, gathered, held, vec_ref, w_sems.at[5])
    ready = load_weights(plan, 0, gathered, w, w_sems)
    outs = []

    targets = [(pp, pp_out), (x0, x0_out), (n1, n1_out), (mixed, mixed_out), (o, o_out),
               (x1, x1_out), (n2, n2_out), (g, g_out), (gp, gp_out), (y, y_out),
               (latent, latent_out)]

    def saved(ref):
        for k, (source, target) in enumerate(targets):
            if source is ref:
                copy = pltpu.make_async_copy(source, target, out_sems.at[k])
                copy.start()
                outs.append(copy)

    def gather(image, carry):
        chosen = picks(perm, image)
        pp[image] = dot(chosen, patches[image]).astype(BF16)
        here = pl.ds(pl.multiple_of(image * ROWS_E, 16), ROWS_E)
        xe[here, :] = pp[image, 0:ROWS_E, :]
        few = chosen[0:ROWS_E, :]
        x0[here, :] = (dot(few, pos[0]) + dot(few, pos[1])) + dot(few, pos[2])
        return carry

    lax.fori_loop(0, sh.images, gather, 0)
    saved(pp)
    vec = finish_vec()
    ready("patch")

    def put(pair):
        part = vec_ref[0:1, lanes(pair)]

        def step(at):
            here = pl.ds(at, 16)
            x0[here, lanes(pair)] = (acc[here, :] + part) + x0[here, lanes(pair)]

        for_rows(sh.count, 16, step, 4)

    times_columns(xe, w["patch"], D // 128, PIX, acc, put)
    saved(x0)
    block_forward(
        sh, x0, n1, mixed, o, x1, n2, g, gp, y, w, vec, lambda i: info[1 + i], acc, ready, saved
    )
    norm_forward(y, vec("gf"), vec("bf"), latent, sh.count, D)
    saved(latent)
    for copy in outs:
        copy.wait()


def lasting(microseconds):
    return pl.CostEstimate(
        flops=int(microseconds * 1e9), bytes_accessed=1 << 20, transcendentals=0
    )


def saved_shapes(sh):
    count, width, hidden = sh.count, sh.width, sh.hidden
    return [
        ((count, width), F32),
        ((count, width), BF16),
        ((count, 3 * width), BF16),
        ((count, width), BF16),
        ((count, width), F32),
        ((count, width), BF16),
        ((count, hidden), BF16),
        ((count, hidden), F32),
        ((count, width), F32),
    ]


def encoder(plan, sh, info, gathered, patches, perm, pos):
    saved = saved_shapes(sh)
    pp_shape = ((sh.images, ROWS_D, PIX), BF16)
    latent_shape = ((sh.count, D), BF16)
    outs = [pp_shape, *saved, latent_shape]
    holders = len({v[2] for v in plan.sections[0].vectors.values()})
    return pl.pallas_call(
        lambda *refs: encoder_kernel(plan, sh, refs),
        out_shape=[jax.ShapeDtypeStruct(*s) for s in outs],
        in_specs=[IN_SMEM, ANY, IN_VMEM, IN_VMEM, IN_VMEM],
        out_specs=[ANY] * len(outs),
        scratch_shapes=[
            *weight_scratch(ENC, W_ENC),
            pltpu.VMEM((holders, VEC_UNITS, 16, 128), BF16),
            pltpu.VMEM((8, D), F32),
            pltpu.VMEM(*pp_shape),
            pltpu.VMEM((sh.count, PIX), BF16),
            *[pltpu.VMEM(*s) for s in saved],
            pltpu.VMEM(*latent_shape),
            pltpu.VMEM((sh.count, 256), F32),
            pltpu.SemaphoreType.DMA((6,)),
            pltpu.SemaphoreType.DMA((len(outs),)),
        ],
        compiler_params=pltpu.CompilerParams(vmem_limit_bytes=VMEM_BYTES),
        cost_estimate=lasting(50),
        name="encoder_forward",
    )(info, gathered, patches, perm, pos)


W_DEC = ["embed", "qkv", "proj", "fc1", "fc2", "head"]


def decoder_kernel(plan, sh, refs):
    info, scale, gathered, latent_in, pp_in, perm, pos = refs[:7]
    targets, refs = refs[7:19], refs[19:]
    (grad_latent, loss_out,
     w_embed, w_qkv, w_proj, w_fc1, w_fc2, w_head, held, vec_ref, pp, latent, embedded, x0, n1,
     mixed, o, x1, n2, g, gp, y, f, dn, guess, acc, acc_e, turned, turned_e, stage, vec_stage, w_sems,
     in_sems, grad_sems) = refs
    w = dict(zip(W_DEC, (w_embed, w_qkv, w_proj, w_fc1, w_fc2, w_head)))
    copy_latent = pltpu.make_async_copy(latent_in, latent, in_sems.at[0])
    copy_pp = pltpu.make_async_copy(pp_in, pp, in_sems.at[1])
    copy_latent.start()
    finish_vec = load_vectors(plan, 1, gathered, held, vec_ref, w_sems.at[6])
    ready = load_weights(plan, 1, gathered, w, w_sems)
    copy_pp.start()
    images, count = sh.images, sh.count
    count_e = images * ROWS_E
    vec = finish_vec()
    copy_latent.wait()
    ready("embed")

    def put_embedded(pair):
        def step(at):
            embedded[pl.ds(at, 16), lanes(pair)] = acc_e[pl.ds(at, 16), :]

        for_rows(count_e, 16, step, 4)

    times_columns(latent, w["embed"], DD // 128, D, acc_e, put_embedded)

    def tokens(image, carry):
        chosen = picks(perm, image)
        place = (dot(chosen, pos[0]) + dot(chosen, pos[1])) + dot(chosen, pos[2])
        start = pl.multiple_of(image * ROWS_D, 16)
        kept = info[1 + image]
        token = vec_ref[0:1, :]
        few = embedded[pl.ds(pl.multiple_of(image * ROWS_E, 16), ROWS_E), :]
        rank = lax.broadcasted_iota(jnp.int32, (ROWS_E, DD), 0)
        x0[pl.ds(start, ROWS_E), :] = jnp.where(rank < kept, few, token) + place[:ROWS_E, :]
        x0[pl.ds(start + ROWS_E, ROWS_D - ROWS_E), :] = token + place[ROWS_E:, :]
        return carry

    lax.fori_loop(0, images, tokens, 0)
    block_forward(
        sh, x0, n1, mixed, o, x1, n2, g, gp, y, w, vec, lambda i: NP, acc, ready, lambda ref: None
    )
    norm_forward(y, vec("gf"), vec("bf"), f, count, DD)
    ready("head")
    copy_pp.wait()
    factor = scale[0]

    def predict_image(image, total):
        start = pl.multiple_of(image * ROWS_D, 16)
        kept = info[1 + image]
        here = pl.ds(start, ROWS_D)
        for pair in range(PIX // 256):
            guess[:, pair * 256 : pair * 256 + 256] = dot(
                f[here, :], columns(w["head"], PIX // 128, DD, pair)
            )

        def rows(i, total):
            at = pl.multiple_of(i * 16, 16)
            target, _ = norm_rows(pp[image, pl.ds(at, 16), :].astype(F32), PIX)
            off = guess[pl.ds(at, 16), :] - target
            rank = lax.broadcasted_iota(jnp.int32, (16, PIX), 0) + at
            off = jnp.where((rank >= kept) & (rank < NP), off, 0.0)
            pp[image, pl.ds(at, 16), :] = (off * factor).astype(BF16)
            return total + jnp.sum((off * off).reshape(2, 8, PIX), axis=0)

        return lax.fori_loop(0, ROWS_D // 16, rows, total)

    total = lax.fori_loop(0, images, predict_image, jnp.zeros((8, PIX), F32))
    total = jnp.sum(jnp.sum(total, axis=0, keepdims=True), axis=1, keepdims=True)
    loss_out[...] = jnp.broadcast_to(total * (1.0 / PIX), (8, 128))

    grads = Gradients(plan, 1, info[0], stage, grad_sems, targets)
    values = {}
    back = Backward(
        sh, w, vec, lambda i: NP, grads, values, acc, turned, lambda name, ref: None
    )
    dpred = pp.reshape(count, PIX)
    grads.weight("head", f, DD, dpred, turned)

    def put_dn(here, there, value):
        dn[here, there] = value

    back.bands(dpred, "head", DD, put_dn)

    def from_dn(at, size):
        return dn[pl.ds(at, size), :]

    def put_y(at, size, value):
        y[pl.ds(at, size), :] = value

    values["gf"], values["bf"] = norm_backward(y, vec("gf"), from_dn, put_y, count, DD)
    back.second_product(y, f, g, gp)
    back.first_product(y, g, n2, x1, dn)
    dmixed = g.at[:, pl.ds(0, 3 * DD)]
    back.attention(y, f, o, mixed, dmixed)
    back.mixing(y, dmixed, n1, x0, dn)

    def split(image, total):
        start = pl.multiple_of(image * ROWS_D, 16)
        kept = info[1 + image]

        def rows(i, total):
            at = pl.multiple_of(i * 16, 16)
            grad = y[pl.ds(start + at, 16), :]
            rank = lax.broadcasted_iota(jnp.int32, (16, DD), 0) + at
            free = jnp.where(rank >= kept, grad, 0.0)

            @pl.when(i < ROWS_E // 16)
            def _():
                taken = jnp.where(rank < kept, grad, 0.0).astype(BF16)
                n1[pl.ds(pl.multiple_of(image * ROWS_E, 16) + at, 16), :] = taken

            return total + jnp.sum(free.reshape(2, 8, DD), axis=0)

        return lax.fori_loop(0, ROWS_D // 16, rows, total)

    total = lax.fori_loop(0, images, split, jnp.zeros((8, DD), F32))
    values["mask"] = jnp.sum(total, axis=0, keepdims=True)
    placed = n1.at[pl.ds(0, count_e)]
    grads.weight("embed", latent, D, placed, turned_e)

    def latent_band(band, carry):
        acc_e[...] = dot_nt(placed[...], row_band(w["embed"], DD // 128, band))

        def step(at):
            grad_latent[pl.ds(at, 16), lanes(band)] = acc_e[pl.ds(at, 16), :].astype(BF16)

        for_rows(count_e, 16, step, 4)
        return carry

    lax.fori_loop(0, D // 256, latent_band, 0)
    grads.finish(values, vec_stage)


def grad_shapes(plan, s):
    cuts = plan.part_cuts
    return [
        jax.ShapeDtypeStruct((count, cuts[part + 1] - cuts[part], 16, 128), F32)
        for _, count in plan.bins(s)
        for _ in range(2)
        for part in range(3)
    ]


def decoder(plan, sh, info, scale, gathered, latent, pp, perm, pos):
    count_e = sh.images * ROWS_E
    holders = len({v[2] for v in plan.sections[1].vectors.values()})
    saved = saved_shapes(sh)
    most = max(plan.sections[1].panels.values())
    return pl.pallas_call(
        lambda *refs: decoder_kernel(plan, sh, refs),
        out_shape=[
            *grad_shapes(plan, 1),
            jax.ShapeDtypeStruct((count_e, D), BF16),
            jax.ShapeDtypeStruct((8, 128), F32),
        ],
        in_specs=[IN_SMEM, IN_SMEM, ANY, ANY, ANY, IN_VMEM, IN_VMEM],
        out_specs=[*[ANY] * 12, IN_VMEM, IN_VMEM],
        scratch_shapes=[
            *weight_scratch(DEC, W_DEC),
            pltpu.VMEM((holders, VEC_UNITS, 16, 128), BF16),
            pltpu.VMEM((8, DD), F32),
            pltpu.VMEM((sh.images, ROWS_D, PIX), BF16),
            pltpu.VMEM((count_e, D), BF16),
            pltpu.VMEM((count_e, DD), F32),
            *[pltpu.VMEM(*s) for s in saved],
            pltpu.VMEM((sh.count, DD), BF16),
            pltpu.VMEM((sh.count, DD), F32),
            pltpu.VMEM((ROWS_D, PIX), F32),
            pltpu.VMEM((sh.count, 256), F32),
            pltpu.VMEM((count_e, 256), F32),
            pltpu.VMEM((256, sh.count), BF16),
            pltpu.VMEM((256, count_e), BF16),
            pltpu.VMEM((2, 16 * most, 16, 128), F32),
            pltpu.VMEM((holders, VEC_UNITS, 16, 128), F32),
            pltpu.SemaphoreType.DMA((7,)),
            pltpu.SemaphoreType.DMA((2,)),
            pltpu.SemaphoreType.DMA((3,)),
        ],
        compiler_params=pltpu.CompilerParams(vmem_limit_bytes=VMEM_BYTES),
        cost_estimate=lasting(160),
        name="decoder_both",
    )(info, scale, gathered, latent, pp, perm, pos)


class Stage:
    def __init__(self, plan, sh, weights, reads, temps, outs, most, cost, name, body):
        self.plan, self.sh, self.weights, self.reads = plan, sh, weights, reads
        self.temps, self.outs, self.most, self.cost, self.name = temps, outs, most, cost, name
        self.body = body

    def kernel(self, blocks, *refs):
        refs = list(refs)

        def take(count):
            got = refs[:count]
            del refs[:count]
            return got

        plan, sh = self.plan, self.sh
        info, gathered = take(2)
        sources = dict(zip(self.reads, take(len(self.reads))))
        take(blocks)
        targets = take(len(grad_shapes(plan, 0)))
        results = dict(zip(self.outs, take(len(self.outs))))
        w = dict(zip(self.weights, take(len(self.weights))))
        here = dict(zip(self.reads, take(len(self.reads))))
        temps = dict(zip(self.temps, take(len(self.temps))))
        held, vec_ref, acc, turned, stage, vec_stage, w_sems, in_sems, grad_sems = refs
        finish_vec = load_vectors(plan, 0, gathered, held, vec_ref, w_sems.at[len(w)])
        loads = {}
        for k, (name, ref) in enumerate(here.items()):
            if name == "xe":
                copies = [
                    pltpu.make_async_copy(
                        sources[name].at[i, pl.ds(0, ROWS_E)],
                        ref.at[pl.ds(i * ROWS_E, ROWS_E)],
                        in_sems.at[k],
                    )
                    for i in range(sh.images)
                ]
            else:
                copies = [pltpu.make_async_copy(sources[name], ref, in_sems.at[k])]
            for copy in copies:
                copy.start()
            loads[id(ref)] = copies
        weights_ready = load_weights(plan, 0, gathered, w, w_sems)
        vec = finish_vec()

        def ready(name, ref=None):
            for copy in loads.pop(id(ref), ()):
                copy.wait()
            if name is not None:
                weights_ready(name)

        values = {}
        grads = Gradients(plan, 0, info[0], stage, grad_sems, targets)
        back = Backward(
            sh, w, vec, lambda i: info[1 + i], grads, values, acc, turned, ready
        )
        self.body(back, {**here, **temps}, results)
        assert not loads
        grads.finish(values, vec_stage)

    def __call__(self, info, gathered, arrays, blocks):
        plan, sh = self.plan, self.sh
        count, width, hidden = sh.count, sh.width, sh.hidden
        known = {
            "dz": ((count, width), BF16),
            "y": ((count, width), F32),
            "dy": ((count, width), F32),
            "x0": ((count, width), F32),
            "x1": ((count, width), F32),
            "dn": ((count, width), F32),
            "n1": ((count, width), BF16),
            "n2": ((count, width), BF16),
            "o": ((count, width), BF16),
            "dyb": ((count, width), BF16),
            "xe": ((count, PIX), BF16),
            "mixed": ((count, 3 * width), BF16),
            "dmixed": ((count, 3 * width), BF16),
            "g": ((count, hidden), BF16),
            "gp": ((count, hidden), F32),
        }
        holders = len({v[2] for v in plan.sections[0].vectors.values()})
        targets = grad_shapes(plan, 0)
        before = 2 + len(self.reads)
        got = pl.pallas_call(
            functools.partial(self.kernel, len(blocks)),
            out_shape=[*targets, *[jax.ShapeDtypeStruct(*known[n]) for n in self.outs]],
            in_specs=[IN_SMEM, *[ANY] * (1 + len(self.reads) + len(blocks))],
            out_specs=[*[ANY] * len(targets), *[IN_VMEM] * len(self.outs)],
            input_output_aliases={before + i: i for i in range(len(blocks))},
            scratch_shapes=[
                *weight_scratch(ENC, self.weights),
                *[pltpu.VMEM(*known[n]) for n in self.reads],
                *[pltpu.VMEM(*known[n]) for n in self.temps],
                pltpu.VMEM((holders, VEC_UNITS, 16, 128), BF16),
                pltpu.VMEM((8, D), F32),
                pltpu.VMEM((count, 256), F32),
                pltpu.VMEM((256, count), BF16),
                pltpu.VMEM((2, 16 * self.most, 16, 128), F32),
                pltpu.VMEM((holders, VEC_UNITS, 16, 128), F32),
                pltpu.SemaphoreType.DMA((len(self.weights) + 1,)),
                pltpu.SemaphoreType.DMA((len(self.reads),)),
                pltpu.SemaphoreType.DMA((3,)),
            ],
            compiler_params=pltpu.CompilerParams(vmem_limit_bytes=VMEM_BYTES),
            cost_estimate=lasting(self.cost),
            name=self.name,
        )(info, gathered, *[arrays[n] for n in self.reads], *blocks)
        return got[: len(targets)], dict(zip(self.outs, got[len(targets) :]))


def back_second(back, r, out):
    sh = back.sh
    back.ready(None, r["dz"])
    back.ready(None, r["y"])

    def from_latent(at, size):
        return r["dz"][pl.ds(at, size), :].astype(F32)

    def put(at, size, value):
        out["dy"][pl.ds(at, size), :] = value

    back.values["gf"], back.values["bf"] = norm_backward(
        r["y"], back.vec("gf"), from_latent, put, sh.count, D
    )
    back.second_product(out["dy"], r["dyb"], r["g"], r["gp"])

    def step(at):
        out["g"][pl.ds(at, 16), :] = r["g"][pl.ds(at, 16), :]

    for_rows(sh.count, 16, step, 2)


def copy_rows(count, source, target):
    def step(at):
        target[pl.ds(at, 16), :] = source[pl.ds(at, 16), :]

    for_rows(count, 16, step, 4)


def back_first(back, r, out):
    back.ready(None, r["dy"])
    back.ready(None, r["g"])
    copy_rows(back.sh.count, r["dy"], out["dy"])
    back.first_product(out["dy"], r["g"], r["n2"], r["x1"], r["dn"])


def back_attention(back, r, out):
    back.ready(None, r["dy"])
    back.attention(r["dy"], r["dyb"], r["o"], r["mixed"], out["dmixed"])


def back_mixing(back, r, out):
    back.ready(None, r["dy"])
    back.ready(None, r["dmixed"])
    back.mixing(r["dy"], r["dmixed"], r["n1"], r["x0"], r["dn"])

    def body(i, total):
        at = pl.multiple_of(i * 16, 16)
        grad = r["dy"][pl.ds(at, 16), :]
        r["dyb"][pl.ds(at, 16), :] = grad.astype(BF16)
        return total + jnp.sum(grad.reshape(2, 8, D), axis=0)

    total = lax.fori_loop(0, back.sh.count // 16, body, jnp.zeros((8, D), F32))
    back.values["patch_b"] = jnp.sum(total, axis=0, keepdims=True)
    back.ready(None, r["xe"])
    back.grads.weight("patch", r["xe"], PIX, r["dyb"], back.turned)


def encoder_back_stages(plan, sh):
    most = {n: plan.sections[0].panels[n] for n in ("fc1", "fc2", "qkv", "proj")}
    return [
        Stage(plan, sh, ["fc2"], ["y", "dz", "g", "gp"], ["dyb"], ["dy", "g"], most["fc2"], 25,
              "encoder_back_fc2", back_second),
        Stage(plan, sh, ["fc1"], ["g", "dy", "n2", "x1"], ["dn"], ["dy"], most["fc1"], 20,
              "encoder_back_fc1", back_first),
        Stage(plan, sh, ["proj"], ["dy", "o", "mixed"], ["dyb"], ["dmixed"], most["proj"], 35,
              "encoder_back_attention", back_attention),
        Stage(plan, sh, ["qkv"], ["dy", "dmixed", "n1", "x0", "xe"], ["dn", "dyb"], [],
              most["qkv"], 25, "encoder_back_qkv", back_mixing),
    ]


def pick(value, index, axis):
    return lax.dynamic_index_in_dim(value, index, axis, keepdims=False)


def total_of(terms):
    total = terms[0]
    for term in terms[1:]:
        total = total + term
    return total


def tie(*trees):
    return lax.optimization_barrier(trees)


class Flow:
    def __init__(self, dp, keep, send, first):
        self.dp = dp
        self.me = lax.axis_index("dp")
        self.keep, self.given = keep, send
        count = keep[0].shape[0]
        self.bits = count.bit_length() - 1
        assert count == 1 << self.bits and dp & (dp - 1) == 0
        self.all_bits = dp.bit_length() - 1
        self.first = first
        low = [b for b in range(0, self.bits, 1)]
        if dp == 64:
            low = [b for b in (0, 2, 4, 1, 3) if b < self.bits]
        turn = min(3, len(low))
        self.orders = [low[p % turn :][: turn - p % turn] + low[: p % turn] + low[turn:] for p in range(3)]
        self.left = [list(range(self.bits - 1, -1, -1)) for _ in range(3)]
        self.step = -1
        self.terms = None

    def done(self):
        return self.step == self.all_bits

    def payload(self):
        if self.step < 0:
            return list(self.given)
        out = []
        for part in range(3):
            if self.step < self.bits:
                bit = self.orders[part][self.step]
                dim = self.left[part].index(bit)
                other = 1 - (self.me >> bit & 1)
                out.append(total_of([pick(t, other, dim) for t in self.terms[part]]))
            else:
                out.append(total_of(self.terms[part]))
        return out

    def send(self, payload):
        if self.step < 0:
            return [lax.ppermute(p, "section", [(0, 1), (1, 0)]) for p in payload]
        out = []
        for part in range(3):
            if self.step < self.bits:
                flip = 1 << self.orders[part][self.step]
                pairs = [(i, i ^ flip) for i in range(self.dp)]
            else:
                flip = 1 << self.step
                pairs = [(i, i ^ flip) for i in range(self.dp) if (i ^ self.first) & flip]
            out.append(lax.ppermute(payload[part], "dp", pairs))
        return out

    def take(self, got):
        if self.step < 0:
            self.terms = [
                [v.reshape((2,) * self.bits + v.shape[1:]) for v in pair]
                for pair in zip(self.keep, got)
            ]
        elif self.step < self.bits:
            for part in range(3):
                bit = self.orders[part][self.step]
                dim = self.left[part].index(bit)
                mine = self.me >> bit & 1
                self.terms[part] = [pick(t, mine, dim) for t in self.terms[part]] + [got[part]]
                self.left[part].remove(bit)
        else:
            self.terms = [t + [g] for t, g in zip(self.terms, got)]
        self.step += 1

    def result(self):
        return jnp.concatenate([total_of(t) for t in self.terms], axis=0)


def move_on(flows, *others):
    flows = [f for f in flows if f is not None and not f.done()]
    payloads, others = tie([f.payload() for f in flows], others)
    return flows, [f.send(p) for f, p in zip(flows, payloads)], others


def arrive(flows, got):
    for flow, values in zip(flows, got):
        flow.take(values)


def sum_everywhere(dp, value):
    value = value + lax.ppermute(value, "section", [(0, 1), (1, 0)])
    bits = dp.bit_length() - 1
    for low in range(0, bits, 2):
        got = [
            lax.ppermute(value, "dp", [(i, i ^ (flip << low)) for i in range(dp)])
            for flip in range(1, 1 << min(2, bits - low))
        ]
        value = value + got[0]
        if len(got) == 3:
            value = value + (got[1] + got[2])
    return value


def sincos(width):
    places = np.arange(NP).astype(np.float32)[:, None]
    column = np.arange(width)
    rates = np.exp(
        -(np.float32(2.0) * (column // 2).astype(np.float32) / np.float32(width))
        * np.float32(math.log(10000.0))
    ).astype(np.float32)
    phases = (places * rates[None, :]).astype(np.float32)
    table = np.where(
        column[None, :] % 2 == 0, np.sin(phases.astype(np.float64)), np.cos(phases.astype(np.float64))
    ).astype(np.float32)
    parts = []
    left = np.zeros((ROWS_D, width), np.float32)
    left[:NP] = table
    for _ in range(3):
        high = left.astype(jnp.bfloat16)
        parts.append(high)
        left = left - high.astype(np.float32)
    return np.stack(parts)


def on_device(patches, keep, perm, master, first, second, ema):
    dp = lax.axis_size("dp")
    section = lax.axis_index("section")
    me = lax.axis_index("dp")
    shard = master.shape[1]
    plan = Plan(dp, shard // 128)
    rows, half = plan.shard_rows, plan.half
    swap = [(0, 1), (1, 0)]
    states = [v.reshape(rows, 1, 128) for v in (master, first, second, ema)]

    following = lax.ppermute(
        states[0][: plan.head_rows], "dp", [(i, i - 1) for i in range(1, dp)]
    )
    index = jnp.asarray(plan.pack_index)[section, me]
    packed = pack(plan, index, states[0], following)
    mine = lax.dynamic_slice_in_dim(packed, section * half, half, 0)
    given = lax.ppermute(
        lax.dynamic_slice_in_dim(packed, (1 - section) * half, half, 0), "section", swap
    )
    half_e = jnp.where(section == 0, mine, given)
    half_d = jnp.where(section == 0, given, mine)
    gathered_e = lax.all_gather(half_e, ("section", "dp"), axis=0, tiled=True)
    gathered_e = gathered_e.reshape(2, dp, half, 16, 128)
    half_d, _ = tie(half_d, gathered_e[0, 0, 0])
    gathered_d = lax.all_gather(half_d, ("section", "dp"), axis=0, tiled=True)
    gathered_d = gathered_d.reshape(2, dp, half, 16, 128)

    count = sum_everywhere(dp, jnp.sum(NP - keep).astype(F32)) * 0.5
    images = patches.shape[0] // 2
    mine = section * images
    patches = lax.dynamic_slice_in_dim(patches, mine, images, 0)
    patches = jnp.pad(patches, ((0, 0), (0, ROWS_D - NP), (0, 0)))
    order = lax.dynamic_slice_in_dim(perm, mine, images, 0)
    order = jnp.pad(order, ((0, 0), (0, ROWS_D - NP)), constant_values=ROWS_D - 1)
    order = order.reshape(images * ROWS_D, 1)
    kept = lax.dynamic_slice_in_dim(keep, mine, images, 0)
    info = jnp.concatenate([section[None].astype(jnp.int32), kept])
    scale = ((1.0 / count) * (1.0 / PIX) * 2.0).reshape(1)

    shape_e = Shape(images, ROWS_E, D, HEADS_E, FF_E)
    shape_d = Shape(images, ROWS_D, DD, HEADS_D, FF_D)
    pp, *saved, latent = encoder(
        plan, shape_e, info, gathered_e, patches, order, jnp.asarray(sincos(D))
    )
    arrays = dict(zip(("x0", "n1", "mixed", "o", "x1", "n2", "g", "gp", "y"), saved))
    arrays["xe"] = pp
    *sums_d, arrays["dz"], loss = decoder(
        plan, shape_d, info, scale, gathered_d, latent, pp, order, jnp.asarray(sincos(DD))
    )

    stages = encoder_back_stages(plan, shape_e)
    tail_parts = plan.tail_parts()
    tail_got = [lax.ppermute(sums_d[9 + p], "section", swap) for p in tail_parts]
    main = Flow(dp, sums_d[0:3], sums_d[3:6], 0)
    low = high = None
    blocks = []
    for number, stage in enumerate(stages):
        flows, got, (arrays, blocks) = move_on([main, high], arrays, blocks)
        blocks, made = stage(info, gathered_e, arrays, blocks)
        arrays = {**arrays, **made}
        got, arrays, blocks = tie(got, arrays, blocks)
        arrive(flows, got)
        if number == 0:
            tail_sum = lax.psum(
                [sums_d[6 + p] + g for p, g in zip(tail_parts, tail_got)], "dp"
            )
        if number == 1:
            high = Flow(dp, blocks[6:9], blocks[9:12], dp // 2)
    low = Flow(dp, blocks[0:3], blocks[3:6], 0)
    every = [main, high, low]
    while not all(f.done() for f in every):
        flows, got, _ = move_on(every)
        arrive(flows, got)

    cuts = plan.part_cuts
    first_tail, tail_blocks = plan.bins(1)[1]
    tail_at = jnp.clip(me - first_tail, 0, tail_blocks - 1)
    tail_sum = dict(zip(tail_parts, tail_sum))
    sum_tail = jnp.concatenate(
        [
            pick(tail_sum[p], tail_at, 0)
            if p in tail_sum
            else jnp.zeros((cuts[p + 1] - cuts[p], 16, 128), F32)
            for p in range(3)
        ],
        axis=0,
    )
    sum_d = jnp.where(me < first_tail, main.result(), sum_tail)
    sum_e = jnp.where(me < dp // 2, low.result(), high.result())
    half_mine = jnp.where(section == 0, sum_e, sum_d)
    half_other = lax.ppermute(jnp.where(section == 0, sum_d, sum_e), "section", swap)
    block = jnp.where(
        section == 0,
        jnp.concatenate([half_mine, half_other], axis=0),
        jnp.concatenate([half_other, half_mine], axis=0),
    )
    start = jnp.asarray(plan.tail_start)[section, me]
    tail = jnp.concatenate(
        [
            lax.dynamic_slice_in_dim(block, start, plan.tail_units, 0),
            block[plan.vec_unit :],
        ],
        axis=0,
    )
    tail = lax.ppermute(tail, "dp", [(i, i + 1) for i in range(dp - 1)])
    index = jnp.asarray(plan.unpack_index)[section, me]
    total, squares = unpack(plan, index, block, tail)

    sums = sum_everywhere(dp, jnp.stack([jnp.sum(squares), loss[0, 0]]))
    norm = jnp.sqrt(sums[0])
    factor = jnp.minimum(1.0, clip_limit / (norm + norm_epsilon))
    made = update(plan, factor.reshape(1), total, states)
    return (*[v.reshape(1, shard) for v in made], norm, sums[1], count)


def solution(mesh):
    return jax.shard_map(
        on_device,
        mesh=mesh,
        in_specs=(
            P("dp", None, None),
            P("dp"),
            P("dp", None),
            P("section", "dp"),
            P("section", "dp"),
            P("section", "dp"),
            P("section", "dp"),
        ),
        out_specs=(
            P("section", "dp"),
            P("section", "dp"),
            P("section", "dp"),
            P("section", "dp"),
            P(),
            P(),
            P(),
        ),
        check_vma=False,
    )
```

```python
import functools
import math

import jax
import jax.numpy as jnp
import numpy as np
from jax import lax
from jax.experimental import pallas as pl
from jax.experimental.pallas import tpu as pltpu
from jax.sharding import PartitionSpec as P

D = 768
HEADS_E = 12
FF_E = 3072
DD = 512
HEADS_D = 16
FF_D = 2048
PIX = 768
NP = 196
SLOTS = 98
STEP = 10

norm_epsilon = 1e-06
clip_limit = 0.01
learn_rate = 0.02
beta_one = 0.9
beta_two = 0.999
adam_epsilon = 1e-08
weight_decay = 0.05
average_keep = 0.8

F32 = jnp.float32
BF16 = jnp.bfloat16
ROWS_E = 112
ROWS_D = 208
GROUP = 16
VEC_UNITS = 2
VMEM_BYTES = 60 * 1024 * 1024
ANY = pl.BlockSpec(memory_space=pl.ANY)
IN_VMEM = pl.BlockSpec(memory_space=pltpu.VMEM)
IN_SMEM = pl.BlockSpec(memory_space=pltpu.SMEM)

ENC = [
    ("patch", (PIX, D)),
    ("patch_b", (D,)),
    ("g1", (D,)),
    ("b1", (D,)),
    ("qkv", (D, 3 * D)),
    ("proj", (D, D)),
    ("g2", (D,)),
    ("b2", (D,)),
    ("fc1", (D, FF_E)),
    ("fc2", (FF_E, D)),
    ("gf", (D,)),
    ("bf", (D,)),
]
DEC = [
    ("embed", (D, DD)),
    ("mask", (DD,)),
    ("g1", (DD,)),
    ("b1", (DD,)),
    ("qkv", (DD, 3 * DD)),
    ("proj", (DD, DD)),
    ("g2", (DD,)),
    ("b2", (DD,)),
    ("fc1", (DD, FF_D)),
    ("fc2", (FF_D, DD)),
    ("gf", (DD,)),
    ("bf", (DD,)),
    ("head", (DD, PIX)),
]


class Section:
    def __init__(self, layout, dp, shard_rows):
        self.dp = dp
        self.shard_rows = shard_rows
        self.groups = []
        self.vectors = {}
        self.panels = {}
        fill = [0] * dp
        vector_fill = [0] * dp
        row = 0
        for name, shape in layout:
            panels = shape[-1] // 128
            self.panels[name] = panels
            if len(shape) == 2:
                for group in range(shape[0] // GROUP):
                    block = row // shard_rows
                    self.groups.append((name, group, row, panels, block, fill[block]))
                    fill[block] += panels
                    row += GROUP * panels
            else:
                block = row // shard_rows
                self.vectors[name] = (row, panels, block, vector_fill[block])
                vector_fill[block] += panels
                row += panels
        self.rows = row
        self.fill = fill
        assert max(vector_fill) <= 16 * VEC_UNITS
        self.blocks_used = max(b for b in range(dp) if fill[b] or vector_fill[b]) + 1

    def pieces(self, name, first=0, count=None):
        out = []
        for tensor, group, _, panels, block, unit in self.groups:
            if tensor != name or group < first or (count is not None and group >= first + count):
                continue
            if out and out[-1][0] == block and out[-1][1] + out[-1][3] * panels == unit:
                out[-1][3] += 1
            else:
                out.append([block, unit, group, 1])
        return [tuple(p) for p in out]

    def runs(self, name, cuts, first=0, count=None):
        panels = self.panels[name]
        out = []
        for block, unit, group, groups in self.pieces(name, first, count):
            at, left = (group - first) * panels, groups * panels
            while left:
                place = max(i for i in range(len(cuts) - 1) if cuts[i] <= unit)
                take = min(left, cuts[place + 1] - unit)
                out.append((block, place, unit - cuts[place], at, take))
                unit, at, left = unit + take, at + take, left - take
        return out


class Plan:
    def __init__(self, dp, shard_rows):
        self.dp = dp
        self.shard_rows = shard_rows
        self.sections = [Section(ENC, dp, shard_rows), Section(DEC, dp, shard_rows)]
        units = max(max(s.fill) for s in self.sections)
        units += (units + VEC_UNITS) % 2
        self.vec_unit = units
        self.units = units + VEC_UNITS
        self.half = self.units // 2
        half = self.half
        self.quarter = -(-half // 2)
        self.part_cuts = [0, -(-half // 3), -(-2 * half // 3), half]
        self.half_cuts = [0, half, self.units]
        self.head_rows = 8 * -(-max(16 * max(s.panels.values()) for s in self.sections) // 8)
        self.tail_units = max(max(s.panels.values()) for s in self.sections)
        self.pack_base = 8 * -(-shard_rows // 8)
        self.pack_rows = shard_rows + self.head_rows
        self.pack_index = np.zeros((2, dp, self.units * 16), np.int32)
        self.tail_rows = 16 * (self.tail_units + VEC_UNITS)
        self.zero_row = self.units * 16 + self.tail_rows
        self.unpack_index = np.full((2, dp, shard_rows), self.zero_row, np.int32)
        self.tail_start = np.zeros((2, dp), np.int32)
        for s, section in enumerate(self.sections):
            for b in range(dp):
                self.tail_start[s, b] = max(section.fill[b] - self.tail_units, 0)
            for name, group, row, panels, block, unit in section.groups:
                for panel in range(panels):
                    for r in range(GROUP):
                        self.place(s, block, (unit + panel) * 16 + r, row + r * panels + panel)
            for row, panels, block, at in section.vectors.values():
                for panel in range(panels):
                    self.place(s, block, self.vec_unit * 16 + at + panel, row + panel)

    def bins(self, s):
        if s == 0:
            return [(0, self.dp // 2), (self.dp // 2, self.dp - self.dp // 2)]
        used = self.sections[1].blocks_used
        main = 1 << (used.bit_length() - 1)
        return [(0, main), (main, max(used - main, 1))]

    def tail_used(self):
        first, count = self.bins(1)[1]
        section = self.sections[1]
        assert count == 1 and all(v[2] < first for v in section.vectors.values())
        used = section.fill[first]
        return min(used, self.half), max(used - self.half, 0)

    def bin_units(self, s):
        return [self.half, self.half if s == 0 else max(self.tail_used())]

    def place(self, s, block, block_row, flat_row):
        local = flat_row - block * self.shard_rows
        assert 0 <= local < self.pack_rows
        gap = self.pack_base - self.shard_rows if local >= self.shard_rows else 0
        self.pack_index[s, block, block_row] = local + gap
        owner, at = divmod(flat_row, self.shard_rows)
        if owner == block:
            self.unpack_index[s, owner, at] = block_row
        else:
            assert owner == block + 1
            if block_row >= self.vec_unit * 16:
                source = self.tail_units * 16 + block_row - self.vec_unit * 16
            else:
                source = block_row - int(self.tail_start[s, block]) * 16
                assert 0 <= source < self.tail_units * 16
            self.unpack_index[s, owner, at] = self.units * 16 + source


def move_rows_in(index_ref, held, done, count):
    def eight(i, carry):
        for j in range(8):
            row = i * 8 + j
            done[pl.ds(row, 1), :] = held[pl.ds(index_ref[row], 1), :]
        return carry

    lax.fori_loop(0, count // 8, eight, 0)
    for row in range(count // 8 * 8, count):
        done[pl.ds(row, 1), :] = held[pl.ds(index_ref[row], 1), :]


def pack_kernel(base, index_ref, flat, following, out_ref, held, done, sems):
    rows, more = flat.shape[0], following.shape[0]
    copies = [
        pltpu.make_async_copy(flat.at[:, 0], held.at[pl.ds(0, rows)], sems.at[0]),
        pltpu.make_async_copy(following.at[:, 0], held.at[pl.ds(base, more)], sems.at[1]),
    ]
    for copy in copies:
        copy.start()
    for copy in copies:
        copy.wait()
    count = done.shape[0]
    move_rows_in(index_ref, held, done, count)
    out_ref[...] = done[...].reshape(out_ref.shape).astype(BF16)


def pack(plan, index, flat, following):
    count = plan.units * 16
    return pl.pallas_call(
        functools.partial(pack_kernel, plan.pack_base),
        out_shape=jax.ShapeDtypeStruct((plan.units, 16, 128), BF16),
        in_specs=[IN_SMEM, ANY, ANY],
        out_specs=IN_VMEM,
        scratch_shapes=[
            pltpu.VMEM((plan.pack_base + plan.head_rows, 128), F32),
            pltpu.VMEM((count, 128), F32),
            pltpu.SemaphoreType.DMA((2,)),
        ],
        compiler_params=pltpu.CompilerParams(vmem_limit_bytes=32 * 1024 * 1024),
        name="pack_rows",
    )(index, flat, following)


def unpack_kernel(zero_row, rows, index_ref, block, tail, out_ref, held):
    at = 0
    for source in (block, tail):
        size = source.shape[0] * 16
        held[pl.ds(at, size), :] = source[...].reshape(size, 128)
        at += size
    held[pl.ds(zero_row, 8), :] = jnp.zeros((8, 128), F32)
    out_ref[pl.ds(out_ref.shape[0] - 16, 16), :] = jnp.zeros((16, 128), F32)
    move_rows_in(index_ref, held, out_ref, rows)


def unpack(plan, index, block, tail):
    rows = plan.shard_rows
    padded = 16 * -(-rows // 16)
    return pl.pallas_call(
        functools.partial(unpack_kernel, plan.zero_row, rows),
        out_shape=jax.ShapeDtypeStruct((padded, 128), F32),
        in_specs=[IN_SMEM, IN_VMEM, IN_VMEM],
        out_specs=IN_VMEM,
        scratch_shapes=[pltpu.VMEM((plan.zero_row + 8, 128), F32)],
        compiler_params=pltpu.CompilerParams(vmem_limit_bytes=32 * 1024 * 1024),
        name="unpack_rows",
    )(index, block, tail)


def update_kernel(rows, chunk, factor_ref, total, *refs):
    states, outs, held, made, in_sems, out_sems = (
        refs[:4], refs[4:8], refs[8:12], refs[12:16], refs[16], refs[17],
    )
    starts = list(range(0, rows, chunk))
    sizes = [min(chunk, rows - at) for at in starts]
    loads = [
        [
            pltpu.make_async_copy(
                source.at[pl.ds(at, size), 0], ref.at[pl.ds(at, size)], in_sems.at[k, j]
            )
            for j, (source, ref) in enumerate(zip(states, held))
        ]
        for k, (at, size) in enumerate(zip(starts, sizes))
    ]
    for group in loads:
        for copy in group:
            copy.start()
    stores = []
    factor = factor_ref[0]
    for k, (at, size) in enumerate(zip(starts, sizes)):
        for copy in loads[k]:
            copy.wait()

        def body(i, carry):
            here = pl.ds(pl.multiple_of(at + i * 16, 8), 16)
            master, first, second, ema = (ref[here, :] for ref in held)
            clipped = total[here, :] * factor
            new_first = beta_one * first + (1.0 - beta_one) * clipped
            new_second = beta_two * second + (1.0 - beta_two) * clipped * clipped
            first_hat = new_first * (1.0 / (1.0 - beta_one**STEP))
            second_hat = new_second * (1.0 / (1.0 - beta_two**STEP))
            new_master = master - learn_rate * (
                first_hat / (jnp.sqrt(second_hat) + adam_epsilon) + weight_decay * master
            )
            made[0][here, :] = new_master
            made[1][here, :] = new_first
            made[2][here, :] = new_second
            made[3][here, :] = average_keep * ema + (1.0 - average_keep) * new_master
            return carry

        lax.fori_loop(0, -(-size // 16), body, 0, unroll=2)
        for j in range(4):
            copy = pltpu.make_async_copy(
                made[j].at[pl.ds(at, size)], outs[j].at[pl.ds(at, size), 0], out_sems.at[k, j]
            )
            copy.start()
            stores.append(copy)
    for copy in stores:
        copy.wait()


def update(plan, factor, total, states):
    rows = plan.shard_rows
    chunk = 16 * -(-rows // (16 * 4))
    padded = 16 * -(-rows // 16)
    count = -(-rows // chunk)
    return pl.pallas_call(
        functools.partial(update_kernel, rows, chunk),
        out_shape=[jax.ShapeDtypeStruct((rows, 1, 128), F32)] * 4,
        in_specs=[IN_SMEM, IN_VMEM, *[ANY] * 4],
        out_specs=[ANY] * 4,
        scratch_shapes=[
            *[pltpu.VMEM((padded, 128), F32)] * 8,
            pltpu.SemaphoreType.DMA((count, 4)),
            pltpu.SemaphoreType.DMA((count, 4)),
        ],
        compiler_params=pltpu.CompilerParams(vmem_limit_bytes=VMEM_BYTES),
        name="update_states",
    )(factor, total, *states)


def dot(a, b):
    return lax.dot_general(a, b, (((1,), (0,)), ((), ())), preferred_element_type=F32)


def dot_nt(a, b):
    return lax.dot_general(a, b, (((1,), (1,)), ((), ())), preferred_element_type=F32)


def dot_tn(a, b):
    return lax.dot_general(a, b, (((0,), (0,)), ((), ())), preferred_element_type=F32)


def total_of(terms):
    total = terms[0]
    for term in terms[1:]:
        total = total + term
    return total


def for_rows(count, size, step, unroll=1):
    def body(i, carry):
        step(pl.multiple_of(i * size, size))
        return carry

    lax.fori_loop(0, count // size, body, 0, unroll=unroll)


def columns(weight, panels, depth, pair):
    halves = [
        weight[:, 2 * pair + i].reshape(depth, 128)
        for i in range(2)
    ]
    return jnp.concatenate(halves, axis=1)


def row_band(weight, panels, band):
    parts = [weight[pl.ds(band * 16, 16), i].reshape(256, 128) for i in range(panels)]
    return jnp.concatenate(parts, axis=1)


def row_chunks(count):
    size = next(n for n in (208, 224, 112, 104, 16) if count % n == 0)
    return [slice(at, at + size) for at in range(0, count, size)]


def times_columns(left, weight, panels, depth, finish):
    def body(pair, carry):
        right = columns(weight, panels, depth, pair)
        for here in row_chunks(left.shape[0]):
            finish(pair, here, dot(left[here, :], right))
        return carry

    lax.fori_loop(0, panels // 2, body, 0)


def times_bands(left, weight, panels, count, finish):
    def body(band, carry):
        right = row_band(weight, panels, band)
        for here in row_chunks(left.shape[0]):
            finish(here, lanes(band), dot_nt(left[here, :], right))
        return carry

    lax.fori_loop(0, count // 256, body, 0)


def lanes(pair):
    return pl.ds(pl.multiple_of(pair * 256, 256), 256)


def norm_block(count):
    return next(n for n in (224, 208, 112, 104, 16) if count % n == 0)


def norm_rows(x, width):
    mean = jnp.sum(x, axis=1, keepdims=True) * (1.0 / width)
    centre = x - mean
    spread = jnp.sum(centre * centre, axis=1, keepdims=True) * (1.0 / width)
    rstd = lax.rsqrt(spread + norm_epsilon)
    return centre * rstd, rstd


def norm_forward(x_ref, gain, shift, out_ref, count, width):
    size = norm_block(count)

    def step(at):
        hat, _ = norm_rows(x_ref[pl.ds(at, size), :], width)
        out_ref[pl.ds(at, size), :] = (hat * gain + shift).astype(out_ref.dtype)

    for_rows(count, size, step)


def norm_backward(x_ref, gain, grad_of, put, count, width):
    size = norm_block(count)

    def body(i, carry):
        gain_sum, shift_sum = carry
        at = pl.multiple_of(i * size, size)
        hat, rstd = norm_rows(x_ref[pl.ds(at, size), :], width)
        grad = grad_of(at, size)
        gain_sum = gain_sum + jnp.sum((grad * hat).reshape(size // 8, 8, width), axis=0)
        shift_sum = shift_sum + jnp.sum(grad.reshape(size // 8, 8, width), axis=0)
        scaled = grad * gain
        first = jnp.sum(scaled, axis=1, keepdims=True) * (1.0 / width)
        second = jnp.sum(scaled * hat, axis=1, keepdims=True) * (1.0 / width)
        put(at, size, rstd * (scaled - first - hat * second))
        return gain_sum, shift_sum

    zero = jnp.zeros((8, width), F32)
    gain_sum, shift_sum = lax.fori_loop(0, count // size, body, (zero, zero))
    return jnp.sum(gain_sum, axis=0, keepdims=True), jnp.sum(shift_sum, axis=0, keepdims=True)


def head_masks(size):
    lane = lax.broadcasted_iota(jnp.int32, (1, 128), 1)
    return [
        jnp.where((lane >= h * size) & (lane < (h + 1) * size), 1.0, 0.0).astype(BF16)
        for h in range(128 // size)
    ]


def softmax_columns(scores, limit):
    key = lax.broadcasted_iota(jnp.int32, scores.shape, 0)
    scores = jnp.where(key < limit, scores, -1e30)
    top = jnp.max(scores, axis=0, keepdims=True)
    raised = jnp.exp(scores - top)
    return raised * (1.0 / jnp.sum(raised, axis=0, keepdims=True))


def softmax_rows(scores, limit):
    key = lax.broadcasted_iota(jnp.int32, scores.shape, 1)
    scores = jnp.where(key < limit, scores, -1e30)
    top = jnp.max(scores, axis=1, keepdims=True)
    raised = jnp.exp(scores - top)
    return raised * (1.0 / jnp.sum(raised, axis=1, keepdims=True))


def attention_forward(mixed, out, limit_of, images, rows, width, size):
    panels = width // 128
    masks = head_masks(size)

    def body(step, carry):
        image, panel = step // panels, step % panels
        here = pl.ds(pl.multiple_of(image * rows, 16), rows)

        def part(third):
            return mixed[here, pl.ds(pl.multiple_of((third * panels + panel) * 128, 128), 128)]

        query, keys, values = part(0), part(1), part(2)
        limit = limit_of(image)
        probs = [softmax_rows(dot_nt(query * mask, keys), limit).astype(BF16) for mask in masks]
        total = total_of([dot(p, values) * m.astype(F32) for p, m in zip(probs, masks)])
        out[here, pl.ds(pl.multiple_of(panel * 128, 128), 128)] = total.astype(BF16)
        return carry

    lax.fori_loop(0, images * panels, body, 0, unroll=4)


def attention_backward(mixed, grad_out, grad_mixed, limit_of, images, rows, width, size):
    panels = width // 128
    masks = head_masks(size)

    def body(step, carry):
        image, panel = step // panels, step % panels
        here = pl.ds(pl.multiple_of(image * rows, 16), rows)

        def place(third):
            return pl.ds(pl.multiple_of((third * panels + panel) * 128, 128), 128)

        query, keys, values = (mixed[here, place(third)] for third in range(3))
        grad = grad_out[here, place(0)]
        turned = keys.T
        limit = limit_of(image)
        zero = jnp.zeros((rows, 128), F32)
        grad_query, grad_keys, grad_values = [], zero, zero
        for h, mask in enumerate(masks):
            masked_query = query * mask
            masked_grad = grad * mask
            probs = softmax_columns(dot_nt(keys, masked_query), limit)
            grad_probs = dot_nt(values, masked_grad)
            inner = jnp.sum(probs * grad_probs, axis=0, keepdims=True)
            grad_scores = (probs * (grad_probs - inner)).astype(BF16)
            grad_values = grad_values + dot(probs.astype(BF16), masked_grad)
            grad_keys = grad_keys + dot(grad_scores, masked_query)
            grad_query.append(dot(turned[h * size : h * size + size, :], grad_scores))
        grad_query = jnp.concatenate(grad_query, axis=0) * (1.0 / math.sqrt(size))
        grad_mixed[here, place(0)] = grad_query.astype(BF16).T
        grad_mixed[here, place(1)] = grad_keys.astype(BF16)
        grad_mixed[here, place(2)] = grad_values.astype(BF16)
        return carry

    lax.fori_loop(0, images * panels, body, 0, unroll=2)


def gelu_parts(value):
    bell = 0.5 * (1.0 + lax.erf(value * math.sqrt(0.5)))
    slope = bell + value * (jnp.exp(value * value * -0.5) * (1.0 / math.sqrt(2.0 * math.pi)))
    return value * bell, slope


class Shape:
    def __init__(self, images, rows, width, heads, hidden):
        self.images, self.rows, self.width = images, rows, width
        self.size = width // heads
        self.hidden = hidden
        self.count = images * rows


def block_forward(sh, x0, n1, mixed, o, x1, n2, g, gp, y, w, vec, limit_of, ready, saved):
    width, hidden, count = sh.width, sh.hidden, sh.count
    panels = width // 128
    norm_forward(x0, vec("g1"), vec("b1"), n1, count, width)
    saved(n1)
    ready("qkv")

    def put_mixed(pair, here, value):
        scale = jnp.where(pair < panels // 2, 1.0 / math.sqrt(sh.size), 1.0)
        mixed[here, lanes(pair)] = (value * scale).astype(BF16)

    times_columns(n1, w["qkv"], 3 * panels, width, put_mixed)
    saved(mixed)
    attention_forward(mixed, o, limit_of, sh.images, sh.rows, width, sh.size)
    saved(o)
    ready("proj")

    def put_sum(base, out):
        def finish(pair, here, value):
            out[here, lanes(pair)] = base[here, lanes(pair)] + value

        return finish

    times_columns(o, w["proj"], panels, width, put_sum(x0, x1))
    saved(x1)
    norm_forward(x1, vec("g2"), vec("b2"), n2, count, width)
    saved(n2)
    ready("fc1")

    def put_hidden(pair, here, value):
        value, slope = gelu_parts(value)
        g[here, lanes(pair)] = value.astype(BF16)
        gp[here, lanes(pair)] = slope

    times_columns(n2, w["fc1"], hidden // 128, width, put_hidden)
    saved(g)
    saved(gp)
    ready("fc2")
    times_columns(g, w["fc2"], panels, hidden, put_sum(x1, y))
    saved(y)


class Gradients:
    def __init__(self, plan, s, own, stage, sems, targets):
        self.plan, self.section, self.own = plan, plan.sections[s], own
        self.bins = plan.bins(s)
        self.stage, self.sems, self.targets = stage, sems, targets
        self.turn = 0
        self.flying = [[], []]

    def copy_out(self, source, block, side, unit, take, sem):
        which = max(i for i, (first, _) in enumerate(self.bins) if first <= block)
        block = block - self.bins[which][0]
        keep, send = self.targets[2 * which], self.targets[2 * which + 1]

        def to(target):
            return pltpu.make_async_copy(source, target.at[block, pl.ds(unit, take)], sem)

        @pl.when(self.own == side)
        def _():
            to(keep).start()

        @pl.when(self.own != side)
        def _():
            to(send).start()

        return to(keep)

    def drain(self, slot):
        for copy in self.flying[slot]:
            copy.wait()
        self.flying[slot] = []

    def weight(self, name, left, depth, right, turned):
        panels = self.section.panels[name]
        for band in range(depth // 256):
            slot = self.turn % 2
            self.turn += 1
            self.drain(slot)
            stage = self.stage.at[slot]
            turned[...] = left[:, band * 256 : band * 256 + 256].T

            def body(pair, carry):
                value = dot(turned[...], right[:, lanes(pair)])
                for i in range(2):
                    stage[pl.ds(2 * pair + i, 16, stride=panels)] = value[
                        :, i * 128 : i * 128 + 128
                    ].reshape(16, 16, 128)
                return carry

            lax.fori_loop(0, panels // 2, body, 0)
            for block, side, unit, at, take in self.section.runs(
                name, self.plan.half_cuts, band * 16, 16
            ):
                self.flying[slot].append(
                    self.copy_out(
                        stage.at[pl.ds(at, take)], block, side, unit, take, self.sems.at[slot]
                    )
                )

    def finish(self, values, scratch):
        vectors = self.section.vectors
        blocks = sorted({vectors[name][2] for name in values})
        for k, block in enumerate(blocks):
            scratch[k] = jnp.zeros((VEC_UNITS, 16, 128), F32)
            for name, (_, panels, at_block, at) in vectors.items():
                if at_block != block:
                    continue
                for panel in range(panels):
                    unit, row = divmod(at + panel, 16)
                    scratch[k, unit, row : row + 1, :] = values[name][
                        :, panel * 128 : panel * 128 + 128
                    ]
        unit = self.plan.vec_unit - self.plan.half
        copies = [
            self.copy_out(scratch.at[k], block, 1, unit, VEC_UNITS, self.sems.at[2])
            for k, block in enumerate(blocks)
        ]
        for copy in copies:
            copy.wait()
        self.drain(0)
        self.drain(1)


class Backward:
    def __init__(self, sh, w, vec, limit_of, grads, values, turned, ready):
        self.sh, self.w, self.vec, self.limit_of = sh, w, vec, limit_of
        self.grads, self.values, self.turned, self.ready = grads, values, turned, ready
        self.panels = sh.width // 128

    def round_stream(self, dy, dyb):
        def step(at):
            dyb[pl.ds(at, 16), :] = dy[pl.ds(at, 16), :].astype(BF16)

        for_rows(self.sh.count, 16, step, 4)

    def bands(self, left, name, count, put):
        times_bands(left, self.w[name], self.grads.section.panels[name], count, put)

    def through_norm(self, x, dn, dy, gain, shift, dn_is=None):
        def from_dn(at, size):
            return dn[pl.ds(at, size), :]

        def into_stream(at, size, value):
            dy[pl.ds(at, size), :] = dy[pl.ds(at, size), :] + value

        self.values[gain], self.values[shift] = norm_backward(
            x, self.vec(gain), from_dn, into_stream, self.sh.count, self.sh.width
        )

    def second_product(self, dy, dyb, g, gp):
        self.round_stream(dy, dyb)
        self.ready("fc2", g)
        self.grads.weight("fc2", g, self.sh.hidden, dyb, self.turned)
        self.ready(None, gp)

        def put(here, there, value):
            g[here, there] = (value * gp[here, there]).astype(BF16)

        self.bands(dyb, "fc2", self.sh.hidden, put)

    def first_product(self, dy, g, n2, x1, dn):
        def put(here, there, value):
            dn[here, there] = value

        self.ready("fc1", n2)
        self.grads.weight("fc1", n2, self.sh.width, g, self.turned)
        self.bands(g, "fc1", self.sh.width, put)
        self.ready(None, x1)
        self.through_norm(x1, dn, dy, "g2", "b2")

    def attention(self, dy, dyb, o, mixed, dmixed):
        sh = self.sh
        self.round_stream(dy, dyb)
        self.ready("proj", o)
        self.grads.weight("proj", o, sh.width, dyb, self.turned)

        def put(here, there, value):
            o[here, there] = value.astype(BF16)

        self.bands(dyb, "proj", sh.width, put)
        self.ready(None, mixed)
        attention_backward(mixed, o, dmixed, self.limit_of, sh.images, sh.rows, sh.width, sh.size)

    def mixing(self, dy, dmixed, n1, x0, dn):
        def put(here, there, value):
            dn[here, there] = value

        self.ready("qkv", n1)
        self.grads.weight("qkv", n1, self.sh.width, dmixed, self.turned)
        self.bands(dmixed, "qkv", self.sh.width, put)
        self.ready(None, x0)
        self.through_norm(x0, dn, dy, "g1", "b1")


def held_at(plan, s, gathered, block, side, unit, take):
    if s == 0:
        return [(gathered[0].at[side, block, pl.ds(unit, take)], 0, take)]
    if block == plan.bins(1)[1][0]:
        return [(gathered[1].at[side, pl.ds(unit, take)], 0, take)]
    out = []
    quarter = plan.quarter
    if unit < quarter:
        few = min(take, quarter - unit)
        out.append((gathered[0].at[side, 2 * block, pl.ds(unit, few)], 0, few))
    if unit + take > quarter:
        skip = max(quarter - unit, 0)
        few = take - skip
        source = gathered[0].at[side, 2 * block + 1, pl.ds(unit + skip - quarter, few)]
        out.append((source, skip, few))
    return out


def load_vectors(plan, s, gathered, held, vec_ref, sem):
    section = plan.sections[s]
    blocks = sorted({v[2] for v in section.vectors.values()})
    copies = [
        pltpu.make_async_copy(source, held.at[k, pl.ds(skip, few)], sem)
        for k, block in enumerate(blocks)
        for source, skip, few in held_at(
            plan, s, gathered, block, 1, plan.vec_unit - plan.half, VEC_UNITS
        )
    ]
    for copy in copies:
        copy.start()
    names = {name: i for i, name in enumerate(section.vectors)}

    def finish():
        for copy in copies:
            copy.wait()
        for k, block in enumerate(blocks):
            rows = held[k].reshape(16 * VEC_UNITS, 128).astype(F32)
            for name, (_, panels, at_block, at) in section.vectors.items():
                if at_block != block:
                    continue
                i = names[name]
                for panel in range(panels):
                    vec_ref[i : i + 1, panel * 128 : panel * 128 + 128] = rows[
                        at + panel : at + panel + 1, :
                    ]
        return lambda name: vec_ref[names[name] : names[name] + 1, :]

    return finish


def load_weights(plan, s, gathered, w, sems):
    section = plan.sections[s]
    copies = {}
    for k, (name, ref) in enumerate(w.items()):
        panels = section.panels[name]
        flat = ref.reshape(ref.shape[0] * panels, 16, 128)
        copies[name] = [
            pltpu.make_async_copy(source, flat.at[pl.ds(at + skip, few)], sems.at[k])
            for block, side, unit, at, take in section.runs(name, plan.half_cuts)
            for source, skip, few in held_at(plan, s, gathered, block, side, unit, take)
        ]
        for copy in copies[name]:
            copy.start()

    def ready(name):
        for copy in copies.get(name, ()):
            copy.wait()

    return ready


def weight_scratch(layout, names):
    shapes = dict(layout)
    return [
        pltpu.VMEM((shapes[n][0] // GROUP, shapes[n][1] // 128, GROUP, 128), BF16)
        for n in names
    ]


def picks(perm_ref, image):
    here = pl.ds(pl.multiple_of(image * ROWS_D, 16), ROWS_D)
    patch = lax.broadcasted_iota(jnp.int32, (ROWS_D, ROWS_D), 1)
    return jnp.where(perm_ref[here, :] == patch, 1.0, 0.0).astype(BF16)


W_ENC = ["patch", "qkv", "proj", "fc1", "fc2"]


def encoder_kernel(plan, sh, refs):
    (info, gathered, patches, perm, pos, pp_out, x0_out, n1_out, mixed_out, o_out, x1_out, n2_out,
     g_out, gp_out, y_out, latent_out, w_patch, w_qkv, w_proj, w_fc1, w_fc2, held, vec_ref, pp, xe,
     x0, n1, mixed, o, x1, n2, g, gp, y, latent, w_sems, out_sems) = refs
    w = dict(zip(W_ENC, (w_patch, w_qkv, w_proj, w_fc1, w_fc2)))
    finish_vec = load_vectors(plan, 0, [gathered], held, vec_ref, w_sems.at[5])
    ready = load_weights(plan, 0, [gathered], w, w_sems)
    outs = []

    targets = [(pp, pp_out), (x0, x0_out), (n1, n1_out), (mixed, mixed_out), (o, o_out),
               (x1, x1_out), (n2, n2_out), (g, g_out), (gp, gp_out), (y, y_out),
               (latent, latent_out)]

    def saved(ref):
        for k, (source, target) in enumerate(targets):
            if source is ref:
                copy = pltpu.make_async_copy(source, target, out_sems.at[k])
                copy.start()
                outs.append(copy)

    def gather(image, carry):
        chosen = picks(perm, image)
        pp[image] = dot(chosen, patches[image]).astype(BF16)
        here = pl.ds(pl.multiple_of(image * ROWS_E, 16), ROWS_E)
        xe[here, :] = pp[image, 0:ROWS_E, :]
        few = chosen[0:ROWS_E, :]
        x0[here, :] = (dot(few, pos[0]) + dot(few, pos[1])) + dot(few, pos[2])
        return carry

    lax.fori_loop(0, sh.images, gather, 0)
    saved(pp)
    vec = finish_vec()
    ready("patch")

    def put(pair, here, value):
        part = vec_ref[0:1, lanes(pair)]
        x0[here, lanes(pair)] = (value + part) + x0[here, lanes(pair)]

    times_columns(xe, w["patch"], D // 128, PIX, put)
    saved(x0)
    block_forward(
        sh, x0, n1, mixed, o, x1, n2, g, gp, y, w, vec, lambda i: info[1 + i], ready, saved
    )
    norm_forward(y, vec("gf"), vec("bf"), latent, sh.count, D)
    saved(latent)
    for copy in outs:
        copy.wait()


def lasting(microseconds):
    return pl.CostEstimate(
        flops=int(microseconds * 1e9), bytes_accessed=1 << 20, transcendentals=0
    )


def saved_shapes(sh):
    count, width, hidden = sh.count, sh.width, sh.hidden
    return [
        ((count, width), F32),
        ((count, width), BF16),
        ((count, 3 * width), BF16),
        ((count, width), BF16),
        ((count, width), F32),
        ((count, width), BF16),
        ((count, hidden), BF16),
        ((count, hidden), F32),
        ((count, width), F32),
    ]


def encoder(plan, sh, info, gathered, patches, perm, pos):
    saved = saved_shapes(sh)
    pp_shape = ((sh.images, ROWS_D, PIX), BF16)
    latent_shape = ((sh.count, D), BF16)
    outs = [pp_shape, *saved, latent_shape]
    holders = len({v[2] for v in plan.sections[0].vectors.values()})
    return pl.pallas_call(
        lambda *refs: encoder_kernel(plan, sh, refs),
        out_shape=[jax.ShapeDtypeStruct(*s) for s in outs],
        in_specs=[IN_SMEM, ANY, IN_VMEM, IN_VMEM, IN_VMEM],
        out_specs=[ANY] * len(outs),
        scratch_shapes=[
            *weight_scratch(ENC, W_ENC),
            pltpu.VMEM((holders, VEC_UNITS, 16, 128), BF16),
            pltpu.VMEM((8, D), F32),
            pltpu.VMEM(*pp_shape),
            pltpu.VMEM((sh.count, PIX), BF16),
            *[pltpu.VMEM(*s) for s in saved],
            pltpu.VMEM(*latent_shape),
            pltpu.SemaphoreType.DMA((6,)),
            pltpu.SemaphoreType.DMA((len(outs),)),
        ],
        compiler_params=pltpu.CompilerParams(vmem_limit_bytes=VMEM_BYTES),
        cost_estimate=lasting(50),
        name="encoder_forward",
    )(info, gathered, patches, perm, pos)


W_DEC = ["embed", "qkv", "proj", "fc1", "fc2", "head"]


def decoder_kernel(plan, sh, refs):
    info, scale, gathered, gathered_tail, latent_in, pp_in, perm, pos = refs[:8]
    gathered = [gathered, gathered_tail]
    targets, refs = refs[8:12], refs[12:]
    (grad_latent, loss_out,
     w_embed, w_qkv, w_proj, w_fc1, w_fc2, w_head, held, vec_ref, pp, latent, embedded, x0, n1,
     mixed, o, x1, n2, g, gp, y, f, dn, guess, turned, turned_e, stage, vec_stage, w_sems,
     in_sems, grad_sems) = refs
    w = dict(zip(W_DEC, (w_embed, w_qkv, w_proj, w_fc1, w_fc2, w_head)))
    copy_latent = pltpu.make_async_copy(latent_in, latent, in_sems.at[0])
    copy_pp = pltpu.make_async_copy(pp_in, pp, in_sems.at[1])
    copy_latent.start()
    finish_vec = load_vectors(plan, 1, gathered, held, vec_ref, w_sems.at[6])
    ready = load_weights(plan, 1, gathered, w, w_sems)
    copy_pp.start()
    images, count = sh.images, sh.count
    count_e = images * ROWS_E
    vec = finish_vec()
    copy_latent.wait()
    ready("embed")

    def put_embedded(pair, here, value):
        embedded[here, lanes(pair)] = value

    times_columns(latent, w["embed"], DD // 128, D, put_embedded)

    def tokens(image, carry):
        chosen = picks(perm, image)
        place = (dot(chosen, pos[0]) + dot(chosen, pos[1])) + dot(chosen, pos[2])
        start = pl.multiple_of(image * ROWS_D, 16)
        kept = info[1 + image]
        token = vec_ref[0:1, :]
        few = embedded[pl.ds(pl.multiple_of(image * ROWS_E, 16), ROWS_E), :]
        rank = lax.broadcasted_iota(jnp.int32, (ROWS_E, DD), 0)
        x0[pl.ds(start, ROWS_E), :] = jnp.where(rank < kept, few, token) + place[:ROWS_E, :]
        x0[pl.ds(start + ROWS_E, ROWS_D - ROWS_E), :] = token + place[ROWS_E:, :]
        return carry

    lax.fori_loop(0, images, tokens, 0)
    block_forward(
        sh, x0, n1, mixed, o, x1, n2, g, gp, y, w, vec, lambda i: NP, ready, lambda ref: None
    )
    norm_forward(y, vec("gf"), vec("bf"), f, count, DD)
    ready("head")
    copy_pp.wait()
    factor = scale[0]

    def predict_image(image, total):
        start = pl.multiple_of(image * ROWS_D, 16)
        kept = info[1 + image]
        here = pl.ds(start, ROWS_D)
        for pair in range(PIX // 256):
            guess[:, pair * 256 : pair * 256 + 256] = dot(
                f[here, :], columns(w["head"], PIX // 128, DD, pair)
            )

        def rows(i, total):
            at = pl.multiple_of(i * 16, 16)
            target, _ = norm_rows(pp[image, pl.ds(at, 16), :].astype(F32), PIX)
            off = guess[pl.ds(at, 16), :] - target
            rank = lax.broadcasted_iota(jnp.int32, (16, PIX), 0) + at
            off = jnp.where((rank >= kept) & (rank < NP), off, 0.0)
            pp[image, pl.ds(at, 16), :] = (off * factor).astype(BF16)
            return total + jnp.sum((off * off).reshape(2, 8, PIX), axis=0)

        return lax.fori_loop(0, ROWS_D // 16, rows, total)

    total = lax.fori_loop(0, images, predict_image, jnp.zeros((8, PIX), F32))
    total = jnp.sum(jnp.sum(total, axis=0, keepdims=True), axis=1, keepdims=True)
    loss_out[...] = jnp.broadcast_to(total * (1.0 / PIX), (8, 128))

    grads = Gradients(plan, 1, info[0], stage, grad_sems, targets)
    values = {}
    back = Backward(
        sh, w, vec, lambda i: NP, grads, values, turned, lambda name, ref: None
    )
    dpred = pp.reshape(count, PIX)
    grads.weight("head", f, DD, dpred, turned)

    def put_dn(here, there, value):
        dn[here, there] = value

    back.bands(dpred, "head", DD, put_dn)

    def from_dn(at, size):
        return dn[pl.ds(at, size), :]

    def put_y(at, size, value):
        y[pl.ds(at, size), :] = value

    values["gf"], values["bf"] = norm_backward(y, vec("gf"), from_dn, put_y, count, DD)
    back.second_product(y, f, g, gp)
    back.first_product(y, g, n2, x1, dn)
    dmixed = g.at[:, pl.ds(0, 3 * DD)]
    back.attention(y, f, o, mixed, dmixed)
    back.mixing(y, dmixed, n1, x0, dn)

    def split(image, total):
        start = pl.multiple_of(image * ROWS_D, 16)
        kept = info[1 + image]

        def rows(i, total):
            at = pl.multiple_of(i * 16, 16)
            grad = y[pl.ds(start + at, 16), :]
            rank = lax.broadcasted_iota(jnp.int32, (16, DD), 0) + at
            free = jnp.where(rank >= kept, grad, 0.0)

            @pl.when(i < ROWS_E // 16)
            def _():
                taken = jnp.where(rank < kept, grad, 0.0).astype(BF16)
                n1[pl.ds(pl.multiple_of(image * ROWS_E, 16) + at, 16), :] = taken

            return total + jnp.sum(free.reshape(2, 8, DD), axis=0)

        return lax.fori_loop(0, ROWS_D // 16, rows, total)

    total = lax.fori_loop(0, images, split, jnp.zeros((8, DD), F32))
    values["mask"] = jnp.sum(total, axis=0, keepdims=True)
    placed = n1.at[pl.ds(0, count_e)]
    grads.weight("embed", latent, D, placed, turned_e)

    def put_latent(here, there, value):
        grad_latent[here, there] = value.astype(BF16)

    times_bands(placed, w["embed"], DD // 128, D, put_latent)
    grads.finish(values, vec_stage)


def grad_shapes(plan, s):
    return [
        jax.ShapeDtypeStruct((count, units, 16, 128), F32)
        for (_, count), units in zip(plan.bins(s), plan.bin_units(s))
        for _ in range(2)
    ]


def decoder(plan, sh, info, scale, gathered, latent, pp, perm, pos):
    count_e = sh.images * ROWS_E
    holders = len({v[2] for v in plan.sections[1].vectors.values()})
    saved = saved_shapes(sh)
    most = max(plan.sections[1].panels.values())
    return pl.pallas_call(
        lambda *refs: decoder_kernel(plan, sh, refs),
        out_shape=[
            *grad_shapes(plan, 1),
            jax.ShapeDtypeStruct((count_e, D), BF16),
            jax.ShapeDtypeStruct((8, 128), F32),
        ],
        in_specs=[IN_SMEM, IN_SMEM, ANY, ANY, ANY, ANY, IN_VMEM, IN_VMEM],
        out_specs=[*[ANY] * 4, IN_VMEM, IN_VMEM],
        scratch_shapes=[
            *weight_scratch(DEC, W_DEC),
            pltpu.VMEM((holders, VEC_UNITS, 16, 128), BF16),
            pltpu.VMEM((8, DD), F32),
            pltpu.VMEM((sh.images, ROWS_D, PIX), BF16),
            pltpu.VMEM((count_e, D), BF16),
            pltpu.VMEM((count_e, DD), F32),
            *[pltpu.VMEM(*s) for s in saved],
            pltpu.VMEM((sh.count, DD), BF16),
            pltpu.VMEM((sh.count, DD), F32),
            pltpu.VMEM((ROWS_D, PIX), F32),
            pltpu.VMEM((256, sh.count), BF16),
            pltpu.VMEM((256, count_e), BF16),
            pltpu.VMEM((2, 16 * most, 16, 128), F32),
            pltpu.VMEM((holders, VEC_UNITS, 16, 128), F32),
            pltpu.SemaphoreType.DMA((7,)),
            pltpu.SemaphoreType.DMA((2,)),
            pltpu.SemaphoreType.DMA((3,)),
        ],
        compiler_params=pltpu.CompilerParams(vmem_limit_bytes=VMEM_BYTES),
        cost_estimate=lasting(160),
        name="decoder_both",
    )(info, scale, *gathered, latent, pp, perm, pos)


class Stage:
    def __init__(self, plan, sh, weights, reads, temps, outs, most, cost, name, body, bins=2):
        self.plan, self.sh, self.weights, self.reads = plan, sh, weights, reads
        self.temps, self.outs, self.most, self.cost, self.name = temps, outs, most, cost, name
        self.body = body
        self.bins = bins

    def kernel(self, blocks, *refs):
        refs = list(refs)

        def take(count):
            got = refs[:count]
            del refs[:count]
            return got

        plan, sh = self.plan, self.sh
        info, gathered = take(2)
        sources = dict(zip(self.reads, take(len(self.reads))))
        take(blocks)
        targets = take(2 * self.bins)
        results = dict(zip(self.outs, take(len(self.outs))))
        w = dict(zip(self.weights, take(len(self.weights))))
        here = dict(zip(self.reads, take(len(self.reads))))
        temps = dict(zip(self.temps, take(len(self.temps))))
        held, vec_ref, turned, stage, vec_stage, w_sems, in_sems, grad_sems = refs
        finish_vec = load_vectors(plan, 0, [gathered], held, vec_ref, w_sems.at[len(w)])
        loads = {}
        for k, (name, ref) in enumerate(here.items()):
            if name == "xe":
                copies = [
                    pltpu.make_async_copy(
                        sources[name].at[i, pl.ds(0, ROWS_E)],
                        ref.at[pl.ds(i * ROWS_E, ROWS_E)],
                        in_sems.at[k],
                    )
                    for i in range(sh.images)
                ]
            else:
                copies = [pltpu.make_async_copy(sources[name], ref, in_sems.at[k])]
            for copy in copies:
                copy.start()
            loads[id(ref)] = copies
        weights_ready = load_weights(plan, 0, [gathered], w, w_sems)
        vec = finish_vec()

        def ready(name, ref=None):
            for copy in loads.pop(id(ref), ()):
                copy.wait()
            if name is not None:
                weights_ready(name)

        values = {}
        grads = Gradients(plan, 0, info[0], stage, grad_sems, targets)
        back = Backward(
            sh, w, vec, lambda i: info[1 + i], grads, values, turned, ready
        )
        self.body(back, {**here, **temps}, results)
        assert not loads
        grads.finish(values, vec_stage)

    def __call__(self, info, gathered, arrays, blocks):
        plan, sh = self.plan, self.sh
        count, width, hidden = sh.count, sh.width, sh.hidden
        known = {
            "dz": ((count, width), BF16),
            "y": ((count, width), F32),
            "dy": ((count, width), F32),
            "x0": ((count, width), F32),
            "x1": ((count, width), F32),
            "dn": ((count, width), F32),
            "n1": ((count, width), BF16),
            "n2": ((count, width), BF16),
            "o": ((count, width), BF16),
            "dyb": ((count, width), BF16),
            "xe": ((count, PIX), BF16),
            "mixed": ((count, 3 * width), BF16),
            "dmixed": ((count, 3 * width), BF16),
            "g": ((count, hidden), BF16),
            "gp": ((count, hidden), F32),
        }
        holders = len({v[2] for v in plan.sections[0].vectors.values()})
        targets = grad_shapes(plan, 0)[: 2 * self.bins]
        before = 2 + len(self.reads)
        got = pl.pallas_call(
            functools.partial(self.kernel, len(blocks)),
            out_shape=[*targets, *[jax.ShapeDtypeStruct(*known[n]) for n in self.outs]],
            in_specs=[IN_SMEM, *[ANY] * (1 + len(self.reads) + len(blocks))],
            out_specs=[*[ANY] * len(targets), *[IN_VMEM] * len(self.outs)],
            input_output_aliases={before + i: i for i in range(len(blocks))},
            scratch_shapes=[
                *weight_scratch(ENC, self.weights),
                *[pltpu.VMEM(*known[n]) for n in self.reads],
                *[pltpu.VMEM(*known[n]) for n in self.temps],
                pltpu.VMEM((holders, VEC_UNITS, 16, 128), BF16),
                pltpu.VMEM((8, D), F32),
                pltpu.VMEM((256, count), BF16),
                pltpu.VMEM((2, 16 * self.most, 16, 128), F32),
                pltpu.VMEM((holders, VEC_UNITS, 16, 128), F32),
                pltpu.SemaphoreType.DMA((len(self.weights) + 1,)),
                pltpu.SemaphoreType.DMA((len(self.reads),)),
                pltpu.SemaphoreType.DMA((3,)),
            ],
            compiler_params=pltpu.CompilerParams(vmem_limit_bytes=VMEM_BYTES),
            cost_estimate=lasting(self.cost),
            name=self.name,
        )(info, gathered, *[arrays[n] for n in self.reads], *blocks)
        return got[: len(targets)], dict(zip(self.outs, got[len(targets) :]))


def back_second(back, r, out):
    sh = back.sh
    back.ready(None, r["dz"])
    back.ready(None, r["y"])

    def from_latent(at, size):
        return r["dz"][pl.ds(at, size), :].astype(F32)

    def put(at, size, value):
        out["dy"][pl.ds(at, size), :] = value

    back.values["gf"], back.values["bf"] = norm_backward(
        r["y"], back.vec("gf"), from_latent, put, sh.count, D
    )
    back.second_product(out["dy"], r["dyb"], r["g"], r["gp"])

    def step(at):
        out["g"][pl.ds(at, 16), :] = r["g"][pl.ds(at, 16), :]

    for_rows(sh.count, 16, step, 2)


def copy_rows(count, source, target):
    def step(at):
        target[pl.ds(at, 16), :] = source[pl.ds(at, 16), :]

    for_rows(count, 16, step, 4)


def back_first(back, r, out):
    back.ready(None, r["dy"])
    back.ready(None, r["g"])
    copy_rows(back.sh.count, r["dy"], out["dy"])
    back.first_product(out["dy"], r["g"], r["n2"], r["x1"], r["dn"])


def back_attention(back, r, out):
    back.ready(None, r["dy"])
    back.attention(r["dy"], r["dyb"], r["o"], r["mixed"], out["dmixed"])


def back_mixing(back, r, out):
    back.ready(None, r["dy"])
    back.ready(None, r["dmixed"])
    back.mixing(r["dy"], r["dmixed"], r["n1"], r["x0"], r["dn"])

    def body(i, total):
        at = pl.multiple_of(i * 16, 16)
        grad = r["dy"][pl.ds(at, 16), :]
        r["dyb"][pl.ds(at, 16), :] = grad.astype(BF16)
        return total + jnp.sum(grad.reshape(2, 8, D), axis=0)

    total = lax.fori_loop(0, back.sh.count // 16, body, jnp.zeros((8, D), F32))
    back.values["patch_b"] = jnp.sum(total, axis=0, keepdims=True)
    back.ready(None, r["xe"])
    back.grads.weight("patch", r["xe"], PIX, r["dyb"], back.turned)


def encoder_back_stages(plan, sh):
    most = {n: plan.sections[0].panels[n] for n in ("fc1", "fc2", "qkv", "proj")}
    return [
        Stage(plan, sh, ["fc2"], ["y", "dz", "g", "gp"], ["dyb"], ["dy", "g"], most["fc2"], 25,
              "encoder_back_fc2", back_second),
        Stage(plan, sh, ["fc1"], ["g", "dy", "n2", "x1"], ["dn"], ["dy"], most["fc1"], 20,
              "encoder_back_fc1", back_first),
        Stage(plan, sh, ["proj"], ["dy", "o", "mixed"], ["dyb"], ["dmixed"], most["proj"], 35,
              "encoder_back_attention", back_attention, 1),
        Stage(plan, sh, ["qkv"], ["dy", "dmixed", "n1", "x0", "xe"], ["dn", "dyb"], [],
              most["qkv"], 25, "encoder_back_qkv", back_mixing, 1),
    ]


def pick(value, index, axis):
    return lax.dynamic_index_in_dim(value, index, axis, keepdims=False)


def tie(*trees):
    return lax.optimization_barrier(trees)


class Term:
    def __init__(self, base, bits, first, last, fixed=()):
        self.base, self.bits, self.first, self.last = base, bits, first, last
        self.fixed = dict(fixed)

    def at(self, bit, index):
        return Term(self.base, self.bits, self.first, self.last, {**self.fixed, bit: index})

    def value(self):
        zero = jnp.zeros((), jnp.int32)
        starts = [self.fixed.get(b, zero).astype(jnp.int32) for b in self.bits]
        sizes = [1 if b in self.fixed else 2 for b in self.bits]
        left = [n for n in sizes if n == 2]
        starts += [jnp.full((), self.first, jnp.int32), zero, zero]
        count = self.last - self.first
        out = lax.dynamic_slice(self.base, starts, [*sizes, count, 16, 128])
        return out.reshape(*left, count, 16, 128)


def sum_of(terms):
    return total_of([term.value() for term in terms])


class Flow:
    def __init__(self, dp, keep, send, first, parts=3):
        self.dp = dp
        self.me = lax.axis_index("dp")
        self.keep, self.given = keep, send
        count, units = keep.shape[:2]
        self.bits = count.bit_length() - 1
        assert count == 1 << self.bits and dp & (dp - 1) == 0
        self.all_bits = dp.bit_length() - 1
        self.first = first
        low = list(range(self.bits))
        if dp == 64:
            low = [b for b in (0, 2, 4, 1, 3) if b < self.bits]
        turn = max(min(3, len(low)), 1)
        self.cuts = [units * p // parts for p in range(parts + 1)]
        self.orders = [low[p % turn : turn] + low[: p % turn] + low[turn:] for p in range(parts)]
        self.step = -1
        self.terms = None

    def done(self):
        return self.step == self.all_bits

    def payload(self):
        if self.step < 0:
            return [self.given]
        if self.step >= self.bits:
            return [self.result()]
        out = []
        for terms, order in zip(self.terms, self.orders):
            bit = order[self.step]
            other = 1 - (self.me >> bit & 1)
            out.append(sum_of([t.at(bit, other) for t in terms]))
        return out

    def send(self, payload):
        if self.step < 0:
            return [lax.ppermute(payload[0], "section", [(0, 1), (1, 0)])]
        if self.step >= self.bits:
            flip = 1 << self.step
            pairs = [(i, i ^ flip) for i in range(self.dp) if (i ^ self.first) & flip]
            return [lax.ppermute(payload[0], "dp", pairs)]
        out = []
        for value, order in zip(payload, self.orders):
            flip = 1 << order[self.step]
            out.append(lax.ppermute(value, "dp", [(i, i ^ flip) for i in range(self.dp)]))
        return out

    def take(self, got):
        ranges = list(zip(self.cuts[:-1], self.cuts[1:]))
        if self.step < 0:
            bits = list(range(self.bits - 1, -1, -1))
            shape = (2,) * self.bits + self.keep.shape[1:]
            self.terms = [
                [Term(v.reshape(shape), bits, *r) for v in (self.keep, got[0])] for r in ranges
            ]
        elif self.step < self.bits:
            for k, (order, value) in enumerate(zip(self.orders, got)):
                bit = order[self.step]
                mine = self.me >> bit & 1
                gone = order[: self.step + 1]
                bits = [b for b in range(self.bits - 1, -1, -1) if b not in gone]
                self.terms[k] = [t.at(bit, mine) for t in self.terms[k]]
                self.terms[k].append(Term(value, bits, 0, value.shape[-3]))
        else:
            for k, r in enumerate(ranges):
                self.terms[k].append(Term(got[0], [], *r))
        self.step += 1

    def result(self):
        return jnp.concatenate([sum_of(t) for t in self.terms], axis=0)


def move_on(flows, *others):
    flows = [f for f in flows if f is not None and not f.done()]
    payloads, others = tie([f.payload() for f in flows], others)
    return flows, [f.send(p) for f, p in zip(flows, payloads)], others


def arrive(flows, got):
    for flow, values in zip(flows, got):
        flow.take(values)


def sum_everywhere(dp, value):
    value = value + lax.ppermute(value, "section", [(0, 1), (1, 0)])
    bits = dp.bit_length() - 1
    for low in range(0, bits, 2):
        got = [
            lax.ppermute(value, "dp", [(i, i ^ (flip << low)) for i in range(dp)])
            for flip in range(1, 1 << min(2, bits - low))
        ]
        value = value + got[0]
        if len(got) == 3:
            value = value + (got[1] + got[2])
    return value


def squares_of(plan, s, value, section, me):
    section_plan = plan.sections[s]
    vectors = np.zeros((plan.dp,), np.int32)
    for _, panels, block, at in section_plan.vectors.values():
        vectors[block] = max(vectors[block], at + panels)
    filled = jnp.asarray(np.asarray(section_plan.fill, np.int32) * 16)[me]
    vectors = jnp.asarray(vectors)[me]
    shape = value.shape
    row = lax.broadcasted_iota(jnp.int32, shape, 0) * 16 + lax.broadcasted_iota(jnp.int32, shape, 1)
    row = row + section * (plan.half * 16)
    extra = row - plan.vec_unit * 16
    valid = (row < filled) | ((extra >= 0) & (extra < vectors))
    return jnp.sum(jnp.where(valid, value * value, 0.0))


def gather_decoder(plan, half_d, section, me, after):
    dp, quarter = plan.dp, plan.quarter
    first = plan.bins(1)[1][0]
    assert 2 * first == dp
    used = max(plan.tail_used())
    spread = jnp.pad(half_d, ((0, 2 * quarter - plan.half), (0, 0), (0, 0)))
    spread = total_of(
        [
            lax.ppermute(
                spread[i * quarter : (i + 1) * quarter],
                "dp",
                [(b, 2 * b + i) for b in range(first)],
            )
            for i in range(2)
        ]
    )
    rest = jnp.where(me == first, half_d[:used], jnp.zeros((), BF16))
    holders = [first]
    for bit in reversed(range(dp.bit_length() - 1)):
        rest = rest + lax.ppermute(rest, "dp", [(i, i ^ 1 << bit) for i in holders])
        holders = holders + [i ^ 1 << bit for i in holders]
    other = lax.ppermute(rest, "section", [(0, 1), (1, 0)])
    rest = jnp.where(section == 0, jnp.stack([rest, other]), jnp.stack([other, rest]))
    spread, _ = tie(spread, after[0, 0, 0])
    gathered = lax.all_gather(spread, ("section", "dp"), axis=0, tiled=True)
    return gathered.reshape(2, dp, quarter, 16, 128), rest


def sincos(width):
    places = np.arange(NP).astype(np.float32)[:, None]
    column = np.arange(width)
    rates = np.exp(
        -(np.float32(2.0) * (column // 2).astype(np.float32) / np.float32(width))
        * np.float32(math.log(10000.0))
    ).astype(np.float32)
    phases = (places * rates[None, :]).astype(np.float32)
    table = np.where(
        column[None, :] % 2 == 0, np.sin(phases.astype(np.float64)), np.cos(phases.astype(np.float64))
    ).astype(np.float32)
    parts = []
    left = np.zeros((ROWS_D, width), np.float32)
    left[:NP] = table
    for _ in range(3):
        high = left.astype(jnp.bfloat16)
        parts.append(high)
        left = left - high.astype(np.float32)
    return np.stack(parts)


def on_device(patches, keep, perm, master, first, second, ema):
    dp = lax.axis_size("dp")
    section = lax.axis_index("section")
    me = lax.axis_index("dp")
    shard = master.shape[1]
    plan = Plan(dp, shard // 128)
    rows, half = plan.shard_rows, plan.half
    swap = [(0, 1), (1, 0)]
    states = [v.reshape(rows, 1, 128) for v in (master, first, second, ema)]

    following = lax.ppermute(
        states[0][: plan.head_rows], "dp", [(i, i - 1) for i in range(1, dp)]
    )
    index = jnp.asarray(plan.pack_index)[section, me]
    packed = pack(plan, index, states[0], following)
    mine = lax.dynamic_slice_in_dim(packed, section * half, half, 0)
    given = lax.ppermute(
        lax.dynamic_slice_in_dim(packed, (1 - section) * half, half, 0), "section", swap
    )
    half_e = jnp.where(section == 0, mine, given)
    half_d = jnp.where(section == 0, given, mine)
    gathered_e = lax.all_gather(half_e, ("section", "dp"), axis=0, tiled=True)
    gathered_e = gathered_e.reshape(2, dp, half, 16, 128)
    gathered_d = gather_decoder(plan, half_d, section, me, gathered_e)

    count = sum_everywhere(dp, jnp.sum(NP - keep).astype(F32)) * 0.5
    images = patches.shape[0] // 2
    mine = section * images
    patches = lax.dynamic_slice_in_dim(patches, mine, images, 0)
    patches = jnp.pad(patches, ((0, 0), (0, ROWS_D - NP), (0, 0)))
    order = lax.dynamic_slice_in_dim(perm, mine, images, 0)
    order = jnp.pad(order, ((0, 0), (0, ROWS_D - NP)), constant_values=ROWS_D - 1)
    order = order.reshape(images * ROWS_D, 1)
    kept = lax.dynamic_slice_in_dim(keep, mine, images, 0)
    info = jnp.concatenate([section[None].astype(jnp.int32), kept])
    scale = ((1.0 / count) * (1.0 / PIX) * 2.0).reshape(1)

    shape_e = Shape(images, ROWS_E, D, HEADS_E, FF_E)
    shape_d = Shape(images, ROWS_D, DD, HEADS_D, FF_D)
    pp, *saved, latent = encoder(
        plan, shape_e, info, gathered_e, patches, order, jnp.asarray(sincos(D))
    )
    arrays = dict(zip(("x0", "n1", "mixed", "o", "x1", "n2", "g", "gp", "y"), saved))
    arrays["xe"] = pp
    *sums_d, arrays["dz"], loss = decoder(
        plan, shape_d, info, scale, gathered_d, latent, pp, order, jnp.asarray(sincos(DD))
    )

    stages = encoder_back_stages(plan, shape_e)
    first_tail = plan.bins(1)[1][0]
    main = Flow(dp, sums_d[0], sums_d[1], 0)
    rest = Flow(dp, sums_d[2], sums_d[3], first_tail, 1)
    flows, got, _ = move_on([main])
    got, arrays = tie(got, arrays)
    arrive(flows, got)
    low = high = None
    blocks = []
    for number, stage in enumerate(stages):
        flows, got, (arrays, blocks) = move_on([main, rest, high], arrays, blocks)
        blocks, made = stage(info, gathered_e, arrays, blocks)
        arrays = {**arrays, **made}
        got, arrays, blocks = tie(got, arrays, blocks)
        arrive(flows, got)
        if number == 1:
            high = Flow(dp, blocks[2], blocks[3], dp // 2)
            blocks = blocks[:2]
    low = Flow(dp, blocks[0], blocks[1], 0)
    every = [main, rest, high, low]
    while not all(f.done() for f in every):
        flows, got, _ = move_on(every)
        arrive(flows, got)

    sum_tail = rest.result()
    sum_tail = jnp.pad(sum_tail, ((0, half - sum_tail.shape[0]), (0, 0), (0, 0)))
    sum_d = jnp.where(me < first_tail, main.result(), sum_tail)
    sum_e = jnp.where(me < dp // 2, low.result(), high.result())
    squares = [
        squares_of(plan, s, v, section, me) for s, v in enumerate((sum_e, sum_d))
    ]
    sums = sum_everywhere(dp, jnp.stack([squares[0] + squares[1], loss[0, 0]]))
    half_mine = jnp.where(section == 0, sum_e, sum_d)
    half_other = lax.ppermute(jnp.where(section == 0, sum_d, sum_e), "section", swap)
    block = jnp.where(
        section == 0,
        jnp.concatenate([half_mine, half_other], axis=0),
        jnp.concatenate([half_other, half_mine], axis=0),
    )
    start = jnp.asarray(plan.tail_start)[section, me]
    tail = jnp.concatenate(
        [
            lax.dynamic_slice_in_dim(block, start, plan.tail_units, 0),
            block[plan.vec_unit :],
        ],
        axis=0,
    )
    tail = lax.ppermute(tail, "dp", [(i, i + 1) for i in range(dp - 1)])
    index = jnp.asarray(plan.unpack_index)[section, me]
    total = unpack(plan, index, block, tail)
    norm = jnp.sqrt(sums[0])
    factor = jnp.minimum(1.0, clip_limit / (norm + norm_epsilon))
    made = update(plan, factor.reshape(1), total, states)
    return (*[v.reshape(1, shard) for v in made], norm, sums[1], count)


def solution(mesh):
    return jax.shard_map(
        on_device,
        mesh=mesh,
        in_specs=(
            P("dp", None, None),
            P("dp"),
            P("dp", None),
            P("section", "dp"),
            P("section", "dp"),
            P("section", "dp"),
            P("section", "dp"),
        ),
        out_specs=(
            P("section", "dp"),
            P("section", "dp"),
            P("section", "dp"),
            P("section", "dp"),
            P(),
            P(),
            P(),
        ),
        check_vma=False,
    )
```

```python
import functools
import math

import jax
import jax.numpy as jnp
import numpy as np
from jax import lax
from jax.experimental import pallas as pl
from jax.experimental.pallas import tpu as pltpu
from jax.sharding import PartitionSpec as P

D = 768
HEADS_E = 12
FF_E = 3072
DD = 512
HEADS_D = 16
FF_D = 2048
PIX = 768
NP = 196
SLOTS = 98
STEP = 10

norm_epsilon = 1e-06
clip_limit = 0.01
learn_rate = 0.02
beta_one = 0.9
beta_two = 0.999
adam_epsilon = 1e-08
weight_decay = 0.05
average_keep = 0.8

F32 = jnp.float32
BF16 = jnp.bfloat16
ROWS_E = 112
ROWS_D = 208
GROUP = 16
VEC_UNITS = 2
VMEM_BYTES = 60 * 1024 * 1024
COST = 2e8
ANY = pl.BlockSpec(memory_space=pl.ANY)
IN_VMEM = pl.BlockSpec(memory_space=pltpu.VMEM)
IN_SMEM = pl.BlockSpec(memory_space=pltpu.SMEM)

ENC = [
    ("patch", (PIX, D)),
    ("patch_b", (D,)),
    ("g1", (D,)),
    ("b1", (D,)),
    ("qkv", (D, 3 * D)),
    ("proj", (D, D)),
    ("g2", (D,)),
    ("b2", (D,)),
    ("fc1", (D, FF_E)),
    ("fc2", (FF_E, D)),
    ("gf", (D,)),
    ("bf", (D,)),
]
DEC = [
    ("embed", (D, DD)),
    ("mask", (DD,)),
    ("g1", (DD,)),
    ("b1", (DD,)),
    ("qkv", (DD, 3 * DD)),
    ("proj", (DD, DD)),
    ("g2", (DD,)),
    ("b2", (DD,)),
    ("fc1", (DD, FF_D)),
    ("fc2", (FF_D, DD)),
    ("gf", (DD,)),
    ("bf", (DD,)),
    ("head", (DD, PIX)),
]


class Section:
    def __init__(self, layout, dp, shard_rows):
        self.dp = dp
        self.shard_rows = shard_rows
        self.groups = []
        self.vectors = {}
        self.panels = {}
        fill = [0] * dp
        vector_fill = [0] * dp
        row = 0
        for name, shape in layout:
            panels = shape[-1] // 128
            self.panels[name] = panels
            if len(shape) == 2:
                for group in range(shape[0] // GROUP):
                    block = row // shard_rows
                    self.groups.append((name, group, row, panels, block, fill[block]))
                    fill[block] += panels
                    row += GROUP * panels
            else:
                block = row // shard_rows
                self.vectors[name] = (row, panels, block, vector_fill[block])
                vector_fill[block] += panels
                row += panels
        self.rows = row
        self.fill = fill
        assert max(vector_fill) <= 16 * VEC_UNITS
        self.blocks_used = max(b for b in range(dp) if fill[b] or vector_fill[b]) + 1

    def pieces(self, name, first=0, count=None):
        out = []
        for tensor, group, _, panels, block, unit in self.groups:
            if tensor != name or group < first or (count is not None and group >= first + count):
                continue
            if out and out[-1][0] == block and out[-1][1] + out[-1][3] * panels == unit:
                out[-1][3] += 1
            else:
                out.append([block, unit, group, 1])
        return [tuple(p) for p in out]

    def runs(self, name, cuts, first=0, count=None):
        panels = self.panels[name]
        out = []
        for block, unit, group, groups in self.pieces(name, first, count):
            at, left = (group - first) * panels, groups * panels
            while left:
                place = max(i for i in range(len(cuts) - 1) if cuts[i] <= unit)
                take = min(left, cuts[place + 1] - unit)
                out.append((block, place, unit - cuts[place], at, take))
                unit, at, left = unit + take, at + take, left - take
        return out


class Plan:
    def __init__(self, dp, shard_rows):
        self.dp = dp
        self.shard_rows = shard_rows
        self.sections = [Section(ENC, dp, shard_rows), Section(DEC, dp, shard_rows)]
        units = max(max(s.fill) for s in self.sections)
        units += (units + VEC_UNITS) % 2
        self.vec_unit = units
        self.units = units + VEC_UNITS
        self.half = self.units // 2
        half = self.half
        self.quarter = -(-half // 2)
        self.part_cuts = [0, -(-half // 3), -(-2 * half // 3), half]
        self.half_cuts = [0, half, self.units]
        self.head_rows = 8 * -(-max(16 * max(s.panels.values()) for s in self.sections) // 8)
        self.tail_units = max(max(s.panels.values()) for s in self.sections)
        self.pack_base = 8 * -(-shard_rows // 8)
        self.pack_rows = shard_rows + self.head_rows
        self.pack_index = np.zeros((2, dp, self.units * 16), np.int32)
        self.tail_rows = 16 * (self.tail_units + VEC_UNITS)
        self.zero_row = self.units * 16 + self.tail_rows
        self.unpack_index = np.full((2, dp, shard_rows), self.zero_row, np.int32)
        self.tail_start = np.zeros((2, dp), np.int32)
        for s, section in enumerate(self.sections):
            for b in range(dp):
                self.tail_start[s, b] = max(section.fill[b] - self.tail_units, 0)
            for name, group, row, panels, block, unit in section.groups:
                for panel in range(panels):
                    for r in range(GROUP):
                        self.place(s, block, (unit + panel) * 16 + r, row + r * panels + panel)
            for row, panels, block, at in section.vectors.values():
                for panel in range(panels):
                    self.place(s, block, self.vec_unit * 16 + at + panel, row + panel)

    def bins(self, s):
        if s == 0:
            return [(0, self.dp // 2), (self.dp // 2, self.dp - self.dp // 2)]
        used = self.sections[1].blocks_used
        main = 1 << (used.bit_length() - 1)
        return [(0, main), (main, max(used - main, 1))]

    def tail_used(self):
        first, count = self.bins(1)[1]
        section = self.sections[1]
        assert count == 1 and all(v[2] < first for v in section.vectors.values())
        used = section.fill[first]
        return min(used, self.half), max(used - self.half, 0)

    def bin_units(self, s):
        return [self.half, self.half if s == 0 else max(self.tail_used())]

    def place(self, s, block, block_row, flat_row):
        local = flat_row - block * self.shard_rows
        assert 0 <= local < self.pack_rows
        gap = self.pack_base - self.shard_rows if local >= self.shard_rows else 0
        self.pack_index[s, block, block_row] = local + gap
        owner, at = divmod(flat_row, self.shard_rows)
        if owner == block:
            self.unpack_index[s, owner, at] = block_row
        else:
            assert owner == block + 1
            if block_row >= self.vec_unit * 16:
                source = self.tail_units * 16 + block_row - self.vec_unit * 16
            else:
                source = block_row - int(self.tail_start[s, block]) * 16
                assert 0 <= source < self.tail_units * 16
            self.unpack_index[s, owner, at] = self.units * 16 + source


def move_rows_in(index_ref, held, done, count):
    def eight(i, carry):
        for j in range(8):
            row = i * 8 + j
            done[pl.ds(row, 1), :] = held[pl.ds(index_ref[row], 1), :]
        return carry

    lax.fori_loop(0, count // 8, eight, 0)
    for row in range(count // 8 * 8, count):
        done[pl.ds(row, 1), :] = held[pl.ds(index_ref[row], 1), :]


def pack_kernel(base, index_ref, flat, following, out_ref, held, done, sems):
    rows, more = flat.shape[0], following.shape[0]
    copies = [
        pltpu.make_async_copy(flat.at[:, 0], held.at[pl.ds(0, rows)], sems.at[0]),
        pltpu.make_async_copy(following.at[:, 0], held.at[pl.ds(base, more)], sems.at[1]),
    ]
    for copy in copies:
        copy.start()
    for copy in copies:
        copy.wait()
    count = done.shape[0]
    move_rows_in(index_ref, held, done, count)
    out_ref[...] = done[...].reshape(out_ref.shape).astype(BF16)


def pack(plan, index, flat, following):
    count = plan.units * 16
    return pl.pallas_call(
        functools.partial(pack_kernel, plan.pack_base),
        out_shape=jax.ShapeDtypeStruct((plan.units, 16, 128), BF16),
        in_specs=[IN_SMEM, ANY, ANY],
        out_specs=IN_VMEM,
        scratch_shapes=[
            pltpu.VMEM((plan.pack_base + plan.head_rows, 128), F32),
            pltpu.VMEM((count, 128), F32),
            pltpu.SemaphoreType.DMA((2,)),
        ],
        compiler_params=pltpu.CompilerParams(vmem_limit_bytes=32 * 1024 * 1024),
        name="pack_rows",
    )(index, flat, following)


def unpack_kernel(zero_row, rows, index_ref, block, tail, out_ref, held):
    at = 0
    for source in (block, tail):
        size = source.shape[0] * 16
        held[pl.ds(at, size), :] = source[...].reshape(size, 128)
        at += size
    held[pl.ds(zero_row, 8), :] = jnp.zeros((8, 128), F32)
    out_ref[pl.ds(out_ref.shape[0] - 16, 16), :] = jnp.zeros((16, 128), F32)
    move_rows_in(index_ref, held, out_ref, rows)


def unpack(plan, index, block, tail):
    rows = plan.shard_rows
    padded = 16 * -(-rows // 16)
    return pl.pallas_call(
        functools.partial(unpack_kernel, plan.zero_row, rows),
        out_shape=jax.ShapeDtypeStruct((padded, 128), F32),
        in_specs=[IN_SMEM, IN_VMEM, IN_VMEM],
        out_specs=IN_VMEM,
        scratch_shapes=[pltpu.VMEM((plan.zero_row + 8, 128), F32)],
        compiler_params=pltpu.CompilerParams(vmem_limit_bytes=32 * 1024 * 1024),
        name="unpack_rows",
    )(index, block, tail)


def update_kernel(rows, chunk, factor_ref, total, *refs):
    states, outs, held, made, in_sems, out_sems = (
        refs[:4], refs[4:8], refs[8:12], refs[12:16], refs[16], refs[17],
    )
    starts = list(range(0, rows, chunk))
    sizes = [min(chunk, rows - at) for at in starts]
    loads = [
        [
            pltpu.make_async_copy(
                source.at[pl.ds(at, size), 0], ref.at[pl.ds(at, size)], in_sems.at[k, j]
            )
            for j, (source, ref) in enumerate(zip(states, held))
        ]
        for k, (at, size) in enumerate(zip(starts, sizes))
    ]
    for group in loads:
        for copy in group:
            copy.start()
    stores = []
    factor = factor_ref[0]
    for k, (at, size) in enumerate(zip(starts, sizes)):
        for copy in loads[k]:
            copy.wait()

        def body(i, carry):
            here = pl.ds(pl.multiple_of(at + i * 16, 8), 16)
            master, first, second, ema = (ref[here, :] for ref in held)
            clipped = total[here, :] * factor
            new_first = beta_one * first + (1.0 - beta_one) * clipped
            new_second = beta_two * second + (1.0 - beta_two) * clipped * clipped
            first_hat = new_first * (1.0 / (1.0 - beta_one**STEP))
            second_hat = new_second * (1.0 / (1.0 - beta_two**STEP))
            new_master = master - learn_rate * (
                first_hat / (jnp.sqrt(second_hat) + adam_epsilon) + weight_decay * master
            )
            made[0][here, :] = new_master
            made[1][here, :] = new_first
            made[2][here, :] = new_second
            made[3][here, :] = average_keep * ema + (1.0 - average_keep) * new_master
            return carry

        lax.fori_loop(0, -(-size // 16), body, 0, unroll=2)
        for j in range(4):
            copy = pltpu.make_async_copy(
                made[j].at[pl.ds(at, size)], outs[j].at[pl.ds(at, size), 0], out_sems.at[k, j]
            )
            copy.start()
            stores.append(copy)
    for copy in stores:
        copy.wait()


def update(plan, factor, total, states):
    rows = plan.shard_rows
    chunk = 16 * -(-rows // (16 * 4))
    padded = 16 * -(-rows // 16)
    count = -(-rows // chunk)
    return pl.pallas_call(
        functools.partial(update_kernel, rows, chunk),
        out_shape=[jax.ShapeDtypeStruct((rows, 1, 128), F32)] * 4,
        in_specs=[IN_SMEM, IN_VMEM, *[ANY] * 4],
        out_specs=[ANY] * 4,
        scratch_shapes=[
            *[pltpu.VMEM((padded, 128), F32)] * 8,
            pltpu.SemaphoreType.DMA((count, 4)),
            pltpu.SemaphoreType.DMA((count, 4)),
        ],
        compiler_params=pltpu.CompilerParams(vmem_limit_bytes=VMEM_BYTES),
        name="update_states",
    )(factor, total, *states)


def dot(a, b):
    return lax.dot_general(a, b, (((1,), (0,)), ((), ())), preferred_element_type=F32)


def dot_nt(a, b):
    return lax.dot_general(a, b, (((1,), (1,)), ((), ())), preferred_element_type=F32)


def dot_tn(a, b):
    return lax.dot_general(a, b, (((0,), (0,)), ((), ())), preferred_element_type=F32)


def total_of(terms):
    total = terms[0]
    for term in terms[1:]:
        total = total + term
    return total


def for_rows(count, size, step, unroll=1):
    def body(i, carry):
        step(pl.multiple_of(i * size, size))
        return carry

    lax.fori_loop(0, count // size, body, 0, unroll=unroll)


def columns(weight, depth, first, count):
    parts = [weight[:, first + i].reshape(depth, 128) for i in range(count)]
    return jnp.concatenate(parts, axis=1)


def row_band(weight, panels, band):
    parts = [weight[pl.ds(band * 16, 16), i].reshape(256, 128) for i in range(panels)]
    return jnp.concatenate(parts, axis=1)


def row_chunks(count):
    size = next(n for n in (208, 224, 112, 104, 16) if count % n == 0)
    return [slice(at, at + size) for at in range(0, count, size)]


def wide_chunks(count):
    size = next(n for n in (416, 336, 112, 104, 16) if count % n == 0)
    return [slice(at, at + size) for at in range(0, count, size)]


def times_columns(left, weight, panels, depth, finish):
    group = 4 if panels % 4 == 0 else 2

    def body(index, carry):
        right = columns(weight, depth, group * index, group)
        width = group * 128
        there = pl.ds(pl.multiple_of(index * width, width), width)
        for here in row_chunks(left.shape[0]):
            finish(index * width, here, there, dot(left[here, :], right))
        return carry

    lax.fori_loop(0, panels // group, body, 0)


def times_bands(left, weight, panels, count, finish):
    def body(band, carry):
        right = row_band(weight, panels, band)
        for here in wide_chunks(left.shape[0]):
            finish(here, lanes(band), dot_nt(left[here, :], right))
        return carry

    lax.fori_loop(0, count // 256, body, 0)


def lanes(pair):
    return pl.ds(pl.multiple_of(pair * 256, 256), 256)


def norm_block(count):
    return next(n for n in (224, 208, 112, 104, 16) if count % n == 0)


def norm_rows(x, width):
    mean = jnp.sum(x, axis=1, keepdims=True) * (1.0 / width)
    centre = x - mean
    spread = jnp.sum(centre * centre, axis=1, keepdims=True) * (1.0 / width)
    rstd = lax.rsqrt(spread + norm_epsilon)
    return centre * rstd, rstd


def norm_forward(x_ref, gain, shift, out_ref, count, width):
    size = norm_block(count)

    def step(at):
        hat, _ = norm_rows(x_ref[pl.ds(at, size), :], width)
        out_ref[pl.ds(at, size), :] = (hat * gain + shift).astype(out_ref.dtype)

    for_rows(count, size, step)


def norm_backward(x_ref, gain, grad_of, put, count, width):
    size = norm_block(count)

    def body(i, carry):
        gain_sum, shift_sum = carry
        at = pl.multiple_of(i * size, size)
        hat, rstd = norm_rows(x_ref[pl.ds(at, size), :], width)
        grad = grad_of(at, size)
        gain_sum = gain_sum + jnp.sum((grad * hat).reshape(size // 8, 8, width), axis=0)
        shift_sum = shift_sum + jnp.sum(grad.reshape(size // 8, 8, width), axis=0)
        scaled = grad * gain
        first = jnp.sum(scaled, axis=1, keepdims=True) * (1.0 / width)
        second = jnp.sum(scaled * hat, axis=1, keepdims=True) * (1.0 / width)
        put(at, size, rstd * (scaled - first - hat * second))
        return gain_sum, shift_sum

    zero = jnp.zeros((8, width), F32)
    gain_sum, shift_sum = lax.fori_loop(0, count // size, body, (zero, zero))
    return jnp.sum(gain_sum, axis=0, keepdims=True), jnp.sum(shift_sum, axis=0, keepdims=True)


def head_masks(size):
    lane = lax.broadcasted_iota(jnp.int32, (1, 128), 1)
    return [
        jnp.where((lane >= h * size) & (lane < (h + 1) * size), 1.0, 0.0).astype(BF16)
        for h in range(128 // size)
    ]


def softmax_columns(scores, limit):
    key = lax.broadcasted_iota(jnp.int32, scores.shape, 0)
    scores = jnp.where(key < limit, scores, -1e30)
    top = jnp.max(scores, axis=0, keepdims=True)
    raised = jnp.exp(scores - top)
    return raised * (1.0 / jnp.sum(raised, axis=0, keepdims=True))


def softmax_rows(scores, limit):
    key = lax.broadcasted_iota(jnp.int32, scores.shape, 1)
    scores = jnp.where(key < limit, scores, -1e30)
    top = jnp.max(scores, axis=1, keepdims=True)
    raised = jnp.exp(scores - top)
    return raised * (1.0 / jnp.sum(raised, axis=1, keepdims=True))


def attention_forward(mixed, out, limit_of, images, rows, width, size):
    panels = width // 128
    masks = head_masks(size)

    def body(step, carry):
        image, panel = step // panels, step % panels
        here = pl.ds(pl.multiple_of(image * rows, 16), rows)

        def part(third):
            return mixed[here, pl.ds(pl.multiple_of((third * panels + panel) * 128, 128), 128)]

        query, keys, values = part(0), part(1), part(2)
        limit = limit_of(image)
        probs = [softmax_rows(dot_nt(query * mask, keys), limit).astype(BF16) for mask in masks]
        total = total_of([dot(p, values) * m.astype(F32) for p, m in zip(probs, masks)])
        out[here, pl.ds(pl.multiple_of(panel * 128, 128), 128)] = total.astype(BF16)
        return carry

    lax.fori_loop(0, images * panels, body, 0, unroll=6)


def attention_backward(mixed, grad_out, grad_mixed, limit_of, images, rows, width, size):
    panels = width // 128
    masks = head_masks(size)

    def body(step, carry):
        image, panel = step // panels, step % panels
        here = pl.ds(pl.multiple_of(image * rows, 16), rows)

        def place(third):
            return pl.ds(pl.multiple_of((third * panels + panel) * 128, 128), 128)

        query, keys, values = (mixed[here, place(third)] for third in range(3))
        grad = grad_out[here, place(0)]
        turned = keys.T
        limit = limit_of(image)
        zero = jnp.zeros((rows, 128), F32)
        grad_query, grad_keys, grad_values = [], zero, zero
        for h, mask in enumerate(masks):
            masked_query = query * mask
            masked_grad = grad * mask
            probs = softmax_columns(dot_nt(keys, masked_query), limit)
            grad_probs = dot_nt(values, masked_grad)
            inner = jnp.sum(probs * grad_probs, axis=0, keepdims=True)
            grad_scores = (probs * (grad_probs - inner)).astype(BF16)
            grad_values = grad_values + dot(probs.astype(BF16), masked_grad)
            grad_keys = grad_keys + dot(grad_scores, masked_query)
            grad_query.append(dot(turned[h * size : h * size + size, :], grad_scores))
        grad_query = jnp.concatenate(grad_query, axis=0) * (1.0 / math.sqrt(size))
        grad_mixed[here, place(0)] = grad_query.astype(BF16).T
        grad_mixed[here, place(1)] = grad_keys.astype(BF16)
        grad_mixed[here, place(2)] = grad_values.astype(BF16)
        return carry

    lax.fori_loop(0, images * panels, body, 0, unroll=3)


def gelu_parts(value):
    bell = 0.5 * (1.0 + lax.erf(value * math.sqrt(0.5)))
    slope = bell + value * (jnp.exp(value * value * -0.5) * (1.0 / math.sqrt(2.0 * math.pi)))
    return value * bell, slope


class Shape:
    def __init__(self, images, rows, width, heads, hidden):
        self.images, self.rows, self.width = images, rows, width
        self.size = width // heads
        self.hidden = hidden
        self.count = images * rows


def block_forward(sh, x0, n1, mixed, o, x1, n2, g, gp, y, w, vec, limit_of, ready, saved):
    width, hidden, count = sh.width, sh.hidden, sh.count
    panels = width // 128
    norm_forward(x0, vec("g1"), vec("b1"), n1, count, width)
    saved(n1)
    ready("qkv")

    def put_mixed(start, here, there, value):
        scale = jnp.where(start < width, 1.0 / math.sqrt(sh.size), 1.0)
        mixed[here, there] = (value * scale).astype(BF16)

    times_columns(n1, w["qkv"], 3 * panels, width, put_mixed)
    saved(mixed)
    attention_forward(mixed, o, limit_of, sh.images, sh.rows, width, sh.size)
    saved(o)
    ready("proj")

    def put_sum(base, out):
        def finish(_, here, there, value):
            out[here, there] = base[here, there] + value

        return finish

    times_columns(o, w["proj"], panels, width, put_sum(x0, x1))
    saved(x1)
    norm_forward(x1, vec("g2"), vec("b2"), n2, count, width)
    saved(n2)
    ready("fc1")

    def put_hidden(_, here, there, value):
        value, slope = gelu_parts(value)
        g[here, there] = value.astype(BF16)
        gp[here, there] = slope

    times_columns(n2, w["fc1"], hidden // 128, width, put_hidden)
    saved(g)
    saved(gp)
    ready("fc2")
    times_columns(g, w["fc2"], panels, hidden, put_sum(x1, y))
    saved(y)


class Gradients:
    def __init__(self, plan, s, own, stage, sems, targets):
        self.plan, self.section, self.own = plan, plan.sections[s], own
        self.bins = plan.bins(s)
        self.stage, self.sems, self.targets = stage, sems, targets
        self.turn = 0
        self.flying = [[], []]

    def copy_out(self, source, block, side, unit, take, sem):
        which = max(i for i, (first, _) in enumerate(self.bins) if first <= block)
        block = block - self.bins[which][0]
        keep, send = self.targets[2 * which], self.targets[2 * which + 1]

        def to(target):
            return pltpu.make_async_copy(source, target.at[block, pl.ds(unit, take)], sem)

        @pl.when(self.own == side)
        def _():
            to(keep).start()

        @pl.when(self.own != side)
        def _():
            to(send).start()

        return to(keep)

    def drain(self, slot):
        for copy in self.flying[slot]:
            copy.wait()
        self.flying[slot] = []

    def weight(self, name, left, depth, right, turned):
        panels = self.section.panels[name]
        for band in range(depth // 256):
            slot = self.turn % 2
            self.turn += 1
            self.drain(slot)
            stage = self.stage.at[slot]
            turned[...] = left[:, band * 256 : band * 256 + 256].T

            def body(pair, carry):
                value = dot(turned[...], right[:, lanes(pair)])
                for i in range(2):
                    stage[pl.ds(2 * pair + i, 16, stride=panels)] = value[
                        :, i * 128 : i * 128 + 128
                    ].reshape(16, 16, 128)
                return carry

            lax.fori_loop(0, panels // 2, body, 0)
            for block, side, unit, at, take in self.section.runs(
                name, self.plan.half_cuts, band * 16, 16
            ):
                self.flying[slot].append(
                    self.copy_out(
                        stage.at[pl.ds(at, take)], block, side, unit, take, self.sems.at[slot]
                    )
                )

    def finish(self, values, scratch):
        vectors = self.section.vectors
        blocks = sorted({vectors[name][2] for name in values})
        for k, block in enumerate(blocks):
            scratch[k] = jnp.zeros((VEC_UNITS, 16, 128), F32)
            for name, (_, panels, at_block, at) in vectors.items():
                if at_block != block:
                    continue
                for panel in range(panels):
                    unit, row = divmod(at + panel, 16)
                    scratch[k, unit, row : row + 1, :] = values[name][
                        :, panel * 128 : panel * 128 + 128
                    ]
        unit = self.plan.vec_unit - self.plan.half
        copies = [
            self.copy_out(scratch.at[k], block, 1, unit, VEC_UNITS, self.sems.at[2])
            for k, block in enumerate(blocks)
        ]
        for copy in copies:
            copy.wait()
        self.drain(0)
        self.drain(1)


class Backward:
    def __init__(self, sh, w, vec, limit_of, grads, values, turned, ready):
        self.sh, self.w, self.vec, self.limit_of = sh, w, vec, limit_of
        self.grads, self.values, self.turned, self.ready = grads, values, turned, ready
        self.panels = sh.width // 128

    def round_stream(self, dy, dyb):
        def step(at):
            dyb[pl.ds(at, 16), :] = dy[pl.ds(at, 16), :].astype(BF16)

        for_rows(self.sh.count, 16, step, 4)

    def bands(self, left, name, count, put):
        times_bands(left, self.w[name], self.grads.section.panels[name], count, put)

    def through_norm(self, x, dn, dy, gain, shift, dn_is=None):
        def from_dn(at, size):
            return dn[pl.ds(at, size), :]

        def into_stream(at, size, value):
            dy[pl.ds(at, size), :] = dy[pl.ds(at, size), :] + value

        self.values[gain], self.values[shift] = norm_backward(
            x, self.vec(gain), from_dn, into_stream, self.sh.count, self.sh.width
        )

    def second_product(self, dy, dyb, g, gp):
        self.round_stream(dy, dyb)
        self.ready("fc2", g)
        self.grads.weight("fc2", g, self.sh.hidden, dyb, self.turned)
        self.ready(None, gp)

        def put(here, there, value):
            g[here, there] = (value * gp[here, there]).astype(BF16)

        self.bands(dyb, "fc2", self.sh.hidden, put)

    def first_product(self, dy, g, n2, x1, dn):
        def put(here, there, value):
            dn[here, there] = value

        self.ready("fc1", n2)
        self.grads.weight("fc1", n2, self.sh.width, g, self.turned)
        self.bands(g, "fc1", self.sh.width, put)
        self.ready(None, x1)
        self.through_norm(x1, dn, dy, "g2", "b2")

    def projection(self, dy, dyb, o, grad):
        sh = self.sh
        self.round_stream(dy, dyb)
        self.ready("proj", o)
        self.grads.weight("proj", o, sh.width, dyb, self.turned)

        def put(here, there, value):
            grad[here, there] = value.astype(BF16)

        self.bands(dyb, "proj", sh.width, put)

    def attention(self, grad, mixed, dmixed):
        sh = self.sh
        self.ready(None, grad)
        self.ready(None, mixed)
        attention_backward(mixed, grad, dmixed, self.limit_of, sh.images, sh.rows, sh.width, sh.size)

    def mixing(self, dy, dmixed, n1, x0, dn):
        def put(here, there, value):
            dn[here, there] = value

        self.ready("qkv", n1)
        self.grads.weight("qkv", n1, self.sh.width, dmixed, self.turned)
        self.bands(dmixed, "qkv", self.sh.width, put)
        self.ready(None, x0)
        self.through_norm(x0, dn, dy, "g1", "b1")


def held_at(plan, s, gathered, block, side, unit, take):
    if s == 0:
        return [(gathered[0].at[side, block, pl.ds(unit, take)], 0, take)]
    if block == plan.bins(1)[1][0]:
        return [(gathered[1].at[side, pl.ds(unit, take)], 0, take)]
    out = []
    quarter = plan.quarter
    if unit < quarter:
        few = min(take, quarter - unit)
        out.append((gathered[0].at[side, 2 * block, pl.ds(unit, few)], 0, few))
    if unit + take > quarter:
        skip = max(quarter - unit, 0)
        few = take - skip
        source = gathered[0].at[side, 2 * block + 1, pl.ds(unit + skip - quarter, few)]
        out.append((source, skip, few))
    return out


def load_vectors(plan, s, gathered, held, vec_ref, sem):
    section = plan.sections[s]
    blocks = sorted({v[2] for v in section.vectors.values()})
    copies = [
        pltpu.make_async_copy(source, held.at[k, pl.ds(skip, few)], sem)
        for k, block in enumerate(blocks)
        for source, skip, few in held_at(
            plan, s, gathered, block, 1, plan.vec_unit - plan.half, VEC_UNITS
        )
    ]
    for copy in copies:
        copy.start()
    names = {name: i for i, name in enumerate(section.vectors)}

    def finish():
        for copy in copies:
            copy.wait()
        for k, block in enumerate(blocks):
            rows = held[k].reshape(16 * VEC_UNITS, 128).astype(F32)
            for name, (_, panels, at_block, at) in section.vectors.items():
                if at_block != block:
                    continue
                i = names[name]
                for panel in range(panels):
                    vec_ref[i : i + 1, panel * 128 : panel * 128 + 128] = rows[
                        at + panel : at + panel + 1, :
                    ]
        return lambda name: vec_ref[names[name] : names[name] + 1, :]

    return finish


def load_weights(plan, s, gathered, w, sems):
    section = plan.sections[s]
    copies = {}
    for k, (name, ref) in enumerate(w.items()):
        panels = section.panels[name]
        flat = ref.reshape(ref.shape[0] * panels, 16, 128)
        copies[name] = [
            pltpu.make_async_copy(source, flat.at[pl.ds(at + skip, few)], sems.at[k])
            for block, side, unit, at, take in section.runs(name, plan.half_cuts)
            for source, skip, few in held_at(plan, s, gathered, block, side, unit, take)
        ]
        for copy in copies[name]:
            copy.start()

    def ready(name):
        for copy in copies.get(name, ()):
            copy.wait()

    return ready


def weight_scratch(layout, names):
    shapes = dict(layout)
    return [
        pltpu.VMEM((shapes[n][0] // GROUP, shapes[n][1] // 128, GROUP, 128), BF16)
        for n in names
    ]


def picks(perm_ref, image):
    here = pl.ds(pl.multiple_of(image * ROWS_D, 16), ROWS_D)
    patch = lax.broadcasted_iota(jnp.int32, (ROWS_D, ROWS_D), 1)
    return jnp.where(perm_ref[here, :] == patch, 1.0, 0.0).astype(BF16)


W_ENC = ["patch", "qkv", "proj", "fc1", "fc2"]


def encoder_kernel(plan, sh, refs):
    (info, gathered, patches, perm, pos, pp_out, x0_out, n1_out, mixed_out, o_out, x1_out, n2_out,
     g_out, gp_out, y_out, latent_out, w_patch, w_qkv, w_proj, w_fc1, w_fc2, held, vec_ref, pp, xe,
     x0, n1, mixed, o, x1, n2, g, gp, y, latent, w_sems, out_sems) = refs
    w = dict(zip(W_ENC, (w_patch, w_qkv, w_proj, w_fc1, w_fc2)))
    finish_vec = load_vectors(plan, 0, [gathered], held, vec_ref, w_sems.at[5])
    ready = load_weights(plan, 0, [gathered], w, w_sems)
    outs = []

    targets = [(pp, pp_out), (x0, x0_out), (n1, n1_out), (mixed, mixed_out), (o, o_out),
               (x1, x1_out), (n2, n2_out), (g, g_out), (gp, gp_out), (y, y_out),
               (latent, latent_out)]

    def saved(ref):
        for k, (source, target) in enumerate(targets):
            if source is ref:
                copy = pltpu.make_async_copy(source, target, out_sems.at[k])
                copy.start()
                outs.append(copy)

    def gather(image, carry):
        chosen = picks(perm, image)
        pp[image] = dot(chosen, patches[image]).astype(BF16)
        here = pl.ds(pl.multiple_of(image * ROWS_E, 16), ROWS_E)
        xe[here, :] = pp[image, 0:ROWS_E, :]
        few = chosen[0:ROWS_E, :]
        x0[here, :] = (dot(few, pos[0]) + dot(few, pos[1])) + dot(few, pos[2])
        return carry

    lax.fori_loop(0, sh.images, gather, 0)
    saved(pp)
    vec = finish_vec()
    ready("patch")

    def put(_, here, there, value):
        x0[here, there] = (value + vec_ref[0:1, there]) + x0[here, there]

    times_columns(xe, w["patch"], D // 128, PIX, put)
    saved(x0)
    block_forward(
        sh, x0, n1, mixed, o, x1, n2, g, gp, y, w, vec, lambda i: info[1 + i], ready, saved
    )
    norm_forward(y, vec("gf"), vec("bf"), latent, sh.count, D)
    saved(latent)
    for copy in outs:
        copy.wait()


def lasting(microseconds):
    return pl.CostEstimate(
        flops=int(microseconds * COST), bytes_accessed=1 << 20, transcendentals=0
    )


def saved_shapes(sh):
    count, width, hidden = sh.count, sh.width, sh.hidden
    return [
        ((count, width), F32),
        ((count, width), BF16),
        ((count, 3 * width), BF16),
        ((count, width), BF16),
        ((count, width), F32),
        ((count, width), BF16),
        ((count, hidden), BF16),
        ((count, hidden), F32),
        ((count, width), F32),
    ]


def encoder(plan, sh, info, gathered, patches, perm, pos):
    saved = saved_shapes(sh)
    pp_shape = ((sh.images, ROWS_D, PIX), BF16)
    latent_shape = ((sh.count, D), BF16)
    outs = [pp_shape, *saved, latent_shape]
    holders = len({v[2] for v in plan.sections[0].vectors.values()})
    return pl.pallas_call(
        lambda *refs: encoder_kernel(plan, sh, refs),
        out_shape=[jax.ShapeDtypeStruct(*s) for s in outs],
        in_specs=[IN_SMEM, ANY, IN_VMEM, IN_VMEM, IN_VMEM],
        out_specs=[ANY] * len(outs),
        scratch_shapes=[
            *weight_scratch(ENC, W_ENC),
            pltpu.VMEM((holders, VEC_UNITS, 16, 128), BF16),
            pltpu.VMEM((8, D), F32),
            pltpu.VMEM(*pp_shape),
            pltpu.VMEM((sh.count, PIX), BF16),
            *[pltpu.VMEM(*s) for s in saved],
            pltpu.VMEM(*latent_shape),
            pltpu.SemaphoreType.DMA((6,)),
            pltpu.SemaphoreType.DMA((len(outs),)),
        ],
        compiler_params=pltpu.CompilerParams(vmem_limit_bytes=VMEM_BYTES),
        cost_estimate=lasting(50),
        name="encoder_forward",
    )(info, gathered, patches, perm, pos)


W_DEC = ["embed", "qkv", "proj", "fc1", "fc2", "head"]


def decoder_kernel(plan, sh, refs):
    info, scale, gathered, gathered_tail, latent_in, pp_in, perm, pos = refs[:8]
    gathered = [gathered, gathered_tail]
    targets, refs = refs[8:12], refs[12:]
    (grad_latent, loss_out,
     w_embed, w_qkv, w_proj, w_fc1, w_fc2, w_head, held, vec_ref, pp, latent, embedded, x0, n1,
     mixed, o, x1, n2, g, gp, y, f, dn, guess, turned, turned_e, stage, vec_stage, w_sems,
     in_sems, grad_sems) = refs
    w = dict(zip(W_DEC, (w_embed, w_qkv, w_proj, w_fc1, w_fc2, w_head)))
    copy_latent = pltpu.make_async_copy(latent_in, latent, in_sems.at[0])
    copy_pp = pltpu.make_async_copy(pp_in, pp, in_sems.at[1])
    copy_latent.start()
    finish_vec = load_vectors(plan, 1, gathered, held, vec_ref, w_sems.at[6])
    ready = load_weights(plan, 1, gathered, w, w_sems)
    copy_pp.start()
    images, count = sh.images, sh.count
    count_e = images * ROWS_E
    vec = finish_vec()
    copy_latent.wait()
    ready("embed")

    def put_embedded(_, here, there, value):
        embedded[here, there] = value

    times_columns(latent, w["embed"], DD // 128, D, put_embedded)

    def tokens(image, carry):
        chosen = picks(perm, image)
        place = (dot(chosen, pos[0]) + dot(chosen, pos[1])) + dot(chosen, pos[2])
        start = pl.multiple_of(image * ROWS_D, 16)
        kept = info[1 + image]
        token = vec_ref[0:1, :]
        few = embedded[pl.ds(pl.multiple_of(image * ROWS_E, 16), ROWS_E), :]
        rank = lax.broadcasted_iota(jnp.int32, (ROWS_E, DD), 0)
        x0[pl.ds(start, ROWS_E), :] = jnp.where(rank < kept, few, token) + place[:ROWS_E, :]
        x0[pl.ds(start + ROWS_E, ROWS_D - ROWS_E), :] = token + place[ROWS_E:, :]
        return carry

    lax.fori_loop(0, images, tokens, 0)
    block_forward(
        sh, x0, n1, mixed, o, x1, n2, g, gp, y, w, vec, lambda i: NP, ready, lambda ref: None
    )
    norm_forward(y, vec("gf"), vec("bf"), f, count, DD)
    ready("head")
    copy_pp.wait()
    factor = scale[0]

    def predict_image(image, total):
        start = pl.multiple_of(image * ROWS_D, 16)
        kept = info[1 + image]
        here = pl.ds(start, ROWS_D)
        for pair in range(PIX // 256):
            guess[:, pair * 256 : pair * 256 + 256] = dot(
                f[here, :], columns(w["head"], DD, 2 * pair, 2)
            )

        def rows(i, total):
            at = pl.multiple_of(i * 16, 16)
            target, _ = norm_rows(pp[image, pl.ds(at, 16), :].astype(F32), PIX)
            off = guess[pl.ds(at, 16), :] - target
            rank = lax.broadcasted_iota(jnp.int32, (16, PIX), 0) + at
            off = jnp.where((rank >= kept) & (rank < NP), off, 0.0)
            pp[image, pl.ds(at, 16), :] = (off * factor).astype(BF16)
            return total + jnp.sum((off * off).reshape(2, 8, PIX), axis=0)

        return lax.fori_loop(0, ROWS_D // 16, rows, total)

    total = lax.fori_loop(0, images, predict_image, jnp.zeros((8, PIX), F32))
    total = jnp.sum(jnp.sum(total, axis=0, keepdims=True), axis=1, keepdims=True)
    loss_out[...] = jnp.broadcast_to(total * (1.0 / PIX), (8, 128))

    grads = Gradients(plan, 1, info[0], stage, grad_sems, targets)
    values = {}
    back = Backward(
        sh, w, vec, lambda i: NP, grads, values, turned, lambda name, ref: None
    )
    dpred = pp.reshape(count, PIX)
    grads.weight("head", f, DD, dpred, turned)

    def put_dn(here, there, value):
        dn[here, there] = value

    back.bands(dpred, "head", DD, put_dn)

    def from_dn(at, size):
        return dn[pl.ds(at, size), :]

    def put_y(at, size, value):
        y[pl.ds(at, size), :] = value

    values["gf"], values["bf"] = norm_backward(y, vec("gf"), from_dn, put_y, count, DD)
    back.second_product(y, f, g, gp)
    back.first_product(y, g, n2, x1, dn)
    dmixed = g.at[:, pl.ds(0, 3 * DD)]
    back.projection(y, f, o, o)
    back.attention(o, mixed, dmixed)
    back.mixing(y, dmixed, n1, x0, dn)

    def split(image, total):
        start = pl.multiple_of(image * ROWS_D, 16)
        kept = info[1 + image]

        def rows(i, total):
            at = pl.multiple_of(i * 16, 16)
            grad = y[pl.ds(start + at, 16), :]
            rank = lax.broadcasted_iota(jnp.int32, (16, DD), 0) + at
            free = jnp.where(rank >= kept, grad, 0.0)

            @pl.when(i < ROWS_E // 16)
            def _():
                taken = jnp.where(rank < kept, grad, 0.0).astype(BF16)
                n1[pl.ds(pl.multiple_of(image * ROWS_E, 16) + at, 16), :] = taken

            return total + jnp.sum(free.reshape(2, 8, DD), axis=0)

        return lax.fori_loop(0, ROWS_D // 16, rows, total)

    total = lax.fori_loop(0, images, split, jnp.zeros((8, DD), F32))
    values["mask"] = jnp.sum(total, axis=0, keepdims=True)
    placed = n1.at[pl.ds(0, count_e)]
    grads.weight("embed", latent, D, placed, turned_e)

    def put_latent(here, there, value):
        grad_latent[here, there] = value.astype(BF16)

    times_bands(placed, w["embed"], DD // 128, D, put_latent)
    grads.finish(values, vec_stage)


def grad_shapes(plan, s):
    return [
        jax.ShapeDtypeStruct((count, units, 16, 128), F32)
        for (_, count), units in zip(plan.bins(s), plan.bin_units(s))
        for _ in range(2)
    ]


def decoder(plan, sh, info, scale, gathered, latent, pp, perm, pos):
    count_e = sh.images * ROWS_E
    holders = len({v[2] for v in plan.sections[1].vectors.values()})
    saved = saved_shapes(sh)
    most = max(plan.sections[1].panels.values())
    return pl.pallas_call(
        lambda *refs: decoder_kernel(plan, sh, refs),
        out_shape=[
            *grad_shapes(plan, 1),
            jax.ShapeDtypeStruct((count_e, D), BF16),
            jax.ShapeDtypeStruct((8, 128), F32),
        ],
        in_specs=[IN_SMEM, IN_SMEM, ANY, ANY, ANY, ANY, IN_VMEM, IN_VMEM],
        out_specs=[*[ANY] * 4, IN_VMEM, IN_VMEM],
        scratch_shapes=[
            *weight_scratch(DEC, W_DEC),
            pltpu.VMEM((holders, VEC_UNITS, 16, 128), BF16),
            pltpu.VMEM((8, DD), F32),
            pltpu.VMEM((sh.images, ROWS_D, PIX), BF16),
            pltpu.VMEM((count_e, D), BF16),
            pltpu.VMEM((count_e, DD), F32),
            *[pltpu.VMEM(*s) for s in saved],
            pltpu.VMEM((sh.count, DD), BF16),
            pltpu.VMEM((sh.count, DD), F32),
            pltpu.VMEM((ROWS_D, PIX), F32),
            pltpu.VMEM((256, sh.count), BF16),
            pltpu.VMEM((256, count_e), BF16),
            pltpu.VMEM((2, 16 * most, 16, 128), F32),
            pltpu.VMEM((holders, VEC_UNITS, 16, 128), F32),
            pltpu.SemaphoreType.DMA((7,)),
            pltpu.SemaphoreType.DMA((2,)),
            pltpu.SemaphoreType.DMA((3,)),
        ],
        compiler_params=pltpu.CompilerParams(vmem_limit_bytes=VMEM_BYTES),
        cost_estimate=lasting(160),
        name="decoder_both",
    )(info, scale, *gathered, latent, pp, perm, pos)


class Stage:
    def __init__(self, plan, sh, weights, reads, temps, outs, most, cost, name, body, bins=2):
        self.plan, self.sh, self.weights, self.reads = plan, sh, weights, reads
        self.temps, self.outs, self.most, self.cost, self.name = temps, outs, most, cost, name
        self.body = body
        self.bins = bins

    def kernel(self, blocks, *refs):
        refs = list(refs)

        def take(count):
            got = refs[:count]
            del refs[:count]
            return got

        plan, sh = self.plan, self.sh
        info, gathered = take(2)
        sources = dict(zip(self.reads, take(len(self.reads))))
        take(blocks)
        targets = take(2 * self.bins)
        results = dict(zip(self.outs, take(len(self.outs))))
        w = dict(zip(self.weights, take(len(self.weights))))
        here = dict(zip(self.reads, take(len(self.reads))))
        temps = dict(zip(self.temps, take(len(self.temps))))
        held, vec_ref, turned, stage, vec_stage, w_sems, in_sems, grad_sems = refs
        finish_vec = load_vectors(plan, 0, [gathered], held, vec_ref, w_sems.at[len(w)])
        loads = {}
        for k, (name, ref) in enumerate(here.items()):
            if name == "xe":
                copies = [
                    pltpu.make_async_copy(
                        sources[name].at[i, pl.ds(0, ROWS_E)],
                        ref.at[pl.ds(i * ROWS_E, ROWS_E)],
                        in_sems.at[k],
                    )
                    for i in range(sh.images)
                ]
            else:
                copies = [pltpu.make_async_copy(sources[name], ref, in_sems.at[k])]
            for copy in copies:
                copy.start()
            loads[id(ref)] = copies
        weights_ready = load_weights(plan, 0, [gathered], w, w_sems)
        vec = finish_vec()

        def ready(name, ref=None):
            for copy in loads.pop(id(ref), ()):
                copy.wait()
            if name is not None:
                weights_ready(name)

        values = {}
        grads = Gradients(plan, 0, info[0], stage, grad_sems, targets)
        back = Backward(
            sh, w, vec, lambda i: info[1 + i], grads, values, turned, ready
        )
        self.body(back, {**here, **temps}, results)
        assert not loads
        grads.finish(values, vec_stage)

    def __call__(self, info, gathered, arrays, blocks):
        plan, sh = self.plan, self.sh
        count, width, hidden = sh.count, sh.width, sh.hidden
        known = {
            "dz": ((count, width), BF16),
            "y": ((count, width), F32),
            "dy": ((count, width), F32),
            "x0": ((count, width), F32),
            "x1": ((count, width), F32),
            "dn": ((count, width), F32),
            "n1": ((count, width), BF16),
            "n2": ((count, width), BF16),
            "o": ((count, width), BF16),
            "dyb": ((count, width), BF16),
            "do": ((count, width), BF16),
            "xe": ((count, PIX), BF16),
            "mixed": ((count, 3 * width), BF16),
            "dmixed": ((count, 3 * width), BF16),
            "g": ((count, hidden), BF16),
            "gp": ((count, hidden), F32),
        }
        holders = len({v[2] for v in plan.sections[0].vectors.values()})
        targets = grad_shapes(plan, 0)[: 2 * self.bins]
        before = 2 + len(self.reads)
        got = pl.pallas_call(
            functools.partial(self.kernel, len(blocks)),
            out_shape=[*targets, *[jax.ShapeDtypeStruct(*known[n]) for n in self.outs]],
            in_specs=[IN_SMEM, *[ANY] * (1 + len(self.reads) + len(blocks))],
            out_specs=[*[ANY] * len(targets), *[IN_VMEM] * len(self.outs)],
            input_output_aliases={before + i: i for i in range(len(blocks))},
            scratch_shapes=[
                *weight_scratch(ENC, self.weights),
                *[pltpu.VMEM(*known[n]) for n in self.reads],
                *[pltpu.VMEM(*known[n]) for n in self.temps],
                pltpu.VMEM((holders, VEC_UNITS, 16, 128), BF16),
                pltpu.VMEM((8, D), F32),
                pltpu.VMEM((256, count), BF16),
                pltpu.VMEM((2, 16 * self.most, 16, 128), F32),
                pltpu.VMEM((holders, VEC_UNITS, 16, 128), F32),
                pltpu.SemaphoreType.DMA((len(self.weights) + 1,)),
                pltpu.SemaphoreType.DMA((len(self.reads),)),
                pltpu.SemaphoreType.DMA((3,)),
            ],
            compiler_params=pltpu.CompilerParams(vmem_limit_bytes=VMEM_BYTES),
            cost_estimate=lasting(self.cost),
            name=self.name,
        )(info, gathered, *[arrays[n] for n in self.reads], *blocks)
        return got[: len(targets)], dict(zip(self.outs, got[len(targets) :]))


def back_second(back, r, out):
    sh = back.sh
    back.ready(None, r["dz"])
    back.ready(None, r["y"])

    def from_latent(at, size):
        return r["dz"][pl.ds(at, size), :].astype(F32)

    def put(at, size, value):
        out["dy"][pl.ds(at, size), :] = value

    back.values["gf"], back.values["bf"] = norm_backward(
        r["y"], back.vec("gf"), from_latent, put, sh.count, D
    )
    back.second_product(out["dy"], r["dyb"], r["g"], r["gp"])

    def step(at):
        out["g"][pl.ds(at, 16), :] = r["g"][pl.ds(at, 16), :]

    for_rows(sh.count, 16, step, 2)


def copy_rows(count, source, target):
    def step(at):
        target[pl.ds(at, 16), :] = source[pl.ds(at, 16), :]

    for_rows(count, 16, step, 4)


def back_first(back, r, out):
    back.ready(None, r["dy"])
    back.ready(None, r["g"])
    copy_rows(back.sh.count, r["dy"], out["dy"])
    back.first_product(out["dy"], r["g"], r["n2"], r["x1"], r["dn"])


def back_projection(back, r, out):
    back.ready(None, r["dy"])
    back.projection(r["dy"], r["dyb"], r["o"], out["do"])


def back_attention(back, r, out):
    back.attention(r["do"], r["mixed"], out["dmixed"])


def back_mixing(back, r, out):
    back.ready(None, r["dy"])
    back.ready(None, r["dmixed"])
    back.mixing(r["dy"], r["dmixed"], r["n1"], r["x0"], r["dn"])

    def body(i, total):
        at = pl.multiple_of(i * 16, 16)
        grad = r["dy"][pl.ds(at, 16), :]
        r["dyb"][pl.ds(at, 16), :] = grad.astype(BF16)
        return total + jnp.sum(grad.reshape(2, 8, D), axis=0)

    total = lax.fori_loop(0, back.sh.count // 16, body, jnp.zeros((8, D), F32))
    back.values["patch_b"] = jnp.sum(total, axis=0, keepdims=True)
    back.ready(None, r["xe"])
    back.grads.weight("patch", r["xe"], PIX, r["dyb"], back.turned)


def encoder_back_stages(plan, sh):
    most = {n: plan.sections[0].panels[n] for n in ("fc1", "fc2", "qkv", "proj")}
    return [
        Stage(plan, sh, ["fc2"], ["y", "dz", "g", "gp"], ["dyb"], ["dy", "g"], most["fc2"], 25,
              "encoder_back_fc2", back_second),
        Stage(plan, sh, ["fc1"], ["g", "dy", "n2", "x1"], ["dn"], ["dy"], most["fc1"], 20,
              "encoder_back_fc1", back_first),
        Stage(plan, sh, ["proj"], ["dy", "o"], ["dyb"], ["do"], most["proj"], 10,
              "encoder_back_proj", back_projection, 1),
        Stage(plan, sh, [], ["do", "mixed"], [], ["dmixed"], 1, 25,
              "encoder_back_attention", back_attention, 0),
        Stage(plan, sh, ["qkv"], ["dy", "dmixed", "n1", "x0", "xe"], ["dn", "dyb"], [],
              most["qkv"], 25, "encoder_back_qkv", back_mixing, 1),
    ]


def pick(value, index, axis):
    return lax.dynamic_index_in_dim(value, index, axis, keepdims=False)


def tie(*trees):
    return lax.optimization_barrier(trees)


class Term:
    def __init__(self, base, bits, first, last, fixed=()):
        self.base, self.bits, self.first, self.last = base, bits, first, last
        self.fixed = dict(fixed)

    def at(self, bit, index):
        return Term(self.base, self.bits, self.first, self.last, {**self.fixed, bit: index})

    def value(self):
        zero = jnp.zeros((), jnp.int32)
        starts = [self.fixed.get(b, zero).astype(jnp.int32) for b in self.bits]
        sizes = [1 if b in self.fixed else 2 for b in self.bits]
        left = [n for n in sizes if n == 2]
        starts += [jnp.full((), self.first, jnp.int32), zero, zero]
        count = self.last - self.first
        out = lax.dynamic_slice(self.base, starts, [*sizes, count, 16, 128])
        return out.reshape(*left, count, 16, 128)


def sum_of(terms):
    return total_of([term.value() for term in terms])


class Flow:
    def __init__(self, dp, keep, send, first, parts=3):
        self.dp = dp
        self.me = lax.axis_index("dp")
        self.keep, self.given = keep, send
        count, units = keep.shape[:2]
        self.bits = count.bit_length() - 1
        assert count == 1 << self.bits and dp & (dp - 1) == 0
        self.all_bits = dp.bit_length() - 1
        self.first = first
        low = list(range(self.bits))
        if dp == 64:
            low = [b for b in (0, 2, 4, 1, 3) if b < self.bits]
        turn = max(min(3, len(low)), 1)
        self.cuts = [units * p // parts for p in range(parts + 1)]
        self.orders = [low[p % turn : turn] + low[: p % turn] + low[turn:] for p in range(parts)]
        self.step = -1
        self.terms = None

    def done(self):
        return self.step == self.all_bits

    def last(self):
        return self.step == self.all_bits - 1

    def payload(self):
        if self.step < 0:
            return [self.given]
        if self.step >= self.bits:
            return [self.result()]
        out = []
        for terms, order in zip(self.terms, self.orders):
            bit = order[self.step]
            other = 1 - (self.me >> bit & 1)
            out.append(sum_of([t.at(bit, other) for t in terms]))
        return out

    def send(self, payload):
        if self.step < 0:
            return [lax.ppermute(payload[0], "section", [(0, 1), (1, 0)])]
        if self.step >= self.bits:
            flip = 1 << self.step
            pairs = [(i, i ^ flip) for i in range(self.dp) if (i ^ self.first) & flip]
            return [lax.ppermute(payload[0], "dp", pairs)]
        out = []
        for value, order in zip(payload, self.orders):
            flip = 1 << order[self.step]
            out.append(lax.ppermute(value, "dp", [(i, i ^ flip) for i in range(self.dp)]))
        return out

    def take(self, got):
        ranges = list(zip(self.cuts[:-1], self.cuts[1:]))
        if self.step < 0:
            bits = list(range(self.bits - 1, -1, -1))
            shape = (2,) * self.bits + self.keep.shape[1:]
            self.terms = [
                [Term(v.reshape(shape), bits, *r) for v in (self.keep, got[0])] for r in ranges
            ]
        elif self.step < self.bits:
            for k, (order, value) in enumerate(zip(self.orders, got)):
                bit = order[self.step]
                mine = self.me >> bit & 1
                gone = order[: self.step + 1]
                bits = [b for b in range(self.bits - 1, -1, -1) if b not in gone]
                self.terms[k] = [t.at(bit, mine) for t in self.terms[k]]
                self.terms[k].append(Term(value, bits, 0, value.shape[-3]))
        else:
            for k, r in enumerate(ranges):
                self.terms[k].append(Term(got[0], [], *r))
        self.step += 1

    def result(self):
        return jnp.concatenate([sum_of(t) for t in self.terms], axis=0)


def move_on(flows, *others):
    flows = [f for f in flows if f is not None and not f.done()]
    payloads, others = tie([f.payload() for f in flows], others)
    return flows, [f.send(p) for f, p in zip(flows, payloads)], others


def arrive(flows, got):
    for flow, values in zip(flows, got):
        flow.take(values)


def sum_everywhere(dp, value):
    value = value + lax.ppermute(value, "section", [(0, 1), (1, 0)])
    bits = dp.bit_length() - 1
    for low in range(0, bits, 2):
        got = [
            lax.ppermute(value, "dp", [(i, i ^ (flip << low)) for i in range(dp)])
            for flip in range(1, 1 << min(2, bits - low))
        ]
        value = value + got[0]
        if len(got) == 3:
            value = value + (got[1] + got[2])
    return value


def squares_of(plan, s, value, section, me):
    section_plan = plan.sections[s]
    vectors = np.zeros((plan.dp,), np.int32)
    for _, panels, block, at in section_plan.vectors.values():
        vectors[block] = max(vectors[block], at + panels)
    filled = jnp.asarray(np.asarray(section_plan.fill, np.int32) * 16)[me]
    vectors = jnp.asarray(vectors)[me]
    shape = value.shape
    row = lax.broadcasted_iota(jnp.int32, shape, 0) * 16 + lax.broadcasted_iota(jnp.int32, shape, 1)
    row = row + section * (plan.half * 16)
    extra = row - plan.vec_unit * 16
    valid = (row < filled) | ((extra >= 0) & (extra < vectors))
    return jnp.sum(jnp.where(valid, value * value, 0.0))


def gather_decoder(plan, half_d, section, me, after):
    dp, quarter = plan.dp, plan.quarter
    first = plan.bins(1)[1][0]
    assert 2 * first == dp
    used = max(plan.tail_used())
    spread = jnp.pad(half_d, ((0, 2 * quarter - plan.half), (0, 0), (0, 0)))
    spread = total_of(
        [
            lax.ppermute(
                spread[i * quarter : (i + 1) * quarter],
                "dp",
                [(b, 2 * b + i) for b in range(first)],
            )
            for i in range(2)
        ]
    )
    rest = jnp.where(me == first, half_d[:used], jnp.zeros((), BF16))
    holders = [first]
    for bit in reversed(range(dp.bit_length() - 1)):
        rest = rest + lax.ppermute(rest, "dp", [(i, i ^ 1 << bit) for i in holders])
        holders = holders + [i ^ 1 << bit for i in holders]
    other = lax.ppermute(rest, "section", [(0, 1), (1, 0)])
    rest = jnp.where(section == 0, jnp.stack([rest, other]), jnp.stack([other, rest]))
    spread, _ = tie(spread, after[0, 0, 0])
    gathered = lax.all_gather(spread, ("section", "dp"), axis=0, tiled=True)
    return gathered.reshape(2, dp, quarter, 16, 128), rest


def sincos(width):
    places = np.arange(NP).astype(np.float32)[:, None]
    column = np.arange(width)
    rates = np.exp(
        -(np.float32(2.0) * (column // 2).astype(np.float32) / np.float32(width))
        * np.float32(math.log(10000.0))
    ).astype(np.float32)
    phases = (places * rates[None, :]).astype(np.float32)
    table = np.where(
        column[None, :] % 2 == 0, np.sin(phases.astype(np.float64)), np.cos(phases.astype(np.float64))
    ).astype(np.float32)
    parts = []
    left = np.zeros((ROWS_D, width), np.float32)
    left[:NP] = table
    for _ in range(3):
        high = left.astype(jnp.bfloat16)
        parts.append(high)
        left = left - high.astype(np.float32)
    return np.stack(parts)


def on_device(patches, keep, perm, master, first, second, ema):
    dp = lax.axis_size("dp")
    section = lax.axis_index("section")
    me = lax.axis_index("dp")
    shard = master.shape[1]
    plan = Plan(dp, shard // 128)
    rows, half = plan.shard_rows, plan.half
    swap = [(0, 1), (1, 0)]
    states = [v.reshape(rows, 1, 128) for v in (master, first, second, ema)]

    following = lax.ppermute(
        states[0][: plan.head_rows], "dp", [(i, i - 1) for i in range(1, dp)]
    )
    index = jnp.asarray(plan.pack_index)[section, me]
    packed = pack(plan, index, states[0], following)
    mine = lax.dynamic_slice_in_dim(packed, section * half, half, 0)
    given = lax.ppermute(
        lax.dynamic_slice_in_dim(packed, (1 - section) * half, half, 0), "section", swap
    )
    half_e = jnp.where(section == 0, mine, given)
    half_d = jnp.where(section == 0, given, mine)
    gathered_e = lax.all_gather(half_e, ("section", "dp"), axis=0, tiled=True)
    gathered_e = gathered_e.reshape(2, dp, half, 16, 128)
    gathered_d = gather_decoder(plan, half_d, section, me, gathered_e)

    count = sum_everywhere(dp, jnp.sum(NP - keep).astype(F32)) * 0.5
    images = patches.shape[0] // 2
    mine = section * images
    patches = lax.dynamic_slice_in_dim(patches, mine, images, 0)
    patches = jnp.pad(patches, ((0, 0), (0, ROWS_D - NP), (0, 0)))
    order = lax.dynamic_slice_in_dim(perm, mine, images, 0)
    order = jnp.pad(order, ((0, 0), (0, ROWS_D - NP)), constant_values=ROWS_D - 1)
    order = order.reshape(images * ROWS_D, 1)
    kept = lax.dynamic_slice_in_dim(keep, mine, images, 0)
    info = jnp.concatenate([section[None].astype(jnp.int32), kept])
    scale = ((1.0 / count) * (1.0 / PIX) * 2.0).reshape(1)

    shape_e = Shape(images, ROWS_E, D, HEADS_E, FF_E)
    shape_d = Shape(images, ROWS_D, DD, HEADS_D, FF_D)
    pp, *saved, latent = encoder(
        plan, shape_e, info, gathered_e, patches, order, jnp.asarray(sincos(D))
    )
    arrays = dict(zip(("x0", "n1", "mixed", "o", "x1", "n2", "g", "gp", "y"), saved))
    arrays["xe"] = pp
    *sums_d, arrays["dz"], loss = decoder(
        plan, shape_d, info, scale, gathered_d, latent, pp, order, jnp.asarray(sincos(DD))
    )

    stages = encoder_back_stages(plan, shape_e)
    first_tail = plan.bins(1)[1][0]
    main = Flow(dp, sums_d[0], sums_d[1], 0)
    rest = Flow(dp, sums_d[2], sums_d[3], first_tail, 1)
    flows, got, _ = move_on([main, rest])
    got, arrays = tie(got, arrays)
    arrive(flows, got)
    low = high = None
    blocks = []
    late = []
    for number, stage in enumerate(stages):
        flows, got, (arrays, blocks) = move_on([main, rest, high], arrays, blocks)
        if stage.bins:
            blocks, made = stage(info, gathered_e, arrays, blocks)
        else:
            _, made = stage(info, gathered_e, arrays, [])
        arrays = {**arrays, **made}
        kept = [g for f, g in zip(flows, got) if not f.last()]
        kept, late, arrays, blocks = tie(kept, late, arrays, blocks)
        late = [g for f, g in zip(flows, got) if f.last()]
        kept = iter(kept)
        arrive(flows, [g if f.last() else next(kept) for f, g in zip(flows, got)])
        if number == 1:
            high = Flow(dp, blocks[2], blocks[3], dp // 2)
            blocks = blocks[:2]
    low = Flow(dp, blocks[0], blocks[1], 0)
    every = [main, rest, high, low]
    while not all(f.done() for f in every):
        flows, got, _ = move_on(every)
        arrive(flows, got)

    sum_tail = rest.result()
    sum_tail = jnp.pad(sum_tail, ((0, half - sum_tail.shape[0]), (0, 0), (0, 0)))
    sum_d = jnp.where(me < first_tail, main.result(), sum_tail)
    sum_e = jnp.where(me < dp // 2, low.result(), high.result())
    squares = [
        squares_of(plan, s, v, section, me) for s, v in enumerate((sum_e, sum_d))
    ]
    sums = sum_everywhere(dp, jnp.stack([squares[0] + squares[1], loss[0, 0]]))
    half_mine = jnp.where(section == 0, sum_e, sum_d)
    half_other = lax.ppermute(jnp.where(section == 0, sum_d, sum_e), "section", swap)
    block = jnp.where(
        section == 0,
        jnp.concatenate([half_mine, half_other], axis=0),
        jnp.concatenate([half_other, half_mine], axis=0),
    )
    start = jnp.asarray(plan.tail_start)[section, me]
    tail = jnp.concatenate(
        [
            lax.dynamic_slice_in_dim(block, start, plan.tail_units, 0),
            block[plan.vec_unit :],
        ],
        axis=0,
    )
    tail = lax.ppermute(tail, "dp", [(i, i + 1) for i in range(dp - 1)])
    index = jnp.asarray(plan.unpack_index)[section, me]
    total = unpack(plan, index, block, tail)
    norm = jnp.sqrt(sums[0])
    factor = jnp.minimum(1.0, clip_limit / (norm + norm_epsilon))
    made = update(plan, factor.reshape(1), total, states)
    return (*[v.reshape(1, shard) for v in made], norm, sums[1], count)


def solution(mesh):
    return jax.shard_map(
        on_device,
        mesh=mesh,
        in_specs=(
            P("dp", None, None),
            P("dp"),
            P("dp", None),
            P("section", "dp"),
            P("section", "dp"),
            P("section", "dp"),
            P("section", "dp"),
        ),
        out_specs=(
            P("section", "dp"),
            P("section", "dp"),
            P("section", "dp"),
            P("section", "dp"),
            P(),
            P(),
            P(),
        ),
        check_vma=False,
    )
```

```python
import functools
import math

import jax
import jax.numpy as jnp
import numpy as np
from jax import lax
from jax.experimental import pallas as pl
from jax.experimental.pallas import tpu as pltpu
from jax.sharding import PartitionSpec as P

D = 768
HEADS_E = 12
FF_E = 3072
DD = 512
HEADS_D = 16
FF_D = 2048
PIX = 768
NP = 196
SLOTS = 98
STEP = 10

norm_epsilon = 1e-06
clip_limit = 0.01
learn_rate = 0.02
beta_one = 0.9
beta_two = 0.999
adam_epsilon = 1e-08
weight_decay = 0.05
average_keep = 0.8

F32 = jnp.float32
BF16 = jnp.bfloat16
ROWS_E = 112
ROWS_D = 208
GROUP = 16
VEC_UNITS = 2
VMEM_BYTES = 60 * 1024 * 1024
COST = 2e8
ANY = pl.BlockSpec(memory_space=pl.ANY)
IN_VMEM = pl.BlockSpec(memory_space=pltpu.VMEM)
IN_SMEM = pl.BlockSpec(memory_space=pltpu.SMEM)

ENC = [
    ("patch", (PIX, D)),
    ("patch_b", (D,)),
    ("g1", (D,)),
    ("b1", (D,)),
    ("qkv", (D, 3 * D)),
    ("proj", (D, D)),
    ("g2", (D,)),
    ("b2", (D,)),
    ("fc1", (D, FF_E)),
    ("fc2", (FF_E, D)),
    ("gf", (D,)),
    ("bf", (D,)),
]
DEC = [
    ("embed", (D, DD)),
    ("mask", (DD,)),
    ("g1", (DD,)),
    ("b1", (DD,)),
    ("qkv", (DD, 3 * DD)),
    ("proj", (DD, DD)),
    ("g2", (DD,)),
    ("b2", (DD,)),
    ("fc1", (DD, FF_D)),
    ("fc2", (FF_D, DD)),
    ("gf", (DD,)),
    ("bf", (DD,)),
    ("head", (DD, PIX)),
]


class Section:
    def __init__(self, layout, dp, shard_rows):
        self.dp = dp
        self.shard_rows = shard_rows
        self.groups = []
        self.vectors = {}
        self.panels = {}
        fill = [0] * dp
        vector_fill = [0] * dp
        row = 0
        for name, shape in layout:
            panels = shape[-1] // 128
            self.panels[name] = panels
            if len(shape) == 2:
                for group in range(shape[0] // GROUP):
                    block = row // shard_rows
                    self.groups.append((name, group, row, panels, block, fill[block]))
                    fill[block] += panels
                    row += GROUP * panels
            else:
                block = row // shard_rows
                self.vectors[name] = (row, panels, block, vector_fill[block])
                vector_fill[block] += panels
                row += panels
        self.rows = row
        self.fill = fill
        assert max(vector_fill) <= 16 * VEC_UNITS
        self.blocks_used = max(b for b in range(dp) if fill[b] or vector_fill[b]) + 1

    def pieces(self, name, first=0, count=None):
        out = []
        for tensor, group, _, panels, block, unit in self.groups:
            if tensor != name or group < first or (count is not None and group >= first + count):
                continue
            if out and out[-1][0] == block and out[-1][1] + out[-1][3] * panels == unit:
                out[-1][3] += 1
            else:
                out.append([block, unit, group, 1])
        return [tuple(p) for p in out]

    def runs(self, name, cuts, first=0, count=None):
        panels = self.panels[name]
        out = []
        for block, unit, group, groups in self.pieces(name, first, count):
            at, left = (group - first) * panels, groups * panels
            while left:
                place = max(i for i in range(len(cuts) - 1) if cuts[i] <= unit)
                take = min(left, cuts[place + 1] - unit)
                out.append((block, place, unit - cuts[place], at, take))
                unit, at, left = unit + take, at + take, left - take
        return out


class Plan:
    def __init__(self, dp, shard_rows):
        self.dp = dp
        self.shard_rows = shard_rows
        self.sections = [Section(ENC, dp, shard_rows), Section(DEC, dp, shard_rows)]
        units = max(max(s.fill) for s in self.sections)
        units += (units + VEC_UNITS) % 2
        self.vec_unit = units
        self.units = units + VEC_UNITS
        self.half = self.units // 2
        half = self.half
        self.quarter = -(-half // 2)
        self.part_cuts = [0, -(-half // 3), -(-2 * half // 3), half]
        self.half_cuts = [0, half, self.units]
        self.head_rows = 8 * -(-max(16 * max(s.panels.values()) for s in self.sections) // 8)
        self.tail_units = max(max(s.panels.values()) for s in self.sections)
        self.pack_base = 8 * -(-shard_rows // 8)
        self.pack_rows = shard_rows + self.head_rows
        self.pack_index = np.zeros((2, dp, self.units * 16), np.int32)
        self.tail_rows = 16 * (self.tail_units + VEC_UNITS)
        self.zero_row = self.units * 16 + self.tail_rows
        self.unpack_index = np.full((2, dp, shard_rows), self.zero_row, np.int32)
        self.tail_start = np.zeros((2, dp), np.int32)
        for s, section in enumerate(self.sections):
            for b in range(dp):
                self.tail_start[s, b] = max(section.fill[b] - self.tail_units, 0)
            for name, group, row, panels, block, unit in section.groups:
                for panel in range(panels):
                    for r in range(GROUP):
                        self.place(s, block, (unit + panel) * 16 + r, row + r * panels + panel)
            for row, panels, block, at in section.vectors.values():
                for panel in range(panels):
                    self.place(s, block, self.vec_unit * 16 + at + panel, row + panel)

    def bins(self, s):
        if s == 0:
            return [(0, self.dp // 2), (self.dp // 2, self.dp - self.dp // 2)]
        used = self.sections[1].blocks_used
        main = 1 << (used.bit_length() - 1)
        return [(0, main), (main, max(used - main, 1))]

    def tail_used(self):
        first, count = self.bins(1)[1]
        section = self.sections[1]
        assert count == 1 and all(v[2] < first for v in section.vectors.values())
        used = section.fill[first]
        return min(used, self.half), max(used - self.half, 0)

    def bin_units(self, s):
        return [self.half, self.half if s == 0 else max(self.tail_used())]

    def place(self, s, block, block_row, flat_row):
        local = flat_row - block * self.shard_rows
        assert 0 <= local < self.pack_rows
        gap = self.pack_base - self.shard_rows if local >= self.shard_rows else 0
        self.pack_index[s, block, block_row] = local + gap
        owner, at = divmod(flat_row, self.shard_rows)
        if owner == block:
            self.unpack_index[s, owner, at] = block_row
        else:
            assert owner == block + 1
            if block_row >= self.vec_unit * 16:
                source = self.tail_units * 16 + block_row - self.vec_unit * 16
            else:
                source = block_row - int(self.tail_start[s, block]) * 16
                assert 0 <= source < self.tail_units * 16
            self.unpack_index[s, owner, at] = self.units * 16 + source


def move_rows_in(index_ref, held, done, count):
    def eight(i, carry):
        for j in range(8):
            row = i * 8 + j
            done[pl.ds(row, 1), :] = held[pl.ds(index_ref[row], 1), :]
        return carry

    lax.fori_loop(0, count // 8, eight, 0)
    for row in range(count // 8 * 8, count):
        done[pl.ds(row, 1), :] = held[pl.ds(index_ref[row], 1), :]


def pack_kernel(base, index_ref, flat, following, out_ref, held, done, sems):
    rows, more = flat.shape[0], following.shape[0]
    copies = [
        pltpu.make_async_copy(flat.at[:, 0], held.at[pl.ds(0, rows)], sems.at[0]),
        pltpu.make_async_copy(following.at[:, 0], held.at[pl.ds(base, more)], sems.at[1]),
    ]
    for copy in copies:
        copy.start()
    for copy in copies:
        copy.wait()
    count = done.shape[0]
    move_rows_in(index_ref, held, done, count)
    out_ref[...] = done[...].reshape(out_ref.shape).astype(BF16)


def pack(plan, index, flat, following):
    count = plan.units * 16
    return pl.pallas_call(
        functools.partial(pack_kernel, plan.pack_base),
        out_shape=jax.ShapeDtypeStruct((plan.units, 16, 128), BF16),
        in_specs=[IN_SMEM, ANY, ANY],
        out_specs=IN_VMEM,
        scratch_shapes=[
            pltpu.VMEM((plan.pack_base + plan.head_rows, 128), F32),
            pltpu.VMEM((count, 128), F32),
            pltpu.SemaphoreType.DMA((2,)),
        ],
        compiler_params=pltpu.CompilerParams(vmem_limit_bytes=32 * 1024 * 1024),
        name="pack_rows",
    )(index, flat, following)


def unpack_kernel(zero_row, rows, index_ref, block, tail, out_ref, held):
    at = 0
    for source in (block, tail):
        size = source.shape[0] * 16
        held[pl.ds(at, size), :] = source[...].reshape(size, 128)
        at += size
    held[pl.ds(zero_row, 8), :] = jnp.zeros((8, 128), F32)
    out_ref[pl.ds(out_ref.shape[0] - 16, 16), :] = jnp.zeros((16, 128), F32)
    move_rows_in(index_ref, held, out_ref, rows)


def unpack(plan, index, block, tail):
    rows = plan.shard_rows
    padded = 16 * -(-rows // 16)
    return pl.pallas_call(
        functools.partial(unpack_kernel, plan.zero_row, rows),
        out_shape=jax.ShapeDtypeStruct((padded, 128), F32),
        in_specs=[IN_SMEM, IN_VMEM, IN_VMEM],
        out_specs=IN_VMEM,
        scratch_shapes=[pltpu.VMEM((plan.zero_row + 8, 128), F32)],
        compiler_params=pltpu.CompilerParams(vmem_limit_bytes=32 * 1024 * 1024),
        cost_estimate=lasting(6),
        name="unpack_rows",
    )(index, block, tail)


def update_kernel(rows, chunk, factor_ref, total, *refs):
    states, outs, held, made, in_sems, out_sems = (
        refs[:4], refs[4:8], refs[8:12], refs[12:16], refs[16], refs[17],
    )
    starts = list(range(0, rows, chunk))
    sizes = [min(chunk, rows - at) for at in starts]
    loads = [
        [
            pltpu.make_async_copy(
                source.at[pl.ds(at, size), 0], ref.at[pl.ds(at, size)], in_sems.at[k, j]
            )
            for j, (source, ref) in enumerate(zip(states, held))
        ]
        for k, (at, size) in enumerate(zip(starts, sizes))
    ]
    for group in loads:
        for copy in group:
            copy.start()
    stores = []
    factor = factor_ref[0]
    for k, (at, size) in enumerate(zip(starts, sizes)):
        for copy in loads[k]:
            copy.wait()

        def body(i, carry):
            here = pl.ds(pl.multiple_of(at + i * 16, 8), 16)
            master, first, second, ema = (ref[here, :] for ref in held)
            clipped = total[here, :] * factor
            new_first = beta_one * first + (1.0 - beta_one) * clipped
            new_second = beta_two * second + (1.0 - beta_two) * clipped * clipped
            first_hat = new_first * (1.0 / (1.0 - beta_one**STEP))
            second_hat = new_second * (1.0 / (1.0 - beta_two**STEP))
            new_master = master - learn_rate * (
                first_hat / (jnp.sqrt(second_hat) + adam_epsilon) + weight_decay * master
            )
            made[0][here, :] = new_master
            made[1][here, :] = new_first
            made[2][here, :] = new_second
            made[3][here, :] = average_keep * ema + (1.0 - average_keep) * new_master
            return carry

        lax.fori_loop(0, -(-size // 16), body, 0, unroll=2)
        for j in range(4):
            copy = pltpu.make_async_copy(
                made[j].at[pl.ds(at, size)], outs[j].at[pl.ds(at, size), 0], out_sems.at[k, j]
            )
            copy.start()
            stores.append(copy)
    for copy in stores:
        copy.wait()


def update(plan, factor, total, states):
    rows = plan.shard_rows
    chunk = 16 * -(-rows // (16 * 4))
    padded = 16 * -(-rows // 16)
    count = -(-rows // chunk)
    return pl.pallas_call(
        functools.partial(update_kernel, rows, chunk),
        out_shape=[jax.ShapeDtypeStruct((rows, 1, 128), F32)] * 4,
        in_specs=[IN_SMEM, IN_VMEM, *[ANY] * 4],
        out_specs=[ANY] * 4,
        scratch_shapes=[
            *[pltpu.VMEM((padded, 128), F32)] * 8,
            pltpu.SemaphoreType.DMA((count, 4)),
            pltpu.SemaphoreType.DMA((count, 4)),
        ],
        compiler_params=pltpu.CompilerParams(vmem_limit_bytes=VMEM_BYTES),
        name="update_states",
    )(factor, total, *states)


def dot(a, b):
    return lax.dot_general(a, b, (((1,), (0,)), ((), ())), preferred_element_type=F32)


def dot_nt(a, b):
    return lax.dot_general(a, b, (((1,), (1,)), ((), ())), preferred_element_type=F32)


def dot_tn(a, b):
    return lax.dot_general(a, b, (((0,), (0,)), ((), ())), preferred_element_type=F32)


def total_of(terms):
    total = terms[0]
    for term in terms[1:]:
        total = total + term
    return total


def for_rows(count, size, step, unroll=1):
    def body(i, carry):
        step(pl.multiple_of(i * size, size))
        return carry

    lax.fori_loop(0, count // size, body, 0, unroll=unroll)


def columns(weight, depth, first, count):
    parts = [weight[:, first + i].reshape(depth, 128) for i in range(count)]
    return jnp.concatenate(parts, axis=1)


def row_band(weight, panels, band):
    parts = [weight[pl.ds(band * 16, 16), i].reshape(256, 128) for i in range(panels)]
    return jnp.concatenate(parts, axis=1)


def row_chunks(count):
    size = next(n for n in (208, 224, 112, 104, 16) if count % n == 0)
    return [slice(at, at + size) for at in range(0, count, size)]


def wide_chunks(count):
    size = next(n for n in (416, 336, 112, 104, 16) if count % n == 0)
    return [slice(at, at + size) for at in range(0, count, size)]


def times_columns(left, weight, panels, depth, finish):
    group = 4 if panels % 4 == 0 else 2

    def body(index, carry):
        right = columns(weight, depth, group * index, group)
        width = group * 128
        there = pl.ds(pl.multiple_of(index * width, width), width)
        for here in row_chunks(left.shape[0]):
            finish(index * width, here, there, dot(left[here, :], right))
        return carry

    lax.fori_loop(0, panels // group, body, 0)


def times_bands(left, weight, panels, count, finish):
    def body(band, carry):
        right = row_band(weight, panels, band)
        for here in wide_chunks(left.shape[0]):
            finish(here, lanes(band), dot_nt(left[here, :], right))
        return carry

    lax.fori_loop(0, count // 256, body, 0)


def lanes(pair):
    return pl.ds(pl.multiple_of(pair * 256, 256), 256)


def norm_block(count):
    return next(n for n in (224, 208, 112, 104, 16) if count % n == 0)


def norm_rows(x, width):
    mean = jnp.sum(x, axis=1, keepdims=True) * (1.0 / width)
    centre = x - mean
    spread = jnp.sum(centre * centre, axis=1, keepdims=True) * (1.0 / width)
    rstd = lax.rsqrt(spread + norm_epsilon)
    return centre * rstd, rstd


def norm_forward(x_ref, gain, shift, out_ref, count, width):
    size = norm_block(count)

    def step(at):
        hat, _ = norm_rows(x_ref[pl.ds(at, size), :], width)
        out_ref[pl.ds(at, size), :] = (hat * gain + shift).astype(out_ref.dtype)

    for_rows(count, size, step)


def norm_backward(x_ref, gain, grad_of, put, count, width):
    size = norm_block(count)

    def body(i, carry):
        gain_sum, shift_sum = carry
        at = pl.multiple_of(i * size, size)
        hat, rstd = norm_rows(x_ref[pl.ds(at, size), :], width)
        grad = grad_of(at, size)
        gain_sum = gain_sum + jnp.sum((grad * hat).reshape(size // 8, 8, width), axis=0)
        shift_sum = shift_sum + jnp.sum(grad.reshape(size // 8, 8, width), axis=0)
        scaled = grad * gain
        first = jnp.sum(scaled, axis=1, keepdims=True) * (1.0 / width)
        second = jnp.sum(scaled * hat, axis=1, keepdims=True) * (1.0 / width)
        put(at, size, rstd * (scaled - first - hat * second))
        return gain_sum, shift_sum

    zero = jnp.zeros((8, width), F32)
    gain_sum, shift_sum = lax.fori_loop(0, count // size, body, (zero, zero))
    return jnp.sum(gain_sum, axis=0, keepdims=True), jnp.sum(shift_sum, axis=0, keepdims=True)


def head_masks(size):
    lane = lax.broadcasted_iota(jnp.int32, (1, 128), 1)
    return [
        jnp.where((lane >= h * size) & (lane < (h + 1) * size), 1.0, 0.0).astype(BF16)
        for h in range(128 // size)
    ]


def softmax_columns(scores, limit):
    key = lax.broadcasted_iota(jnp.int32, scores.shape, 0)
    scores = jnp.where(key < limit, scores, -1e30)
    top = jnp.max(scores, axis=0, keepdims=True)
    raised = jnp.exp(scores - top)
    return raised * (1.0 / jnp.sum(raised, axis=0, keepdims=True))


def softmax_rows(scores, limit):
    key = lax.broadcasted_iota(jnp.int32, scores.shape, 1)
    scores = jnp.where(key < limit, scores, -1e30)
    top = jnp.max(scores, axis=1, keepdims=True)
    raised = jnp.exp(scores - top)
    return raised * (1.0 / jnp.sum(raised, axis=1, keepdims=True))


def attention_forward(mixed, out, limit_of, images, rows, width, size):
    panels = width // 128
    masks = head_masks(size)

    def body(step, carry):
        image, panel = step // panels, step % panels
        here = pl.ds(pl.multiple_of(image * rows, 16), rows)

        def part(third):
            return mixed[here, pl.ds(pl.multiple_of((third * panels + panel) * 128, 128), 128)]

        query, keys, values = part(0), part(1), part(2)
        limit = limit_of(image)
        probs = [softmax_rows(dot_nt(query * mask, keys), limit).astype(BF16) for mask in masks]
        total = total_of([dot(p, values) * m.astype(F32) for p, m in zip(probs, masks)])
        out[here, pl.ds(pl.multiple_of(panel * 128, 128), 128)] = total.astype(BF16)
        return carry

    lax.fori_loop(0, images * panels, body, 0, unroll=6)


def attention_backward(mixed, grad_out, grad_mixed, limit_of, images, rows, width, size):
    panels = width // 128
    masks = head_masks(size)

    def body(step, carry):
        image, panel = step // panels, step % panels
        here = pl.ds(pl.multiple_of(image * rows, 16), rows)

        def place(third):
            return pl.ds(pl.multiple_of((third * panels + panel) * 128, 128), 128)

        query, keys, values = (mixed[here, place(third)] for third in range(3))
        grad = grad_out[here, place(0)]
        turned = keys.T
        limit = limit_of(image)
        zero = jnp.zeros((rows, 128), F32)
        grad_query, grad_keys, grad_values = [], zero, zero
        for h, mask in enumerate(masks):
            masked_query = query * mask
            masked_grad = grad * mask
            probs = softmax_columns(dot_nt(keys, masked_query), limit)
            grad_probs = dot_nt(values, masked_grad)
            inner = jnp.sum(probs * grad_probs, axis=0, keepdims=True)
            grad_scores = (probs * (grad_probs - inner)).astype(BF16)
            grad_values = grad_values + dot(probs.astype(BF16), masked_grad)
            grad_keys = grad_keys + dot(grad_scores, masked_query)
            grad_query.append(dot(turned[h * size : h * size + size, :], grad_scores))
        grad_query = jnp.concatenate(grad_query, axis=0) * (1.0 / math.sqrt(size))
        grad_mixed[here, place(0)] = grad_query.astype(BF16).T
        grad_mixed[here, place(1)] = grad_keys.astype(BF16)
        grad_mixed[here, place(2)] = grad_values.astype(BF16)
        return carry

    lax.fori_loop(0, images * panels, body, 0, unroll=3)


def gelu_parts(value):
    bell = 0.5 * (1.0 + lax.erf(value * math.sqrt(0.5)))
    slope = bell + value * (jnp.exp(value * value * -0.5) * (1.0 / math.sqrt(2.0 * math.pi)))
    return value * bell, slope


class Shape:
    def __init__(self, images, rows, width, heads, hidden):
        self.images, self.rows, self.width = images, rows, width
        self.size = width // heads
        self.hidden = hidden
        self.count = images * rows


def block_forward(sh, x0, n1, mixed, o, x1, n2, g, gp, y, w, vec, limit_of, ready, saved):
    width, hidden, count = sh.width, sh.hidden, sh.count
    panels = width // 128
    norm_forward(x0, vec("g1"), vec("b1"), n1, count, width)
    saved(n1)
    ready("qkv")

    def put_mixed(start, here, there, value):
        scale = jnp.where(start < width, 1.0 / math.sqrt(sh.size), 1.0)
        mixed[here, there] = (value * scale).astype(BF16)

    times_columns(n1, w["qkv"], 3 * panels, width, put_mixed)
    saved(mixed)
    attention_forward(mixed, o, limit_of, sh.images, sh.rows, width, sh.size)
    saved(o)
    ready("proj")

    def put_sum(base, out):
        def finish(_, here, there, value):
            out[here, there] = base[here, there] + value

        return finish

    times_columns(o, w["proj"], panels, width, put_sum(x0, x1))
    saved(x1)
    norm_forward(x1, vec("g2"), vec("b2"), n2, count, width)
    saved(n2)
    ready("fc1")

    def put_hidden(_, here, there, value):
        value, slope = gelu_parts(value)
        g[here, there] = value.astype(BF16)
        gp[here, there] = slope

    times_columns(n2, w["fc1"], hidden // 128, width, put_hidden)
    saved(g)
    saved(gp)
    ready("fc2")
    times_columns(g, w["fc2"], panels, hidden, put_sum(x1, y))
    saved(y)


class Gradients:
    def __init__(self, plan, s, own, stage, sems, targets):
        self.plan, self.section, self.own = plan, plan.sections[s], own
        self.bins = plan.bins(s)
        self.stage, self.sems, self.targets = stage, sems, targets
        self.turn = 0
        self.flying = [[], []]

    def copy_out(self, source, block, side, unit, take, sem):
        which = max(i for i, (first, _) in enumerate(self.bins) if first <= block)
        block = block - self.bins[which][0]
        keep, send = self.targets[2 * which], self.targets[2 * which + 1]

        def to(target):
            return pltpu.make_async_copy(source, target.at[block, pl.ds(unit, take)], sem)

        @pl.when(self.own == side)
        def _():
            to(keep).start()

        @pl.when(self.own != side)
        def _():
            to(send).start()

        return to(keep)

    def drain(self, slot):
        for copy in self.flying[slot]:
            copy.wait()
        self.flying[slot] = []

    def weight(self, name, left, depth, right, turned):
        panels = self.section.panels[name]
        for band in range(depth // 256):
            slot = self.turn % 2
            self.turn += 1
            self.drain(slot)
            stage = self.stage.at[slot]
            turned[...] = left[:, band * 256 : band * 256 + 256].T

            def body(pair, carry):
                value = dot(turned[...], right[:, lanes(pair)])
                for i in range(2):
                    stage[pl.ds(2 * pair + i, 16, stride=panels)] = value[
                        :, i * 128 : i * 128 + 128
                    ].reshape(16, 16, 128)
                return carry

            lax.fori_loop(0, panels // 2, body, 0)
            for block, side, unit, at, take in self.section.runs(
                name, self.plan.half_cuts, band * 16, 16
            ):
                self.flying[slot].append(
                    self.copy_out(
                        stage.at[pl.ds(at, take)], block, side, unit, take, self.sems.at[slot]
                    )
                )

    def finish(self, values, scratch):
        vectors = self.section.vectors
        blocks = sorted({vectors[name][2] for name in values})
        for k, block in enumerate(blocks):
            scratch[k] = jnp.zeros((VEC_UNITS, 16, 128), F32)
            for name, (_, panels, at_block, at) in vectors.items():
                if at_block != block:
                    continue
                for panel in range(panels):
                    unit, row = divmod(at + panel, 16)
                    scratch[k, unit, row : row + 1, :] = values[name][
                        :, panel * 128 : panel * 128 + 128
                    ]
        unit = self.plan.vec_unit - self.plan.half
        copies = [
            self.copy_out(scratch.at[k], block, 1, unit, VEC_UNITS, self.sems.at[2])
            for k, block in enumerate(blocks)
        ]
        for copy in copies:
            copy.wait()
        self.drain(0)
        self.drain(1)


class Backward:
    def __init__(self, sh, w, vec, limit_of, grads, values, turned, ready):
        self.sh, self.w, self.vec, self.limit_of = sh, w, vec, limit_of
        self.grads, self.values, self.turned, self.ready = grads, values, turned, ready
        self.panels = sh.width // 128

    def round_stream(self, dy, dyb):
        def step(at):
            dyb[pl.ds(at, 16), :] = dy[pl.ds(at, 16), :].astype(BF16)

        for_rows(self.sh.count, 16, step, 4)

    def bands(self, left, name, count, put):
        times_bands(left, self.w[name], self.grads.section.panels[name], count, put)

    def through_norm(self, x, dn, dy, gain, shift, dn_is=None):
        def from_dn(at, size):
            return dn[pl.ds(at, size), :]

        def into_stream(at, size, value):
            dy[pl.ds(at, size), :] = dy[pl.ds(at, size), :] + value

        self.values[gain], self.values[shift] = norm_backward(
            x, self.vec(gain), from_dn, into_stream, self.sh.count, self.sh.width
        )

    def second_product(self, dy, dyb, g, gp):
        self.round_stream(dy, dyb)
        self.ready("fc2", g)
        self.grads.weight("fc2", g, self.sh.hidden, dyb, self.turned)
        self.ready(None, gp)

        def put(here, there, value):
            g[here, there] = (value * gp[here, there]).astype(BF16)

        self.bands(dyb, "fc2", self.sh.hidden, put)

    def first_product(self, dy, g, n2, x1, dn):
        def put(here, there, value):
            dn[here, there] = value

        self.ready("fc1", n2)
        self.grads.weight("fc1", n2, self.sh.width, g, self.turned)
        self.bands(g, "fc1", self.sh.width, put)
        self.ready(None, x1)
        self.through_norm(x1, dn, dy, "g2", "b2")

    def projection(self, dy, dyb, o, grad):
        sh = self.sh
        self.round_stream(dy, dyb)
        self.ready("proj", o)
        self.grads.weight("proj", o, sh.width, dyb, self.turned)

        def put(here, there, value):
            grad[here, there] = value.astype(BF16)

        self.bands(dyb, "proj", sh.width, put)

    def attention(self, grad, mixed, dmixed):
        sh = self.sh
        self.ready(None, grad)
        self.ready(None, mixed)
        attention_backward(mixed, grad, dmixed, self.limit_of, sh.images, sh.rows, sh.width, sh.size)

    def mixing(self, dy, dmixed, n1, x0, dn):
        def put(here, there, value):
            dn[here, there] = value

        self.ready("qkv", n1)
        self.grads.weight("qkv", n1, self.sh.width, dmixed, self.turned)
        self.bands(dmixed, "qkv", self.sh.width, put)
        self.ready(None, x0)
        self.through_norm(x0, dn, dy, "g1", "b1")


def held_at(plan, s, gathered, block, side, unit, take):
    if s == 0:
        return [(gathered[0].at[side, block, pl.ds(unit, take)], 0, take)]
    if block == plan.bins(1)[1][0]:
        return [(gathered[1].at[side, pl.ds(unit, take)], 0, take)]
    out = []
    quarter = plan.quarter
    if unit < quarter:
        few = min(take, quarter - unit)
        out.append((gathered[0].at[side, 2 * block, pl.ds(unit, few)], 0, few))
    if unit + take > quarter:
        skip = max(quarter - unit, 0)
        few = take - skip
        source = gathered[0].at[side, 2 * block + 1, pl.ds(unit + skip - quarter, few)]
        out.append((source, skip, few))
    return out


def load_vectors(plan, s, gathered, held, vec_ref, sem):
    section = plan.sections[s]
    blocks = sorted({v[2] for v in section.vectors.values()})
    copies = [
        pltpu.make_async_copy(source, held.at[k, pl.ds(skip, few)], sem)
        for k, block in enumerate(blocks)
        for source, skip, few in held_at(
            plan, s, gathered, block, 1, plan.vec_unit - plan.half, VEC_UNITS
        )
    ]
    for copy in copies:
        copy.start()
    names = {name: i for i, name in enumerate(section.vectors)}

    def finish():
        for copy in copies:
            copy.wait()
        for k, block in enumerate(blocks):
            rows = held[k].reshape(16 * VEC_UNITS, 128).astype(F32)
            for name, (_, panels, at_block, at) in section.vectors.items():
                if at_block != block:
                    continue
                i = names[name]
                for panel in range(panels):
                    vec_ref[i : i + 1, panel * 128 : panel * 128 + 128] = rows[
                        at + panel : at + panel + 1, :
                    ]
        return lambda name: vec_ref[names[name] : names[name] + 1, :]

    return finish


def load_weights(plan, s, gathered, w, sems):
    section = plan.sections[s]
    copies = {}
    for k, (name, ref) in enumerate(w.items()):
        panels = section.panels[name]
        flat = ref.reshape(ref.shape[0] * panels, 16, 128)
        copies[name] = [
            pltpu.make_async_copy(source, flat.at[pl.ds(at + skip, few)], sems.at[k])
            for block, side, unit, at, take in section.runs(name, plan.half_cuts)
            for source, skip, few in held_at(plan, s, gathered, block, side, unit, take)
        ]
        for copy in copies[name]:
            copy.start()

    def ready(name):
        for copy in copies.get(name, ()):
            copy.wait()

    return ready


def weight_scratch(layout, names):
    shapes = dict(layout)
    return [
        pltpu.VMEM((shapes[n][0] // GROUP, shapes[n][1] // 128, GROUP, 128), BF16)
        for n in names
    ]


def picks(perm_ref, image):
    here = pl.ds(pl.multiple_of(image * ROWS_D, 16), ROWS_D)
    patch = lax.broadcasted_iota(jnp.int32, (ROWS_D, ROWS_D), 1)
    return jnp.where(perm_ref[here, :] == patch, 1.0, 0.0).astype(BF16)


W_ENC = ["patch", "qkv", "proj", "fc1", "fc2"]


def encoder_kernel(plan, sh, refs):
    (info, gathered, patches, perm, pos, pp_out, x0_out, n1_out, mixed_out, o_out, x1_out, n2_out,
     g_out, gp_out, y_out, latent_out, w_patch, w_qkv, w_proj, w_fc1, w_fc2, held, vec_ref, pp, xe,
     x0, n1, mixed, o, x1, n2, g, gp, y, latent, w_sems, out_sems) = refs
    w = dict(zip(W_ENC, (w_patch, w_qkv, w_proj, w_fc1, w_fc2)))
    finish_vec = load_vectors(plan, 0, [gathered], held, vec_ref, w_sems.at[5])
    ready = load_weights(plan, 0, [gathered], w, w_sems)
    outs = []

    targets = [(pp, pp_out), (x0, x0_out), (n1, n1_out), (mixed, mixed_out), (o, o_out),
               (x1, x1_out), (n2, n2_out), (g, g_out), (gp, gp_out), (y, y_out),
               (latent, latent_out)]

    def saved(ref):
        for k, (source, target) in enumerate(targets):
            if source is ref:
                copy = pltpu.make_async_copy(source, target, out_sems.at[k])
                copy.start()
                outs.append(copy)

    def gather(image, carry):
        chosen = picks(perm, image)
        pp[image] = dot(chosen, patches[image]).astype(BF16)
        here = pl.ds(pl.multiple_of(image * ROWS_E, 16), ROWS_E)
        xe[here, :] = pp[image, 0:ROWS_E, :]
        few = chosen[0:ROWS_E, :]
        x0[here, :] = (dot(few, pos[0]) + dot(few, pos[1])) + dot(few, pos[2])
        return carry

    lax.fori_loop(0, sh.images, gather, 0)
    saved(pp)
    vec = finish_vec()
    ready("patch")

    def put(_, here, there, value):
        x0[here, there] = (value + vec_ref[0:1, there]) + x0[here, there]

    times_columns(xe, w["patch"], D // 128, PIX, put)
    saved(x0)
    block_forward(
        sh, x0, n1, mixed, o, x1, n2, g, gp, y, w, vec, lambda i: info[1 + i], ready, saved
    )
    norm_forward(y, vec("gf"), vec("bf"), latent, sh.count, D)
    saved(latent)
    for copy in outs:
        copy.wait()


def lasting(microseconds):
    return pl.CostEstimate(
        flops=int(microseconds * COST), bytes_accessed=1 << 20, transcendentals=0
    )


def saved_shapes(sh):
    count, width, hidden = sh.count, sh.width, sh.hidden
    return [
        ((count, width), F32),
        ((count, width), BF16),
        ((count, 3 * width), BF16),
        ((count, width), BF16),
        ((count, width), F32),
        ((count, width), BF16),
        ((count, hidden), BF16),
        ((count, hidden), F32),
        ((count, width), F32),
    ]


def encoder(plan, sh, info, gathered, patches, perm, pos):
    saved = saved_shapes(sh)
    pp_shape = ((sh.images, ROWS_D, PIX), BF16)
    latent_shape = ((sh.count, D), BF16)
    outs = [pp_shape, *saved, latent_shape]
    holders = len({v[2] for v in plan.sections[0].vectors.values()})
    return pl.pallas_call(
        lambda *refs: encoder_kernel(plan, sh, refs),
        out_shape=[jax.ShapeDtypeStruct(*s) for s in outs],
        in_specs=[IN_SMEM, ANY, IN_VMEM, IN_VMEM, IN_VMEM],
        out_specs=[ANY] * len(outs),
        scratch_shapes=[
            *weight_scratch(ENC, W_ENC),
            pltpu.VMEM((holders, VEC_UNITS, 16, 128), BF16),
            pltpu.VMEM((8, D), F32),
            pltpu.VMEM(*pp_shape),
            pltpu.VMEM((sh.count, PIX), BF16),
            *[pltpu.VMEM(*s) for s in saved],
            pltpu.VMEM(*latent_shape),
            pltpu.SemaphoreType.DMA((6,)),
            pltpu.SemaphoreType.DMA((len(outs),)),
        ],
        compiler_params=pltpu.CompilerParams(vmem_limit_bytes=VMEM_BYTES),
        cost_estimate=lasting(50),
        name="encoder_forward",
    )(info, gathered, patches, perm, pos)


W_DEC = ["embed", "qkv", "proj", "fc1", "fc2", "head"]


def decoder_kernel(plan, sh, refs):
    info, scale, gathered, gathered_tail, latent_in, pp_in, perm, pos = refs[:8]
    gathered = [gathered, gathered_tail]
    targets, refs = refs[8:12], refs[12:]
    (grad_latent, loss_out,
     w_embed, w_qkv, w_proj, w_fc1, w_fc2, w_head, held, vec_ref, pp, latent, embedded, x0, n1,
     mixed, o, x1, n2, g, gp, y, f, dn, guess, turned, turned_e, stage, vec_stage, w_sems,
     in_sems, grad_sems) = refs
    w = dict(zip(W_DEC, (w_embed, w_qkv, w_proj, w_fc1, w_fc2, w_head)))
    copy_latent = pltpu.make_async_copy(latent_in, latent, in_sems.at[0])
    copy_pp = pltpu.make_async_copy(pp_in, pp, in_sems.at[1])
    copy_latent.start()
    finish_vec = load_vectors(plan, 1, gathered, held, vec_ref, w_sems.at[6])
    ready = load_weights(plan, 1, gathered, w, w_sems)
    copy_pp.start()
    images, count = sh.images, sh.count
    count_e = images * ROWS_E
    vec = finish_vec()
    copy_latent.wait()
    ready("embed")

    def put_embedded(_, here, there, value):
        embedded[here, there] = value

    times_columns(latent, w["embed"], DD // 128, D, put_embedded)

    def tokens(image, carry):
        chosen = picks(perm, image)
        place = (dot(chosen, pos[0]) + dot(chosen, pos[1])) + dot(chosen, pos[2])
        start = pl.multiple_of(image * ROWS_D, 16)
        kept = info[1 + image]
        token = vec_ref[0:1, :]
        few = embedded[pl.ds(pl.multiple_of(image * ROWS_E, 16), ROWS_E), :]
        rank = lax.broadcasted_iota(jnp.int32, (ROWS_E, DD), 0)
        x0[pl.ds(start, ROWS_E), :] = jnp.where(rank < kept, few, token) + place[:ROWS_E, :]
        x0[pl.ds(start + ROWS_E, ROWS_D - ROWS_E), :] = token + place[ROWS_E:, :]
        return carry

    lax.fori_loop(0, images, tokens, 0)
    block_forward(
        sh, x0, n1, mixed, o, x1, n2, g, gp, y, w, vec, lambda i: NP, ready, lambda ref: None
    )
    norm_forward(y, vec("gf"), vec("bf"), f, count, DD)
    ready("head")
    copy_pp.wait()
    factor = scale[0]

    def predict_image(image, total):
        start = pl.multiple_of(image * ROWS_D, 16)
        kept = info[1 + image]
        here = pl.ds(start, ROWS_D)
        for pair in range(PIX // 256):
            guess[:, pair * 256 : pair * 256 + 256] = dot(
                f[here, :], columns(w["head"], DD, 2 * pair, 2)
            )

        target, _ = norm_rows(pp[image].astype(F32), PIX)
        off = guess[...] - target
        rank = lax.broadcasted_iota(jnp.int32, (ROWS_D, 1), 0)
        off = jnp.where((rank >= kept) & (rank < NP), off, 0.0)
        pp[image] = (off * factor).astype(BF16)
        return total + jnp.sum((off * off).reshape(ROWS_D // 8, 8, PIX), axis=0)

    total = lax.fori_loop(0, images, predict_image, jnp.zeros((8, PIX), F32))
    total = jnp.sum(jnp.sum(total, axis=0, keepdims=True), axis=1, keepdims=True)
    loss_out[...] = jnp.broadcast_to(total * (1.0 / PIX), (8, 128))

    grads = Gradients(plan, 1, info[0], stage, grad_sems, targets)
    values = {}
    back = Backward(
        sh, w, vec, lambda i: NP, grads, values, turned, lambda name, ref: None
    )
    dpred = pp.reshape(count, PIX)
    grads.weight("head", f, DD, dpred, turned)

    def put_dn(here, there, value):
        dn[here, there] = value

    back.bands(dpred, "head", DD, put_dn)

    def from_dn(at, size):
        return dn[pl.ds(at, size), :]

    def put_y(at, size, value):
        y[pl.ds(at, size), :] = value

    values["gf"], values["bf"] = norm_backward(y, vec("gf"), from_dn, put_y, count, DD)
    back.second_product(y, f, g, gp)
    back.first_product(y, g, n2, x1, dn)
    dmixed = g.at[:, pl.ds(0, 3 * DD)]
    back.projection(y, f, o, o)
    back.attention(o, mixed, dmixed)
    back.mixing(y, dmixed, n1, x0, dn)

    def split(image, total):
        start = pl.multiple_of(image * ROWS_D, 16)
        kept = info[1 + image]

        grad = y[pl.ds(start, ROWS_D), :]
        rank = lax.broadcasted_iota(jnp.int32, (ROWS_D, 1), 0)
        few = pl.ds(pl.multiple_of(image * ROWS_E, 16), ROWS_E)
        taken = jnp.where(rank[:ROWS_E] < kept, grad[:ROWS_E], 0.0)
        n1[few, :] = taken.astype(BF16)
        free = jnp.where(rank >= kept, grad, 0.0)
        return total + jnp.sum(free.reshape(ROWS_D // 8, 8, DD), axis=0)

    total = lax.fori_loop(0, images, split, jnp.zeros((8, DD), F32))
    values["mask"] = jnp.sum(total, axis=0, keepdims=True)
    placed = n1.at[pl.ds(0, count_e)]
    grads.weight("embed", latent, D, placed, turned_e)

    def put_latent(here, there, value):
        grad_latent[here, there] = value.astype(BF16)

    times_bands(placed, w["embed"], DD // 128, D, put_latent)
    grads.finish(values, vec_stage)


def grad_shapes(plan, s):
    return [
        jax.ShapeDtypeStruct((count, units, 16, 128), F32)
        for (_, count), units in zip(plan.bins(s), plan.bin_units(s))
        for _ in range(2)
    ]


def decoder(plan, sh, info, scale, gathered, latent, pp, perm, pos):
    count_e = sh.images * ROWS_E
    holders = len({v[2] for v in plan.sections[1].vectors.values()})
    saved = saved_shapes(sh)
    most = max(plan.sections[1].panels.values())
    return pl.pallas_call(
        lambda *refs: decoder_kernel(plan, sh, refs),
        out_shape=[
            *grad_shapes(plan, 1),
            jax.ShapeDtypeStruct((count_e, D), BF16),
            jax.ShapeDtypeStruct((8, 128), F32),
        ],
        in_specs=[IN_SMEM, IN_SMEM, ANY, ANY, ANY, ANY, IN_VMEM, IN_VMEM],
        out_specs=[*[ANY] * 4, IN_VMEM, IN_VMEM],
        scratch_shapes=[
            *weight_scratch(DEC, W_DEC),
            pltpu.VMEM((holders, VEC_UNITS, 16, 128), BF16),
            pltpu.VMEM((8, DD), F32),
            pltpu.VMEM((sh.images, ROWS_D, PIX), BF16),
            pltpu.VMEM((count_e, D), BF16),
            pltpu.VMEM((count_e, DD), F32),
            *[pltpu.VMEM(*s) for s in saved],
            pltpu.VMEM((sh.count, DD), BF16),
            pltpu.VMEM((sh.count, DD), F32),
            pltpu.VMEM((ROWS_D, PIX), F32),
            pltpu.VMEM((256, sh.count), BF16),
            pltpu.VMEM((256, count_e), BF16),
            pltpu.VMEM((2, 16 * most, 16, 128), F32),
            pltpu.VMEM((holders, VEC_UNITS, 16, 128), F32),
            pltpu.SemaphoreType.DMA((7,)),
            pltpu.SemaphoreType.DMA((2,)),
            pltpu.SemaphoreType.DMA((3,)),
        ],
        compiler_params=pltpu.CompilerParams(vmem_limit_bytes=VMEM_BYTES),
        cost_estimate=lasting(160),
        name="decoder_both",
    )(info, scale, *gathered, latent, pp, perm, pos)


class Stage:
    def __init__(self, plan, sh, weights, reads, temps, outs, most, cost, name, body, bins=2):
        self.plan, self.sh, self.weights, self.reads = plan, sh, weights, reads
        self.temps, self.outs, self.most, self.cost, self.name = temps, outs, most, cost, name
        self.body = body
        self.bins = bins

    def kernel(self, blocks, *refs):
        refs = list(refs)

        def take(count):
            got = refs[:count]
            del refs[:count]
            return got

        plan, sh = self.plan, self.sh
        info, gathered = take(2)
        sources = dict(zip(self.reads, take(len(self.reads))))
        take(blocks)
        targets = take(2 * self.bins)
        results = dict(zip(self.outs, take(len(self.outs))))
        w = dict(zip(self.weights, take(len(self.weights))))
        here = dict(zip(self.reads, take(len(self.reads))))
        temps = dict(zip(self.temps, take(len(self.temps))))
        held, vec_ref, turned, stage, vec_stage, w_sems, in_sems, grad_sems = refs
        finish_vec = load_vectors(plan, 0, [gathered], held, vec_ref, w_sems.at[len(w)])
        loads = {}
        for k, (name, ref) in enumerate(here.items()):
            if name == "xe":
                copies = [
                    pltpu.make_async_copy(
                        sources[name].at[i, pl.ds(0, ROWS_E)],
                        ref.at[pl.ds(i * ROWS_E, ROWS_E)],
                        in_sems.at[k],
                    )
                    for i in range(sh.images)
                ]
            else:
                copies = [pltpu.make_async_copy(sources[name], ref, in_sems.at[k])]
            for copy in copies:
                copy.start()
            loads[id(ref)] = copies
        weights_ready = load_weights(plan, 0, [gathered], w, w_sems)
        vec = finish_vec()

        def ready(name, ref=None):
            for copy in loads.pop(id(ref), ()):
                copy.wait()
            if name is not None:
                weights_ready(name)

        values = {}
        grads = Gradients(plan, 0, info[0], stage, grad_sems, targets)
        back = Backward(
            sh, w, vec, lambda i: info[1 + i], grads, values, turned, ready
        )
        back.out_sem = in_sems.at[len(self.reads)]
        self.body(back, {**here, **temps}, results)
        assert not loads
        grads.finish(values, vec_stage)

    def __call__(self, info, gathered, arrays, blocks):
        plan, sh = self.plan, self.sh
        count, width, hidden = sh.count, sh.width, sh.hidden
        known = {
            "dz": ((count, width), BF16),
            "y": ((count, width), F32),
            "dy": ((count, width), F32),
            "x0": ((count, width), F32),
            "x1": ((count, width), F32),
            "dn": ((count, width), F32),
            "n1": ((count, width), BF16),
            "n2": ((count, width), BF16),
            "o": ((count, width), BF16),
            "dyb": ((count, width), BF16),
            "do": ((count, width), BF16),
            "xe": ((count, PIX), BF16),
            "mixed": ((count, 3 * width), BF16),
            "dmixed": ((count, 3 * width), BF16),
            "g": ((count, hidden), BF16),
            "gp": ((count, hidden), F32),
        }
        holders = len({v[2] for v in plan.sections[0].vectors.values()})
        targets = grad_shapes(plan, 0)[: 2 * self.bins]
        before = 2 + len(self.reads)
        got = pl.pallas_call(
            functools.partial(self.kernel, len(blocks)),
            out_shape=[*targets, *[jax.ShapeDtypeStruct(*known[n]) for n in self.outs]],
            in_specs=[IN_SMEM, *[ANY] * (1 + len(self.reads) + len(blocks))],
            out_specs=[*[ANY] * len(targets), *[ANY if n == "g" else IN_VMEM for n in self.outs]],
            input_output_aliases={before + i: i for i in range(len(blocks))},
            scratch_shapes=[
                *weight_scratch(ENC, self.weights),
                *[pltpu.VMEM(*known[n]) for n in self.reads],
                *[pltpu.VMEM(*known[n]) for n in self.temps],
                pltpu.VMEM((holders, VEC_UNITS, 16, 128), BF16),
                pltpu.VMEM((8, D), F32),
                pltpu.VMEM((256, count), BF16),
                pltpu.VMEM((2, 16 * self.most, 16, 128), F32),
                pltpu.VMEM((holders, VEC_UNITS, 16, 128), F32),
                pltpu.SemaphoreType.DMA((len(self.weights) + 1,)),
                pltpu.SemaphoreType.DMA((len(self.reads) + 1,)),
                pltpu.SemaphoreType.DMA((3,)),
            ],
            compiler_params=pltpu.CompilerParams(vmem_limit_bytes=VMEM_BYTES),
            cost_estimate=lasting(self.cost),
            name=self.name,
        )(info, gathered, *[arrays[n] for n in self.reads], *blocks)
        return got[: len(targets)], dict(zip(self.outs, got[len(targets) :]))


def back_second(back, r, out):
    sh = back.sh
    back.ready(None, r["dz"])
    back.ready(None, r["y"])

    def from_latent(at, size):
        return r["dz"][pl.ds(at, size), :].astype(F32)

    def put(at, size, value):
        out["dy"][pl.ds(at, size), :] = value

    back.values["gf"], back.values["bf"] = norm_backward(
        r["y"], back.vec("gf"), from_latent, put, sh.count, D
    )
    back.second_product(out["dy"], r["dyb"], r["g"], r["gp"])
    copy = pltpu.make_async_copy(r["g"], out["g"], back.out_sem)
    copy.start()
    back.grads.drain(0)
    back.grads.drain(1)
    copy.wait()


def copy_rows(count, source, target):
    def step(at):
        target[pl.ds(at, 16), :] = source[pl.ds(at, 16), :]

    for_rows(count, 16, step, 4)


def back_first(back, r, out):
    back.ready(None, r["dy"])
    back.ready(None, r["g"])
    copy_rows(back.sh.count, r["dy"], out["dy"])
    back.first_product(out["dy"], r["g"], r["n2"], r["x1"], r["dn"])


def back_projection(back, r, out):
    back.ready(None, r["dy"])
    back.projection(r["dy"], r["dyb"], r["o"], out["do"])


def back_attention(back, r, out):
    back.attention(r["do"], r["mixed"], out["dmixed"])


def back_mixing(back, r, out):
    back.ready(None, r["dy"])
    back.ready(None, r["dmixed"])
    back.mixing(r["dy"], r["dmixed"], r["n1"], r["x0"], r["dn"])

    def body(i, total):
        at = pl.multiple_of(i * 16, 16)
        grad = r["dy"][pl.ds(at, 16), :]
        r["dyb"][pl.ds(at, 16), :] = grad.astype(BF16)
        return total + jnp.sum(grad.reshape(2, 8, D), axis=0)

    total = lax.fori_loop(0, back.sh.count // 16, body, jnp.zeros((8, D), F32))
    back.values["patch_b"] = jnp.sum(total, axis=0, keepdims=True)
    back.ready(None, r["xe"])
    back.grads.weight("patch", r["xe"], PIX, r["dyb"], back.turned)


def encoder_back_stages(plan, sh):
    most = {n: plan.sections[0].panels[n] for n in ("fc1", "fc2", "qkv", "proj")}
    return [
        Stage(plan, sh, ["fc2"], ["y", "dz", "g", "gp"], ["dyb"], ["dy", "g"], most["fc2"], 25,
              "encoder_back_fc2", back_second),
        Stage(plan, sh, ["fc1"], ["g", "dy", "n2", "x1"], ["dn"], ["dy"], most["fc1"], 20,
              "encoder_back_fc1", back_first),
        Stage(plan, sh, ["proj"], ["dy", "o"], ["dyb"], ["do"], most["proj"], 10,
              "encoder_back_proj", back_projection, 1),
        Stage(plan, sh, [], ["do", "mixed"], [], ["dmixed"], 1, 25,
              "encoder_back_attention", back_attention, 0),
        Stage(plan, sh, ["qkv"], ["dy", "dmixed", "n1", "x0", "xe"], ["dn", "dyb"], [],
              most["qkv"], 25, "encoder_back_qkv", back_mixing, 1),
    ]


def pick(value, index, axis):
    return lax.dynamic_index_in_dim(value, index, axis, keepdims=False)


def tie(*trees):
    return lax.optimization_barrier(trees)


class Term:
    def __init__(self, base, bits, first, last, fixed=()):
        self.base, self.bits, self.first, self.last = base, bits, first, last
        self.fixed = dict(fixed)

    def at(self, bit, index):
        return Term(self.base, self.bits, self.first, self.last, {**self.fixed, bit: index})

    def value(self):
        zero = jnp.zeros((), jnp.int32)
        starts = [self.fixed.get(b, zero).astype(jnp.int32) for b in self.bits]
        sizes = [1 if b in self.fixed else 2 for b in self.bits]
        left = [n for n in sizes if n == 2]
        starts += [jnp.full((), self.first, jnp.int32), zero, zero]
        count = self.last - self.first
        out = lax.dynamic_slice(self.base, starts, [*sizes, count, 16, 128])
        return out.reshape(*left, count, 16, 128)


def sum_of(terms):
    return total_of([term.value() for term in terms])


class Flow:
    def __init__(self, dp, keep, send, first, shares=(1, 1, 1)):
        parts = len(shares)
        self.dp = dp
        self.me = lax.axis_index("dp")
        self.keep, self.given = keep, send
        count, units = keep.shape[:2]
        self.bits = count.bit_length() - 1
        assert count == 1 << self.bits and dp & (dp - 1) == 0
        self.all_bits = dp.bit_length() - 1
        self.first = first
        low = list(range(self.bits))
        if dp == 64:
            low = [b for b in (0, 2, 4, 1, 3) if b < self.bits]
        turn = max(min(3, len(low)), 1)
        self.cuts = [units * sum(shares[:p]) // sum(shares) for p in range(parts + 1)]
        self.orders = [low[p % turn : turn] + low[: p % turn] + low[turn:] for p in range(parts)]
        self.step = -1
        self.terms = None

    def done(self):
        return self.step == self.all_bits

    def last(self):
        return self.step == self.all_bits - 1

    def payload(self):
        if self.step < 0:
            return [self.given]
        if self.step >= self.bits:
            return [self.result()]
        out = []
        for terms, order in zip(self.terms, self.orders):
            bit = order[self.step]
            other = 1 - (self.me >> bit & 1)
            out.append(sum_of([t.at(bit, other) for t in terms]))
        return out

    def send(self, payload):
        if self.step < 0:
            return [lax.ppermute(payload[0], "section", [(0, 1), (1, 0)])]
        if self.step >= self.bits:
            flip = 1 << self.step
            pairs = [(i, i ^ flip) for i in range(self.dp) if (i ^ self.first) & flip]
            return [lax.ppermute(payload[0], "dp", pairs)]
        out = []
        for value, order in zip(payload, self.orders):
            flip = 1 << order[self.step]
            out.append(lax.ppermute(value, "dp", [(i, i ^ flip) for i in range(self.dp)]))
        return out

    def take(self, got):
        ranges = list(zip(self.cuts[:-1], self.cuts[1:]))
        if self.step < 0:
            bits = list(range(self.bits - 1, -1, -1))
            shape = (2,) * self.bits + self.keep.shape[1:]
            self.terms = [
                [Term(v.reshape(shape), bits, *r) for v in (self.keep, got[0])] for r in ranges
            ]
        elif self.step < self.bits:
            for k, (order, value) in enumerate(zip(self.orders, got)):
                bit = order[self.step]
                mine = self.me >> bit & 1
                gone = order[: self.step + 1]
                bits = [b for b in range(self.bits - 1, -1, -1) if b not in gone]
                self.terms[k] = [t.at(bit, mine) for t in self.terms[k]]
                self.terms[k].append(Term(value, bits, 0, value.shape[-3]))
        else:
            for k, r in enumerate(ranges):
                self.terms[k].append(Term(got[0], [], *r))
        self.step += 1

    def result(self):
        return jnp.concatenate([sum_of(t) for t in self.terms], axis=0)


def move_on(flows, *others):
    flows = [f for f in flows if f is not None and not f.done()]
    payloads, others = tie([f.payload() for f in flows], others)
    return flows, [f.send(p) for f, p in zip(flows, payloads)], others


def arrive(flows, got):
    for flow, values in zip(flows, got):
        flow.take(values)


def sum_in_chip(value):
    return value + lax.ppermute(value, "section", [(0, 1), (1, 0)])


def sum_over_dp(dp, value, low):
    bits = dp.bit_length() - 1
    got = [
        lax.ppermute(value, "dp", [(i, i ^ (flip << low)) for i in range(dp)])
        for flip in range(1, 1 << min(2, bits - low))
    ]
    value = value + got[0]
    if len(got) == 3:
        value = value + (got[1] + got[2])
    return value


def sum_everywhere(dp, value):
    value = sum_in_chip(value)
    for low in range(0, dp.bit_length() - 1, 2):
        value = sum_over_dp(dp, value, low)
    return value


def squares_of(plan, s, value, section, me):
    section_plan = plan.sections[s]
    vectors = np.zeros((plan.dp,), np.int32)
    for _, panels, block, at in section_plan.vectors.values():
        vectors[block] = max(vectors[block], at + panels)
    filled = jnp.asarray(np.asarray(section_plan.fill, np.int32) * 16)[me]
    vectors = jnp.asarray(vectors)[me]
    shape = value.shape
    row = lax.broadcasted_iota(jnp.int32, shape, 0) * 16 + lax.broadcasted_iota(jnp.int32, shape, 1)
    row = row + section * (plan.half * 16)
    extra = row - plan.vec_unit * 16
    valid = (row < filled) | ((extra >= 0) & (extra < vectors))
    return jnp.sum(jnp.where(valid, value * value, 0.0))


def gather_decoder(plan, half_d, section, me, after):
    dp, quarter = plan.dp, plan.quarter
    first = plan.bins(1)[1][0]
    assert 2 * first == dp
    used = max(plan.tail_used())
    spread = jnp.pad(half_d, ((0, 2 * quarter - plan.half), (0, 0), (0, 0)))
    spread = total_of(
        [
            lax.ppermute(
                spread[i * quarter : (i + 1) * quarter],
                "dp",
                [(b, 2 * b + i) for b in range(first)],
            )
            for i in range(2)
        ]
    )
    rest = jnp.where(me == first, half_d[:used], jnp.zeros((), BF16))
    holders = [first]
    for bit in reversed(range(dp.bit_length() - 1)):
        rest = rest + lax.ppermute(rest, "dp", [(i, i ^ 1 << bit) for i in holders])
        holders = holders + [i ^ 1 << bit for i in holders]
    other = lax.ppermute(rest, "section", [(0, 1), (1, 0)])
    rest = jnp.where(section == 0, jnp.stack([rest, other]), jnp.stack([other, rest]))
    spread, _ = tie(spread, after[0, 0, 0])
    gathered = lax.all_gather(spread, ("section", "dp"), axis=0, tiled=True)
    return gathered.reshape(2, dp, quarter, 16, 128), rest


def sincos(width):
    places = np.arange(NP).astype(np.float32)[:, None]
    column = np.arange(width)
    rates = np.exp(
        -(np.float32(2.0) * (column // 2).astype(np.float32) / np.float32(width))
        * np.float32(math.log(10000.0))
    ).astype(np.float32)
    phases = (places * rates[None, :]).astype(np.float32)
    table = np.where(
        column[None, :] % 2 == 0, np.sin(phases.astype(np.float64)), np.cos(phases.astype(np.float64))
    ).astype(np.float32)
    parts = []
    left = np.zeros((ROWS_D, width), np.float32)
    left[:NP] = table
    for _ in range(3):
        high = left.astype(jnp.bfloat16)
        parts.append(high)
        left = left - high.astype(np.float32)
    return np.stack(parts)


def on_device(patches, keep, perm, master, first, second, ema):
    dp = lax.axis_size("dp")
    section = lax.axis_index("section")
    me = lax.axis_index("dp")
    shard = master.shape[1]
    plan = Plan(dp, shard // 128)
    rows, half = plan.shard_rows, plan.half
    swap = [(0, 1), (1, 0)]
    states = [v.reshape(rows, 1, 128) for v in (master, first, second, ema)]

    following = lax.ppermute(
        states[0][: plan.head_rows], "dp", [(i, i - 1) for i in range(1, dp)]
    )
    index = jnp.asarray(plan.pack_index)[section, me]
    packed = pack(plan, index, states[0], following)
    mine = lax.dynamic_slice_in_dim(packed, section * half, half, 0)
    given = lax.ppermute(
        lax.dynamic_slice_in_dim(packed, (1 - section) * half, half, 0), "section", swap
    )
    half_e = jnp.where(section == 0, mine, given)
    half_d = jnp.where(section == 0, given, mine)
    gathered_e = lax.all_gather(half_e, ("section", "dp"), axis=0, tiled=True)
    gathered_e = gathered_e.reshape(2, dp, half, 16, 128)
    gathered_d = gather_decoder(plan, half_d, section, me, gathered_e)

    count = sum_everywhere(dp, jnp.sum(NP - keep).astype(F32)) * 0.5
    images = patches.shape[0] // 2
    mine = section * images
    patches = lax.dynamic_slice_in_dim(patches, mine, images, 0)
    patches = jnp.pad(patches, ((0, 0), (0, ROWS_D - NP), (0, 0)))
    order = lax.dynamic_slice_in_dim(perm, mine, images, 0)
    order = jnp.pad(order, ((0, 0), (0, ROWS_D - NP)), constant_values=ROWS_D - 1)
    order = order.reshape(images * ROWS_D, 1)
    kept = lax.dynamic_slice_in_dim(keep, mine, images, 0)
    info = jnp.concatenate([section[None].astype(jnp.int32), kept])
    scale = ((1.0 / count) * (1.0 / PIX) * 2.0).reshape(1)

    shape_e = Shape(images, ROWS_E, D, HEADS_E, FF_E)
    shape_d = Shape(images, ROWS_D, DD, HEADS_D, FF_D)
    pp, *saved, latent = encoder(
        plan, shape_e, info, gathered_e, patches, order, jnp.asarray(sincos(D))
    )
    arrays = dict(zip(("x0", "n1", "mixed", "o", "x1", "n2", "g", "gp", "y"), saved))
    arrays["xe"] = pp
    *sums_d, arrays["dz"], loss = decoder(
        plan, shape_d, info, scale, gathered_d, latent, pp, order, jnp.asarray(sincos(DD))
    )

    stages = encoder_back_stages(plan, shape_e)
    first_tail = plan.bins(1)[1][0]
    main = Flow(dp, sums_d[0], sums_d[1], 0)
    rest = Flow(dp, sums_d[2], sums_d[3], first_tail, (1,))
    flows, got, _ = move_on([main, rest])
    got, arrays = tie(got, arrays)
    arrive(flows, got)
    low = high = None
    blocks = []
    late = []
    for number, stage in enumerate(stages):
        flows, got, (arrays, blocks) = move_on([main, rest, high], arrays, blocks)
        if stage.bins:
            blocks, made = stage(info, gathered_e, arrays, blocks)
        else:
            _, made = stage(info, gathered_e, arrays, [])
        arrays = {**arrays, **made}
        kept = [g for f, g in zip(flows, got) if not f.last()]
        kept, late, arrays, blocks = tie(kept, late, arrays, blocks)
        late = [g for f, g in zip(flows, got) if f.last()]
        kept = iter(kept)
        arrive(flows, [g if f.last() else next(kept) for f, g in zip(flows, got)])
        if number == 1:
            high = Flow(dp, blocks[2], blocks[3], dp // 2, (4, 4, 2))
            blocks = blocks[:2]
    low = Flow(dp, blocks[0], blocks[1], 0)
    every = [main, rest, high, low]
    while not all(f.done() for f in every):
        flows, got, _ = move_on(every)
        arrive(flows, got)

    sum_tail = rest.result()
    sum_tail = jnp.pad(sum_tail, ((0, half - sum_tail.shape[0]), (0, 0), (0, 0)))
    sum_d = jnp.where(me < first_tail, main.result(), sum_tail)
    sum_e = jnp.where(me < dp // 2, low.result(), high.result())
    squares = [
        squares_of(plan, s, v, section, me) for s, v in enumerate((sum_e, sum_d))
    ]
    half_mine = jnp.where(section == 0, sum_e, sum_d)
    half_other = lax.ppermute(jnp.where(section == 0, sum_d, sum_e), "section", swap)
    sums = sum_in_chip(jnp.stack([squares[0] + squares[1], loss[0, 0]]))
    sums, half_other = tie(sums, half_other)
    sums = sum_over_dp(dp, sums, 0)
    block = jnp.where(
        section == 0,
        jnp.concatenate([half_mine, half_other], axis=0),
        jnp.concatenate([half_other, half_mine], axis=0),
    )
    start = jnp.asarray(plan.tail_start)[section, me]
    tail = jnp.concatenate(
        [
            lax.dynamic_slice_in_dim(block, start, plan.tail_units, 0),
            block[plan.vec_unit :],
        ],
        axis=0,
    )
    sums, tail = tie(sums, tail)
    tail = lax.ppermute(tail, "dp", [(i, i + 1) for i in range(dp - 1)])
    for low in range(2, dp.bit_length() - 1, 2):
        sums = sum_over_dp(dp, sums, low)
    index = jnp.asarray(plan.unpack_index)[section, me]
    total = unpack(plan, index, block, tail)
    norm = jnp.sqrt(sums[0])
    factor = jnp.minimum(1.0, clip_limit / (norm + norm_epsilon))
    made = update(plan, factor.reshape(1), total, states)
    return (*[v.reshape(1, shard) for v in made], norm, sums[1], count)


def solution(mesh):
    return jax.shard_map(
        on_device,
        mesh=mesh,
        in_specs=(
            P("dp", None, None),
            P("dp"),
            P("dp", None),
            P("section", "dp"),
            P("section", "dp"),
            P("section", "dp"),
            P("section", "dp"),
        ),
        out_specs=(
            P("section", "dp"),
            P("section", "dp"),
            P("section", "dp"),
            P("section", "dp"),
            P(),
            P(),
            P(),
        ),
        check_vma=False,
    )
```

```python
import functools
import math

import jax
import jax.numpy as jnp
import numpy as np
from jax import lax
from jax.experimental import pallas as pl
from jax.experimental.pallas import tpu as pltpu
from jax.sharding import PartitionSpec as P

D = 768
HEADS_E = 12
FF_E = 3072
DD = 512
HEADS_D = 16
FF_D = 2048
PIX = 768
NP = 196
SLOTS = 98
STEP = 10

norm_epsilon = 1e-06
clip_limit = 0.01
learn_rate = 0.02
beta_one = 0.9
beta_two = 0.999
adam_epsilon = 1e-08
weight_decay = 0.05
average_keep = 0.8

F32 = jnp.float32
BF16 = jnp.bfloat16
ROWS_E = 112
ROWS_D = 208
GROUP = 16
VEC_UNITS = 2
VMEM_BYTES = 60 * 1024 * 1024
COST = 2e8
ANY = pl.BlockSpec(memory_space=pl.ANY)
IN_VMEM = pl.BlockSpec(memory_space=pltpu.VMEM)
IN_SMEM = pl.BlockSpec(memory_space=pltpu.SMEM)

ENC = [
    ("patch", (PIX, D)),
    ("patch_b", (D,)),
    ("g1", (D,)),
    ("b1", (D,)),
    ("qkv", (D, 3 * D)),
    ("proj", (D, D)),
    ("g2", (D,)),
    ("b2", (D,)),
    ("fc1", (D, FF_E)),
    ("fc2", (FF_E, D)),
    ("gf", (D,)),
    ("bf", (D,)),
]
DEC = [
    ("embed", (D, DD)),
    ("mask", (DD,)),
    ("g1", (DD,)),
    ("b1", (DD,)),
    ("qkv", (DD, 3 * DD)),
    ("proj", (DD, DD)),
    ("g2", (DD,)),
    ("b2", (DD,)),
    ("fc1", (DD, FF_D)),
    ("fc2", (FF_D, DD)),
    ("gf", (DD,)),
    ("bf", (DD,)),
    ("head", (DD, PIX)),
]


class Section:
    def __init__(self, layout, dp, shard_rows):
        self.dp = dp
        self.shard_rows = shard_rows
        self.groups = []
        self.vectors = {}
        self.panels = {}
        fill = [0] * dp
        vector_fill = [0] * dp
        row = 0
        for name, shape in layout:
            panels = shape[-1] // 128
            self.panels[name] = panels
            if len(shape) == 2:
                for group in range(shape[0] // GROUP):
                    block = row // shard_rows
                    self.groups.append((name, group, row, panels, block, fill[block]))
                    fill[block] += panels
                    row += GROUP * panels
            else:
                block = row // shard_rows
                self.vectors[name] = (row, panels, block, vector_fill[block])
                vector_fill[block] += panels
                row += panels
        self.rows = row
        self.fill = fill
        assert max(vector_fill) <= 16 * VEC_UNITS
        self.blocks_used = max(b for b in range(dp) if fill[b] or vector_fill[b]) + 1

    def pieces(self, name, first=0, count=None):
        out = []
        for tensor, group, _, panels, block, unit in self.groups:
            if tensor != name or group < first or (count is not None and group >= first + count):
                continue
            if out and out[-1][0] == block and out[-1][1] + out[-1][3] * panels == unit:
                out[-1][3] += 1
            else:
                out.append([block, unit, group, 1])
        return [tuple(p) for p in out]

    def runs(self, name, cuts, first=0, count=None):
        panels = self.panels[name]
        out = []
        for block, unit, group, groups in self.pieces(name, first, count):
            at, left = (group - first) * panels, groups * panels
            while left:
                place = max(i for i in range(len(cuts) - 1) if cuts[i] <= unit)
                take = min(left, cuts[place + 1] - unit)
                out.append((block, place, unit - cuts[place], at, take))
                unit, at, left = unit + take, at + take, left - take
        return out


class Plan:
    def __init__(self, dp, shard_rows):
        self.dp = dp
        self.shard_rows = shard_rows
        self.sections = [Section(ENC, dp, shard_rows), Section(DEC, dp, shard_rows)]
        units = max(max(s.fill) for s in self.sections)
        units += (units + VEC_UNITS) % 2
        self.vec_unit = units
        self.units = units + VEC_UNITS
        self.half = self.units // 2
        half = self.half
        self.quarter = -(-half // 2)
        self.part_cuts = [0, -(-half // 3), -(-2 * half // 3), half]
        self.half_cuts = [0, half, self.units]
        self.head_rows = 8 * -(-max(16 * max(s.panels.values()) for s in self.sections) // 8)
        self.tail_units = max(max(s.panels.values()) for s in self.sections)
        self.pack_base = 8 * -(-shard_rows // 8)
        self.pack_rows = shard_rows + self.head_rows
        self.pack_index = np.zeros((2, dp, self.units * 16), np.int32)
        self.tail_rows = 16 * (self.tail_units + VEC_UNITS)
        self.zero_row = self.units * 16 + self.tail_rows
        self.unpack_index = np.full((2, dp, shard_rows), self.zero_row, np.int32)
        self.tail_start = np.zeros((2, dp), np.int32)
        for s, section in enumerate(self.sections):
            for b in range(dp):
                self.tail_start[s, b] = max(section.fill[b] - self.tail_units, 0)
            for name, group, row, panels, block, unit in section.groups:
                for panel in range(panels):
                    for r in range(GROUP):
                        self.place(s, block, (unit + panel) * 16 + r, row + r * panels + panel)
            for row, panels, block, at in section.vectors.values():
                for panel in range(panels):
                    self.place(s, block, self.vec_unit * 16 + at + panel, row + panel)

    def bins(self, s):
        if s == 0:
            return [(0, self.dp // 2), (self.dp // 2, self.dp - self.dp // 2)]
        used = self.sections[1].blocks_used
        main = 1 << (used.bit_length() - 1)
        return [(0, main), (main, max(used - main, 1))]

    def tail_used(self):
        first, count = self.bins(1)[1]
        section = self.sections[1]
        assert count == 1 and all(v[2] < first for v in section.vectors.values())
        used = section.fill[first]
        return min(used, self.half), max(used - self.half, 0)

    def bin_units(self, s):
        return [self.half, self.half if s == 0 else max(self.tail_used())]

    def place(self, s, block, block_row, flat_row):
        local = flat_row - block * self.shard_rows
        assert 0 <= local < self.pack_rows
        gap = self.pack_base - self.shard_rows if local >= self.shard_rows else 0
        self.pack_index[s, block, block_row] = local + gap
        owner, at = divmod(flat_row, self.shard_rows)
        if owner == block:
            self.unpack_index[s, owner, at] = block_row
        else:
            assert owner == block + 1
            if block_row >= self.vec_unit * 16:
                source = self.tail_units * 16 + block_row - self.vec_unit * 16
            else:
                source = block_row - int(self.tail_start[s, block]) * 16
                assert 0 <= source < self.tail_units * 16
            self.unpack_index[s, owner, at] = self.units * 16 + source


def move_rows_in(index_ref, held, done, count):
    def eight(i, carry):
        for j in range(8):
            row = i * 8 + j
            done[pl.ds(row, 1), :] = held[pl.ds(index_ref[row], 1), :]
        return carry

    lax.fori_loop(0, count // 8, eight, 0)
    for row in range(count // 8 * 8, count):
        done[pl.ds(row, 1), :] = held[pl.ds(index_ref[row], 1), :]


def pack_kernel(base, index_ref, flat, following, out_ref, held, done, sems):
    rows, more = flat.shape[0], following.shape[0]
    copies = [
        pltpu.make_async_copy(flat.at[:, 0], held.at[pl.ds(0, rows)], sems.at[0]),
        pltpu.make_async_copy(following.at[:, 0], held.at[pl.ds(base, more)], sems.at[1]),
    ]
    for copy in copies:
        copy.start()
    for copy in copies:
        copy.wait()
    count = done.shape[0]
    move_rows_in(index_ref, held, done, count)
    out_ref[...] = done[...].reshape(out_ref.shape).astype(BF16)


def pack(plan, index, flat, following):
    count = plan.units * 16
    return pl.pallas_call(
        functools.partial(pack_kernel, plan.pack_base),
        out_shape=jax.ShapeDtypeStruct((plan.units, 16, 128), BF16),
        in_specs=[IN_SMEM, ANY, ANY],
        out_specs=IN_VMEM,
        scratch_shapes=[
            pltpu.VMEM((plan.pack_base + plan.head_rows, 128), F32),
            pltpu.VMEM((count, 128), F32),
            pltpu.SemaphoreType.DMA((2,)),
        ],
        compiler_params=pltpu.CompilerParams(vmem_limit_bytes=32 * 1024 * 1024),
        name="pack_rows",
    )(index, flat, following)


def unpack_kernel(zero_row, rows, index_ref, block, tail, out_ref, held):
    at = 0
    for source in (block, tail):
        size = source.shape[0] * 16
        held[pl.ds(at, size), :] = source[...].reshape(size, 128)
        at += size
    held[pl.ds(zero_row, 8), :] = jnp.zeros((8, 128), F32)
    out_ref[pl.ds(out_ref.shape[0] - 16, 16), :] = jnp.zeros((16, 128), F32)
    move_rows_in(index_ref, held, out_ref, rows)


def unpack(plan, index, block, tail):
    rows = plan.shard_rows
    padded = 16 * -(-rows // 16)
    return pl.pallas_call(
        functools.partial(unpack_kernel, plan.zero_row, rows),
        out_shape=jax.ShapeDtypeStruct((padded, 128), F32),
        in_specs=[IN_SMEM, IN_VMEM, IN_VMEM],
        out_specs=IN_VMEM,
        scratch_shapes=[pltpu.VMEM((plan.zero_row + 8, 128), F32)],
        compiler_params=pltpu.CompilerParams(vmem_limit_bytes=32 * 1024 * 1024),
        cost_estimate=lasting(6),
        name="unpack_rows",
    )(index, block, tail)


def update_kernel(rows, chunk, factor_ref, total, *refs):
    states, outs, held, made, in_sems, out_sems = (
        refs[:4], refs[4:8], refs[8:12], refs[12:16], refs[16], refs[17],
    )
    starts = list(range(0, rows, chunk))
    sizes = [min(chunk, rows - at) for at in starts]
    loads = [
        [
            pltpu.make_async_copy(
                source.at[pl.ds(at, size), 0], ref.at[pl.ds(at, size)], in_sems.at[k, j]
            )
            for j, (source, ref) in enumerate(zip(states, held))
        ]
        for k, (at, size) in enumerate(zip(starts, sizes))
    ]
    for group in loads:
        for copy in group:
            copy.start()
    stores = []
    factor = factor_ref[0]
    for k, (at, size) in enumerate(zip(starts, sizes)):
        for copy in loads[k]:
            copy.wait()

        def body(i, carry):
            here = pl.ds(pl.multiple_of(at + i * 16, 8), 16)
            master, first, second, ema = (ref[here, :] for ref in held)
            clipped = total[here, :] * factor
            new_first = beta_one * first + (1.0 - beta_one) * clipped
            new_second = beta_two * second + (1.0 - beta_two) * clipped * clipped
            first_hat = new_first * (1.0 / (1.0 - beta_one**STEP))
            second_hat = new_second * (1.0 / (1.0 - beta_two**STEP))
            new_master = master - learn_rate * (
                first_hat / (jnp.sqrt(second_hat) + adam_epsilon) + weight_decay * master
            )
            made[0][here, :] = new_master
            made[1][here, :] = new_first
            made[2][here, :] = new_second
            made[3][here, :] = average_keep * ema + (1.0 - average_keep) * new_master
            return carry

        lax.fori_loop(0, -(-size // 16), body, 0, unroll=2)
        for j in range(4):
            copy = pltpu.make_async_copy(
                made[j].at[pl.ds(at, size)], outs[j].at[pl.ds(at, size), 0], out_sems.at[k, j]
            )
            copy.start()
            stores.append(copy)
    for copy in stores:
        copy.wait()


def update(plan, factor, total, states):
    rows = plan.shard_rows
    chunk = 16 * -(-rows // (16 * 4))
    padded = 16 * -(-rows // 16)
    count = -(-rows // chunk)
    return pl.pallas_call(
        functools.partial(update_kernel, rows, chunk),
        out_shape=[jax.ShapeDtypeStruct((rows, 1, 128), F32)] * 4,
        in_specs=[IN_SMEM, IN_VMEM, *[ANY] * 4],
        out_specs=[ANY] * 4,
        scratch_shapes=[
            *[pltpu.VMEM((padded, 128), F32)] * 8,
            pltpu.SemaphoreType.DMA((count, 4)),
            pltpu.SemaphoreType.DMA((count, 4)),
        ],
        compiler_params=pltpu.CompilerParams(vmem_limit_bytes=VMEM_BYTES),
        name="update_states",
    )(factor, total, *states)


def dot(a, b):
    return lax.dot_general(a, b, (((1,), (0,)), ((), ())), preferred_element_type=F32)


def dot_nt(a, b):
    return lax.dot_general(a, b, (((1,), (1,)), ((), ())), preferred_element_type=F32)


def dot_tn(a, b):
    return lax.dot_general(a, b, (((0,), (0,)), ((), ())), preferred_element_type=F32)


def total_of(terms):
    total = terms[0]
    for term in terms[1:]:
        total = total + term
    return total


def for_rows(count, size, step, unroll=1):
    def body(i, carry):
        step(pl.multiple_of(i * size, size))
        return carry

    lax.fori_loop(0, count // size, body, 0, unroll=unroll)


def columns(weight, depth, first, count):
    parts = [weight[:, first + i].reshape(depth, 128) for i in range(count)]
    return jnp.concatenate(parts, axis=1)


def row_band(weight, panels, band):
    parts = [weight[pl.ds(band * 16, 16), i].reshape(256, 128) for i in range(panels)]
    return jnp.concatenate(parts, axis=1)


def row_chunks(count):
    size = next(n for n in (208, 224, 112, 104, 16) if count % n == 0)
    return [slice(at, at + size) for at in range(0, count, size)]


def wide_chunks(count):
    size = next(n for n in (416, 336, 112, 104, 16) if count % n == 0)
    return [slice(at, at + size) for at in range(0, count, size)]


def times_columns(left, weight, panels, depth, finish):
    group = 4 if panels % 4 == 0 else 2

    def body(index, carry):
        right = columns(weight, depth, group * index, group)
        width = group * 128
        there = pl.ds(pl.multiple_of(index * width, width), width)
        for here in row_chunks(left.shape[0]):
            finish(index * width, here, there, dot(left[here, :], right))
        return carry

    lax.fori_loop(0, panels // group, body, 0)


def times_bands(left, weight, panels, count, finish):
    def body(band, carry):
        right = row_band(weight, panels, band)
        for here in wide_chunks(left.shape[0]):
            finish(here, lanes(band), dot_nt(left[here, :], right))
        return carry

    lax.fori_loop(0, count // 256, body, 0)


def lanes(pair):
    return pl.ds(pl.multiple_of(pair * 256, 256), 256)


def norm_block(count):
    return next(n for n in (416, 336, 112, 104, 16) if count % n == 0)


def norm_rows(x, width):
    mean = jnp.sum(x, axis=1, keepdims=True) * (1.0 / width)
    centre = x - mean
    spread = jnp.sum(centre * centre, axis=1, keepdims=True) * (1.0 / width)
    rstd = lax.rsqrt(spread + norm_epsilon)
    return centre * rstd, rstd


def norm_forward(x_ref, gain, shift, out_ref, count, width):
    size = norm_block(count)

    def step(at):
        hat, _ = norm_rows(x_ref[pl.ds(at, size), :], width)
        out_ref[pl.ds(at, size), :] = (hat * gain + shift).astype(out_ref.dtype)

    for_rows(count, size, step)


def norm_backward(x_ref, gain, grad_of, put, count, width):
    size = norm_block(count)

    def body(i, carry):
        gain_sum, shift_sum = carry
        at = pl.multiple_of(i * size, size)
        hat, rstd = norm_rows(x_ref[pl.ds(at, size), :], width)
        grad = grad_of(at, size)
        gain_sum = gain_sum + jnp.sum((grad * hat).reshape(size // 8, 8, width), axis=0)
        shift_sum = shift_sum + jnp.sum(grad.reshape(size // 8, 8, width), axis=0)
        scaled = grad * gain
        first = jnp.sum(scaled, axis=1, keepdims=True) * (1.0 / width)
        second = jnp.sum(scaled * hat, axis=1, keepdims=True) * (1.0 / width)
        put(at, size, rstd * (scaled - first - hat * second))
        return gain_sum, shift_sum

    zero = jnp.zeros((8, width), F32)
    gain_sum, shift_sum = lax.fori_loop(0, count // size, body, (zero, zero))
    return jnp.sum(gain_sum, axis=0, keepdims=True), jnp.sum(shift_sum, axis=0, keepdims=True)


def head_masks(size):
    lane = lax.broadcasted_iota(jnp.int32, (1, 128), 1)
    return [
        jnp.where((lane >= h * size) & (lane < (h + 1) * size), 1.0, 0.0).astype(BF16)
        for h in range(128 // size)
    ]


def softmax_columns(scores, limit):
    key = lax.broadcasted_iota(jnp.int32, scores.shape, 0)
    scores = jnp.where(key < limit, scores, -1e30)
    top = jnp.max(scores, axis=0, keepdims=True)
    raised = jnp.exp(scores - top)
    return raised * (1.0 / jnp.sum(raised, axis=0, keepdims=True))


def softmax_rows(scores, limit):
    key = lax.broadcasted_iota(jnp.int32, scores.shape, 1)
    scores = jnp.where(key < limit, scores, -1e30)
    top = jnp.max(scores, axis=1, keepdims=True)
    raised = jnp.exp(scores - top)
    return raised * (1.0 / jnp.sum(raised, axis=1, keepdims=True))


def attention_forward(mixed, out, limit_of, images, rows, width, size):
    panels = width // 128
    masks = head_masks(size)

    def body(step, carry):
        image, panel = step // panels, step % panels
        here = pl.ds(pl.multiple_of(image * rows, 16), rows)

        def part(third):
            return mixed[here, pl.ds(pl.multiple_of((third * panels + panel) * 128, 128), 128)]

        query, keys, values = part(0), part(1), part(2)
        limit = limit_of(image)
        probs = [softmax_rows(dot_nt(query * mask, keys), limit).astype(BF16) for mask in masks]
        total = total_of([dot(p, values) * m.astype(F32) for p, m in zip(probs, masks)])
        out[here, pl.ds(pl.multiple_of(panel * 128, 128), 128)] = total.astype(BF16)
        return carry

    lax.fori_loop(0, images * panels, body, 0, unroll=6)


def attention_backward(mixed, grad_out, grad_mixed, limit_of, images, rows, width, size):
    panels = width // 128
    masks = head_masks(size)

    def body(step, carry):
        image, panel = step // panels, step % panels
        here = pl.ds(pl.multiple_of(image * rows, 16), rows)

        def place(third):
            return pl.ds(pl.multiple_of((third * panels + panel) * 128, 128), 128)

        query, keys, values = (mixed[here, place(third)] for third in range(3))
        grad = grad_out[here, place(0)]
        turned = keys.T
        limit = limit_of(image)
        zero = jnp.zeros((rows, 128), F32)
        grad_query, grad_keys, grad_values = [], zero, zero
        for h, mask in enumerate(masks):
            masked_query = query * mask
            masked_grad = grad * mask
            probs = softmax_columns(dot_nt(keys, masked_query), limit)
            grad_probs = dot_nt(values, masked_grad)
            inner = jnp.sum(probs * grad_probs, axis=0, keepdims=True)
            grad_scores = (probs * (grad_probs - inner)).astype(BF16)
            grad_values = grad_values + dot(probs.astype(BF16), masked_grad)
            grad_keys = grad_keys + dot(grad_scores, masked_query)
            grad_query.append(dot(turned[h * size : h * size + size, :], grad_scores))
        grad_query = jnp.concatenate(grad_query, axis=0) * (1.0 / math.sqrt(size))
        grad_mixed[here, place(0)] = grad_query.astype(BF16).T
        grad_mixed[here, place(1)] = grad_keys.astype(BF16)
        grad_mixed[here, place(2)] = grad_values.astype(BF16)
        return carry

    lax.fori_loop(0, images * panels, body, 0, unroll=3)


def gelu_parts(value):
    bell = 0.5 * (1.0 + lax.erf(value * math.sqrt(0.5)))
    slope = bell + value * (jnp.exp(value * value * -0.5) * (1.0 / math.sqrt(2.0 * math.pi)))
    return value * bell, slope


class Shape:
    def __init__(self, images, rows, width, heads, hidden):
        self.images, self.rows, self.width = images, rows, width
        self.size = width // heads
        self.hidden = hidden
        self.count = images * rows


def block_forward(sh, x0, n1, mixed, o, x1, n2, g, gp, y, w, vec, limit_of, ready, saved):
    width, hidden, count = sh.width, sh.hidden, sh.count
    panels = width // 128
    norm_forward(x0, vec("g1"), vec("b1"), n1, count, width)
    saved(n1)
    ready("qkv")

    def put_mixed(start, here, there, value):
        scale = jnp.where(start < width, 1.0 / math.sqrt(sh.size), 1.0)
        mixed[here, there] = (value * scale).astype(BF16)

    times_columns(n1, w["qkv"], 3 * panels, width, put_mixed)
    saved(mixed)
    attention_forward(mixed, o, limit_of, sh.images, sh.rows, width, sh.size)
    saved(o)
    ready("proj")

    def put_sum(base, out):
        def finish(_, here, there, value):
            out[here, there] = base[here, there] + value

        return finish

    times_columns(o, w["proj"], panels, width, put_sum(x0, x1))
    saved(x1)
    norm_forward(x1, vec("g2"), vec("b2"), n2, count, width)
    saved(n2)
    ready("fc1")

    def put_hidden(_, here, there, value):
        value, slope = gelu_parts(value)
        g[here, there] = value.astype(BF16)
        gp[here, there] = slope

    times_columns(n2, w["fc1"], hidden // 128, width, put_hidden)
    saved(g)
    saved(gp)
    ready("fc2")
    times_columns(g, w["fc2"], panels, hidden, put_sum(x1, y))
    saved(y)


class Gradients:
    def __init__(self, plan, s, own, stage, sems, targets):
        self.plan, self.section, self.own = plan, plan.sections[s], own
        self.bins = plan.bins(s)
        self.stage, self.sems, self.targets = stage, sems, targets
        self.turn = 0
        self.flying = [[], []]

    def copy_out(self, source, block, side, unit, take, sem):
        which = max(i for i, (first, _) in enumerate(self.bins) if first <= block)
        block = block - self.bins[which][0]
        keep, send = self.targets[2 * which], self.targets[2 * which + 1]

        def to(target):
            return pltpu.make_async_copy(source, target.at[block, pl.ds(unit, take)], sem)

        @pl.when(self.own == side)
        def _():
            to(keep).start()

        @pl.when(self.own != side)
        def _():
            to(send).start()

        return to(keep)

    def drain(self, slot):
        for copy in self.flying[slot]:
            copy.wait()
        self.flying[slot] = []

    def weight(self, name, left, depth, right, turned):
        panels = self.section.panels[name]
        for band in range(depth // 256):
            slot = self.turn % 2
            self.turn += 1
            self.drain(slot)
            stage = self.stage.at[slot]
            turned[...] = left[:, band * 256 : band * 256 + 256].T

            def body(pair, carry):
                value = dot(turned[...], right[:, lanes(pair)])
                for i in range(2):
                    stage[pl.ds(2 * pair + i, 16, stride=panels)] = value[
                        :, i * 128 : i * 128 + 128
                    ].reshape(16, 16, 128)
                return carry

            lax.fori_loop(0, panels // 2, body, 0)
            for block, side, unit, at, take in self.section.runs(
                name, self.plan.half_cuts, band * 16, 16
            ):
                self.flying[slot].append(
                    self.copy_out(
                        stage.at[pl.ds(at, take)], block, side, unit, take, self.sems.at[slot]
                    )
                )

    def finish(self, values, scratch):
        vectors = self.section.vectors
        blocks = sorted({vectors[name][2] for name in values})
        for k, block in enumerate(blocks):
            scratch[k] = jnp.zeros((VEC_UNITS, 16, 128), F32)
            for name, (_, panels, at_block, at) in vectors.items():
                if at_block != block:
                    continue
                for panel in range(panels):
                    unit, row = divmod(at + panel, 16)
                    scratch[k, unit, row : row + 1, :] = values[name][
                        :, panel * 128 : panel * 128 + 128
                    ]
        unit = self.plan.vec_unit - self.plan.half
        copies = [
            self.copy_out(scratch.at[k], block, 1, unit, VEC_UNITS, self.sems.at[2])
            for k, block in enumerate(blocks)
        ]
        for copy in copies:
            copy.wait()
        self.drain(0)
        self.drain(1)


class Backward:
    def __init__(self, sh, w, vec, limit_of, grads, values, turned, ready):
        self.sh, self.w, self.vec, self.limit_of = sh, w, vec, limit_of
        self.grads, self.values, self.turned, self.ready = grads, values, turned, ready
        self.panels = sh.width // 128

    def round_stream(self, dy, dyb):
        def step(at):
            dyb[pl.ds(at, 16), :] = dy[pl.ds(at, 16), :].astype(BF16)

        for_rows(self.sh.count, 16, step, 4)

    def bands(self, left, name, count, put):
        times_bands(left, self.w[name], self.grads.section.panels[name], count, put)

    def through_norm(self, x, dn, dy, gain, shift, dn_is=None):
        def from_dn(at, size):
            return dn[pl.ds(at, size), :]

        def into_stream(at, size, value):
            dy[pl.ds(at, size), :] = dy[pl.ds(at, size), :] + value

        self.values[gain], self.values[shift] = norm_backward(
            x, self.vec(gain), from_dn, into_stream, self.sh.count, self.sh.width
        )

    def second_product(self, dy, dyb, g, gp):
        self.round_stream(dy, dyb)
        self.ready("fc2", g)
        self.grads.weight("fc2", g, self.sh.hidden, dyb, self.turned)
        self.ready(None, gp)

        def put(here, there, value):
            g[here, there] = (value * gp[here, there]).astype(BF16)

        self.bands(dyb, "fc2", self.sh.hidden, put)

    def first_product(self, dy, g, n2, x1, dn):
        def put(here, there, value):
            dn[here, there] = value

        self.ready("fc1", n2)
        self.grads.weight("fc1", n2, self.sh.width, g, self.turned)
        self.bands(g, "fc1", self.sh.width, put)
        self.ready(None, x1)
        self.through_norm(x1, dn, dy, "g2", "b2")

    def projection(self, dy, dyb, o, grad):
        sh = self.sh
        self.round_stream(dy, dyb)
        self.ready("proj", o)
        self.grads.weight("proj", o, sh.width, dyb, self.turned)

        def put(here, there, value):
            grad[here, there] = value.astype(BF16)

        self.bands(dyb, "proj", sh.width, put)

    def attention(self, grad, mixed, dmixed):
        sh = self.sh
        self.ready(None, grad)
        self.ready(None, mixed)
        attention_backward(mixed, grad, dmixed, self.limit_of, sh.images, sh.rows, sh.width, sh.size)

    def mixing(self, dy, dmixed, n1, x0, dn):
        def put(here, there, value):
            dn[here, there] = value

        self.ready("qkv", n1)
        self.grads.weight("qkv", n1, self.sh.width, dmixed, self.turned)
        self.bands(dmixed, "qkv", self.sh.width, put)
        self.ready(None, x0)
        self.through_norm(x0, dn, dy, "g1", "b1")


def held_at(plan, s, gathered, block, side, unit, take):
    if s == 0:
        return [(gathered[0].at[side, block, pl.ds(unit, take)], 0, take)]
    if block == plan.bins(1)[1][0]:
        return [(gathered[1].at[side, pl.ds(unit, take)], 0, take)]
    out = []
    quarter = plan.quarter
    if unit < quarter:
        few = min(take, quarter - unit)
        out.append((gathered[0].at[side, 2 * block, pl.ds(unit, few)], 0, few))
    if unit + take > quarter:
        skip = max(quarter - unit, 0)
        few = take - skip
        source = gathered[0].at[side, 2 * block + 1, pl.ds(unit + skip - quarter, few)]
        out.append((source, skip, few))
    return out


def load_vectors(plan, s, gathered, held, vec_ref, sem):
    section = plan.sections[s]
    blocks = sorted({v[2] for v in section.vectors.values()})
    copies = [
        pltpu.make_async_copy(source, held.at[k, pl.ds(skip, few)], sem)
        for k, block in enumerate(blocks)
        for source, skip, few in held_at(
            plan, s, gathered, block, 1, plan.vec_unit - plan.half, VEC_UNITS
        )
    ]
    for copy in copies:
        copy.start()
    names = {name: i for i, name in enumerate(section.vectors)}

    def finish():
        for copy in copies:
            copy.wait()
        for k, block in enumerate(blocks):
            rows = held[k].reshape(16 * VEC_UNITS, 128).astype(F32)
            for name, (_, panels, at_block, at) in section.vectors.items():
                if at_block != block:
                    continue
                i = names[name]
                for panel in range(panels):
                    vec_ref[i : i + 1, panel * 128 : panel * 128 + 128] = rows[
                        at + panel : at + panel + 1, :
                    ]
        return lambda name: vec_ref[names[name] : names[name] + 1, :]

    return finish


def load_weights(plan, s, gathered, w, sems):
    section = plan.sections[s]
    copies = {}
    for k, (name, ref) in enumerate(w.items()):
        panels = section.panels[name]
        flat = ref.reshape(ref.shape[0] * panels, 16, 128)
        copies[name] = [
            pltpu.make_async_copy(source, flat.at[pl.ds(at + skip, few)], sems.at[k])
            for block, side, unit, at, take in section.runs(name, plan.half_cuts)
            for source, skip, few in held_at(plan, s, gathered, block, side, unit, take)
        ]
        for copy in copies[name]:
            copy.start()

    def ready(name):
        for copy in copies.get(name, ()):
            copy.wait()

    return ready


def weight_scratch(layout, names):
    shapes = dict(layout)
    return [
        pltpu.VMEM((shapes[n][0] // GROUP, shapes[n][1] // 128, GROUP, 128), BF16)
        for n in names
    ]


def picks(perm_ref, image):
    here = pl.ds(pl.multiple_of(image * ROWS_D, 16), ROWS_D)
    patch = lax.broadcasted_iota(jnp.int32, (ROWS_D, ROWS_D), 1)
    return jnp.where(perm_ref[here, :] == patch, 1.0, 0.0).astype(BF16)


W_ENC = ["patch", "qkv", "proj", "fc1", "fc2"]


def encoder_kernel(plan, sh, refs):
    (info, gathered, patches, perm, pos, pp_out, x0_out, n1_out, mixed_out, o_out, x1_out, n2_out,
     g_out, gp_out, y_out, latent_out, w_patch, w_qkv, w_proj, w_fc1, w_fc2, held, vec_ref, pp, xe,
     x0, n1, mixed, o, x1, n2, g, gp, y, latent, w_sems, out_sems) = refs
    w = dict(zip(W_ENC, (w_patch, w_qkv, w_proj, w_fc1, w_fc2)))
    finish_vec = load_vectors(plan, 0, [gathered], held, vec_ref, w_sems.at[5])
    ready = load_weights(plan, 0, [gathered], w, w_sems)
    outs = []

    targets = [(pp, pp_out), (x0, x0_out), (n1, n1_out), (mixed, mixed_out), (o, o_out),
               (x1, x1_out), (n2, n2_out), (g, g_out), (gp, gp_out), (y, y_out),
               (latent, latent_out)]

    def saved(ref):
        for k, (source, target) in enumerate(targets):
            if source is ref:
                copy = pltpu.make_async_copy(source, target, out_sems.at[k])
                copy.start()
                outs.append(copy)

    def gather(image, carry):
        chosen = picks(perm, image)
        pp[image] = dot(chosen, patches[image]).astype(BF16)
        here = pl.ds(pl.multiple_of(image * ROWS_E, 16), ROWS_E)
        xe[here, :] = pp[image, 0:ROWS_E, :]
        few = chosen[0:ROWS_E, :]
        x0[here, :] = (dot(few, pos[0]) + dot(few, pos[1])) + dot(few, pos[2])
        return carry

    lax.fori_loop(0, sh.images, gather, 0)
    saved(pp)
    vec = finish_vec()
    ready("patch")

    def put(_, here, there, value):
        x0[here, there] = (value + vec_ref[0:1, there]) + x0[here, there]

    times_columns(xe, w["patch"], D // 128, PIX, put)
    saved(x0)
    block_forward(
        sh, x0, n1, mixed, o, x1, n2, g, gp, y, w, vec, lambda i: info[1 + i], ready, saved
    )
    norm_forward(y, vec("gf"), vec("bf"), latent, sh.count, D)
    saved(latent)
    for copy in outs:
        copy.wait()


def lasting(microseconds):
    return pl.CostEstimate(
        flops=int(microseconds * COST), bytes_accessed=1 << 20, transcendentals=0
    )


def saved_shapes(sh):
    count, width, hidden = sh.count, sh.width, sh.hidden
    return [
        ((count, width), F32),
        ((count, width), BF16),
        ((count, 3 * width), BF16),
        ((count, width), BF16),
        ((count, width), F32),
        ((count, width), BF16),
        ((count, hidden), BF16),
        ((count, hidden), F32),
        ((count, width), F32),
    ]


def encoder(plan, sh, info, gathered, patches, perm, pos):
    saved = saved_shapes(sh)
    pp_shape = ((sh.images, ROWS_D, PIX), BF16)
    latent_shape = ((sh.count, D), BF16)
    outs = [pp_shape, *saved, latent_shape]
    holders = len({v[2] for v in plan.sections[0].vectors.values()})
    return pl.pallas_call(
        lambda *refs: encoder_kernel(plan, sh, refs),
        out_shape=[jax.ShapeDtypeStruct(*s) for s in outs],
        in_specs=[IN_SMEM, ANY, IN_VMEM, IN_VMEM, IN_VMEM],
        out_specs=[ANY] * len(outs),
        scratch_shapes=[
            *weight_scratch(ENC, W_ENC),
            pltpu.VMEM((holders, VEC_UNITS, 16, 128), BF16),
            pltpu.VMEM((8, D), F32),
            pltpu.VMEM(*pp_shape),
            pltpu.VMEM((sh.count, PIX), BF16),
            *[pltpu.VMEM(*s) for s in saved],
            pltpu.VMEM(*latent_shape),
            pltpu.SemaphoreType.DMA((6,)),
            pltpu.SemaphoreType.DMA((len(outs),)),
        ],
        compiler_params=pltpu.CompilerParams(vmem_limit_bytes=VMEM_BYTES),
        cost_estimate=lasting(50),
        name="encoder_forward",
    )(info, gathered, patches, perm, pos)


W_DEC = ["embed", "qkv", "proj", "fc1", "fc2", "head"]


def decoder_kernel(plan, sh, refs):
    info, scale, gathered, gathered_tail, latent_in, pp_in, perm, pos = refs[:8]
    gathered = [gathered, gathered_tail]
    targets, refs = refs[8:12], refs[12:]
    (grad_latent, loss_out,
     w_embed, w_qkv, w_proj, w_fc1, w_fc2, w_head, held, vec_ref, pp, latent, embedded, x0, n1,
     mixed, o, x1, n2, g, gp, y, f, dn, guess, turned, turned_e, stage, vec_stage, w_sems,
     in_sems, grad_sems) = refs
    w = dict(zip(W_DEC, (w_embed, w_qkv, w_proj, w_fc1, w_fc2, w_head)))
    copy_latent = pltpu.make_async_copy(latent_in, latent, in_sems.at[0])
    copy_pp = pltpu.make_async_copy(pp_in, pp, in_sems.at[1])
    copy_latent.start()
    finish_vec = load_vectors(plan, 1, gathered, held, vec_ref, w_sems.at[6])
    ready = load_weights(plan, 1, gathered, w, w_sems)
    copy_pp.start()
    images, count = sh.images, sh.count
    count_e = images * ROWS_E
    vec = finish_vec()
    copy_latent.wait()
    ready("embed")

    def put_embedded(_, here, there, value):
        embedded[here, there] = value

    times_columns(latent, w["embed"], DD // 128, D, put_embedded)

    def tokens(image, carry):
        chosen = picks(perm, image)
        place = (dot(chosen, pos[0]) + dot(chosen, pos[1])) + dot(chosen, pos[2])
        start = pl.multiple_of(image * ROWS_D, 16)
        kept = info[1 + image]
        token = vec_ref[0:1, :]
        few = embedded[pl.ds(pl.multiple_of(image * ROWS_E, 16), ROWS_E), :]
        rank = lax.broadcasted_iota(jnp.int32, (ROWS_E, DD), 0)
        x0[pl.ds(start, ROWS_E), :] = jnp.where(rank < kept, few, token) + place[:ROWS_E, :]
        x0[pl.ds(start + ROWS_E, ROWS_D - ROWS_E), :] = token + place[ROWS_E:, :]
        return carry

    lax.fori_loop(0, images, tokens, 0)
    block_forward(
        sh, x0, n1, mixed, o, x1, n2, g, gp, y, w, vec, lambda i: NP, ready, lambda ref: None
    )
    norm_forward(y, vec("gf"), vec("bf"), f, count, DD)
    ready("head")
    copy_pp.wait()
    factor = scale[0]

    def predict_image(image, total):
        start = pl.multiple_of(image * ROWS_D, 16)
        kept = info[1 + image]
        here = pl.ds(start, ROWS_D)
        for pair in range(PIX // 256):
            guess[:, pair * 256 : pair * 256 + 256] = dot(
                f[here, :], columns(w["head"], DD, 2 * pair, 2)
            )

        target, _ = norm_rows(pp[image].astype(F32), PIX)
        off = guess[...] - target
        rank = lax.broadcasted_iota(jnp.int32, (ROWS_D, 1), 0)
        off = jnp.where((rank >= kept) & (rank < NP), off, 0.0)
        pp[image] = (off * factor).astype(BF16)
        return total + jnp.sum((off * off).reshape(ROWS_D // 8, 8, PIX), axis=0)

    total = lax.fori_loop(0, images, predict_image, jnp.zeros((8, PIX), F32))
    total = jnp.sum(jnp.sum(total, axis=0, keepdims=True), axis=1, keepdims=True)
    loss_out[...] = jnp.broadcast_to(total * (1.0 / PIX), (8, 128))

    grads = Gradients(plan, 1, info[0], stage, grad_sems, targets)
    values = {}
    back = Backward(
        sh, w, vec, lambda i: NP, grads, values, turned, lambda name, ref: None
    )
    dpred = pp.reshape(count, PIX)
    grads.weight("head", f, DD, dpred, turned)

    def put_dn(here, there, value):
        dn[here, there] = value

    back.bands(dpred, "head", DD, put_dn)

    def from_dn(at, size):
        return dn[pl.ds(at, size), :]

    def put_y(at, size, value):
        y[pl.ds(at, size), :] = value

    values["gf"], values["bf"] = norm_backward(y, vec("gf"), from_dn, put_y, count, DD)
    back.second_product(y, f, g, gp)
    back.first_product(y, g, n2, x1, dn)
    dmixed = g.at[:, pl.ds(0, 3 * DD)]
    back.projection(y, f, o, o)
    back.attention(o, mixed, dmixed)
    back.mixing(y, dmixed, n1, x0, dn)

    def split(image, total):
        start = pl.multiple_of(image * ROWS_D, 16)
        kept = info[1 + image]

        grad = y[pl.ds(start, ROWS_D), :]
        rank = lax.broadcasted_iota(jnp.int32, (ROWS_D, 1), 0)
        few = pl.ds(pl.multiple_of(image * ROWS_E, 16), ROWS_E)
        taken = jnp.where(rank[:ROWS_E] < kept, grad[:ROWS_E], 0.0)
        n1[few, :] = taken.astype(BF16)
        free = jnp.where(rank >= kept, grad, 0.0)
        return total + jnp.sum(free.reshape(ROWS_D // 8, 8, DD), axis=0)

    total = lax.fori_loop(0, images, split, jnp.zeros((8, DD), F32))
    values["mask"] = jnp.sum(total, axis=0, keepdims=True)
    placed = n1.at[pl.ds(0, count_e)]
    grads.weight("embed", latent, D, placed, turned_e)

    def put_latent(here, there, value):
        grad_latent[here, there] = value.astype(BF16)

    times_bands(placed, w["embed"], DD // 128, D, put_latent)
    grads.finish(values, vec_stage)


def grad_shapes(plan, s):
    return [
        jax.ShapeDtypeStruct((count, units, 16, 128), F32)
        for (_, count), units in zip(plan.bins(s), plan.bin_units(s))
        for _ in range(2)
    ]


def decoder(plan, sh, info, scale, gathered, latent, pp, perm, pos):
    count_e = sh.images * ROWS_E
    holders = len({v[2] for v in plan.sections[1].vectors.values()})
    saved = saved_shapes(sh)
    most = max(plan.sections[1].panels.values())
    return pl.pallas_call(
        lambda *refs: decoder_kernel(plan, sh, refs),
        out_shape=[
            *grad_shapes(plan, 1),
            jax.ShapeDtypeStruct((count_e, D), BF16),
            jax.ShapeDtypeStruct((8, 128), F32),
        ],
        in_specs=[IN_SMEM, IN_SMEM, ANY, ANY, ANY, ANY, IN_VMEM, IN_VMEM],
        out_specs=[*[ANY] * 4, IN_VMEM, IN_VMEM],
        scratch_shapes=[
            *weight_scratch(DEC, W_DEC),
            pltpu.VMEM((holders, VEC_UNITS, 16, 128), BF16),
            pltpu.VMEM((8, DD), F32),
            pltpu.VMEM((sh.images, ROWS_D, PIX), BF16),
            pltpu.VMEM((count_e, D), BF16),
            pltpu.VMEM((count_e, DD), F32),
            *[pltpu.VMEM(*s) for s in saved],
            pltpu.VMEM((sh.count, DD), BF16),
            pltpu.VMEM((sh.count, DD), F32),
            pltpu.VMEM((ROWS_D, PIX), F32),
            pltpu.VMEM((256, sh.count), BF16),
            pltpu.VMEM((256, count_e), BF16),
            pltpu.VMEM((2, 16 * most, 16, 128), F32),
            pltpu.VMEM((holders, VEC_UNITS, 16, 128), F32),
            pltpu.SemaphoreType.DMA((7,)),
            pltpu.SemaphoreType.DMA((2,)),
            pltpu.SemaphoreType.DMA((3,)),
        ],
        compiler_params=pltpu.CompilerParams(vmem_limit_bytes=VMEM_BYTES),
        cost_estimate=lasting(160),
        name="decoder_both",
    )(info, scale, *gathered, latent, pp, perm, pos)


class Stage:
    def __init__(self, plan, sh, weights, reads, temps, outs, most, cost, name, body, bins=2):
        self.plan, self.sh, self.weights, self.reads = plan, sh, weights, reads
        self.temps, self.outs, self.most, self.cost, self.name = temps, outs, most, cost, name
        self.body = body
        self.bins = bins

    def kernel(self, blocks, *refs):
        refs = list(refs)

        def take(count):
            got = refs[:count]
            del refs[:count]
            return got

        plan, sh = self.plan, self.sh
        info, gathered = take(2)
        sources = dict(zip(self.reads, take(len(self.reads))))
        take(blocks)
        targets = take(2 * self.bins)
        results = dict(zip(self.outs, take(len(self.outs))))
        w = dict(zip(self.weights, take(len(self.weights))))
        here = dict(zip(self.reads, take(len(self.reads))))
        temps = dict(zip(self.temps, take(len(self.temps))))
        held, vec_ref, turned, stage, vec_stage, w_sems, in_sems, grad_sems = refs
        finish_vec = load_vectors(plan, 0, [gathered], held, vec_ref, w_sems.at[len(w)])
        loads = {}
        for k, (name, ref) in enumerate(here.items()):
            if name == "xe":
                copies = [
                    pltpu.make_async_copy(
                        sources[name].at[i, pl.ds(0, ROWS_E)],
                        ref.at[pl.ds(i * ROWS_E, ROWS_E)],
                        in_sems.at[k],
                    )
                    for i in range(sh.images)
                ]
            else:
                copies = [pltpu.make_async_copy(sources[name], ref, in_sems.at[k])]
            for copy in copies:
                copy.start()
            loads[id(ref)] = copies
        weights_ready = load_weights(plan, 0, [gathered], w, w_sems)
        vec = finish_vec()

        def ready(name, ref=None):
            for copy in loads.pop(id(ref), ()):
                copy.wait()
            if name is not None:
                weights_ready(name)

        values = {}
        grads = Gradients(plan, 0, info[0], stage, grad_sems, targets)
        back = Backward(
            sh, w, vec, lambda i: info[1 + i], grads, values, turned, ready
        )
        back.out_sem = in_sems.at[len(self.reads)]
        self.body(back, {**here, **temps}, results)
        assert not loads
        grads.finish(values, vec_stage)

    def __call__(self, info, gathered, arrays, blocks):
        plan, sh = self.plan, self.sh
        count, width, hidden = sh.count, sh.width, sh.hidden
        known = {
            "dz": ((count, width), BF16),
            "y": ((count, width), F32),
            "dy": ((count, width), F32),
            "x0": ((count, width), F32),
            "x1": ((count, width), F32),
            "dn": ((count, width), F32),
            "n1": ((count, width), BF16),
            "n2": ((count, width), BF16),
            "o": ((count, width), BF16),
            "dyb": ((count, width), BF16),
            "do": ((count, width), BF16),
            "xe": ((count, PIX), BF16),
            "mixed": ((count, 3 * width), BF16),
            "dmixed": ((count, 3 * width), BF16),
            "g": ((count, hidden), BF16),
            "gp": ((count, hidden), F32),
        }
        holders = len({v[2] for v in plan.sections[0].vectors.values()})
        targets = grad_shapes(plan, 0)[: 2 * self.bins]
        before = 2 + len(self.reads)
        got = pl.pallas_call(
            functools.partial(self.kernel, len(blocks)),
            out_shape=[*targets, *[jax.ShapeDtypeStruct(*known[n]) for n in self.outs]],
            in_specs=[IN_SMEM, *[ANY] * (1 + len(self.reads) + len(blocks))],
            out_specs=[*[ANY] * len(targets), *[ANY if n == "g" else IN_VMEM for n in self.outs]],
            input_output_aliases={before + i: i for i in range(len(blocks))},
            scratch_shapes=[
                *weight_scratch(ENC, self.weights),
                *[pltpu.VMEM(*known[n]) for n in self.reads],
                *[pltpu.VMEM(*known[n]) for n in self.temps],
                pltpu.VMEM((holders, VEC_UNITS, 16, 128), BF16),
                pltpu.VMEM((8, D), F32),
                pltpu.VMEM((256, count), BF16),
                pltpu.VMEM((2, 16 * self.most, 16, 128), F32),
                pltpu.VMEM((holders, VEC_UNITS, 16, 128), F32),
                pltpu.SemaphoreType.DMA((len(self.weights) + 1,)),
                pltpu.SemaphoreType.DMA((len(self.reads) + 1,)),
                pltpu.SemaphoreType.DMA((3,)),
            ],
            compiler_params=pltpu.CompilerParams(vmem_limit_bytes=VMEM_BYTES),
            cost_estimate=lasting(self.cost),
            name=self.name,
        )(info, gathered, *[arrays[n] for n in self.reads], *blocks)
        return got[: len(targets)], dict(zip(self.outs, got[len(targets) :]))


def back_second(back, r, out):
    sh = back.sh
    back.ready(None, r["dz"])
    back.ready(None, r["y"])

    def from_latent(at, size):
        return r["dz"][pl.ds(at, size), :].astype(F32)

    def put(at, size, value):
        out["dy"][pl.ds(at, size), :] = value

    back.values["gf"], back.values["bf"] = norm_backward(
        r["y"], back.vec("gf"), from_latent, put, sh.count, D
    )
    back.second_product(out["dy"], r["dyb"], r["g"], r["gp"])
    copy = pltpu.make_async_copy(r["g"], out["g"], back.out_sem)
    copy.start()
    back.grads.drain(0)
    back.grads.drain(1)
    copy.wait()


def copy_rows(count, source, target):
    def step(at):
        target[pl.ds(at, 16), :] = source[pl.ds(at, 16), :]

    for_rows(count, 16, step, 4)


def back_first(back, r, out):
    back.ready(None, r["dy"])
    back.ready(None, r["g"])
    copy_rows(back.sh.count, r["dy"], out["dy"])
    back.first_product(out["dy"], r["g"], r["n2"], r["x1"], r["dn"])


def back_projection(back, r, out):
    back.ready(None, r["dy"])
    back.projection(r["dy"], r["dyb"], r["o"], out["do"])


def back_attention(back, r, out):
    back.attention(r["do"], r["mixed"], out["dmixed"])


def back_mixing(back, r, out):
    back.ready(None, r["dy"])
    back.ready(None, r["dmixed"])
    back.mixing(r["dy"], r["dmixed"], r["n1"], r["x0"], r["dn"])

    def body(i, total):
        at = pl.multiple_of(i * 16, 16)
        grad = r["dy"][pl.ds(at, 16), :]
        r["dyb"][pl.ds(at, 16), :] = grad.astype(BF16)
        return total + jnp.sum(grad.reshape(2, 8, D), axis=0)

    total = lax.fori_loop(0, back.sh.count // 16, body, jnp.zeros((8, D), F32))
    back.values["patch_b"] = jnp.sum(total, axis=0, keepdims=True)
    back.ready(None, r["xe"])
    back.grads.weight("patch", r["xe"], PIX, r["dyb"], back.turned)


def encoder_back_stages(plan, sh):
    most = {n: plan.sections[0].panels[n] for n in ("fc1", "fc2", "qkv", "proj")}
    return [
        Stage(plan, sh, ["fc2"], ["y", "dz", "g", "gp"], ["dyb"], ["dy", "g"], most["fc2"], 25,
              "encoder_back_fc2", back_second),
        Stage(plan, sh, ["fc1"], ["g", "dy", "n2", "x1"], ["dn"], ["dy"], most["fc1"], 20,
              "encoder_back_fc1", back_first),
        Stage(plan, sh, ["proj"], ["dy", "o"], ["dyb"], ["do"], most["proj"], 10,
              "encoder_back_proj", back_projection, 1),
        Stage(plan, sh, [], ["do", "mixed"], [], ["dmixed"], 1, 25,
              "encoder_back_attention", back_attention, 0),
        Stage(plan, sh, ["qkv"], ["dy", "dmixed", "n1", "x0", "xe"], ["dn", "dyb"], [],
              most["qkv"], 25, "encoder_back_qkv", back_mixing, 1),
    ]


def pick(value, index, axis):
    return lax.dynamic_index_in_dim(value, index, axis, keepdims=False)


def tie(*trees):
    return lax.optimization_barrier(trees)


class Term:
    def __init__(self, base, bits, first, last, fixed=()):
        self.base, self.bits, self.first, self.last = base, bits, first, last
        self.fixed = dict(fixed)

    def at(self, bit, index):
        return Term(self.base, self.bits, self.first, self.last, {**self.fixed, bit: index})

    def value(self):
        zero = jnp.zeros((), jnp.int32)
        starts = [self.fixed.get(b, zero).astype(jnp.int32) for b in self.bits]
        sizes = [1 if b in self.fixed else 2 for b in self.bits]
        left = [n for n in sizes if n == 2]
        starts += [jnp.full((), self.first, jnp.int32), zero, zero]
        count = self.last - self.first
        out = lax.dynamic_slice(self.base, starts, [*sizes, count, 16, 128])
        return out.reshape(*left, count, 16, 128)


def sum_of(terms):
    return total_of([term.value() for term in terms])


class Flow:
    def __init__(self, dp, keep, send, first, shares=(1, 1, 1)):
        parts = len(shares)
        self.dp = dp
        self.me = lax.axis_index("dp")
        self.keep, self.given = keep, send
        count, units = keep.shape[:2]
        self.bits = count.bit_length() - 1
        assert count == 1 << self.bits and dp & (dp - 1) == 0
        self.all_bits = dp.bit_length() - 1
        self.first = first
        low = list(range(self.bits))
        if dp == 64:
            low = [b for b in (0, 2, 4, 1, 3) if b < self.bits]
        turn = max(min(3, len(low)), 1)
        self.cuts = [units * sum(shares[:p]) // sum(shares) for p in range(parts + 1)]
        self.orders = [low[p % turn : turn] + low[: p % turn] + low[turn:] for p in range(parts)]
        self.step = -1
        self.terms = None

    def done(self):
        return self.step == self.all_bits

    def last(self):
        return self.step == self.all_bits - 1

    def payload(self):
        if self.step < 0:
            return [self.given]
        if self.step >= self.bits:
            return [self.result()]
        out = []
        for terms, order in zip(self.terms, self.orders):
            bit = order[self.step]
            other = 1 - (self.me >> bit & 1)
            out.append(sum_of([t.at(bit, other) for t in terms]))
        return out

    def send(self, payload):
        if self.step < 0:
            return [lax.ppermute(payload[0], "section", [(0, 1), (1, 0)])]
        if self.step >= self.bits:
            flip = 1 << self.step
            pairs = [(i, i ^ flip) for i in range(self.dp) if (i ^ self.first) & flip]
            return [lax.ppermute(payload[0], "dp", pairs)]
        out = []
        for value, order in zip(payload, self.orders):
            flip = 1 << order[self.step]
            out.append(lax.ppermute(value, "dp", [(i, i ^ flip) for i in range(self.dp)]))
        return out

    def take(self, got):
        ranges = list(zip(self.cuts[:-1], self.cuts[1:]))
        if self.step < 0:
            bits = list(range(self.bits - 1, -1, -1))
            shape = (2,) * self.bits + self.keep.shape[1:]
            self.terms = [
                [Term(v.reshape(shape), bits, *r) for v in (self.keep, got[0])] for r in ranges
            ]
        elif self.step < self.bits:
            for k, (order, value) in enumerate(zip(self.orders, got)):
                bit = order[self.step]
                mine = self.me >> bit & 1
                gone = order[: self.step + 1]
                bits = [b for b in range(self.bits - 1, -1, -1) if b not in gone]
                self.terms[k] = [t.at(bit, mine) for t in self.terms[k]]
                self.terms[k].append(Term(value, bits, 0, value.shape[-3]))
        else:
            for k, r in enumerate(ranges):
                self.terms[k].append(Term(got[0], [], *r))
        self.step += 1

    def result(self):
        return jnp.concatenate([sum_of(t) for t in self.terms], axis=0)


def move_on(flows, *others):
    flows = [f for f in flows if f is not None and not f.done()]
    payloads, others = tie([f.payload() for f in flows], others)
    return flows, [f.send(p) for f, p in zip(flows, payloads)], others


def arrive(flows, got):
    for flow, values in zip(flows, got):
        flow.take(values)


def sum_in_chip(value):
    return value + lax.ppermute(value, "section", [(0, 1), (1, 0)])


def sum_over_dp(dp, value, low):
    bits = dp.bit_length() - 1
    got = [
        lax.ppermute(value, "dp", [(i, i ^ (flip << low)) for i in range(dp)])
        for flip in range(1, 1 << min(2, bits - low))
    ]
    value = value + got[0]
    if len(got) == 3:
        value = value + (got[1] + got[2])
    return value


def sum_everywhere(dp, value):
    value = sum_in_chip(value)
    for low in range(0, dp.bit_length() - 1, 2):
        value = sum_over_dp(dp, value, low)
    return value


def squares_of(plan, s, value, section, me):
    section_plan = plan.sections[s]
    vectors = np.zeros((plan.dp,), np.int32)
    for _, panels, block, at in section_plan.vectors.values():
        vectors[block] = max(vectors[block], at + panels)
    filled = jnp.asarray(np.asarray(section_plan.fill, np.int32) * 16)[me]
    vectors = jnp.asarray(vectors)[me]
    shape = value.shape
    row = lax.broadcasted_iota(jnp.int32, shape, 0) * 16 + lax.broadcasted_iota(jnp.int32, shape, 1)
    row = row + section * (plan.half * 16)
    extra = row - plan.vec_unit * 16
    valid = (row < filled) | ((extra >= 0) & (extra < vectors))
    return jnp.sum(jnp.where(valid, value * value, 0.0))


def gather_decoder(plan, half_d, section, me, after):
    dp, quarter = plan.dp, plan.quarter
    first = plan.bins(1)[1][0]
    assert 2 * first == dp
    used = max(plan.tail_used())
    spread = jnp.pad(half_d, ((0, 2 * quarter - plan.half), (0, 0), (0, 0)))
    spread = total_of(
        [
            lax.ppermute(
                spread[i * quarter : (i + 1) * quarter],
                "dp",
                [(b, 2 * b + i) for b in range(first)],
            )
            for i in range(2)
        ]
    )
    rest = jnp.where(me == first, half_d[:used], jnp.zeros((), BF16))
    holders = [first]
    for bit in reversed(range(dp.bit_length() - 1)):
        rest = rest + lax.ppermute(rest, "dp", [(i, i ^ 1 << bit) for i in holders])
        holders = holders + [i ^ 1 << bit for i in holders]
    other = lax.ppermute(rest, "section", [(0, 1), (1, 0)])
    rest = jnp.where(section == 0, jnp.stack([rest, other]), jnp.stack([other, rest]))
    spread, _ = tie(spread, after[0, 0, 0])
    gathered = lax.all_gather(spread, ("section", "dp"), axis=0, tiled=True)
    return gathered.reshape(2, dp, quarter, 16, 128), rest


def sincos(width):
    places = np.arange(NP).astype(np.float32)[:, None]
    column = np.arange(width)
    rates = np.exp(
        -(np.float32(2.0) * (column // 2).astype(np.float32) / np.float32(width))
        * np.float32(math.log(10000.0))
    ).astype(np.float32)
    phases = (places * rates[None, :]).astype(np.float32)
    table = np.where(
        column[None, :] % 2 == 0, np.sin(phases.astype(np.float64)), np.cos(phases.astype(np.float64))
    ).astype(np.float32)
    parts = []
    left = np.zeros((ROWS_D, width), np.float32)
    left[:NP] = table
    for _ in range(3):
        high = left.astype(jnp.bfloat16)
        parts.append(high)
        left = left - high.astype(np.float32)
    return np.stack(parts)


def on_device(patches, keep, perm, master, first, second, ema):
    dp = lax.axis_size("dp")
    section = lax.axis_index("section")
    me = lax.axis_index("dp")
    shard = master.shape[1]
    plan = Plan(dp, shard // 128)
    rows, half = plan.shard_rows, plan.half
    swap = [(0, 1), (1, 0)]
    states = [v.reshape(rows, 1, 128) for v in (master, first, second, ema)]

    following = lax.ppermute(
        states[0][: plan.head_rows], "dp", [(i, i - 1) for i in range(1, dp)]
    )
    index = jnp.asarray(plan.pack_index)[section, me]
    packed = pack(plan, index, states[0], following)
    mine = lax.dynamic_slice_in_dim(packed, section * half, half, 0)
    given = lax.ppermute(
        lax.dynamic_slice_in_dim(packed, (1 - section) * half, half, 0), "section", swap
    )
    half_e = jnp.where(section == 0, mine, given)
    half_d = jnp.where(section == 0, given, mine)
    gathered_e = lax.all_gather(half_e, ("section", "dp"), axis=0, tiled=True)
    gathered_e = gathered_e.reshape(2, dp, half, 16, 128)
    gathered_d = gather_decoder(plan, half_d, section, me, gathered_e)

    count = sum_everywhere(dp, jnp.sum(NP - keep).astype(F32)) * 0.5
    images = patches.shape[0] // 2
    mine = section * images
    patches = lax.dynamic_slice_in_dim(patches, mine, images, 0)
    patches = jnp.pad(patches, ((0, 0), (0, ROWS_D - NP), (0, 0)))
    order = lax.dynamic_slice_in_dim(perm, mine, images, 0)
    order = jnp.pad(order, ((0, 0), (0, ROWS_D - NP)), constant_values=ROWS_D - 1)
    order = order.reshape(images * ROWS_D, 1)
    kept = lax.dynamic_slice_in_dim(keep, mine, images, 0)
    info = jnp.concatenate([section[None].astype(jnp.int32), kept])
    scale = ((1.0 / count) * (1.0 / PIX) * 2.0).reshape(1)

    shape_e = Shape(images, ROWS_E, D, HEADS_E, FF_E)
    shape_d = Shape(images, ROWS_D, DD, HEADS_D, FF_D)
    pp, *saved, latent = encoder(
        plan, shape_e, info, gathered_e, patches, order, jnp.asarray(sincos(D))
    )
    arrays = dict(zip(("x0", "n1", "mixed", "o", "x1", "n2", "g", "gp", "y"), saved))
    arrays["xe"] = pp
    *sums_d, arrays["dz"], loss = decoder(
        plan, shape_d, info, scale, gathered_d, latent, pp, order, jnp.asarray(sincos(DD))
    )

    stages = encoder_back_stages(plan, shape_e)
    first_tail = plan.bins(1)[1][0]
    main = Flow(dp, sums_d[0], sums_d[1], 0)
    rest = Flow(dp, sums_d[2], sums_d[3], first_tail, (1,))
    flows, got, _ = move_on([main, rest])
    got, arrays = tie(got, arrays)
    arrive(flows, got)
    low = high = None
    blocks = []
    late = []
    for number, stage in enumerate(stages):
        few = None if number in (0, 3) else rest
        flows, got, (arrays, blocks) = move_on([main, few, high], arrays, blocks)
        if stage.bins:
            blocks, made = stage(info, gathered_e, arrays, blocks)
        else:
            _, made = stage(info, gathered_e, arrays, [])
        arrays = {**arrays, **made}
        long = [f is main and f.last() for f in flows]
        kept = [g for g, is_long in zip(got, long) if not is_long]
        kept, late, arrays, blocks = tie(kept, late, arrays, blocks)
        late = [g for g, is_long in zip(got, long) if is_long]
        kept = iter(kept)
        arrive(flows, [g if is_long else next(kept) for g, is_long in zip(got, long)])
        if number == 1:
            high = Flow(dp, blocks[2], blocks[3], dp // 2, (4, 4, 2))
            blocks = blocks[:2]
    low = Flow(dp, blocks[0], blocks[1], 0)
    every = [main, rest, high, low]
    before = ()
    for turn in range(1 + max(f.all_bits - f.step for f in every)):
        flows, got, _ = move_on(every, before if turn == 1 else ())
        before = got
        arrive(flows, got)
    assert all(f.done() for f in every)

    sum_tail = rest.result()
    sum_tail = jnp.pad(sum_tail, ((0, half - sum_tail.shape[0]), (0, 0), (0, 0)))
    sum_d = jnp.where(me < first_tail, main.result(), sum_tail)
    sum_e = jnp.where(me < dp // 2, low.result(), high.result())
    squares = [
        squares_of(plan, s, v, section, me) for s, v in enumerate((sum_e, sum_d))
    ]
    half_mine = jnp.where(section == 0, sum_e, sum_d)
    half_other = lax.ppermute(jnp.where(section == 0, sum_d, sum_e), "section", swap)
    sums = sum_in_chip(jnp.stack([squares[0] + squares[1], loss[0, 0]]))
    sums, half_other = tie(sums, half_other)
    sums = sum_over_dp(dp, sums, 0)
    block = jnp.where(
        section == 0,
        jnp.concatenate([half_mine, half_other], axis=0),
        jnp.concatenate([half_other, half_mine], axis=0),
    )
    start = jnp.asarray(plan.tail_start)[section, me]
    tail = jnp.concatenate(
        [
            lax.dynamic_slice_in_dim(block, start, plan.tail_units, 0),
            block[plan.vec_unit :],
        ],
        axis=0,
    )
    sums, tail = tie(sums, tail)
    tail = lax.ppermute(tail, "dp", [(i, i + 1) for i in range(dp - 1)])
    for low in range(2, dp.bit_length() - 1, 2):
        sums = sum_over_dp(dp, sums, low)
    index = jnp.asarray(plan.unpack_index)[section, me]
    total = unpack(plan, index, block, tail)
    norm = jnp.sqrt(sums[0])
    factor = jnp.minimum(1.0, clip_limit / (norm + norm_epsilon))
    made = update(plan, factor.reshape(1), total, states)
    return (*[v.reshape(1, shard) for v in made], norm, sums[1], count)


def solution(mesh):
    return jax.shard_map(
        on_device,
        mesh=mesh,
        in_specs=(
            P("dp", None, None),
            P("dp"),
            P("dp", None),
            P("section", "dp"),
            P("section", "dp"),
            P("section", "dp"),
            P("section", "dp"),
        ),
        out_specs=(
            P("section", "dp"),
            P("section", "dp"),
            P("section", "dp"),
            P("section", "dp"),
            P(),
            P(),
            P(),
        ),
        check_vma=False,
    )
```

```python
import functools
import math

import jax
import jax.numpy as jnp
import numpy as np
from jax import lax
from jax.experimental import pallas as pl
from jax.experimental.pallas import tpu as pltpu
from jax.sharding import PartitionSpec as P

D = 768
HEADS_E = 12
FF_E = 3072
DD = 512
HEADS_D = 16
FF_D = 2048
PIX = 768
NP = 196
SLOTS = 98
STEP = 10

norm_epsilon = 1e-06
clip_limit = 0.01
learn_rate = 0.02
beta_one = 0.9
beta_two = 0.999
adam_epsilon = 1e-08
weight_decay = 0.05
average_keep = 0.8

F32 = jnp.float32
BF16 = jnp.bfloat16
ROWS_E = 112
ROWS_D = 208
GROUP = 16
VEC_UNITS = 2
VMEM_BYTES = 60 * 1024 * 1024
COST = 2e8
ANY = pl.BlockSpec(memory_space=pl.ANY)
IN_VMEM = pl.BlockSpec(memory_space=pltpu.VMEM)
IN_SMEM = pl.BlockSpec(memory_space=pltpu.SMEM)

ENC = [
    ("patch", (PIX, D)),
    ("patch_b", (D,)),
    ("g1", (D,)),
    ("b1", (D,)),
    ("qkv", (D, 3 * D)),
    ("proj", (D, D)),
    ("g2", (D,)),
    ("b2", (D,)),
    ("fc1", (D, FF_E)),
    ("fc2", (FF_E, D)),
    ("gf", (D,)),
    ("bf", (D,)),
]
DEC = [
    ("embed", (D, DD)),
    ("mask", (DD,)),
    ("g1", (DD,)),
    ("b1", (DD,)),
    ("qkv", (DD, 3 * DD)),
    ("proj", (DD, DD)),
    ("g2", (DD,)),
    ("b2", (DD,)),
    ("fc1", (DD, FF_D)),
    ("fc2", (FF_D, DD)),
    ("gf", (DD,)),
    ("bf", (DD,)),
    ("head", (DD, PIX)),
]


class Section:
    def __init__(self, layout, dp, shard_rows):
        self.dp = dp
        self.shard_rows = shard_rows
        self.groups = []
        self.vectors = {}
        self.panels = {}
        fill = [0] * dp
        vector_fill = [0] * dp
        row = 0
        for name, shape in layout:
            panels = shape[-1] // 128
            self.panels[name] = panels
            if len(shape) == 2:
                for group in range(shape[0] // GROUP):
                    block = row // shard_rows
                    self.groups.append((name, group, row, panels, block, fill[block]))
                    fill[block] += panels
                    row += GROUP * panels
            else:
                block = row // shard_rows
                self.vectors[name] = (row, panels, block, vector_fill[block])
                vector_fill[block] += panels
                row += panels
        self.rows = row
        self.fill = fill
        assert max(vector_fill) <= 16 * VEC_UNITS
        self.blocks_used = max(b for b in range(dp) if fill[b] or vector_fill[b]) + 1

    def pieces(self, name, first=0, count=None):
        out = []
        for tensor, group, _, panels, block, unit in self.groups:
            if tensor != name or group < first or (count is not None and group >= first + count):
                continue
            if out and out[-1][0] == block and out[-1][1] + out[-1][3] * panels == unit:
                out[-1][3] += 1
            else:
                out.append([block, unit, group, 1])
        return [tuple(p) for p in out]

    def runs(self, name, cuts, first=0, count=None):
        panels = self.panels[name]
        out = []
        for block, unit, group, groups in self.pieces(name, first, count):
            at, left = (group - first) * panels, groups * panels
            while left:
                place = max(i for i in range(len(cuts) - 1) if cuts[i] <= unit)
                take = min(left, cuts[place + 1] - unit)
                out.append((block, place, unit - cuts[place], at, take))
                unit, at, left = unit + take, at + take, left - take
        return out


class Plan:
    def __init__(self, dp, shard_rows):
        self.dp = dp
        self.shard_rows = shard_rows
        self.sections = [Section(ENC, dp, shard_rows), Section(DEC, dp, shard_rows)]
        units = max(max(s.fill) for s in self.sections)
        units += (units + VEC_UNITS) % 2
        self.vec_unit = units
        self.units = units + VEC_UNITS
        self.half = self.units // 2
        half = self.half
        self.quarter = -(-half // 2)
        self.part_cuts = [0, -(-half // 3), -(-2 * half // 3), half]
        self.half_cuts = [0, half, self.units]
        self.head_rows = 8 * -(-max(16 * max(s.panels.values()) for s in self.sections) // 8)
        self.tail_units = max(max(s.panels.values()) for s in self.sections)
        self.pack_base = 8 * -(-shard_rows // 8)
        self.pack_rows = shard_rows + self.head_rows
        self.pack_index = np.zeros((2, dp, self.units * 16), np.int32)
        self.tail_rows = 16 * (self.tail_units + VEC_UNITS)
        self.zero_row = self.units * 16 + self.tail_rows
        self.unpack_index = np.full((2, dp, shard_rows), self.zero_row, np.int32)
        self.tail_start = np.zeros((2, dp), np.int32)
        for s, section in enumerate(self.sections):
            for b in range(dp):
                self.tail_start[s, b] = max(section.fill[b] - self.tail_units, 0)
            for name, group, row, panels, block, unit in section.groups:
                for panel in range(panels):
                    for r in range(GROUP):
                        self.place(s, block, (unit + panel) * 16 + r, row + r * panels + panel)
            for row, panels, block, at in section.vectors.values():
                for panel in range(panels):
                    self.place(s, block, self.vec_unit * 16 + at + panel, row + panel)

    def bins(self, s):
        if s == 0:
            return [(0, self.dp // 2), (self.dp // 2, self.dp - self.dp // 2)]
        used = self.sections[1].blocks_used
        main = 1 << (used.bit_length() - 1)
        return [(0, main), (main, max(used - main, 1))]

    def tail_used(self):
        first, count = self.bins(1)[1]
        section = self.sections[1]
        assert count == 1 and all(v[2] < first for v in section.vectors.values())
        used = section.fill[first]
        return min(used, self.half), max(used - self.half, 0)

    def bin_units(self, s):
        return [self.half, self.half if s == 0 else max(self.tail_used())]

    def place(self, s, block, block_row, flat_row):
        local = flat_row - block * self.shard_rows
        assert 0 <= local < self.pack_rows
        gap = self.pack_base - self.shard_rows if local >= self.shard_rows else 0
        self.pack_index[s, block, block_row] = local + gap
        owner, at = divmod(flat_row, self.shard_rows)
        if owner == block:
            self.unpack_index[s, owner, at] = block_row
        else:
            assert owner == block + 1
            if block_row >= self.vec_unit * 16:
                source = self.tail_units * 16 + block_row - self.vec_unit * 16
            else:
                source = block_row - int(self.tail_start[s, block]) * 16
                assert 0 <= source < self.tail_units * 16
            self.unpack_index[s, owner, at] = self.units * 16 + source


def move_rows_in(index_ref, held, done, count):
    def eight(i, carry):
        for j in range(8):
            row = i * 8 + j
            done[pl.ds(row, 1), :] = held[pl.ds(index_ref[row], 1), :]
        return carry

    lax.fori_loop(0, count // 8, eight, 0)
    for row in range(count // 8 * 8, count):
        done[pl.ds(row, 1), :] = held[pl.ds(index_ref[row], 1), :]


def pack_kernel(base, index_ref, flat, following, out_ref, held, done, sems):
    rows, more = flat.shape[0], following.shape[0]
    copies = [
        pltpu.make_async_copy(flat.at[:, 0], held.at[pl.ds(0, rows)], sems.at[0]),
        pltpu.make_async_copy(following.at[:, 0], held.at[pl.ds(base, more)], sems.at[1]),
    ]
    for copy in copies:
        copy.start()
    for copy in copies:
        copy.wait()
    count = done.shape[0]
    move_rows_in(index_ref, held, done, count)
    out_ref[...] = done[...].reshape(out_ref.shape).astype(BF16)


def pack(plan, index, flat, following):
    count = plan.units * 16
    return pl.pallas_call(
        functools.partial(pack_kernel, plan.pack_base),
        out_shape=jax.ShapeDtypeStruct((plan.units, 16, 128), BF16),
        in_specs=[IN_SMEM, ANY, ANY],
        out_specs=IN_VMEM,
        scratch_shapes=[
            pltpu.VMEM((plan.pack_base + plan.head_rows, 128), F32),
            pltpu.VMEM((count, 128), F32),
            pltpu.SemaphoreType.DMA((2,)),
        ],
        compiler_params=pltpu.CompilerParams(vmem_limit_bytes=32 * 1024 * 1024),
        name="pack_rows",
    )(index, flat, following)


def unpack_kernel(zero_row, rows, index_ref, block, tail, out_ref, held):
    at = 0
    for source in (block, tail):
        size = source.shape[0] * 16
        held[pl.ds(at, size), :] = source[...].reshape(size, 128)
        at += size
    held[pl.ds(zero_row, 8), :] = jnp.zeros((8, 128), F32)
    out_ref[pl.ds(out_ref.shape[0] - 16, 16), :] = jnp.zeros((16, 128), F32)
    move_rows_in(index_ref, held, out_ref, rows)


def unpack(plan, index, block, tail):
    rows = plan.shard_rows
    padded = 16 * -(-rows // 16)
    return pl.pallas_call(
        functools.partial(unpack_kernel, plan.zero_row, rows),
        out_shape=jax.ShapeDtypeStruct((padded, 128), F32),
        in_specs=[IN_SMEM, IN_VMEM, IN_VMEM],
        out_specs=IN_VMEM,
        scratch_shapes=[pltpu.VMEM((plan.zero_row + 8, 128), F32)],
        compiler_params=pltpu.CompilerParams(vmem_limit_bytes=32 * 1024 * 1024),
        cost_estimate=lasting(6),
        name="unpack_rows",
    )(index, block, tail)


def update_kernel(rows, chunk, factor_ref, total, *refs):
    states, outs, held, made, in_sems, out_sems = (
        refs[:4], refs[4:8], refs[8:12], refs[12:16], refs[16], refs[17],
    )
    starts = list(range(0, rows, chunk))
    sizes = [min(chunk, rows - at) for at in starts]
    loads = [
        [
            pltpu.make_async_copy(
                source.at[pl.ds(at, size), 0], ref.at[pl.ds(at, size)], in_sems.at[k, j]
            )
            for j, (source, ref) in enumerate(zip(states, held))
        ]
        for k, (at, size) in enumerate(zip(starts, sizes))
    ]
    for group in loads:
        for copy in group:
            copy.start()
    stores = []
    factor = factor_ref[0]
    for k, (at, size) in enumerate(zip(starts, sizes)):
        for copy in loads[k]:
            copy.wait()

        def body(i, carry):
            here = pl.ds(pl.multiple_of(at + i * 16, 8), 16)
            master, first, second, ema = (ref[here, :] for ref in held)
            clipped = total[here, :] * factor
            new_first = beta_one * first + (1.0 - beta_one) * clipped
            new_second = beta_two * second + (1.0 - beta_two) * clipped * clipped
            first_hat = new_first * (1.0 / (1.0 - beta_one**STEP))
            second_hat = new_second * (1.0 / (1.0 - beta_two**STEP))
            new_master = master - learn_rate * (
                first_hat / (jnp.sqrt(second_hat) + adam_epsilon) + weight_decay * master
            )
            made[0][here, :] = new_master
            made[1][here, :] = new_first
            made[2][here, :] = new_second
            made[3][here, :] = average_keep * ema + (1.0 - average_keep) * new_master
            return carry

        lax.fori_loop(0, -(-size // 16), body, 0, unroll=2)
        for j in range(4):
            copy = pltpu.make_async_copy(
                made[j].at[pl.ds(at, size)], outs[j].at[pl.ds(at, size), 0], out_sems.at[k, j]
            )
            copy.start()
            stores.append(copy)
    for copy in stores:
        copy.wait()


def update(plan, factor, total, states):
    rows = plan.shard_rows
    chunk = 16 * -(-rows // (16 * 4))
    padded = 16 * -(-rows // 16)
    count = -(-rows // chunk)
    return pl.pallas_call(
        functools.partial(update_kernel, rows, chunk),
        out_shape=[jax.ShapeDtypeStruct((rows, 1, 128), F32)] * 4,
        in_specs=[IN_SMEM, IN_VMEM, *[ANY] * 4],
        out_specs=[ANY] * 4,
        scratch_shapes=[
            *[pltpu.VMEM((padded, 128), F32)] * 8,
            pltpu.SemaphoreType.DMA((count, 4)),
            pltpu.SemaphoreType.DMA((count, 4)),
        ],
        compiler_params=pltpu.CompilerParams(vmem_limit_bytes=VMEM_BYTES),
        name="update_states",
    )(factor, total, *states)


def dot(a, b):
    return lax.dot_general(a, b, (((1,), (0,)), ((), ())), preferred_element_type=F32)


def dot_nt(a, b):
    return lax.dot_general(a, b, (((1,), (1,)), ((), ())), preferred_element_type=F32)


def dot_tn(a, b):
    return lax.dot_general(a, b, (((0,), (0,)), ((), ())), preferred_element_type=F32)


def total_of(terms):
    total = terms[0]
    for term in terms[1:]:
        total = total + term
    return total


def for_rows(count, size, step, unroll=1):
    def body(i, carry):
        step(pl.multiple_of(i * size, size))
        return carry

    lax.fori_loop(0, count // size, body, 0, unroll=unroll)


def columns(weight, depth, first, count):
    parts = [weight[:, first + i].reshape(depth, 128) for i in range(count)]
    return jnp.concatenate(parts, axis=1)


def row_band(weight, panels, band):
    parts = [weight[pl.ds(band * 16, 16), i].reshape(256, 128) for i in range(panels)]
    return jnp.concatenate(parts, axis=1)


def row_chunks(count):
    size = next(n for n in (208, 224, 112, 104, 16) if count % n == 0)
    return [slice(at, at + size) for at in range(0, count, size)]


def wide_chunks(count):
    size = next(n for n in (416, 336, 112, 104, 16) if count % n == 0)
    return [slice(at, at + size) for at in range(0, count, size)]


def times_columns(left, weight, panels, depth, finish):
    group = 4 if panels % 4 == 0 else 2

    def body(index, carry):
        right = columns(weight, depth, group * index, group)
        width = group * 128
        there = pl.ds(pl.multiple_of(index * width, width), width)
        for here in row_chunks(left.shape[0]):
            finish(index * width, here, there, dot(left[here, :], right))
        return carry

    lax.fori_loop(0, panels // group, body, 0)


def times_bands(left, weight, panels, count, finish):
    def body(band, carry):
        right = row_band(weight, panels, band)
        for here in wide_chunks(left.shape[0]):
            finish(here, lanes(band), dot_nt(left[here, :], right))
        return carry

    lax.fori_loop(0, count // 256, body, 0)


def lanes(pair):
    return pl.ds(pl.multiple_of(pair * 256, 256), 256)


def norm_block(count):
    return next(n for n in (416, 336, 112, 104, 16) if count % n == 0)


def norm_rows(x, width):
    mean = jnp.sum(x, axis=1, keepdims=True) * (1.0 / width)
    centre = x - mean
    spread = jnp.sum(centre * centre, axis=1, keepdims=True) * (1.0 / width)
    rstd = lax.rsqrt(spread + norm_epsilon)
    return centre * rstd, rstd


def norm_forward(x_ref, gain, shift, out_ref, count, width):
    size = norm_block(count)

    def step(at):
        hat, _ = norm_rows(x_ref[pl.ds(at, size), :], width)
        out_ref[pl.ds(at, size), :] = (hat * gain + shift).astype(out_ref.dtype)

    for_rows(count, size, step)


def norm_backward(x_ref, gain, grad_of, put, count, width):
    size = norm_block(count)

    def body(i, carry):
        gain_sum, shift_sum = carry
        at = pl.multiple_of(i * size, size)
        hat, rstd = norm_rows(x_ref[pl.ds(at, size), :], width)
        grad = grad_of(at, size)
        gain_sum = gain_sum + jnp.sum((grad * hat).reshape(size // 8, 8, width), axis=0)
        shift_sum = shift_sum + jnp.sum(grad.reshape(size // 8, 8, width), axis=0)
        scaled = grad * gain
        first = jnp.sum(scaled, axis=1, keepdims=True) * (1.0 / width)
        second = jnp.sum(scaled * hat, axis=1, keepdims=True) * (1.0 / width)
        put(at, size, rstd * (scaled - first - hat * second))
        return gain_sum, shift_sum

    zero = jnp.zeros((8, width), F32)
    gain_sum, shift_sum = lax.fori_loop(0, count // size, body, (zero, zero))
    return jnp.sum(gain_sum, axis=0, keepdims=True), jnp.sum(shift_sum, axis=0, keepdims=True)


def head_masks(size):
    lane = lax.broadcasted_iota(jnp.int32, (1, 128), 1)
    return [
        jnp.where((lane >= h * size) & (lane < (h + 1) * size), 1.0, 0.0).astype(BF16)
        for h in range(128 // size)
    ]


def softmax_columns(scores, limit):
    key = lax.broadcasted_iota(jnp.int32, scores.shape, 0)
    scores = jnp.where(key < limit, scores, -1e30)
    top = jnp.max(scores, axis=0, keepdims=True)
    raised = jnp.exp(scores - top)
    return raised * (1.0 / jnp.sum(raised, axis=0, keepdims=True))


def softmax_rows(scores, limit):
    key = lax.broadcasted_iota(jnp.int32, scores.shape, 1)
    scores = jnp.where(key < limit, scores, -1e30)
    top = jnp.max(scores, axis=1, keepdims=True)
    raised = jnp.exp(scores - top)
    return raised * (1.0 / jnp.sum(raised, axis=1, keepdims=True))


def attention_forward(mixed, out, limit_of, images, rows, width, size):
    panels = width // 128
    masks = head_masks(size)

    def body(step, carry):
        image, panel = step // panels, step % panels
        here = pl.ds(pl.multiple_of(image * rows, 16), rows)

        def part(third):
            return mixed[here, pl.ds(pl.multiple_of((third * panels + panel) * 128, 128), 128)]

        query, keys, values = part(0), part(1), part(2)
        limit = limit_of(image)
        probs = [softmax_rows(dot_nt(query * mask, keys), limit).astype(BF16) for mask in masks]
        total = total_of([dot(p, values) * m.astype(F32) for p, m in zip(probs, masks)])
        out[here, pl.ds(pl.multiple_of(panel * 128, 128), 128)] = total.astype(BF16)
        return carry

    lax.fori_loop(0, images * panels, body, 0, unroll=6)


def attention_backward(mixed, grad_out, grad_mixed, limit_of, images, rows, width, size):
    panels = width // 128
    masks = head_masks(size)

    def body(step, carry):
        image, panel = step // panels, step % panels
        here = pl.ds(pl.multiple_of(image * rows, 16), rows)

        def place(third):
            return pl.ds(pl.multiple_of((third * panels + panel) * 128, 128), 128)

        query, keys, values = (mixed[here, place(third)] for third in range(3))
        grad = grad_out[here, place(0)]
        turned = keys.T
        limit = limit_of(image)
        zero = jnp.zeros((rows, 128), F32)
        grad_query, grad_keys, grad_values = [], zero, zero
        for h, mask in enumerate(masks):
            masked_query = query * mask
            masked_grad = grad * mask
            probs = softmax_columns(dot_nt(keys, masked_query), limit)
            grad_probs = dot_nt(values, masked_grad)
            inner = jnp.sum(probs * grad_probs, axis=0, keepdims=True)
            grad_scores = (probs * (grad_probs - inner)).astype(BF16)
            grad_values = grad_values + dot(probs.astype(BF16), masked_grad)
            grad_keys = grad_keys + dot(grad_scores, masked_query)
            grad_query.append(dot(turned[h * size : h * size + size, :], grad_scores))
        grad_query = jnp.concatenate(grad_query, axis=0) * (1.0 / math.sqrt(size))
        grad_mixed[here, place(0)] = grad_query.astype(BF16).T
        grad_mixed[here, place(1)] = grad_keys.astype(BF16)
        grad_mixed[here, place(2)] = grad_values.astype(BF16)
        return carry

    lax.fori_loop(0, images * panels, body, 0, unroll=4)


def gelu_parts(value):
    bell = 0.5 * (1.0 + lax.erf(value * math.sqrt(0.5)))
    slope = bell + value * (jnp.exp(value * value * -0.5) * (1.0 / math.sqrt(2.0 * math.pi)))
    return value * bell, slope


class Shape:
    def __init__(self, images, rows, width, heads, hidden):
        self.images, self.rows, self.width = images, rows, width
        self.size = width // heads
        self.hidden = hidden
        self.count = images * rows


def block_forward(sh, x0, n1, mixed, o, x1, n2, g, gp, y, w, vec, limit_of, ready, saved):
    width, hidden, count = sh.width, sh.hidden, sh.count
    panels = width // 128
    norm_forward(x0, vec("g1"), vec("b1"), n1, count, width)
    saved(n1)
    ready("qkv")

    def put_mixed(start, here, there, value):
        scale = jnp.where(start < width, 1.0 / math.sqrt(sh.size), 1.0)
        mixed[here, there] = (value * scale).astype(BF16)

    times_columns(n1, w["qkv"], 3 * panels, width, put_mixed)
    saved(mixed)
    attention_forward(mixed, o, limit_of, sh.images, sh.rows, width, sh.size)
    saved(o)
    ready("proj")

    def put_sum(base, out):
        def finish(_, here, there, value):
            out[here, there] = base[here, there] + value

        return finish

    times_columns(o, w["proj"], panels, width, put_sum(x0, x1))
    saved(x1)
    norm_forward(x1, vec("g2"), vec("b2"), n2, count, width)
    saved(n2)
    ready("fc1")

    def put_hidden(_, here, there, value):
        value, slope = gelu_parts(value)
        g[here, there] = value.astype(BF16)
        gp[here, there] = slope

    times_columns(n2, w["fc1"], hidden // 128, width, put_hidden)
    saved(g)
    saved(gp)
    ready("fc2")
    times_columns(g, w["fc2"], panels, hidden, put_sum(x1, y))
    saved(y)


class Gradients:
    def __init__(self, plan, s, own, stage, sems, targets):
        self.plan, self.section, self.own = plan, plan.sections[s], own
        self.bins = plan.bins(s)
        self.stage, self.sems, self.targets = stage, sems, targets
        self.turn = 0
        self.flying = [[], []]

    def copy_out(self, source, block, side, unit, take, sem):
        which = max(i for i, (first, _) in enumerate(self.bins) if first <= block)
        block = block - self.bins[which][0]
        keep, send = self.targets[2 * which], self.targets[2 * which + 1]

        def to(target):
            return pltpu.make_async_copy(source, target.at[block, pl.ds(unit, take)], sem)

        @pl.when(self.own == side)
        def _():
            to(keep).start()

        @pl.when(self.own != side)
        def _():
            to(send).start()

        return to(keep)

    def drain(self, slot):
        for copy in self.flying[slot]:
            copy.wait()
        self.flying[slot] = []

    def weight(self, name, left, depth, right, turned):
        panels = self.section.panels[name]
        for band in range(depth // 256):
            slot = self.turn % 2
            self.turn += 1
            self.drain(slot)
            stage = self.stage.at[slot]
            turned[...] = left[:, band * 256 : band * 256 + 256].T

            def body(pair, carry):
                value = dot(turned[...], right[:, lanes(pair)])
                for i in range(2):
                    stage[pl.ds(2 * pair + i, 16, stride=panels)] = value[
                        :, i * 128 : i * 128 + 128
                    ].reshape(16, 16, 128)
                return carry

            lax.fori_loop(0, panels // 2, body, 0)
            for block, side, unit, at, take in self.section.runs(
                name, self.plan.half_cuts, band * 16, 16
            ):
                self.flying[slot].append(
                    self.copy_out(
                        stage.at[pl.ds(at, take)], block, side, unit, take, self.sems.at[slot]
                    )
                )

    def finish(self, values, scratch):
        vectors = self.section.vectors
        blocks = sorted({vectors[name][2] for name in values})
        for k, block in enumerate(blocks):
            scratch[k] = jnp.zeros((VEC_UNITS, 16, 128), F32)
            for name, (_, panels, at_block, at) in vectors.items():
                if at_block != block:
                    continue
                for panel in range(panels):
                    unit, row = divmod(at + panel, 16)
                    scratch[k, unit, row : row + 1, :] = values[name][
                        :, panel * 128 : panel * 128 + 128
                    ]
        unit = self.plan.vec_unit - self.plan.half
        copies = [
            self.copy_out(scratch.at[k], block, 1, unit, VEC_UNITS, self.sems.at[2])
            for k, block in enumerate(blocks)
        ]
        for copy in copies:
            copy.wait()
        self.drain(0)
        self.drain(1)


class Backward:
    def __init__(self, sh, w, vec, limit_of, grads, values, turned, ready):
        self.sh, self.w, self.vec, self.limit_of = sh, w, vec, limit_of
        self.grads, self.values, self.turned, self.ready = grads, values, turned, ready
        self.panels = sh.width // 128

    def round_stream(self, dy, dyb):
        def step(at):
            dyb[pl.ds(at, 16), :] = dy[pl.ds(at, 16), :].astype(BF16)

        for_rows(self.sh.count, 16, step, 4)

    def bands(self, left, name, count, put):
        times_bands(left, self.w[name], self.grads.section.panels[name], count, put)

    def through_norm(self, x, dn, dy, gain, shift, dn_is=None):
        def from_dn(at, size):
            return dn[pl.ds(at, size), :]

        def into_stream(at, size, value):
            dy[pl.ds(at, size), :] = dy[pl.ds(at, size), :] + value

        self.values[gain], self.values[shift] = norm_backward(
            x, self.vec(gain), from_dn, into_stream, self.sh.count, self.sh.width
        )

    def second_product(self, dy, dyb, g, gp):
        self.round_stream(dy, dyb)
        self.ready("fc2", g)
        self.grads.weight("fc2", g, self.sh.hidden, dyb, self.turned)
        self.ready(None, gp)

        def put(here, there, value):
            g[here, there] = (value * gp[here, there]).astype(BF16)

        self.bands(dyb, "fc2", self.sh.hidden, put)

    def first_product(self, dy, g, n2, x1, dn):
        def put(here, there, value):
            dn[here, there] = value

        self.ready("fc1", n2)
        self.grads.weight("fc1", n2, self.sh.width, g, self.turned)
        self.bands(g, "fc1", self.sh.width, put)
        self.ready(None, x1)
        self.through_norm(x1, dn, dy, "g2", "b2")

    def projection(self, dy, dyb, o, grad):
        sh = self.sh
        self.round_stream(dy, dyb)
        self.ready("proj", o)
        self.grads.weight("proj", o, sh.width, dyb, self.turned)

        def put(here, there, value):
            grad[here, there] = value.astype(BF16)

        self.bands(dyb, "proj", sh.width, put)

    def attention(self, grad, mixed, dmixed):
        sh = self.sh
        self.ready(None, grad)
        self.ready(None, mixed)
        attention_backward(mixed, grad, dmixed, self.limit_of, sh.images, sh.rows, sh.width, sh.size)

    def mixing(self, dy, dmixed, n1, x0, dn):
        def put(here, there, value):
            dn[here, there] = value

        self.ready("qkv", n1)
        self.grads.weight("qkv", n1, self.sh.width, dmixed, self.turned)
        self.bands(dmixed, "qkv", self.sh.width, put)
        self.ready(None, x0)
        self.through_norm(x0, dn, dy, "g1", "b1")


def held_at(plan, s, gathered, block, side, unit, take):
    if s == 0:
        return [(gathered[0].at[side, block, pl.ds(unit, take)], 0, take)]
    if block == plan.bins(1)[1][0]:
        return [(gathered[1].at[side, pl.ds(unit, take)], 0, take)]
    out = []
    quarter = plan.quarter
    if unit < quarter:
        few = min(take, quarter - unit)
        out.append((gathered[0].at[side, 2 * block, pl.ds(unit, few)], 0, few))
    if unit + take > quarter:
        skip = max(quarter - unit, 0)
        few = take - skip
        source = gathered[0].at[side, 2 * block + 1, pl.ds(unit + skip - quarter, few)]
        out.append((source, skip, few))
    return out


def load_vectors(plan, s, gathered, held, vec_ref, sem):
    section = plan.sections[s]
    blocks = sorted({v[2] for v in section.vectors.values()})
    copies = [
        pltpu.make_async_copy(source, held.at[k, pl.ds(skip, few)], sem)
        for k, block in enumerate(blocks)
        for source, skip, few in held_at(
            plan, s, gathered, block, 1, plan.vec_unit - plan.half, VEC_UNITS
        )
    ]
    for copy in copies:
        copy.start()
    names = {name: i for i, name in enumerate(section.vectors)}

    def finish():
        for copy in copies:
            copy.wait()
        for k, block in enumerate(blocks):
            rows = held[k].reshape(16 * VEC_UNITS, 128).astype(F32)
            for name, (_, panels, at_block, at) in section.vectors.items():
                if at_block != block:
                    continue
                i = names[name]
                for panel in range(panels):
                    vec_ref[i : i + 1, panel * 128 : panel * 128 + 128] = rows[
                        at + panel : at + panel + 1, :
                    ]
        return lambda name: vec_ref[names[name] : names[name] + 1, :]

    return finish


def load_weights(plan, s, gathered, w, sems):
    section = plan.sections[s]
    copies = {}
    for k, (name, ref) in enumerate(w.items()):
        panels = section.panels[name]
        flat = ref.reshape(ref.shape[0] * panels, 16, 128)
        copies[name] = [
            pltpu.make_async_copy(source, flat.at[pl.ds(at + skip, few)], sems.at[k])
            for block, side, unit, at, take in section.runs(name, plan.half_cuts)
            for source, skip, few in held_at(plan, s, gathered, block, side, unit, take)
        ]
        for copy in copies[name]:
            copy.start()

    def ready(name):
        for copy in copies.get(name, ()):
            copy.wait()

    return ready


def weight_scratch(layout, names):
    shapes = dict(layout)
    return [
        pltpu.VMEM((shapes[n][0] // GROUP, shapes[n][1] // 128, GROUP, 128), BF16)
        for n in names
    ]


def picks(perm_ref, image):
    here = pl.ds(pl.multiple_of(image * ROWS_D, 16), ROWS_D)
    patch = lax.broadcasted_iota(jnp.int32, (ROWS_D, ROWS_D), 1)
    return jnp.where(perm_ref[here, :] == patch, 1.0, 0.0).astype(BF16)


W_ENC = ["patch", "qkv", "proj", "fc1", "fc2"]


def encoder_kernel(plan, sh, refs):
    (info, gathered, patches, perm, pos, pp_out, x0_out, n1_out, mixed_out, o_out, x1_out, n2_out,
     g_out, gp_out, y_out, latent_out, w_patch, w_qkv, w_proj, w_fc1, w_fc2, held, vec_ref, pp, xe,
     x0, n1, mixed, o, x1, n2, g, gp, y, latent, w_sems, out_sems) = refs
    w = dict(zip(W_ENC, (w_patch, w_qkv, w_proj, w_fc1, w_fc2)))
    finish_vec = load_vectors(plan, 0, [gathered], held, vec_ref, w_sems.at[5])
    ready = load_weights(plan, 0, [gathered], w, w_sems)
    outs = []

    targets = [(pp, pp_out), (x0, x0_out), (n1, n1_out), (mixed, mixed_out), (o, o_out),
               (x1, x1_out), (n2, n2_out), (g, g_out), (gp, gp_out), (y, y_out),
               (latent, latent_out)]

    def saved(ref):
        for k, (source, target) in enumerate(targets):
            if source is ref:
                copy = pltpu.make_async_copy(source, target, out_sems.at[k])
                copy.start()
                outs.append(copy)

    def gather(image, carry):
        chosen = picks(perm, image)
        pp[image] = dot(chosen, patches[image]).astype(BF16)
        here = pl.ds(pl.multiple_of(image * ROWS_E, 16), ROWS_E)
        xe[here, :] = pp[image, 0:ROWS_E, :]
        few = chosen[0:ROWS_E, :]
        x0[here, :] = (dot(few, pos[0]) + dot(few, pos[1])) + dot(few, pos[2])
        return carry

    lax.fori_loop(0, sh.images, gather, 0)
    saved(pp)
    vec = finish_vec()
    ready("patch")

    def put(_, here, there, value):
        x0[here, there] = (value + vec_ref[0:1, there]) + x0[here, there]

    times_columns(xe, w["patch"], D // 128, PIX, put)
    saved(x0)
    block_forward(
        sh, x0, n1, mixed, o, x1, n2, g, gp, y, w, vec, lambda i: info[1 + i], ready, saved
    )
    norm_forward(y, vec("gf"), vec("bf"), latent, sh.count, D)
    saved(latent)
    for copy in outs:
        copy.wait()


def lasting(microseconds):
    return pl.CostEstimate(
        flops=int(microseconds * COST), bytes_accessed=1 << 20, transcendentals=0
    )


def saved_shapes(sh):
    count, width, hidden = sh.count, sh.width, sh.hidden
    return [
        ((count, width), F32),
        ((count, width), BF16),
        ((count, 3 * width), BF16),
        ((count, width), BF16),
        ((count, width), F32),
        ((count, width), BF16),
        ((count, hidden), BF16),
        ((count, hidden), F32),
        ((count, width), F32),
    ]


def encoder(plan, sh, info, gathered, patches, perm, pos):
    saved = saved_shapes(sh)
    pp_shape = ((sh.images, ROWS_D, PIX), BF16)
    latent_shape = ((sh.count, D), BF16)
    outs = [pp_shape, *saved, latent_shape]
    holders = len({v[2] for v in plan.sections[0].vectors.values()})
    return pl.pallas_call(
        lambda *refs: encoder_kernel(plan, sh, refs),
        out_shape=[jax.ShapeDtypeStruct(*s) for s in outs],
        in_specs=[IN_SMEM, ANY, IN_VMEM, IN_VMEM, IN_VMEM],
        out_specs=[ANY] * len(outs),
        scratch_shapes=[
            *weight_scratch(ENC, W_ENC),
            pltpu.VMEM((holders, VEC_UNITS, 16, 128), BF16),
            pltpu.VMEM((8, D), F32),
            pltpu.VMEM(*pp_shape),
            pltpu.VMEM((sh.count, PIX), BF16),
            *[pltpu.VMEM(*s) for s in saved],
            pltpu.VMEM(*latent_shape),
            pltpu.SemaphoreType.DMA((6,)),
            pltpu.SemaphoreType.DMA((len(outs),)),
        ],
        compiler_params=pltpu.CompilerParams(vmem_limit_bytes=VMEM_BYTES),
        cost_estimate=lasting(50),
        name="encoder_forward",
    )(info, gathered, patches, perm, pos)


W_DEC = ["embed", "qkv", "proj", "fc1", "fc2", "head"]


def decoder_kernel(plan, sh, refs):
    info, scale, gathered, gathered_tail, latent_in, pp_in, perm, pos = refs[:8]
    gathered = [gathered, gathered_tail]
    targets, refs = refs[8:12], refs[12:]
    (grad_latent, loss_out,
     w_embed, w_qkv, w_proj, w_fc1, w_fc2, w_head, held, vec_ref, pp, latent, embedded, x0, n1,
     mixed, o, x1, n2, g, gp, y, f, dn, guess, turned, turned_e, stage, vec_stage, w_sems,
     in_sems, grad_sems) = refs
    w = dict(zip(W_DEC, (w_embed, w_qkv, w_proj, w_fc1, w_fc2, w_head)))
    copy_latent = pltpu.make_async_copy(latent_in, latent, in_sems.at[0])
    copy_pp = pltpu.make_async_copy(pp_in, pp, in_sems.at[1])
    copy_latent.start()
    finish_vec = load_vectors(plan, 1, gathered, held, vec_ref, w_sems.at[6])
    ready = load_weights(plan, 1, gathered, w, w_sems)
    copy_pp.start()
    images, count = sh.images, sh.count
    count_e = images * ROWS_E
    vec = finish_vec()
    copy_latent.wait()
    ready("embed")

    def put_embedded(_, here, there, value):
        embedded[here, there] = value

    times_columns(latent, w["embed"], DD // 128, D, put_embedded)

    def tokens(image, carry):
        chosen = picks(perm, image)
        place = (dot(chosen, pos[0]) + dot(chosen, pos[1])) + dot(chosen, pos[2])
        start = pl.multiple_of(image * ROWS_D, 16)
        kept = info[1 + image]
        token = vec_ref[0:1, :]
        few = embedded[pl.ds(pl.multiple_of(image * ROWS_E, 16), ROWS_E), :]
        rank = lax.broadcasted_iota(jnp.int32, (ROWS_E, DD), 0)
        x0[pl.ds(start, ROWS_E), :] = jnp.where(rank < kept, few, token) + place[:ROWS_E, :]
        x0[pl.ds(start + ROWS_E, ROWS_D - ROWS_E), :] = token + place[ROWS_E:, :]
        return carry

    lax.fori_loop(0, images, tokens, 0)
    block_forward(
        sh, x0, n1, mixed, o, x1, n2, g, gp, y, w, vec, lambda i: NP, ready, lambda ref: None
    )
    norm_forward(y, vec("gf"), vec("bf"), f, count, DD)
    ready("head")
    copy_pp.wait()
    factor = scale[0]

    def predict_image(image, total):
        start = pl.multiple_of(image * ROWS_D, 16)
        kept = info[1 + image]
        here = pl.ds(start, ROWS_D)
        for pair in range(PIX // 256):
            guess[:, pair * 256 : pair * 256 + 256] = dot(
                f[here, :], columns(w["head"], DD, 2 * pair, 2)
            )

        target, _ = norm_rows(pp[image].astype(F32), PIX)
        off = guess[...] - target
        rank = lax.broadcasted_iota(jnp.int32, (ROWS_D, 1), 0)
        off = jnp.where((rank >= kept) & (rank < NP), off, 0.0)
        pp[image] = (off * factor).astype(BF16)
        return total + jnp.sum((off * off).reshape(ROWS_D // 8, 8, PIX), axis=0)

    total = lax.fori_loop(0, images, predict_image, jnp.zeros((8, PIX), F32))
    total = jnp.sum(jnp.sum(total, axis=0, keepdims=True), axis=1, keepdims=True)
    loss_out[...] = jnp.broadcast_to(total * (1.0 / PIX), (8, 128))

    grads = Gradients(plan, 1, info[0], stage, grad_sems, targets)
    values = {}
    back = Backward(
        sh, w, vec, lambda i: NP, grads, values, turned, lambda name, ref: None
    )
    dpred = pp.reshape(count, PIX)
    grads.weight("head", f, DD, dpred, turned)

    def put_dn(here, there, value):
        dn[here, there] = value

    back.bands(dpred, "head", DD, put_dn)

    def from_dn(at, size):
        return dn[pl.ds(at, size), :]

    def put_y(at, size, value):
        y[pl.ds(at, size), :] = value

    values["gf"], values["bf"] = norm_backward(y, vec("gf"), from_dn, put_y, count, DD)
    back.second_product(y, f, g, gp)
    back.first_product(y, g, n2, x1, dn)
    dmixed = g.at[:, pl.ds(0, 3 * DD)]
    back.projection(y, f, o, o)
    back.attention(o, mixed, dmixed)
    back.mixing(y, dmixed, n1, x0, dn)

    def split(image, total):
        start = pl.multiple_of(image * ROWS_D, 16)
        kept = info[1 + image]

        grad = y[pl.ds(start, ROWS_D), :]
        rank = lax.broadcasted_iota(jnp.int32, (ROWS_D, 1), 0)
        few = pl.ds(pl.multiple_of(image * ROWS_E, 16), ROWS_E)
        taken = jnp.where(rank[:ROWS_E] < kept, grad[:ROWS_E], 0.0)
        n1[few, :] = taken.astype(BF16)
        free = jnp.where(rank >= kept, grad, 0.0)
        return total + jnp.sum(free.reshape(ROWS_D // 8, 8, DD), axis=0)

    total = lax.fori_loop(0, images, split, jnp.zeros((8, DD), F32))
    values["mask"] = jnp.sum(total, axis=0, keepdims=True)
    placed = n1.at[pl.ds(0, count_e)]
    grads.weight("embed", latent, D, placed, turned_e)

    def put_latent(here, there, value):
        grad_latent[here, there] = value.astype(BF16)

    times_bands(placed, w["embed"], DD // 128, D, put_latent)
    grads.finish(values, vec_stage)


def grad_shapes(plan, s):
    return [
        jax.ShapeDtypeStruct((count, units, 16, 128), F32)
        for (_, count), units in zip(plan.bins(s), plan.bin_units(s))
        for _ in range(2)
    ]


def decoder(plan, sh, info, scale, gathered, latent, pp, perm, pos):
    count_e = sh.images * ROWS_E
    holders = len({v[2] for v in plan.sections[1].vectors.values()})
    saved = saved_shapes(sh)
    most = max(plan.sections[1].panels.values())
    return pl.pallas_call(
        lambda *refs: decoder_kernel(plan, sh, refs),
        out_shape=[
            *grad_shapes(plan, 1),
            jax.ShapeDtypeStruct((count_e, D), BF16),
            jax.ShapeDtypeStruct((8, 128), F32),
        ],
        in_specs=[IN_SMEM, IN_SMEM, ANY, ANY, ANY, ANY, IN_VMEM, IN_VMEM],
        out_specs=[*[ANY] * 4, IN_VMEM, IN_VMEM],
        scratch_shapes=[
            *weight_scratch(DEC, W_DEC),
            pltpu.VMEM((holders, VEC_UNITS, 16, 128), BF16),
            pltpu.VMEM((8, DD), F32),
            pltpu.VMEM((sh.images, ROWS_D, PIX), BF16),
            pltpu.VMEM((count_e, D), BF16),
            pltpu.VMEM((count_e, DD), F32),
            *[pltpu.VMEM(*s) for s in saved],
            pltpu.VMEM((sh.count, DD), BF16),
            pltpu.VMEM((sh.count, DD), F32),
            pltpu.VMEM((ROWS_D, PIX), F32),
            pltpu.VMEM((256, sh.count), BF16),
            pltpu.VMEM((256, count_e), BF16),
            pltpu.VMEM((2, 16 * most, 16, 128), F32),
            pltpu.VMEM((holders, VEC_UNITS, 16, 128), F32),
            pltpu.SemaphoreType.DMA((7,)),
            pltpu.SemaphoreType.DMA((2,)),
            pltpu.SemaphoreType.DMA((3,)),
        ],
        compiler_params=pltpu.CompilerParams(vmem_limit_bytes=VMEM_BYTES),
        cost_estimate=lasting(160),
        name="decoder_both",
    )(info, scale, *gathered, latent, pp, perm, pos)


class Stage:
    def __init__(self, plan, sh, weights, reads, temps, outs, most, cost, name, body, bins=2):
        self.plan, self.sh, self.weights, self.reads = plan, sh, weights, reads
        self.temps, self.outs, self.most, self.cost, self.name = temps, outs, most, cost, name
        self.body = body
        self.bins = bins

    def kernel(self, blocks, *refs):
        refs = list(refs)

        def take(count):
            got = refs[:count]
            del refs[:count]
            return got

        plan, sh = self.plan, self.sh
        info, gathered = take(2)
        sources = dict(zip(self.reads, take(len(self.reads))))
        take(blocks)
        targets = take(2 * self.bins)
        results = dict(zip(self.outs, take(len(self.outs))))
        w = dict(zip(self.weights, take(len(self.weights))))
        here = dict(zip(self.reads, take(len(self.reads))))
        temps = dict(zip(self.temps, take(len(self.temps))))
        held, vec_ref, turned, stage, vec_stage, w_sems, in_sems, grad_sems = refs
        finish_vec = load_vectors(plan, 0, [gathered], held, vec_ref, w_sems.at[len(w)])
        loads = {}
        for k, (name, ref) in enumerate(here.items()):
            if name == "xe":
                copies = [
                    pltpu.make_async_copy(
                        sources[name].at[i, pl.ds(0, ROWS_E)],
                        ref.at[pl.ds(i * ROWS_E, ROWS_E)],
                        in_sems.at[k],
                    )
                    for i in range(sh.images)
                ]
            else:
                copies = [pltpu.make_async_copy(sources[name], ref, in_sems.at[k])]
            for copy in copies:
                copy.start()
            loads[id(ref)] = copies
        weights_ready = load_weights(plan, 0, [gathered], w, w_sems)
        vec = finish_vec()

        def ready(name, ref=None):
            for copy in loads.pop(id(ref), ()):
                copy.wait()
            if name is not None:
                weights_ready(name)

        values = {}
        grads = Gradients(plan, 0, info[0], stage, grad_sems, targets)
        back = Backward(
            sh, w, vec, lambda i: info[1 + i], grads, values, turned, ready
        )
        back.out_sem = in_sems.at[len(self.reads)]
        self.body(back, {**here, **temps}, results)
        assert not loads
        grads.finish(values, vec_stage)

    def __call__(self, info, gathered, arrays, blocks):
        plan, sh = self.plan, self.sh
        count, width, hidden = sh.count, sh.width, sh.hidden
        known = {
            "dz": ((count, width), BF16),
            "y": ((count, width), F32),
            "dy": ((count, width), F32),
            "x0": ((count, width), F32),
            "x1": ((count, width), F32),
            "dn": ((count, width), F32),
            "n1": ((count, width), BF16),
            "n2": ((count, width), BF16),
            "o": ((count, width), BF16),
            "dyb": ((count, width), BF16),
            "do": ((count, width), BF16),
            "xe": ((count, PIX), BF16),
            "mixed": ((count, 3 * width), BF16),
            "dmixed": ((count, 3 * width), BF16),
            "g": ((count, hidden), BF16),
            "gp": ((count, hidden), F32),
        }
        holders = len({v[2] for v in plan.sections[0].vectors.values()})
        targets = grad_shapes(plan, 0)[: 2 * self.bins]
        before = 2 + len(self.reads)
        got = pl.pallas_call(
            functools.partial(self.kernel, len(blocks)),
            out_shape=[*targets, *[jax.ShapeDtypeStruct(*known[n]) for n in self.outs]],
            in_specs=[IN_SMEM, *[ANY] * (1 + len(self.reads) + len(blocks))],
            out_specs=[*[ANY] * len(targets), *[ANY if n == "g" else IN_VMEM for n in self.outs]],
            input_output_aliases={before + i: i for i in range(len(blocks))},
            scratch_shapes=[
                *weight_scratch(ENC, self.weights),
                *[pltpu.VMEM(*known[n]) for n in self.reads],
                *[pltpu.VMEM(*known[n]) for n in self.temps],
                pltpu.VMEM((holders, VEC_UNITS, 16, 128), BF16),
                pltpu.VMEM((8, D), F32),
                pltpu.VMEM((256, count), BF16),
                pltpu.VMEM((2, 16 * self.most, 16, 128), F32),
                pltpu.VMEM((holders, VEC_UNITS, 16, 128), F32),
                pltpu.SemaphoreType.DMA((len(self.weights) + 1,)),
                pltpu.SemaphoreType.DMA((len(self.reads) + 1,)),
                pltpu.SemaphoreType.DMA((3,)),
            ],
            compiler_params=pltpu.CompilerParams(vmem_limit_bytes=VMEM_BYTES),
            cost_estimate=lasting(self.cost),
            name=self.name,
        )(info, gathered, *[arrays[n] for n in self.reads], *blocks)
        return got[: len(targets)], dict(zip(self.outs, got[len(targets) :]))


def back_second(back, r, out):
    sh = back.sh
    back.ready(None, r["dz"])
    back.ready(None, r["y"])

    def from_latent(at, size):
        return r["dz"][pl.ds(at, size), :].astype(F32)

    def put(at, size, value):
        out["dy"][pl.ds(at, size), :] = value

    back.values["gf"], back.values["bf"] = norm_backward(
        r["y"], back.vec("gf"), from_latent, put, sh.count, D
    )
    back.second_product(out["dy"], r["dyb"], r["g"], r["gp"])
    copy = pltpu.make_async_copy(r["g"], out["g"], back.out_sem)
    copy.start()
    back.grads.drain(0)
    back.grads.drain(1)
    copy.wait()


def copy_rows(count, source, target):
    def step(at):
        target[pl.ds(at, 16), :] = source[pl.ds(at, 16), :]

    for_rows(count, 16, step, 4)


def back_first(back, r, out):
    back.ready(None, r["dy"])
    back.ready(None, r["g"])
    copy_rows(back.sh.count, r["dy"], out["dy"])
    back.first_product(out["dy"], r["g"], r["n2"], r["x1"], r["dn"])


def back_projection(back, r, out):
    back.ready(None, r["dy"])
    back.projection(r["dy"], r["dyb"], r["o"], out["do"])


def back_attention(back, r, out):
    back.attention(r["do"], r["mixed"], out["dmixed"])


def back_mixing(back, r, out):
    back.ready(None, r["dy"])
    back.ready(None, r["dmixed"])
    back.mixing(r["dy"], r["dmixed"], r["n1"], r["x0"], r["dn"])

    def body(i, total):
        at = pl.multiple_of(i * 16, 16)
        grad = r["dy"][pl.ds(at, 16), :]
        r["dyb"][pl.ds(at, 16), :] = grad.astype(BF16)
        return total + jnp.sum(grad.reshape(2, 8, D), axis=0)

    total = lax.fori_loop(0, back.sh.count // 16, body, jnp.zeros((8, D), F32))
    back.values["patch_b"] = jnp.sum(total, axis=0, keepdims=True)
    back.ready(None, r["xe"])
    back.grads.weight("patch", r["xe"], PIX, r["dyb"], back.turned)


def encoder_back_stages(plan, sh):
    most = {n: plan.sections[0].panels[n] for n in ("fc1", "fc2", "qkv", "proj")}
    return [
        Stage(plan, sh, ["fc2"], ["y", "dz", "g", "gp"], ["dyb"], ["dy", "g"], most["fc2"], 25,
              "encoder_back_fc2", back_second),
        Stage(plan, sh, ["fc1"], ["g", "dy", "n2", "x1"], ["dn"], ["dy"], most["fc1"], 20,
              "encoder_back_fc1", back_first),
        Stage(plan, sh, ["proj"], ["dy", "o"], ["dyb"], ["do"], most["proj"], 10,
              "encoder_back_proj", back_projection, 1),
        Stage(plan, sh, [], ["do", "mixed"], [], ["dmixed"], 1, 25,
              "encoder_back_attention", back_attention, 0),
        Stage(plan, sh, ["qkv"], ["dy", "dmixed", "n1", "x0", "xe"], ["dn", "dyb"], [],
              most["qkv"], 25, "encoder_back_qkv", back_mixing, 1),
    ]


def pick(value, index, axis):
    return lax.dynamic_index_in_dim(value, index, axis, keepdims=False)


def tie(*trees):
    return lax.optimization_barrier(trees)


class Term:
    def __init__(self, base, bits, first, last, fixed=()):
        self.base, self.bits, self.first, self.last = base, bits, first, last
        self.fixed = dict(fixed)

    def at(self, bit, index):
        return Term(self.base, self.bits, self.first, self.last, {**self.fixed, bit: index})

    def value(self):
        zero = jnp.zeros((), jnp.int32)
        starts = [self.fixed.get(b, zero).astype(jnp.int32) for b in self.bits]
        sizes = [1 if b in self.fixed else 2 for b in self.bits]
        left = [n for n in sizes if n == 2]
        starts += [jnp.full((), self.first, jnp.int32), zero, zero]
        count = self.last - self.first
        out = lax.dynamic_slice(self.base, starts, [*sizes, count, 16, 128])
        return out.reshape(*left, count, 16, 128)


def sum_of(terms):
    return total_of([term.value() for term in terms])


class Flow:
    def __init__(self, dp, keep, send, first, shares=(1, 1, 1)):
        parts = len(shares)
        self.dp = dp
        self.me = lax.axis_index("dp")
        self.keep, self.given = keep, send
        count, units = keep.shape[:2]
        self.bits = count.bit_length() - 1
        assert count == 1 << self.bits and dp & (dp - 1) == 0
        self.all_bits = dp.bit_length() - 1
        self.first = first
        low = list(range(self.bits))
        if dp == 64:
            low = [b for b in (0, 2, 4, 1, 3) if b < self.bits]
        turn = max(min(3, len(low)), 1)
        self.cuts = [units * sum(shares[:p]) // sum(shares) for p in range(parts + 1)]
        self.orders = [low[p % turn : turn] + low[: p % turn] + low[turn:] for p in range(parts)]
        self.step = -1
        self.terms = None

    def done(self):
        return self.step == self.all_bits

    def last(self):
        return self.step == self.all_bits - 1

    def payload(self):
        if self.step < 0:
            return [self.given]
        if self.step >= self.bits:
            return [self.result()]
        out = []
        for terms, order in zip(self.terms, self.orders):
            bit = order[self.step]
            other = 1 - (self.me >> bit & 1)
            out.append(sum_of([t.at(bit, other) for t in terms]))
        return out

    def send(self, payload):
        if self.step < 0:
            return [lax.ppermute(payload[0], "section", [(0, 1), (1, 0)])]
        if self.step >= self.bits:
            flip = 1 << self.step
            pairs = [(i, i ^ flip) for i in range(self.dp) if (i ^ self.first) & flip]
            return [lax.ppermute(payload[0], "dp", pairs)]
        out = []
        for value, order in zip(payload, self.orders):
            flip = 1 << order[self.step]
            out.append(lax.ppermute(value, "dp", [(i, i ^ flip) for i in range(self.dp)]))
        return out

    def take(self, got):
        ranges = list(zip(self.cuts[:-1], self.cuts[1:]))
        if self.step < 0:
            bits = list(range(self.bits - 1, -1, -1))
            shape = (2,) * self.bits + self.keep.shape[1:]
            self.terms = [
                [Term(v.reshape(shape), bits, *r) for v in (self.keep, got[0])] for r in ranges
            ]
        elif self.step < self.bits:
            for k, (order, value) in enumerate(zip(self.orders, got)):
                bit = order[self.step]
                mine = self.me >> bit & 1
                gone = order[: self.step + 1]
                bits = [b for b in range(self.bits - 1, -1, -1) if b not in gone]
                self.terms[k] = [t.at(bit, mine) for t in self.terms[k]]
                self.terms[k].append(Term(value, bits, 0, value.shape[-3]))
        else:
            for k, r in enumerate(ranges):
                self.terms[k].append(Term(got[0], [], *r))
        self.step += 1

    def result(self):
        return jnp.concatenate([sum_of(t) for t in self.terms], axis=0)


def move_on(flows, *others):
    flows = [f for f in flows if f is not None and not f.done()]
    payloads, others = tie([f.payload() for f in flows], others)
    return flows, [f.send(p) for f, p in zip(flows, payloads)], others


def arrive(flows, got):
    for flow, values in zip(flows, got):
        flow.take(values)


def sum_in_chip(value):
    return value + lax.ppermute(value, "section", [(0, 1), (1, 0)])


def sum_over_dp(dp, value, low):
    bits = dp.bit_length() - 1
    got = [
        lax.ppermute(value, "dp", [(i, i ^ (flip << low)) for i in range(dp)])
        for flip in range(1, 1 << min(2, bits - low))
    ]
    value = value + got[0]
    if len(got) == 3:
        value = value + (got[1] + got[2])
    return value


def sum_everywhere(dp, value):
    value = sum_in_chip(value)
    for low in range(0, dp.bit_length() - 1, 2):
        value = sum_over_dp(dp, value, low)
    return value


def squares_of(plan, s, value, section, me):
    section_plan = plan.sections[s]
    vectors = np.zeros((plan.dp,), np.int32)
    for _, panels, block, at in section_plan.vectors.values():
        vectors[block] = max(vectors[block], at + panels)
    filled = jnp.asarray(np.asarray(section_plan.fill, np.int32) * 16)[me]
    vectors = jnp.asarray(vectors)[me]
    shape = value.shape
    row = lax.broadcasted_iota(jnp.int32, shape, 0) * 16 + lax.broadcasted_iota(jnp.int32, shape, 1)
    row = row + section * (plan.half * 16)
    extra = row - plan.vec_unit * 16
    valid = (row < filled) | ((extra >= 0) & (extra < vectors))
    return jnp.sum(jnp.where(valid, value * value, 0.0))


def gather_decoder(plan, half_d, section, me, after):
    dp, quarter = plan.dp, plan.quarter
    first = plan.bins(1)[1][0]
    assert 2 * first == dp
    used = max(plan.tail_used())
    spread = jnp.pad(half_d, ((0, 2 * quarter - plan.half), (0, 0), (0, 0)))
    spread = total_of(
        [
            lax.ppermute(
                spread[i * quarter : (i + 1) * quarter],
                "dp",
                [(b, 2 * b + i) for b in range(first)],
            )
            for i in range(2)
        ]
    )
    rest = jnp.where(me == first, half_d[:used], jnp.zeros((), BF16))
    holders = [first]
    for bit in reversed(range(dp.bit_length() - 1)):
        rest = rest + lax.ppermute(rest, "dp", [(i, i ^ 1 << bit) for i in holders])
        holders = holders + [i ^ 1 << bit for i in holders]
    other = lax.ppermute(rest, "section", [(0, 1), (1, 0)])
    rest = jnp.where(section == 0, jnp.stack([rest, other]), jnp.stack([other, rest]))
    spread, _ = tie(spread, after[0, 0, 0])
    gathered = lax.all_gather(spread, ("section", "dp"), axis=0, tiled=True)
    return gathered.reshape(2, dp, quarter, 16, 128), rest


def sincos(width):
    places = np.arange(NP).astype(np.float32)[:, None]
    column = np.arange(width)
    rates = np.exp(
        -(np.float32(2.0) * (column // 2).astype(np.float32) / np.float32(width))
        * np.float32(math.log(10000.0))
    ).astype(np.float32)
    phases = (places * rates[None, :]).astype(np.float32)
    table = np.where(
        column[None, :] % 2 == 0, np.sin(phases.astype(np.float64)), np.cos(phases.astype(np.float64))
    ).astype(np.float32)
    parts = []
    left = np.zeros((ROWS_D, width), np.float32)
    left[:NP] = table
    for _ in range(3):
        high = left.astype(jnp.bfloat16)
        parts.append(high)
        left = left - high.astype(np.float32)
    return np.stack(parts)


def on_device(patches, keep, perm, master, first, second, ema):
    dp = lax.axis_size("dp")
    section = lax.axis_index("section")
    me = lax.axis_index("dp")
    shard = master.shape[1]
    plan = Plan(dp, shard // 128)
    rows, half = plan.shard_rows, plan.half
    swap = [(0, 1), (1, 0)]
    states = [v.reshape(rows, 1, 128) for v in (master, first, second, ema)]

    following = lax.ppermute(
        states[0][: plan.head_rows], "dp", [(i, i - 1) for i in range(1, dp)]
    )
    index = jnp.asarray(plan.pack_index)[section, me]
    packed = pack(plan, index, states[0], following)
    mine = lax.dynamic_slice_in_dim(packed, section * half, half, 0)
    given = lax.ppermute(
        lax.dynamic_slice_in_dim(packed, (1 - section) * half, half, 0), "section", swap
    )
    half_e = jnp.where(section == 0, mine, given)
    half_d = jnp.where(section == 0, given, mine)
    gathered_e = lax.all_gather(half_e, ("section", "dp"), axis=0, tiled=True)
    gathered_e = gathered_e.reshape(2, dp, half, 16, 128)
    gathered_d = gather_decoder(plan, half_d, section, me, gathered_e)

    count = sum_everywhere(dp, jnp.sum(NP - keep).astype(F32)) * 0.5
    images = patches.shape[0] // 2
    mine = section * images
    patches = lax.dynamic_slice_in_dim(patches, mine, images, 0)
    patches = jnp.pad(patches, ((0, 0), (0, ROWS_D - NP), (0, 0)))
    order = lax.dynamic_slice_in_dim(perm, mine, images, 0)
    order = jnp.pad(order, ((0, 0), (0, ROWS_D - NP)), constant_values=ROWS_D - 1)
    order = order.reshape(images * ROWS_D, 1)
    kept = lax.dynamic_slice_in_dim(keep, mine, images, 0)
    info = jnp.concatenate([section[None].astype(jnp.int32), kept])
    scale = ((1.0 / count) * (1.0 / PIX) * 2.0).reshape(1)

    shape_e = Shape(images, ROWS_E, D, HEADS_E, FF_E)
    shape_d = Shape(images, ROWS_D, DD, HEADS_D, FF_D)
    pp, *saved, latent = encoder(
        plan, shape_e, info, gathered_e, patches, order, jnp.asarray(sincos(D))
    )
    arrays = dict(zip(("x0", "n1", "mixed", "o", "x1", "n2", "g", "gp", "y"), saved))
    arrays["xe"] = pp
    *sums_d, arrays["dz"], loss = decoder(
        plan, shape_d, info, scale, gathered_d, latent, pp, order, jnp.asarray(sincos(DD))
    )

    stages = encoder_back_stages(plan, shape_e)
    first_tail = plan.bins(1)[1][0]
    main = Flow(dp, sums_d[0], sums_d[1], 0)
    rest = Flow(dp, sums_d[2], sums_d[3], first_tail, (1,))
    flows, got, _ = move_on([main, rest])
    got, arrays = tie(got, arrays)
    arrive(flows, got)
    low = high = None
    blocks = []
    late = []
    for number, stage in enumerate(stages):
        few = None if number in (0, 3) else rest
        flows, got, (arrays, blocks) = move_on([main, few, high], arrays, blocks)
        if stage.bins:
            blocks, made = stage(info, gathered_e, arrays, blocks)
        else:
            _, made = stage(info, gathered_e, arrays, [])
        arrays = {**arrays, **made}
        long = [f is main and f.last() for f in flows]
        kept = [g for g, is_long in zip(got, long) if not is_long]
        kept, late, arrays, blocks = tie(kept, late, arrays, blocks)
        late = [g for g, is_long in zip(got, long) if is_long]
        kept = iter(kept)
        arrive(flows, [g if is_long else next(kept) for g, is_long in zip(got, long)])
        if number == 1:
            high = Flow(dp, blocks[2], blocks[3], dp // 2, (5, 5, 2))
            blocks = blocks[:2]
    low = Flow(dp, blocks[0], blocks[1], 0)
    every = [main, rest, high, low]
    before = ()
    for turn in range(1 + max(f.all_bits - f.step for f in every)):
        flows, got, _ = move_on(every, before if turn == 1 else ())
        before = got
        arrive(flows, got)
    assert all(f.done() for f in every)

    sum_tail = rest.result()
    sum_tail = jnp.pad(sum_tail, ((0, half - sum_tail.shape[0]), (0, 0), (0, 0)))
    sum_d = jnp.where(me < first_tail, main.result(), sum_tail)
    sum_e = jnp.where(me < dp // 2, low.result(), high.result())
    squares = [
        squares_of(plan, s, v, section, me) for s, v in enumerate((sum_e, sum_d))
    ]
    half_mine = jnp.where(section == 0, sum_e, sum_d)
    half_other = lax.ppermute(jnp.where(section == 0, sum_d, sum_e), "section", swap)
    sums = sum_in_chip(jnp.stack([squares[0] + squares[1], loss[0, 0]]))
    sums, half_other = tie(sums, half_other)
    sums = sum_over_dp(dp, sums, 0)
    block = jnp.where(
        section == 0,
        jnp.concatenate([half_mine, half_other], axis=0),
        jnp.concatenate([half_other, half_mine], axis=0),
    )
    start = jnp.asarray(plan.tail_start)[section, me]
    tail = jnp.concatenate(
        [
            lax.dynamic_slice_in_dim(block, start, plan.tail_units, 0),
            block[plan.vec_unit :],
        ],
        axis=0,
    )
    sums, tail = tie(sums, tail)
    tail = lax.ppermute(tail, "dp", [(i, i + 1) for i in range(dp - 1)])
    for low in range(2, dp.bit_length() - 1, 2):
        sums = sum_over_dp(dp, sums, low)
    index = jnp.asarray(plan.unpack_index)[section, me]
    total = unpack(plan, index, block, tail)
    norm = jnp.sqrt(sums[0])
    factor = jnp.minimum(1.0, clip_limit / (norm + norm_epsilon))
    made = update(plan, factor.reshape(1), total, states)
    return (*[v.reshape(1, shard) for v in made], norm, sums[1], count)


def solution(mesh):
    return jax.shard_map(
        on_device,
        mesh=mesh,
        in_specs=(
            P("dp", None, None),
            P("dp"),
            P("dp", None),
            P("section", "dp"),
            P("section", "dp"),
            P("section", "dp"),
            P("section", "dp"),
        ),
        out_specs=(
            P("section", "dp"),
            P("section", "dp"),
            P("section", "dp"),
            P("section", "dp"),
            P(),
            P(),
            P(),
        ),
        check_vma=False,
    )
```
